32 devices in a mesh: rep: 2 (over x), shard: 16 (over z, y, core).
Axes of the slice: x: 2, y: 2, z: 4, core: 2. Of those that a mesh axis runs over, the one named last changes fastest.
Arguments:
- hidden_in: bfloat16 [2, 4096, 2048], P(None, ('rep', 'shard')), may hold values from -6 to 6
- segment_ids: int32 [2, 4096], P(None, ('rep', 'shard')), may hold values from 0 to 1, as said below
- out_grad: bfloat16 [2, 4096, 2048], P(None, ('rep', 'shard')), may hold values from -6 to 6
- norm_gain: bfloat16 [2048], P('shard'), may hold values from 0.5 to 1.5
- in_proj: bfloat16 [2048, 8192], P('shard'), may hold values from -0.125 to 0.125
- conv_weight: bfloat16 [4, 4096], P(None, 'shard'), may hold values from -2.5 to 2.5
- conv_bias: bfloat16 [4096], P('shard'), may hold values from -2.5 to 2.5
- x_proj: bfloat16 [4096, 160], P('shard'), may hold values from -0.09375 to 0.09375
- dt_weight: bfloat16 [128, 4096], P(None, 'shard'), may hold values from -0.5 to 0.5
- dt_bias: bfloat16 [4096], P('shard'), may hold values from -5 to -2
- a_log: bfloat16 [16, 4096], P(None, 'shard'), may hold values from -9 to 2.77
- d_skip: bfloat16 [4096], P('shard'), may hold values from -3 to 3
- out_proj: bfloat16 [4096, 2048], P('shard'), may hold values from -0.09375 to 0.09375
Outputs:
- layer_out: bfloat16 [2, 4096, 2048], P(None, ('rep', 'shard'))
- in_grad: float32 [2, 4096, 2048], P(None, ('rep', 'shard'))
- grad_gain: float32 [2048], P('shard')
- grad_in_proj: float32 [2048, 8192], P('shard')
- grad_conv_weight: float32 [4, 4096], P(None, 'shard')
- grad_conv_bias: float32 [4096], P('shard')
- grad_x_proj: float32 [4096, 160], P('shard')
- grad_dt_weight: float32 [128, 4096], P(None, 'shard')
- grad_dt_bias: float32 [4096], P('shard')
- grad_a_log: float32 [16, 4096], P(None, 'shard')
- grad_d_skip: float32 [4096], P('shard')
- grad_out_proj: float32 [4096, 2048], P('shard')
The draws below stay inside these ranges and needn't reach their ends.
Inputs may be any that keep to these rules, and one draw needn't show every extreme that they name: `segment_ids`: ids never fall along a row, start at 0 and rise by exactly one at each document start. In one row drawn from the seed the whole row is a single document of 4096 tokens; every other row holds exactly max(2, 2) documents.
All inputs are finite; a program needn't handle non-finite values.
Results may differ from the reference program's by a relative error of at most 0.0084.
Values may be sent and summed in bfloat16 or wider, within the bound.
A program may use at most 768 MiB of HBM per device.

```python
from functools import partial
import jax
import jax.numpy as jnp
from jax import lax

D = 2048
INNER = 4096
NSTATE = 16
RANK = 128
KCONV = 4
MICRO = 2
DOC_TOKENS = 2048
TOKENS_MB = 4096


def draw_segment_ids(key, part):
    key = jax.random.fold_in(key, 11)
    row_pick = jax.random.randint(jax.random.fold_in(key, 1), (), 0, MICRO)
    doc_count = max(2, TOKENS_MB // DOC_TOKENS)
    id_rows = []
    for row_idx in range(MICRO):
        shuffled = jax.random.permutation(jax.random.fold_in(key, 100 + row_idx), TOKENS_MB - 1)
        start_flags = jnp.zeros((TOKENS_MB,), jnp.int32).at[shuffled[:doc_count - 1] + 1].set(1)
        start_flags = jnp.where(row_pick == row_idx, 0, start_flags)
        id_rows.append(jnp.cumsum(start_flags))
    return jnp.stack(id_rows).astype(jnp.int32)


def draw_a_log(key, part):
    key = jax.random.fold_in(key, 23)
    spread = jax.random.uniform(key, (NSTATE, INNER), jnp.float32, -9.0, 2.77)
    return spread.astype(jnp.bfloat16)


def draw_d_skip(key, part):
    key = jax.random.fold_in(key, 31)
    coin = jax.random.uniform(jax.random.fold_in(key, 1), (INNER,), jnp.float32)
    signs = jnp.where(coin < 0.5, -1.0, 1.0).astype(jnp.float32)
    magnitude = jax.random.uniform(jax.random.fold_in(key, 2), (INNER,), jnp.float32, 0.5, 1.5)
    return (signs * magnitude).astype(jnp.bfloat16)


def steps_of(own_key, dims, shards, least, top_value):
    level = 1.0
    for position, blocks in shards:
        steps = jax.random.uniform(jax.random.fold_in(jax.random.fold_in(own_key, 6), position), (blocks,), jnp.float32, least / len(shards), top_value / len(shards))
        level = level * jnp.repeat(jnp.exp(steps), dims[position] // blocks).reshape((-1,) + (1,) * (len(dims) - 1 - position))
    return level


def normal_values(rng, extent, deviation, bound, cuts=(), kind=jnp.bfloat16):
    values = deviation * jax.random.normal(rng, extent, jnp.float32)
    if cuts:
        values = values * steps_of(rng, extent, cuts, -0.22, 0.18)
    return jnp.clip(values, -bound, bound).astype(kind)


def setup_inputs(seed: int = 0) -> dict:
    streams_of = jax.random.split(jax.random.key(seed), 14)
    hidden_in = normal_values(streams_of[0], (MICRO, TOKENS_MB, D), 1.0, 6.0, ((1, 32),))
    segment_ids = draw_segment_ids(jax.random.fold_in(streams_of[13], 71), 0)
    out_grad = normal_values(streams_of[2], (MICRO, TOKENS_MB, D), 1.0, 6.0, ((1, 32),))
    norm_gain = jnp.clip(1.0 + 0.1 * jax.random.normal(streams_of[3], (D,), jnp.float32), 0.5, 1.5).astype(jnp.bfloat16)
    in_proj = normal_values(streams_of[4], (D, 2 * INNER), D ** -0.5, 0.125, ((0, 16),))
    conv_weight = normal_values(streams_of[5], (KCONV, INNER), 0.5, 2.5, ((1, 16),))
    conv_bias = normal_values(streams_of[6], (INNER,), 0.5, 2.5, ((0, 16),))
    x_proj = normal_values(streams_of[7], (INNER, RANK + 2 * NSTATE), INNER ** -0.5, 0.09375, ((0, 16),))
    dt_weight = normal_values(streams_of[8], (RANK, INNER), RANK ** -0.5, 0.5, ((1, 16),))
    dt_bias = jnp.clip(-5.0 + 3.0 * jax.random.uniform(streams_of[9], (INNER,), jnp.float32) ** steps_of(streams_of[9], (INNER,), ((0, 16),), -0.2, 0.2), -5.0, -2.0).astype(jnp.bfloat16)
    a_log = draw_a_log(jax.random.fold_in(streams_of[13], 71), 0)
    d_skip = draw_d_skip(jax.random.fold_in(streams_of[13], 71), 0)
    out_proj = normal_values(streams_of[12], (INNER, D), INNER ** -0.5, 0.09375, ((0, 16),))
    return dict(hidden_in=hidden_in, segment_ids=segment_ids, out_grad=out_grad, norm_gain=norm_gain, in_proj=in_proj, conv_weight=conv_weight, conv_bias=conv_bias, x_proj=x_proj, dt_weight=dt_weight, dt_bias=dt_bias, a_log=a_log, d_skip=d_skip, out_proj=out_proj)


@jax.custom_vjp
def low(v):
    return lax.optimization_barrier(v.astype(jnp.bfloat16)).astype(jnp.float32)

@jax.custom_vjp
def low_back(v):
    return v

def low_keep(v):
    return (low(v), None)

def low_pass(kept, grad):
    return (grad,)

def back_keep(v):
    return (v, None)

def back_low(kept, grad):
    return (low(grad),)
low.defvjp(low_keep, low_pass)
low_back.defvjp(back_keep, back_low)

def matmul(left_op, right_op):
    return jnp.dot(left_op, right_op, precision=lax.Precision.HIGHEST, preferred_element_type=jnp.float32)

def scan_block(a_mat, running, block_in):

    def advance(carried, pieces):
        step_t, x_t, b_t, c_t, keep_t = pieces
        updated = jnp.exp(step_t[None, :] * a_mat) * keep_t * carried + b_t[:, None] * (step_t * x_t)[None, :]
        return (updated, lax.optimization_barrier(jnp.sum(c_t[:, None] * updated, axis=0)))
    return lax.scan(advance, running, block_in)

def selective(a_mat, step_size, x_conv, b_mat, c_mat, keep_mask):
    length = step_size.shape[0]
    blocks = length // 64
    shaped = tuple((v.reshape((blocks, 64) + v.shape[1:]) for v in (step_size, x_conv, b_mat, c_mat, keep_mask)))
    block_fn = jax.checkpoint(partial(scan_block, a_mat))
    initial = jnp.zeros(a_mat.shape, step_size.dtype)
    last_state, y_blocks = lax.scan(block_fn, initial, shaped)
    return y_blocks.reshape(length, -1)

def layer(inputs, norm_gain, in_proj, conv_weight, conv_bias, x_proj, dt_weight, dt_bias, a_log, d_skip, out_proj, doc_ids):
    length = inputs.shape[0]
    inner_dim = x_proj.shape[0]
    rank_dim = dt_weight.shape[0]
    state_dim = a_log.shape[0]
    kernel = conv_weight.shape[0]
    scale_row = lax.rsqrt(lax.optimization_barrier(jnp.mean(inputs * inputs, axis=1, keepdims=True)) + 1e-05)
    normed = low(inputs * scale_row * norm_gain[None, :])
    projected = low_back(low(matmul(normed, in_proj)))
    x_part = projected[:, :inner_dim]
    z_part = projected[:, inner_dim:]
    convolved = conv_bias[None, :] + conv_weight[kernel - 1][None, :] * x_part
    for offset in range(1, kernel):
        earlier = jnp.concatenate([jnp.zeros((offset, inner_dim), x_part.dtype), x_part[:length - offset]], axis=0)
        prior_ids = jnp.concatenate([jnp.full((offset,), -1, jnp.int32), doc_ids[:length - offset]]).astype(jnp.int32)
        same_doc = (doc_ids == prior_ids).astype(x_part.dtype)
        convolved = convolved + conv_weight[kernel - 1 - offset][None, :] * earlier * same_doc[:, None]
    x_conv = low(jax.nn.silu(convolved))
    dbc_out = low_back(matmul(x_conv, x_proj))
    step_low = low(dbc_out[:, :rank_dim])
    b_mat = dbc_out[:, rank_dim:rank_dim + state_dim]
    c_mat = dbc_out[:, rank_dim + state_dim:]
    step_size = jax.nn.softplus(low_back(matmul(step_low, dt_weight)) + dt_bias[None, :])
    a_mat = -jnp.exp(a_log)
    prior_one = jnp.concatenate([jnp.full((1,), -1, jnp.int32), doc_ids[:length - 1]]).astype(jnp.int32)
    keep_mask = (doc_ids == prior_one).astype(step_size.dtype)
    y_scan = selective(a_mat, step_size, x_conv, b_mat, c_mat, keep_mask)
    y_full = y_scan + d_skip[None, :] * x_conv
    gated_out = low(y_full * jax.nn.silu(z_part))
    return inputs + matmul(gated_out, out_proj)

def reference(hidden_in, segment_ids, out_grad, norm_gain, in_proj, conv_weight, conv_bias, x_proj, dt_weight, dt_bias, a_log, d_skip, out_proj):
    weights = tuple((w.astype(jnp.float32) for w in (norm_gain, in_proj, conv_weight, conv_bias, x_proj, dt_weight, dt_bias, a_log, d_skip, out_proj)))
    outputs = []
    input_grads = []
    totals = tuple((jnp.zeros(w.shape, jnp.float32) for w in weights))
    for row_idx in range(MICRO):
        row_ids = segment_ids[row_idx]

        def forward(inputs, *weight_args):
            return layer(inputs, *weight_args, row_ids)
        result, pullback = jax.vjp(forward, hidden_in[row_idx].astype(jnp.float32), *weights)
        gradients = pullback(out_grad[row_idx].astype(jnp.float32))
        outputs.append(result.astype(jnp.bfloat16))
        input_grads.append(gradients[0])
        totals = tuple((a + b for a, b in zip(totals, gradients[1:])))
    return (jnp.stack(outputs), jnp.stack(input_grads), totals[0], totals[1], totals[2], totals[3], totals[4], totals[5], totals[6], totals[7], totals[8], totals[9])
```

```python
import functools
import jax, jax.numpy as jnp
from jax import lax
from jax.sharding import PartitionSpec as P
from jax.experimental import pallas as pl
from jax.experimental.pallas import tpu as pltpu

TB = 128
UN = 32
FG = 128

def wide(v, e):
    return jnp.concatenate([v] * (e // 128), axis=1) if e > 128 else v

def split3(v):
    def parts(v):
        hi = lax.reduce_precision(v, 8, 7)
        mid = lax.reduce_precision(v - hi, 8, 7)
        lo = lax.reduce_precision(v - hi - mid, 8, 7)
        return [hi, mid, lo]
    n = v.shape[1] // 2
    return jnp.concatenate(parts(v[:, :n]) + parts(v[:, n:]) + [jnp.zeros((v.shape[0], 128 - 6 * n), jnp.float32)], axis=1)

def fill(bcs_ref, bc_scr, n):
    lane = lax.broadcasted_iota(jnp.int32, (n, 128), 1)
    sub = lax.broadcasted_iota(jnp.int32, (n, 128), 0)
    mask = (lane % n) == sub
    r = lax.broadcasted_iota(jnp.int32, (128, 256), 0)
    c = lax.broadcasted_iota(jnp.int32, (128, 256), 1)
    ones = jnp.where((r >= 3 * n) == (c >= 128), 1.0, 0.0).astype(jnp.bfloat16)
    def body(g, _):
        rows = [jnp.where(mask, bcs_ref[pl.ds(g * FG + j, 1), :], 0.0).astype(jnp.bfloat16) for j in range(FG)]
        bc_scr[pl.ds(pl.multiple_of(g * (FG * n), FG * n), FG * n), :] = jnp.dot(jnp.concatenate(rows, axis=0), ones, preferred_element_type=jnp.float32)
        return 0
    lax.fori_loop(0, TB // FG, body, 0)

def fold_rows(vals, sub):
    for k in (1, 2, 4):
        m = (sub & k) == 0
        vals = [jnp.where(m, a, b) + pltpu.roll(jnp.where(m, b, a), 8 - k, 0) for a, b in zip(vals[::2], vals[1::2])]
    return vals[0]

def pass1(sd_ref, dx_ref, dy_ref, bcs_ref, a2_ref, cks_ref, ckp_ref, f_ref, s_scr, p_scr, f_scr, bc_scr, *, n):
    b = pl.program_id(0)
    e = a2_ref.shape[1]
    @pl.when(b == 0)
    def _():
        s_scr[...] = jnp.zeros_like(s_scr)
        p_scr[...] = jnp.ones_like(p_scr)
        f_scr[...] = jnp.zeros_like(f_scr)
    cks_ref[0] = s_scr[...]
    ckp_ref[0] = p_scr[...]
    fill(bcs_ref, bc_scr, n)
    a2 = a2_ref[...]
    def group(g, carry):
        s, p, f = carry
        for j in range(UN):
            t = g * UN + j
            bc = bc_scr[pl.ds(pl.multiple_of(t * n, n), n), :]
            bb, cc = wide(bc[:, :128], e), wide(bc[:, 128:], e)
            a = jnp.exp2(sd_ref[pl.ds(t, 1), :] * a2)
            s = a * s + bb * dx_ref[pl.ds(t, 1), :]
            p = p * a
            f = f + p * (cc * dy_ref[pl.ds(t, 1), :])
        return s, p, f
    s, p, f = lax.fori_loop(0, TB // UN, group, (s_scr[...], p_scr[...], f_scr[...]))
    s_scr[...] = s
    p_scr[...] = p
    f_scr[...] = f
    @pl.when(b == pl.num_programs(0) - 1)
    def _():
        f_ref[0] = s
        f_ref[1] = p
        f_ref[2] = f

def run_pass1(sd, dx, dy, bcs, a2):
    t, e = sd.shape
    n = a2.shape[0]
    nb = t // TB
    row = pl.BlockSpec((TB, e), lambda i: (i, 0))
    return pl.pallas_call(
        functools.partial(pass1, n=n),
        grid=(nb,),
        in_specs=[row, row, row, pl.BlockSpec((TB, 128), lambda i: (i, 0)), pl.BlockSpec((n, e), lambda i: (0, 0))],
        out_specs=[pl.BlockSpec((1, n, e), lambda i: (i, 0, 0)), pl.BlockSpec((1, n, e), lambda i: (i, 0, 0)), pl.BlockSpec((3, n, e), lambda i: (0, 0, 0))],
        out_shape=[jax.ShapeDtypeStruct((nb, n, e), jnp.float32)] * 2 + [jax.ShapeDtypeStruct((3, n, e), jnp.float32)],
        scratch_shapes=[pltpu.VMEM((n, e), jnp.float32)] * 3 + [pltpu.VMEM((TB * n, 256), jnp.float32)],
        compiler_params=pltpu.CompilerParams(vmem_limit_bytes=48 << 20),
    )(sd, dx, dy, bcs, a2)

def pass2(sd_ref, dx_ref, dy_ref, st_ref, bcs_ref, a2_ref, cks_ref, ckp_ref, hin_ref, qin_ref,
          y_ref, da_ref, gb_ref, dbc_ref, ga_ref,
          h_scr, a_scr, q_scr, bc_scr, *, n):
    b = pl.program_id(0)
    e = a2_ref.shape[1]
    @pl.when(b == 0)
    def _():
        q_scr[...] = qin_ref[...]
        ga_ref[...] = jnp.zeros_like(ga_ref)
    fill(bcs_ref, bc_scr, n)
    a2 = a2_ref[...]
    sub = lax.broadcasted_iota(jnp.int32, (8, e), 0)
    h0 = cks_ref[0] + ckp_ref[0] * hin_ref[...]
    h_scr[pl.ds(0, n), :] = h0
    def fwd(g, h):
        ys = []
        for j in range(UN):
            t = g * UN + j
            bc = bc_scr[pl.ds(pl.multiple_of(t * n, n), n), :]
            bb, cc = wide(bc[:, :128], e), wide(bc[:, 128:], e)
            a = jnp.exp2(sd_ref[pl.ds(t, 1), :] * a2)
            h = a * h + bb * dx_ref[pl.ds(t, 1), :]
            a_scr[pl.ds(pl.multiple_of(t * n, n), n), :] = a
            h_scr[pl.ds(pl.multiple_of(t * n + n, n), n), :] = h
            cy = cc * h
            ys.append(cy[:8] + cy[8:])
            if len(ys) == 8:
                y_ref[pl.ds(pl.multiple_of(t - 7, 8), 8), :] = fold_rows(ys, sub)
                ys = []
        return h
    lax.fori_loop(0, TB // UN, fwd, h0)
    lanes = lax.broadcasted_iota(jnp.int32, (n, TB), 1)
    def bwd(g, carry):
        q, ga, hn, db, dc = carry
        das, gbs = [], []
        for j in range(UN):
            t = TB - 1 - (g * UN + j)
            bc = bc_scr[pl.ds(pl.multiple_of(t * n, n), n), :]
            bb, cc = wide(bc[:, :128], e), wide(bc[:, 128:], e)
            a = a_scr[pl.ds(pl.multiple_of(t * n, n), n), :]
            hp = h_scr[pl.ds(pl.multiple_of(t * n, n), n), :]
            dyr = dy_ref[pl.ds(t, 1), :]
            gt = cc * dyr + q
            q = a * gt
            da = q * hp
            ga = ga + da * st_ref[pl.ds(t, 1), :]
            dA = da * a2
            gB = gt * bb
            das.append(dA[:8] + dA[8:])
            gbs.append(gB[:8] + gB[8:])
            pb = gt * dx_ref[pl.ds(t, 1), :]
            pc = dyr * hn
            pb = sum(pb[:, k:k + 128] for k in range(0, e, 128))
            pc = sum(pc[:, k:k + 128] for k in range(0, e, 128))
            db = jnp.where(lanes == t, jnp.sum(pb, axis=1, keepdims=True), db)
            dc = jnp.where(lanes == t, jnp.sum(pc, axis=1, keepdims=True), dc)
            hn = hp
            if len(das) == 8:
                da_ref[pl.ds(pl.multiple_of(t, 8), 8), :] = fold_rows(das[::-1], sub)
                gb_ref[pl.ds(pl.multiple_of(t, 8), 8), :] = fold_rows(gbs[::-1], sub)
                das, gbs = [], []
        return q, ga, hn, db, dc
    z = jnp.zeros((n, TB), jnp.float32)
    q, ga, _, db, dc = lax.fori_loop(0, TB // UN, bwd, (q_scr[...], ga_ref[...], h_scr[pl.ds(TB * n, n), :], z, z))
    q_scr[...] = q
    ga_ref[...] = ga
    dbc_ref[pl.ds(0, n), :] = db
    dbc_ref[pl.ds(n, n), :] = dc

def run_pass2(sd, dx, dy, st, bcs, a2, cks, ckp, hin, qin):
    t, e = sd.shape
    n = a2.shape[0]
    nb = t // TB
    row = pl.BlockSpec((TB, e), lambda i: (nb - 1 - i, 0))
    full = pl.BlockSpec((n, e), lambda i: (0, 0))
    ck = pl.BlockSpec((1, n, e), lambda i: (nb - 1 - i, 0, 0))
    dbcs = pl.BlockSpec((2 * n, TB), lambda i: (0, nb - 1 - i))
    bci = pl.BlockSpec((TB, 128), lambda i: (nb - 1 - i, 0))
    return pl.pallas_call(
        functools.partial(pass2, n=n),
        grid=(nb,),
        in_specs=[row] * 4 + [bci, full, ck, ck, full, full],
        out_specs=[row] * 3 + [dbcs, full],
        out_shape=[jax.ShapeDtypeStruct((t, e), jnp.float32)] * 3 + [jax.ShapeDtypeStruct((2 * n, t), jnp.float32), jax.ShapeDtypeStruct((n, e), jnp.float32)],
        scratch_shapes=[pltpu.VMEM((TB * n + n, e), jnp.float32), pltpu.VMEM((TB * n, e), jnp.float32),
                        pltpu.VMEM((n, e), jnp.float32), pltpu.VMEM((TB * n, 256), jnp.float32)],
        compiler_params=pltpu.CompilerParams(vmem_limit_bytes=48 << 20),
    )(sd, dx, dy, st, bcs, a2, cks, ckp, hin, qin)


def shift_rep(value, steps):
    count = lax.axis_size("rep")
    first, last = max(0, -steps), min(count, count - steps)
    return lax.ppermute(value, "rep", [(i, i + steps) for i in range(first, last)])

def sum_rep(value):
    if lax.axis_size("rep") != 2:
        return lax.psum(value, "rep")
    low = value.astype(jnp.bfloat16)
    other = lax.ppermute(low, "rep", [(0, 1), (1, 0)])
    return low.astype(jnp.float32) + other.astype(jnp.float32)

def nt(a, b):
    return lax.dot_general(a, b, (((1,), (1,)), ((), ())), preferred_element_type=jnp.float32)

def tn(a, b):
    return lax.dot_general(a, b, (((0,), (0,)), ((), ())), preferred_element_type=jnp.float32)

def mm(a, b):
    return jnp.dot(a, b, preferred_element_type=jnp.float32)

def dsilu(v):
    s = jax.nn.sigmoid(v)
    return s * (1.0 + v * (1.0 - s))

def on_device(hidden_in, segment_ids, out_grad, norm_gain, in_proj, conv_weight, conv_bias, x_proj,
              dt_weight, dt_bias, a_log, d_skip, out_proj):
    f32, bf16 = jnp.float32, jnp.bfloat16
    peers, reps = lax.axis_size("shard"), lax.axis_size("rep")
    rep = lax.axis_index("rep")
    m, tl, d = hidden_in.shape
    t = tl * peers
    dl = in_proj.shape[0]
    e = x_proj.shape[0]
    n = a_log.shape[0]
    rank = dt_weight.shape[0]
    taps = conv_weight.shape[0]
    back = taps - 1
    wide32 = lambda v: v.astype(f32)

    u = wide32(hidden_in)
    r = lax.rsqrt(jnp.mean(u * u, axis=2, keepdims=True) + 1e-5)
    nu = (u * r).astype(bf16)
    nu_all = lax.all_gather(nu, "shard", axis=1, tiled=True).reshape(m * t, d)
    dy_all = lax.all_gather(out_grad, "shard", axis=1, tiled=True).reshape(m * t, d)
    ids = lax.all_gather(segment_ids, "shard", axis=1, tiled=True)
    gain = wide32(norm_gain)[:, None]
    w_own = (wide32(in_proj) * gain).astype(bf16)
    w_split = w_own.reshape(dl, 2, peers, e).transpose(2, 0, 1, 3).reshape(peers * dl, 2 * e)
    w_cols = lax.all_to_all(w_split, "shard", 0, 0, tiled=True)

    ids_before = jnp.where(rep > 0, shift_rep(ids[:, t - back:], 1), -1)
    ext_ids = jnp.concatenate([ids_before, ids], axis=1)
    same = [None] + [wide32(ext_ids[:, back - k:back - k + t] == ids)[:, :, None] for k in range(1, taps)]

    xz = mm(nu_all, w_cols).astype(bf16).reshape(m, t, 2 * e)
    x_low = xz[:, :, :e]
    z = wide32(xz[:, :, e:])
    ext_x = jnp.concatenate([shift_rep(x_low[:, t - back:], 1), x_low], axis=1)
    x = wide32(x_low)
    cw = wide32(conv_weight)
    lagged = [x] + [wide32(ext_x[:, back - k:back - k + t]) * same[k] for k in range(1, taps)]
    conv = wide32(conv_bias) + sum(cw[back - k] * lagged[k] for k in range(taps))
    xc_low = jax.nn.silu(conv).astype(bf16)
    xc = wide32(xc_low)
    dbc = lax.psum(mm(xc_low.reshape(m * t, e), x_proj), "shard")
    dt_low = dbc[:, :rank].astype(bf16)
    bcs = split3(dbc[:, rank:]).reshape(m, t, 128)
    pre = (mm(dt_low, dt_weight) + wide32(dt_bias)).reshape(m, t, e)
    step = jax.nn.softplus(pre)
    a_mat = -jnp.exp(wide32(a_log))
    a2 = a_mat * 1.4426950408889634
    sd = jnp.where(same[1] > 0, step, 1e30)
    dx_in = step * xc

    d_gated = nt(dy_all, out_proj).reshape(m, t, e)
    sz = jax.nn.sigmoid(z)
    z_gate = z * sz
    dy_y = d_gated * z_gate

    firsts = [run_pass1(sd[i], dx_in[i], dy_y[i], bcs[i], a2) for i in range(m)]
    ends = lax.all_gather(jnp.stack([f[2] for f in firsts]), "rep")
    h_in = jnp.zeros((m, n, e), f32)
    q_in = jnp.zeros((m, n, e), f32)
    for k in range(reps - 1):
        h_in = jnp.where(k < rep, ends[k, :, 1] * h_in + ends[k, :, 0], h_in)
        o = reps - 1 - k
        q_in = jnp.where(o > rep, ends[o, :, 1] * q_in + ends[o, :, 2], q_in)
    seconds = [run_pass2(sd[i], dx_in[i], dy_y[i], step[i], bcs[i], a2, firsts[i][0], firsts[i][1], h_in[i], q_in[i])
               for i in range(m)]
    y_scan, d_a, gb = (jnp.stack([s[k] for s in seconds]) for k in range(3))
    d_bc = jnp.concatenate([s[3] for s in seconds], axis=1).T
    ga = sum(s[4] for s in seconds)

    skip = wide32(d_skip)
    y = y_scan + skip * xc
    gated = (y * z_gate).astype(bf16).reshape(m * t, e)
    part_out = mm(gated, out_proj).astype(bf16).reshape(m, t, d)
    out_sum = lax.psum_scatter(part_out, "shard", scatter_dimension=1, tiled=True)
    layer_out = (u + wide32(out_sum)).astype(bf16)
    grad_out_proj = tn(gated, dy_all)

    d_z = d_gated * y * (sz * (1.0 + z * (1.0 - sz)))
    d_step = d_a * 0.6931471805599453 + xc * gb
    d_pre = d_step * jax.nn.sigmoid(pre)
    d_pre_low = d_pre.astype(bf16).reshape(m * t, e)
    grad_dt_weight = tn(dt_low, d_pre_low)
    d_dbc = lax.psum(jnp.concatenate([nt(d_pre_low, dt_weight), d_bc], axis=1), "shard").astype(bf16)
    grad_x_proj = tn(xc_low.reshape(m * t, e), d_dbc)
    d_xc = dy_y * skip + step * gb + nt(d_dbc, x_proj).reshape(m, t, e)
    d_conv = d_xc * dsilu(conv)
    grad_conv = jnp.stack([jnp.sum(d_conv * lagged[back - j], axis=(0, 1)) for j in range(taps)])
    d_ext = jnp.pad(cw[back] * d_conv, ((0, 0), (back, 0), (0, 0)))
    for k in range(1, taps):
        d_ext = d_ext + jnp.pad(cw[back - k] * d_conv * same[k], ((0, 0), (back - k, k), (0, 0)))
    tail = shift_rep(d_ext[:, :back].astype(bf16), -1).astype(f32)
    d_x = d_ext[:, back:] + jnp.pad(tail, ((0, 0), (t - back, 0), (0, 0)))
    d_xz = jnp.concatenate([d_x, d_z], axis=2).astype(bf16).reshape(m * t, 2 * e)

    v_part = nt(d_xz, w_cols).astype(bf16).reshape(m, t, d)
    v = wide32(lax.psum_scatter(v_part, "shard", scatter_dimension=1, tiled=True))
    in_grad = wide32(out_grad) + r * v - u * (r * r * r) * jnp.mean(v * u, axis=2, keepdims=True)

    g_cols = sum_rep(tn(nu_all, d_xz)).astype(bf16)
    g_own = wide32(lax.all_to_all(g_cols, "shard", 0, 0, tiled=True))
    g_own = g_own.reshape(peers, dl, 2, e).transpose(1, 2, 0, 3).reshape(dl, 2 * e * peers)
    grad_in_proj = g_own * gain
    grad_gain = jnp.sum(g_own * wide32(in_proj), axis=1)

    grad_out_proj = sum_rep(grad_out_proj)
    small = jnp.concatenate([
        grad_conv, jnp.sum(d_conv, axis=(0, 1))[None], jnp.sum(d_pre, axis=(0, 1))[None],
        jnp.sum(dy_y * xc, axis=(0, 1))[None], ga * a_mat, grad_dt_weight, grad_x_proj.T], axis=0)
    small = sum_rep(small)
    cut, at = [], 0
    for size in (taps, 1, 1, 1, n, rank):
        cut.append(small[at:at + size])
        at += size
    return (layer_out, in_grad, grad_gain, grad_in_proj, cut[0], cut[1][0], small[at:].T, cut[5], cut[2][0],
            cut[4], cut[3][0], grad_out_proj)

def solution(mesh):
    tok, ids = P(None, ("rep", "shard"), None), P(None, ("rep", "shard"))
    row, col, one = P("shard", None), P(None, "shard"), P("shard")
    return jax.shard_map(
        on_device,
        mesh=mesh,
        in_specs=(tok, ids, tok, one, row, col, one, row, col, one, col, one, row),
        out_specs=(tok, tok, one, row, col, one, row, col, one, col, one, row),
        check_vma=False,
    )
```

```python
import functools
import jax
import jax.numpy as jnp
from jax import lax
from jax.sharding import PartitionSpec as P
from jax.experimental import pallas as pl
from jax.experimental.pallas import tpu as pltpu

F32, BF16 = jnp.float32, jnp.bfloat16
LOG2E, LN2 = 1.4426950408889634, 0.6931471805599453
EDGE = 8
VMEM = 56 << 20


def nt(a, b):
    return lax.dot_general(a, b, (((1,), (1,)), ((), ())), preferred_element_type=F32)


def tn(a, b):
    return lax.dot_general(a, b, (((0,), (0,)), ((), ())), preferred_element_type=F32)


def mm(a, b):
    return jnp.dot(a, b, preferred_element_type=F32)


def softplus(v):
    return jnp.maximum(v, 0.0) + jnp.log1p(jnp.exp(-jnp.abs(v)))


def wide(v, e):
    return jnp.concatenate([v] * (e // 128), axis=1) if e > 128 else v


def at(start, size, unit=8):
    return pl.ds(pl.multiple_of(start, unit), size)


def call(kernel, grid, in_specs, out_specs, out_shape, scratch, args, flops=0):
    size = sum(a.size * a.dtype.itemsize for a in args) + sum(s.size * s.dtype.itemsize for s in out_shape)
    return pl.pallas_call(
        kernel, grid=grid, in_specs=in_specs, out_specs=out_specs, out_shape=out_shape,
        scratch_shapes=scratch, compiler_params=pltpu.CompilerParams(vmem_limit_bytes=VMEM),
        cost_estimate=pl.CostEstimate(flops=flops, bytes_accessed=size, transcendentals=0))(*args)


def whole(a):
    return pl.BlockSpec(a.shape, lambda i, r=len(a.shape): (0,) * r)


def block(a, order):
    return pl.BlockSpec((1,) + a.shape[1:], lambda i, r=len(a.shape): (order(i),) + (0,) * (r - 1))


def lags(x_ext, rows):
    return [x_ext[EDGE - k:EDGE - k + rows] for k in range(4)]


def convolve(lag, same, cw, cb):
    out = cb + cw[3:4] * lag[0]
    for k in range(1, 4):
        out = out + cw[3 - k:4 - k] * lag[k] * same[:, k - 1:k]
    return out


def front(nu_ref, w_ref, halo_ref, mask_ref, cw_ref, cb_ref, xp_ref, xz_ref, xc_ref, part_ref, edge_ref, carry, *, m, e):
    @pl.when(pl.program_id(0) == 0)
    def _():
        edge = mm(halo_ref[...], w_ref[:, :e]).astype(BF16)
        edge_ref[...] = edge
        carry[...] = edge.astype(F32)
    xz = mm(nu_ref[0], w_ref[...]).astype(BF16)
    xz_ref[0] = xz
    rows = xz.shape[0] // m
    cw, cb = cw_ref[...], cb_ref[...]
    for i in range(m):
        x = xz[i * rows:(i + 1) * rows, :e].astype(F32)
        ext = jnp.concatenate([carry[i * EDGE:(i + 1) * EDGE], x], axis=0)
        carry[i * EDGE:(i + 1) * EDGE] = x[rows - EDGE:]
        conv = convolve(lags(ext, rows), mask_ref[0, i * rows:(i + 1) * rows], cw, cb)
        xc_ref[0, i * rows:(i + 1) * rows] = (conv * jax.nn.sigmoid(conv)).astype(BF16)
    part_ref[0] = nt(xp_ref[...], xc_ref[0])


def lattice(peers):
    y = 2 if peers <= 16 else 4
    return peers // (2 * y), y, 2


def greet(targets):
    barrier = pltpu.get_barrier_semaphore()
    for target in targets:
        pl.semaphore_signal(barrier, inc=1, device_id={"shard": target}, device_id_type=pl.DeviceIdType.MESH)
    pl.semaphore_wait(barrier, len(targets))


def remote(src, dst, send, recv, target):
    return pltpu.make_async_remote_copy(src_ref=src, dst_ref=dst, send_sem=send, recv_sem=recv,
                                        device_id={"shard": target}, device_id_type=pl.DeviceIdType.MESH)


def spread_low(total, n):
    rows = jnp.concatenate([total, jnp.zeros((256 - total.shape[0], total.shape[1]), F32)], axis=0).T
    rank = total.shape[0] - 2 * n
    out = [rows[:, :rank].astype(BF16)]
    rest = rows[:, rank:]
    hi = rest.astype(BF16)
    mid = (rest - hi.astype(F32)).astype(BF16)
    lo = (rest - hi.astype(F32) - mid.astype(F32)).astype(BF16)
    for k in range(2):
        out += [p[:, k * n:(k + 1) * n] for p in (hi, mid, lo)]
    out.append(jnp.zeros((rows.shape[0], 128 - 6 * n), BF16))
    return jnp.concatenate(out, axis=1)


def spread_plain(total, n):
    return jnp.concatenate([total, jnp.zeros((256 - total.shape[0], total.shape[1]), F32)], axis=0).T.astype(BF16)


def allsum_kernel(part, out, rc, ac, ry, ay, rz, send, recv, *, dims, chunks, finish):
    nz, ny, _ = dims
    me = lax.axis_index("shard")
    c, y, z = me % 2, (me // 2) % ny, me // (2 * ny)
    where = lambda a, b, d: (a * ny + b) * 2 + d
    across = where(z, y, 1 - c)
    ys = [lax.rem(y + k, ny) for k in range(1, ny)]
    zs = [lax.rem(z + k, nz) for k in range(1, nz)]
    greet([across] + [where(z, b, c) for b in ys] + [where(a, y, c) for a in zs])
    width = part.shape[-1] // chunks
    lanes = [pl.ds(q * width, width) for q in range(chunks)]
    rows = [pl.ds(q * width, width) for q in range(chunks)]

    def start(copies):
        for copy in copies:
            copy.start()
        return copies

    def finish_all(copies):
        for copy in copies:
            copy.wait()
    base = [0]

    def sems(count):
        base[0] += count
        return [(send.at[base[0] - count + k], recv.at[base[0] - count + k]) for k in range(count)]

    first = []
    for q in range(chunks):
        (s, r), = sems(1)
        first.append(start([remote(part.at[:, :, 1 - c, :, lanes[q]], rc.at[q], s, r, across)]))
    second = []
    for q in range(chunks):
        finish_all(first[q])
        for a in range(nz):
            for b in range(ny):
                ac[q, a, b] = part[a, b, c, :, q * width:(q + 1) * width] + rc[q, a, b]
        second.append(start([remote(ac.at[q, :, b], ry.at[q, k], *sem, where(z, b, c))
                             for k, (b, sem) in enumerate(zip(ys, sems(ny - 1)))]))
    third = []
    for q in range(chunks):
        finish_all(second[q])
        for a in range(nz):
            got = ac[q, a, y]
            for k in range(ny - 1):
                got = got + ry[q, k, a]
            ay[q, a] = got
        third.append(start([remote(ay.at[q, a], rz.at[q, k], *sem, where(a, y, c))
                            for k, (a, sem) in enumerate(zip(zs, sems(nz - 1)))]))
    fourth = []
    for q in range(chunks):
        finish_all(third[q])
        got = ay[q, z]
        for k in range(nz - 1):
            got = got + rz[q, k]
        out[z, y, c, q * width:(q + 1) * width] = finish(got)
        mine = out.at[z, y, c, rows[q]]
        fourth.append(start([remote(mine, mine, *sem, where(a, y, c)) for a, sem in zip(zs, sems(nz - 1))]))
    fifth = []
    for q in range(chunks):
        finish_all(fourth[q])
        mine = out.at[:, y, c, rows[q]]
        fifth.append(start([remote(mine, mine, *sem, where(z, b, c)) for b, sem in zip(ys, sems(ny - 1))]))
    last = []
    for q in range(chunks):
        finish_all(fifth[q])
        mine = out.at[:, :, c, rows[q]]
        (s, r), = sems(1)
        last.append(start([remote(mine, mine, s, r, across)]))
    for q in range(chunks):
        finish_all(last[q])


def allsum(part, finish, collective_id):
    peers, cols, w = part.shape
    dims = lattice(peers)
    nz, ny, nc = dims
    chunks = w // 128
    copies = 2 * chunks * (1 + ny - 1 + nz - 1)
    out = pl.pallas_call(
        functools.partial(allsum_kernel, dims=dims, chunks=chunks, finish=finish),
        out_shape=jax.ShapeDtypeStruct((nz, ny, nc, w, 256), BF16),
        in_specs=[pl.BlockSpec(memory_space=pltpu.VMEM)],
        out_specs=pl.BlockSpec(memory_space=pltpu.VMEM),
        scratch_shapes=[pltpu.VMEM((chunks, nz, ny, cols, 128), F32), pltpu.VMEM((chunks, nz, ny, cols, 128), F32),
                        pltpu.VMEM((chunks, ny - 1, nz, cols, 128), F32), pltpu.VMEM((chunks, nz, cols, 128), F32),
                        pltpu.VMEM((chunks, nz - 1, cols, 128), F32),
                        pltpu.SemaphoreType.DMA((copies,)), pltpu.SemaphoreType.DMA((copies,))],
        compiler_params=pltpu.CompilerParams(collective_id=collective_id, has_side_effects=True, vmem_limit_bytes=VMEM),
    )(part.reshape(nz, ny, nc, cols, w))
    return out.reshape(peers, w, 256)


def fill(low_ref, bcs_scr, bc_scr, n):
    bcs_scr[...] = low_ref[0, :, 128:].astype(F32)
    lane = lax.broadcasted_iota(jnp.int32, (n, 128), 1)
    sub = lax.broadcasted_iota(jnp.int32, (n, 128), 0)
    mask = (lane % n) == sub
    r = lax.broadcasted_iota(jnp.int32, (128, 256), 0)
    c = lax.broadcasted_iota(jnp.int32, (128, 256), 1)
    ones = jnp.where((r >= 3 * n) == (c >= 128), 1.0, 0.0).astype(BF16)
    group = 128

    def body(g, _):
        rows = [jnp.where(mask, bcs_scr[pl.ds(g * group + j, 1), :], 0.0).astype(BF16) for j in range(group)]
        bc_scr[at(g * (group * n), group * n, 128), :] = mm(jnp.concatenate(rows, axis=0), ones)
        return 0
    lax.fori_loop(0, bcs_scr.shape[0] // group, body, 0)


def fold_rows(vals, sub):
    for k in (1, 2, 4):
        mask = (sub & k) == 0
        vals = [jnp.where(mask, a, b) + pltpu.roll(jnp.where(mask, b, a), 8 - k, 0)
                for a, b in zip(vals[::2], vals[1::2])]
    return vals[0]


def ahead(low_ref, xz_ref, xc_ref, mask_ref, dy_ref, wo_ref, wdt_ref, dtb_ref, a2_ref,
          cks_ref, ckp_ref, end_ref, dg_ref, s_scr, p_scr, f_scr, sd_scr, dx_scr, dy_scr, bcs_scr, bc_scr, *, m, n, e):
    b = pl.program_id(0)
    @pl.when(b == 0)
    def _():
        s_scr[...] = jnp.zeros_like(s_scr)
        p_scr[...] = jnp.ones_like(p_scr)
        f_scr[...] = jnp.zeros_like(f_scr)
    cks_ref[0] = s_scr[...]
    ckp_ref[0] = p_scr[...]
    fill(low_ref, bcs_scr, bc_scr, n)
    step = softplus(mm(low_ref[0, :, :128], wdt_ref[...]) + dtb_ref[...])
    sd_scr[...] = jnp.where(mask_ref[0, :, 0:1] > 0.0, step, 1e30)
    dx_scr[...] = step * xc_ref[0].astype(F32)
    dg = nt(dy_ref[0], wo_ref[...])
    dg_ref[0] = dg
    z = xz_ref[0, :, e:].astype(F32)
    dy_scr[...] = dg * (z * jax.nn.sigmoid(z))
    a2 = a2_ref[...]
    rows = sd_scr.shape[0] // m
    un = 16

    def group(g, carry):
        s, p, f = [list(c) for c in carry]
        for j in range(un):
            for i in range(m):
                t = i * rows + g * un + j
                bc = bc_scr[at(t * n, n, n), :]
                bb, cc = wide(bc[:, :128], e), wide(bc[:, 128:], e)
                a = jnp.exp2(sd_scr[pl.ds(t, 1), :] * a2)
                s[i] = a * s[i] + bb * dx_scr[pl.ds(t, 1), :]
                p[i] = p[i] * a
                f[i] = f[i] + p[i] * (cc * dy_scr[pl.ds(t, 1), :])
        return tuple(s), tuple(p), tuple(f)
    done = lax.fori_loop(0, rows // un, group,
                         tuple(tuple(scr[i] for i in range(m)) for scr in (s_scr, p_scr, f_scr)))
    for scr, vals in zip((s_scr, p_scr, f_scr), done):
        for i in range(m):
            scr[i] = vals[i]

    @pl.when(b == pl.num_programs(0) - 1)
    def _():
        end_ref[0] = s_scr[...]
        end_ref[1] = p_scr[...]
        end_ref[2] = f_scr[...]


def behind(low_ref, xz_ref, xc_ref, mask_ref, dy_ref, dg_ref, nu_ref, cks_ref, ckp_ref,
           wo_ref, wdt_ref, dtb_ref, a2_ref, skip_ref, hin_ref, qin_ref,
           out_ref, dz_ref, dxc_ref, part_ref, go_ref, gdt_ref, ga_ref, vec_ref, gz_ref,
           h_scr, a_scr, q_scr, bcs_scr, bc_scr, pre_scr, st_scr, sd_scr, dx_scr, dy_scr, y_scr, da_scr, gb_scr, *, m, n, e):
    b = pl.program_id(0)
    @pl.when(b == 0)
    def _():
        q_scr[...] = qin_ref[...]
        for ref in (go_ref, gdt_ref, ga_ref, vec_ref, gz_ref):
            ref[...] = jnp.zeros_like(ref)
    fill(low_ref, bcs_scr, bc_scr, n)
    pre = mm(low_ref[0, :, :128], wdt_ref[...]) + dtb_ref[...]
    pre_scr[...] = pre
    step = softplus(pre)
    st_scr[...] = step
    sd_scr[...] = jnp.where(mask_ref[0, :, 0:1] > 0.0, step, 1e30)
    dx_scr[...] = step * xc_ref[0].astype(F32)
    z = xz_ref[0, :, e:].astype(F32)
    dy_scr[...] = dg_ref[0] * (z * jax.nn.sigmoid(z))
    a2 = a2_ref[...]
    sub = lax.broadcasted_iota(jnp.int32, (8, e), 0)
    rows = sd_scr.shape[0] // m
    lanes = lax.broadcasted_iota(jnp.int32, (n, rows), 1)
    un = 32
    for i in range(m):
        r0 = i * rows
        h0 = cks_ref[0, i] + ckp_ref[0, i] * hin_ref[i]
        h_scr[pl.ds(0, n), :] = h0

        def fwd(g, h, r0=r0):
            ys = []
            for j in range(un):
                t = g * un + j
                bc = bc_scr[at((r0 + t) * n, n, n), :]
                bb, cc = wide(bc[:, :128], e), wide(bc[:, 128:], e)
                a = jnp.exp2(sd_scr[pl.ds(r0 + t, 1), :] * a2)
                h = a * h + bb * dx_scr[pl.ds(r0 + t, 1), :]
                a_scr[at(t * n, n, n), :] = a
                h_scr[at(t * n + n, n, n), :] = h
                cy = cc * h
                ys.append(cy[:8] + cy[8:])
                if len(ys) == 8:
                    y_scr[at(r0 + t - 7, 8), :] = fold_rows(ys, sub)
                    ys = []
            return h
        lax.fori_loop(0, rows // un, fwd, h0)

        def bwd(g, carry, r0=r0):
            q, ga, hn, db, dc = carry
            das, gbs = [], []
            for j in range(un):
                t = rows - 1 - (g * un + j)
                bc = bc_scr[at((r0 + t) * n, n, n), :]
                bb, cc = wide(bc[:, :128], e), wide(bc[:, 128:], e)
                a = a_scr[at(t * n, n, n), :]
                hp = h_scr[at(t * n, n, n), :]
                dyr = dy_scr[pl.ds(r0 + t, 1), :]
                gt = cc * dyr + q
                q = a * gt
                da = q * hp
                ga = ga + da * st_scr[pl.ds(r0 + t, 1), :]
                d_a = da * a2
                g_b = gt * bb
                das.append(d_a[:8] + d_a[8:])
                gbs.append(g_b[:8] + g_b[8:])
                pb = gt * dx_scr[pl.ds(r0 + t, 1), :]
                pc = dyr * hn
                pb = sum(pb[:, k:k + 128] for k in range(0, e, 128))
                pc = sum(pc[:, k:k + 128] for k in range(0, e, 128))
                db = jnp.where(lanes == t, jnp.sum(pb, axis=1, keepdims=True), db)
                dc = jnp.where(lanes == t, jnp.sum(pc, axis=1, keepdims=True), dc)
                hn = hp
                if len(das) == 8:
                    da_scr[at(r0 + t, 8), :] = fold_rows(das[::-1], sub)
                    gb_scr[at(r0 + t, 8), :] = fold_rows(gbs[::-1], sub)
                    das, gbs = [], []
            return q, ga, hn, db, dc
        zero = jnp.zeros((n, rows), F32)
        q, ga, _, db, dc = lax.fori_loop(
            0, rows // un, bwd, (q_scr[i], ga_ref[...], h_scr[pl.ds(rows * n, n), :], zero, zero))
        q_scr[i] = q
        ga_ref[...] = ga
        part_ref[0, 128:128 + n, r0:r0 + rows] = db
        part_ref[0, 128 + n:128 + 2 * n, r0:r0 + rows] = dc

    z = xz_ref[0, :, e:].astype(F32)
    sz = jax.nn.sigmoid(z)
    xc = xc_ref[0].astype(F32)
    skip = skip_ref[...]
    y = y_scr[...] + skip * xc
    gated = (y * (z * sz)).astype(BF16)
    out_ref[0] = mm(gated, wo_ref[...]).astype(BF16)
    go_ref[...] += tn(gated, dy_ref[0])
    dz = (dg_ref[0] * y * (sz * (1.0 + z * (1.0 - sz)))).astype(BF16)
    dz_ref[0] = dz
    gz_ref[...] += tn(nu_ref[0], dz)
    gb = gb_scr[...]
    dy_y = dy_scr[...]
    dxc_ref[0] = dy_y * skip + st_scr[...] * gb
    d_pre = (da_scr[...] * LN2 + xc * gb) * jax.nn.sigmoid(pre_scr[...])
    d_low = d_pre.astype(BF16)
    gdt_ref[...] += tn(low_ref[0, :, :128], d_low)
    part_ref[0, :128, :] = nt(wdt_ref[...], d_low)
    vec_ref[0:1] += jnp.sum(d_pre, axis=0, keepdims=True)
    vec_ref[1:2] += jnp.sum(dy_y * xc, axis=0, keepdims=True)


def dsilu(v):
    s = jax.nn.sigmoid(v)
    return s * (1.0 + v * (1.0 - s))


def back(xz_ref, prev_ref, edge_ref, mask_ref, dxc_ref, ddbc_ref, dz_ref, nu_ref, next_ref, w_ref, xpt_ref, cw_ref, cb_ref,
         v_ref, gx_ref, vec_ref, carry, dx_scr, *, m, e):
    b = pl.program_id(0)
    @pl.when(b == 0)
    def _():
        carry[...] = next_ref[...]
        gx_ref[...] = jnp.zeros_like(gx_ref)
        vec_ref[...] = jnp.zeros_like(vec_ref)
    first = b == pl.num_programs(0) - 1
    rows = xz_ref.shape[1] // m
    cw, cb = cw_ref[...], cb_ref[...]
    dxc_all = dxc_ref[0] + mm(ddbc_ref[0], xpt_ref[...])
    for i in range(m):
        part = slice(i * rows, (i + 1) * rows)
        x = xz_ref[0, part, :e].astype(F32)
        before = prev_ref[0, (i + 1) * rows - 2 * EDGE:(i + 1) * rows, :e].astype(F32)[EDGE:]
        before = jnp.where(first, edge_ref[i * EDGE:(i + 1) * EDGE], before)
        lag = lags(jnp.concatenate([before, x], axis=0), rows)
        same = mask_ref[0, part]
        dconv = dxc_all[part] * dsilu(convolve(lag, same, cw, cb))
        vec_ref[4:5] += jnp.sum(dconv, axis=0, keepdims=True)
        vec_ref[3:4] += jnp.sum(dconv * x, axis=0, keepdims=True)
        dx = cw[3:4] * dconv
        for k in range(1, 4):
            masked = dconv * same[:, k - 1:k]
            vec_ref[3 - k:4 - k] += jnp.sum(masked * lag[k], axis=0, keepdims=True)
            sent = cw[3 - k:4 - k] * masked
            ext = jnp.concatenate([sent, carry[k - 1, i]], axis=0)
            dx = dx + ext[k:k + rows]
            carry[k - 1, i] = sent[:EDGE]
        dx_scr[part] = dx
    dx = dx_scr[...].astype(BF16)
    v_ref[0] = nt(jnp.concatenate([dx, dz_ref[0]], axis=1), w_ref[...]).astype(BF16)
    gx_ref[...] += tn(nu_ref[0], dx)


def shift_rep(value, steps):
    count = lax.axis_size("rep")
    first, last = max(0, -steps), min(count, count - steps)
    return lax.ppermute(value, "rep", [(i, i + steps) for i in range(first, last)])


def sum_rep(value):
    if lax.axis_size("rep") != 2:
        return lax.psum(value.astype(F32), "rep")
    low = value.astype(BF16)
    other = lax.ppermute(low, "rep", [(0, 1), (1, 0)])
    return low.astype(F32) + other.astype(F32)


def on_device(hidden_in, segment_ids, out_grad, norm_gain, in_proj, conv_weight, conv_bias, x_proj,
              dt_weight, dt_bias, a_log, d_skip, out_proj):
    peers, reps = lax.axis_size("shard"), lax.axis_size("rep")
    rep = lax.axis_index("rep")
    m, tl, d = hidden_in.shape
    t, w = tl * peers, m * tl
    dl = in_proj.shape[0]
    e = x_proj.shape[0]
    n, rank, taps = a_log.shape[0], dt_weight.shape[0], conv_weight.shape[0]
    w32 = lambda v: v.astype(F32)
    shp = jax.ShapeDtypeStruct
    rising = lambda i: i
    falling = lambda i: peers - 1 - i

    gain = w32(lax.all_gather(norm_gain, "shard", axis=0, tiled=True))
    u = w32(hidden_in)
    r = lax.rsqrt(jnp.mean(u * u, axis=2, keepdims=True) + 1e-5)
    nu = (u * r * gain).astype(BF16).reshape(w, d)
    nu_all = lax.all_gather(nu, "shard")
    dy_all = lax.all_gather(out_grad.reshape(w, d), "shard")
    w_split = in_proj.reshape(dl, 2, peers, e).transpose(2, 0, 1, 3).reshape(peers * dl, 2 * e)
    w_cols = lax.all_to_all(w_split, "shard", 0, 0, tiled=True)

    ids = lax.all_gather(segment_ids, "shard")
    row_ids = ids.transpose(1, 0, 2).reshape(m, t)
    before = jnp.where(rep > 0, shift_rep(row_ids[:, t - taps + 1:], 1), -1)
    ext = jnp.concatenate([before, row_ids], axis=1)
    same = jnp.stack([w32(ext[:, taps - 1 - k:taps - 1 - k + t] == row_ids) for k in range(1, taps)], axis=-1)
    mask = jnp.pad(same, ((0, 0), (0, 0), (0, 8 - same.shape[-1])))
    mask = mask.reshape(m, peers, tl, 8).transpose(1, 0, 2, 3).reshape(peers, w, 8)
    halo = shift_rep(nu_all[peers - 1].reshape(m, tl, d)[:, tl - EDGE:].reshape(m * EDGE, d), 1)

    cw, cb = w32(conv_weight), w32(conv_bias)[None]
    ins = [nu_all, w_cols, halo, mask, cw, cb, x_proj.T]
    outs = [shp((peers, w, 2 * e), BF16), shp((peers, w, e), BF16), shp((peers, rank + 2 * n, w), F32),
            shp((m * EDGE, e), BF16)]
    xz, xc, part, edge = call(
        functools.partial(front, m=m, e=e), (peers,),
        [block(nu_all, rising)] + [whole(a) for a in ins[1:3]] + [block(mask, rising)] + [whole(a) for a in ins[4:]],
        [block(a, rising) for a in outs[:3]] + [whole(outs[3])], outs,
        [pltpu.VMEM((m * EDGE, e), F32)], ins, flops=2 * peers * w * d * 2 * e)

    low = allsum(part, functools.partial(spread_low, n=n), 0)
    a_mat = -jnp.exp(w32(a_log))
    a2 = a_mat * LOG2E
    dtb, skip = w32(dt_bias)[None], w32(d_skip)[None]

    ins = [low, xz, xc, mask, dy_all, out_proj, dt_weight, dtb, a2]
    outs = [shp((peers, m, n, e), F32)] * 2 + [shp((3, m, n, e), F32), shp((peers, w, e), F32)]
    cks, ckp, end, dg = call(
        functools.partial(ahead, m=m, n=n, e=e), (peers,),
        [block(a, rising) for a in ins[:5]] + [whole(a) for a in ins[5:]],
        [block(outs[0], rising), block(outs[1], rising), whole(outs[2]), block(outs[3], rising)], outs,
        [pltpu.VMEM((m, n, e), F32)] * 3 + [pltpu.VMEM((w, e), F32)] * 3 + [pltpu.VMEM((w, 128), F32), pltpu.VMEM((w * n, 256), F32)],
        ins, flops=40 * 10 ** 9)

    ends = lax.all_gather(end, "rep")
    h_in = jnp.zeros((m, n, e), F32)
    q_in = jnp.zeros((m, n, e), F32)
    for k in range(reps - 1):
        o = reps - 1 - k
        h_in = jnp.where(k < rep, ends[k, 1] * h_in + ends[k, 0], h_in)
        q_in = jnp.where(o > rep, ends[o, 1] * q_in + ends[o, 2], q_in)

    ins = [low, xz, xc, mask, dy_all, dg, nu_all, cks, ckp, out_proj, dt_weight, dtb, a2, skip, h_in, q_in]
    outs = [shp((peers, w, d), BF16), shp((peers, w, e), BF16), shp((peers, w, e), F32),
            shp((peers, rank + 2 * n, w), F32), shp((e, d), F32), shp((rank, e), F32), shp((n, e), F32), shp((8, e), F32),
            shp((d, e), F32)]
    part_out, dz, dxc, part, g_out, g_dt, g_a, vec, g_z = call(
        functools.partial(behind, m=m, n=n, e=e), (peers,),
        [block(a, falling) for a in ins[:9]] + [whole(a) for a in ins[9:]],
        [block(a, falling) for a in outs[:4]] + [whole(a) for a in outs[4:]], outs,
        [pltpu.VMEM((tl * n + n, e), F32), pltpu.VMEM((tl * n, e), F32), pltpu.VMEM((m, n, e), F32),
         pltpu.VMEM((w, 128), F32), pltpu.VMEM((w * n, 256), F32)] + [pltpu.VMEM((w, e), F32)] * 8, ins, flops=100 * 10 ** 9)

    out_sum = lax.psum_scatter(part_out, "shard", scatter_dimension=0, tiled=True).reshape(m, tl, d)
    layer_out = (u + w32(out_sum)).astype(BF16)

    ddbc = allsum(part, functools.partial(spread_plain, n=n), 1)
    xpt = jnp.pad(x_proj.T, ((0, 256 - x_proj.shape[1]), (0, 0)))

    x8 = w32(xz[0].reshape(m, tl, 2 * e)[:, :EDGE, :e])
    ext8 = jnp.concatenate([w32(edge).reshape(m, EDGE, e), x8], axis=1)
    same8 = mask[0].reshape(m, tl, 8)[:, :EDGE]
    conv8 = cb + cw[3] * x8
    for k in range(1, taps):
        conv8 = conv8 + cw[3 - k] * ext8[:, EDGE - k:2 * EDGE - k] * same8[:, :, k - 1:k]
    d8 = dxc[0].reshape(m, tl, e)[:, :EDGE] + mm(ddbc[0].reshape(m, tl, -1)[:, :EDGE].reshape(m * EDGE, -1), xpt).reshape(m, EDGE, e)
    d8 = d8 * dsilu(conv8)
    sent = jnp.stack([cw[3 - k] * d8 * same8[:, :, k - 1:k] for k in range(1, taps)])
    follow = shift_rep(sent, -1)

    ins = [xz, xz, w32(edge), mask, dxc, ddbc, dz, nu_all, follow, w_cols, xpt, cw, cb]
    outs = [shp((peers, w, d), BF16), shp((d, e), F32), shp((8, e), F32)]
    earlier = lambda i: jnp.maximum(peers - 2 - i, 0)
    specs = [block(a, falling) for a in ins[:8]] + [whole(a) for a in ins[8:]]
    specs[1], specs[2] = block(xz, earlier), whole(ins[2])
    v_part, g_x, vec2 = call(
        functools.partial(back, m=m, e=e), (peers,), specs,
        [block(outs[0], falling), whole(outs[1]), whole(outs[2])], outs,
        [pltpu.VMEM((taps - 1, m, EDGE, e), F32), pltpu.VMEM((w, e), F32)], ins, flops=2 * peers * w * d * 3 * e)

    v = w32(lax.psum_scatter(v_part, "shard", scatter_dimension=0, tiled=True)).reshape(m, tl, d) * gain
    in_grad = w32(out_grad) + r * v - u * (r * r * r) * jnp.mean(v * u, axis=2, keepdims=True)

    def to_owner(g):
        own = lax.all_to_all(g.astype(BF16), "shard", 0, 0, tiled=True)
        own = own.reshape(peers, dl, e).transpose(1, 0, 2).reshape(dl, peers * e)
        return sum_rep(own)
    grad_in_proj = jnp.concatenate([to_owner(g_x), to_owner(g_z)], axis=1)
    grad_gain = jnp.sum(grad_in_proj * w32(in_proj), axis=1) / w32(norm_gain)

    small = jnp.concatenate([vec, vec2, g_a * a_mat, g_dt, tn(xc.reshape(peers * w, e), ddbc.reshape(peers * w, -1)).T], axis=0)
    small = sum_rep(small)
    vec, vec2, g_a, g_dt, g_xp = (small[:8], small[8:16], small[16:16 + n], small[16 + n:16 + n + rank], small[16 + n + rank:])
    return (layer_out, in_grad, grad_gain, grad_in_proj, vec2[:taps], vec2[taps], g_xp[:rank + 2 * n].T, g_dt, vec[0],
            g_a, vec[1], sum_rep(g_out))


def solution(mesh):
    tok, ids = P(None, ("rep", "shard"), None), P(None, ("rep", "shard"))
    row, col, one = P("shard", None), P(None, "shard"), P("shard")
    return jax.shard_map(
        on_device,
        mesh=mesh,
        in_specs=(tok, ids, tok, one, row, col, one, row, col, one, col, one, row),
        out_specs=(tok, tok, one, row, col, one, row, col, one, col, one, row),
        check_vma=False,
    )
```

```python
import functools
import jax
import jax.numpy as jnp
from jax import lax
from jax.sharding import PartitionSpec as P
from jax.experimental import pallas as pl
from jax.experimental.pallas import tpu as pltpu

F32, BF16 = jnp.float32, jnp.bfloat16
LOG2E, LN2 = 1.4426950408889634, 0.6931471805599453
EDGE = 8
VMEM = 56 << 20


def nt(a, b):
    return lax.dot_general(a, b, (((1,), (1,)), ((), ())), preferred_element_type=F32)


def tn(a, b):
    return lax.dot_general(a, b, (((0,), (0,)), ((), ())), preferred_element_type=F32)


def mm(a, b):
    return jnp.dot(a, b, preferred_element_type=F32)


def softplus(v):
    return jnp.maximum(v, 0.0) + jnp.log1p(jnp.exp(-jnp.abs(v)))


def wide(v, e):
    return jnp.concatenate([v] * (e // 128), axis=1) if e > 128 else v


def at(start, size, unit=8):
    return pl.ds(pl.multiple_of(start, unit), size)


def call(kernel, grid, in_specs, out_specs, out_shape, scratch, args, flops=0):
    size = sum(a.size * a.dtype.itemsize for a in args) + sum(s.size * s.dtype.itemsize for s in out_shape)
    return pl.pallas_call(
        kernel, grid=grid, in_specs=in_specs, out_specs=out_specs, out_shape=out_shape,
        scratch_shapes=scratch, compiler_params=pltpu.CompilerParams(vmem_limit_bytes=VMEM),
        cost_estimate=pl.CostEstimate(flops=flops, bytes_accessed=size, transcendentals=0))(*args)


def whole(a):
    return pl.BlockSpec(a.shape, lambda i, r=len(a.shape): (0,) * r)


def block(a, order):
    return pl.BlockSpec((1,) + a.shape[1:], lambda i, r=len(a.shape): (order(i),) + (0,) * (r - 1))


def lags(x_ext, rows):
    return [x_ext[EDGE - k:EDGE - k + rows] for k in range(4)]


def convolve(lag, same, cw, cb):
    out = cb + cw[3:4] * lag[0]
    for k in range(1, 4):
        out = out + cw[3 - k:4 - k] * lag[k] * same[:, k - 1:k]
    return out


def front(nu_ref, w_ref, halo_ref, mask_ref, cw_ref, cb_ref, xp_ref, xz_ref, xc_ref, part_ref, edge_ref, carry, *, m, e):
    @pl.when(pl.program_id(0) == 0)
    def _():
        edge = mm(halo_ref[...], w_ref[:, :e]).astype(BF16)
        edge_ref[...] = edge
        carry[...] = edge.astype(F32)
    xz = mm(nu_ref[0], w_ref[...]).astype(BF16)
    xz_ref[0] = xz
    rows = xz.shape[0] // m
    cw, cb = cw_ref[...], cb_ref[...]
    for i in range(m):
        x = xz[i * rows:(i + 1) * rows, :e].astype(F32)
        ext = jnp.concatenate([carry[i * EDGE:(i + 1) * EDGE], x], axis=0)
        carry[i * EDGE:(i + 1) * EDGE] = x[rows - EDGE:]
        conv = convolve(lags(ext, rows), mask_ref[0, i * rows:(i + 1) * rows], cw, cb)
        xc_ref[0, i * rows:(i + 1) * rows] = (conv * jax.nn.sigmoid(conv)).astype(BF16)
    part_ref[0] = nt(xp_ref[...], xc_ref[0])


def lattice(peers):
    y = 2 if peers <= 16 else 4
    return peers // (2 * y), y, 2


def greet(targets):
    barrier = pltpu.get_barrier_semaphore()
    for target in targets:
        pl.semaphore_signal(barrier, inc=1, device_id={"shard": target}, device_id_type=pl.DeviceIdType.MESH)
    pl.semaphore_wait(barrier, len(targets))


def remote(src, dst, send, recv, target):
    return pltpu.make_async_remote_copy(src_ref=src, dst_ref=dst, send_sem=send, recv_sem=recv,
                                        device_id={"shard": target}, device_id_type=pl.DeviceIdType.MESH)


def spread_low(total, n):
    rows = jnp.concatenate([total, jnp.zeros((256 - total.shape[0], total.shape[1]), F32)], axis=0).T
    rank = total.shape[0] - 2 * n
    out = [rows[:, :rank].astype(BF16)]
    rest = rows[:, rank:]
    hi = rest.astype(BF16)
    mid = (rest - hi.astype(F32)).astype(BF16)
    lo = (rest - hi.astype(F32) - mid.astype(F32)).astype(BF16)
    for k in range(2):
        out += [p[:, k * n:(k + 1) * n] for p in (hi, mid, lo)]
    out.append(jnp.zeros((rows.shape[0], 128 - 6 * n), BF16))
    return jnp.concatenate(out, axis=1)


def spread_plain(total, n):
    return jnp.concatenate([total, jnp.zeros((256 - total.shape[0], total.shape[1]), F32)], axis=0).T.astype(BF16)


def allsum_kernel(part, out, rc, ac, ry, ay, rz, send, recv, *, dims, chunks, finish):
    nz, ny, _ = dims
    me = lax.axis_index("shard")
    c, y, z = me % 2, (me // 2) % ny, me // (2 * ny)
    where = lambda a, b, d: (a * ny + b) * 2 + d
    across = where(z, y, 1 - c)
    ys = [lax.rem(y + k, ny) for k in range(1, ny)]
    zs = [lax.rem(z + k, nz) for k in range(1, nz)]
    greet([across] + [where(z, b, c) for b in ys] + [where(a, y, c) for a in zs])
    width = part.shape[-1] // chunks
    lanes = [pl.ds(q * width, width) for q in range(chunks)]
    rows = [pl.ds(q * width, width) for q in range(chunks)]

    def start(copies):
        for copy in copies:
            copy.start()
        return copies

    def finish_all(copies):
        for copy in copies:
            copy.wait()
    base = [0]

    def sems(count):
        base[0] += count
        return [(send.at[base[0] - count + k], recv.at[base[0] - count + k]) for k in range(count)]

    first = []
    for q in range(chunks):
        (s, r), = sems(1)
        first.append(start([remote(part.at[:, :, 1 - c, :, lanes[q]], rc.at[q], s, r, across)]))
    second = []
    for q in range(chunks):
        finish_all(first[q])
        for a in range(nz):
            for b in range(ny):
                ac[q, a, b] = part[a, b, c, :, q * width:(q + 1) * width] + rc[q, a, b]
        second.append(start([remote(ac.at[q, :, b], ry.at[q, k], *sem, where(z, b, c))
                             for k, (b, sem) in enumerate(zip(ys, sems(ny - 1)))]))
    third = []
    for q in range(chunks):
        finish_all(second[q])
        for a in range(nz):
            got = ac[q, a, y]
            for k in range(ny - 1):
                got = got + ry[q, k, a]
            ay[q, a] = got
        third.append(start([remote(ay.at[q, a], rz.at[q, k], *sem, where(a, y, c))
                            for k, (a, sem) in enumerate(zip(zs, sems(nz - 1)))]))
    fourth = []
    for q in range(chunks):
        finish_all(third[q])
        got = ay[q, z]
        for k in range(nz - 1):
            got = got + rz[q, k]
        out[z, y, c, q * width:(q + 1) * width] = finish(got)
        mine = out.at[z, y, c, rows[q]]
        fourth.append(start([remote(mine, mine, *sem, where(a, y, c)) for a, sem in zip(zs, sems(nz - 1))]))
    fifth = []
    for q in range(chunks):
        finish_all(fourth[q])
        mine = out.at[:, y, c, rows[q]]
        fifth.append(start([remote(mine, mine, *sem, where(z, b, c)) for b, sem in zip(ys, sems(ny - 1))]))
    last = []
    for q in range(chunks):
        finish_all(fifth[q])
        mine = out.at[:, :, c, rows[q]]
        (s, r), = sems(1)
        last.append(start([remote(mine, mine, s, r, across)]))
    for q in range(chunks):
        finish_all(last[q])


def allsum(part, finish, collective_id):
    peers, cols, w = part.shape
    dims = lattice(peers)
    nz, ny, nc = dims
    chunks = w // 128
    copies = 2 * chunks * (1 + ny - 1 + nz - 1)
    out = pl.pallas_call(
        functools.partial(allsum_kernel, dims=dims, chunks=chunks, finish=finish),
        out_shape=jax.ShapeDtypeStruct((nz, ny, nc, w, 256), BF16),
        in_specs=[pl.BlockSpec(memory_space=pltpu.VMEM)],
        out_specs=pl.BlockSpec(memory_space=pltpu.VMEM),
        scratch_shapes=[pltpu.VMEM((chunks, nz, ny, cols, 128), F32), pltpu.VMEM((chunks, nz, ny, cols, 128), F32),
                        pltpu.VMEM((chunks, ny - 1, nz, cols, 128), F32), pltpu.VMEM((chunks, nz, cols, 128), F32),
                        pltpu.VMEM((chunks, nz - 1, cols, 128), F32),
                        pltpu.SemaphoreType.DMA((copies,)), pltpu.SemaphoreType.DMA((copies,))],
        compiler_params=pltpu.CompilerParams(collective_id=collective_id, has_side_effects=True, vmem_limit_bytes=VMEM),
    )(part.reshape(nz, ny, nc, cols, w))
    return out.reshape(peers, w, 256)


def scatter_kernel(part, out, own, rc, ry, rz, load, send, recv, *, dims, chunks):
    nz, ny, _ = dims
    me = lax.axis_index("shard")
    c, y, z = me % 2, (me // 2) % ny, me // (2 * ny)
    where = lambda a, b, d: (a * ny + b) * 2 + d
    across = where(z, y, 1 - c)
    ys = [lax.rem(y + k, ny) for k in range(1, ny)]
    zs = [lax.rem(z + k, nz) for k in range(1, nz)]
    greet([across] + [where(z, b, c) for b in ys] + [where(a, y, c) for a in zs])
    size = part.shape[3] // chunks
    rows = [pl.ds(q * size, size) for q in range(chunks)]
    per = 1 + ny - 1 + nz - 1

    def pair(q, k):
        return send.at[q * per + k], recv.at[q * per + k]
    loads, first, second, third = [], [], [None] * chunks, [None] * chunks
    for q in range(chunks):
        loads.append(pltpu.make_async_copy(part.at[:, :, c, rows[q]], own.at[:, :, rows[q]], load.at[q]))
        first.append(remote(part.at[:, :, 1 - c, rows[q]], rc.at[:, :, rows[q]], *pair(q, 0), across))
        loads[q].start()
        first[q].start()

    def over_core(q):
        loads[q].wait()
        first[q].wait()

        def add(a, _):
            i, j = a // ny, a % ny
            own[i, j, rows[q]] = (own[i, j, rows[q]].astype(F32) + rc[i, j, rows[q]].astype(F32)).astype(BF16)
            return 0
        lax.fori_loop(0, nz * ny, add, 0)
        second[q] = [remote(own.at[:, b, rows[q]], ry.at[k, :, rows[q]], *pair(q, 1 + k), where(z, b, c))
                     for k, b in enumerate(ys)]
        for copy in second[q]:
            copy.start()

    def over_y(q):
        for copy in second[q]:
            copy.wait()

        def add(a, _):
            total = own[a, y, rows[q]].astype(F32)
            for k in range(ny - 1):
                total = total + ry[k, a, rows[q]].astype(F32)
            own[a, y, rows[q]] = total.astype(BF16)
            return 0
        lax.fori_loop(0, nz, add, 0)
        third[q] = [remote(own.at[a, y, rows[q]], rz.at[k, rows[q]], *pair(q, ny + k), where(a, y, c))
                    for k, a in enumerate(zs)]
        for copy in third[q]:
            copy.start()

    def over_z(q):
        for copy in third[q]:
            copy.wait()
        total = own[z, y, rows[q]].astype(F32)
        for k in range(nz - 1):
            total = total + rz[k, rows[q]].astype(F32)
        out[rows[q]] = total

    for s in range(chunks + 4):
        if s < chunks:
            over_core(s)
        if 0 <= s - 2 < chunks:
            over_y(s - 2)
        if 0 <= s - 4 < chunks:
            over_z(s - 4)


def scatter(part, collective_id):
    peers, w, d = part.shape
    dims = lattice(peers)
    nz, ny, nc = dims
    chunks = w // 32
    copies = chunks * (1 + ny - 1 + nz - 1)
    return pl.pallas_call(
        functools.partial(scatter_kernel, dims=dims, chunks=chunks),
        out_shape=jax.ShapeDtypeStruct((w, d), F32),
        in_specs=[pl.BlockSpec(memory_space=pl.ANY)],
        out_specs=pl.BlockSpec(memory_space=pltpu.VMEM),
        scratch_shapes=[pltpu.VMEM((nz, ny, w, d), BF16), pltpu.VMEM((nz, ny, w, d), BF16),
                        pltpu.VMEM((ny - 1, nz, w, d), BF16), pltpu.VMEM((nz - 1, w, d), BF16),
                        pltpu.SemaphoreType.DMA((chunks,)),
                        pltpu.SemaphoreType.DMA((copies,)), pltpu.SemaphoreType.DMA((copies,))],
        compiler_params=pltpu.CompilerParams(collective_id=collective_id, has_side_effects=True, vmem_limit_bytes=VMEM),
        cost_estimate=pl.CostEstimate(flops=8 * 10 ** 10, bytes_accessed=2 * peers * w * d, transcendentals=0),
    )(part.reshape(nz, ny, nc, w, d))


def fill(low_ref, bcs_scr, bc_scr, n):
    bcs_scr[...] = low_ref[0, :, 128:].astype(F32)
    lane = lax.broadcasted_iota(jnp.int32, (n, 128), 1)
    sub = lax.broadcasted_iota(jnp.int32, (n, 128), 0)
    mask = (lane % n) == sub
    r = lax.broadcasted_iota(jnp.int32, (128, 256), 0)
    c = lax.broadcasted_iota(jnp.int32, (128, 256), 1)
    ones = jnp.where((r >= 3 * n) == (c >= 128), 1.0, 0.0).astype(BF16)
    group = 128

    def body(g, _):
        rows = [jnp.where(mask, bcs_scr[pl.ds(g * group + j, 1), :], 0.0).astype(BF16) for j in range(group)]
        bc_scr[at(g * (group * n), group * n, 128), :] = mm(jnp.concatenate(rows, axis=0), ones)
        return 0
    lax.fori_loop(0, bcs_scr.shape[0] // group, body, 0)


def fold_rows(vals, sub):
    for k in (1, 2, 4):
        mask = (sub & k) == 0
        vals = [jnp.where(mask, a, b) + pltpu.roll(jnp.where(mask, b, a), 8 - k, 0)
                for a, b in zip(vals[::2], vals[1::2])]
    return vals[0]


def ahead(low_ref, xz_ref, xc_ref, mask_ref, dy_ref, wo_ref, wdt_ref, dtb_ref, a2_ref,
          cks_ref, ckp_ref, end_ref, dg_ref, s_scr, p_scr, f_scr, sd_scr, dx_scr, dy_scr, bcs_scr, bc_scr, *, m, n, e):
    b = pl.program_id(0)
    @pl.when(b == 0)
    def _():
        s_scr[...] = jnp.zeros_like(s_scr)
        p_scr[...] = jnp.ones_like(p_scr)
        f_scr[...] = jnp.zeros_like(f_scr)
    cks_ref[0] = s_scr[...]
    ckp_ref[0] = p_scr[...]
    fill(low_ref, bcs_scr, bc_scr, n)
    step = softplus(mm(low_ref[0, :, :128], wdt_ref[...]) + dtb_ref[...])
    sd_scr[...] = jnp.where(mask_ref[0, :, 0:1] > 0.0, step, 1e30)
    dx_scr[...] = step * xc_ref[0].astype(F32)
    dg = nt(dy_ref[0], wo_ref[...])
    dg_ref[0] = dg
    z = xz_ref[0, :, e:].astype(F32)
    dy_scr[...] = dg * (z * jax.nn.sigmoid(z))
    a2 = a2_ref[...]
    rows = sd_scr.shape[0] // m
    un = 16

    def group(g, carry):
        s, p, f = [list(c) for c in carry]
        for j in range(un):
            for i in range(m):
                t = i * rows + g * un + j
                bc = bc_scr[at(t * n, n, n), :]
                bb, cc = wide(bc[:, :128], e), wide(bc[:, 128:], e)
                a = jnp.exp2(sd_scr[pl.ds(t, 1), :] * a2)
                s[i] = a * s[i] + bb * dx_scr[pl.ds(t, 1), :]
                p[i] = p[i] * a
                f[i] = f[i] + p[i] * (cc * dy_scr[pl.ds(t, 1), :])
        return tuple(s), tuple(p), tuple(f)
    done = lax.fori_loop(0, rows // un, group,
                         tuple(tuple(scr[i] for i in range(m)) for scr in (s_scr, p_scr, f_scr)))
    for scr, vals in zip((s_scr, p_scr, f_scr), done):
        for i in range(m):
            scr[i] = vals[i]

    @pl.when(b == pl.num_programs(0) - 1)
    def _():
        end_ref[0] = s_scr[...]
        end_ref[1] = p_scr[...]
        end_ref[2] = f_scr[...]


def behind(low_ref, xz_ref, xc_ref, mask_ref, dy_ref, dg_ref, nu_ref, cks_ref, ckp_ref,
           wo_ref, wdt_ref, dtb_ref, a2_ref, skip_ref, hin_ref, qin_ref,
           out_ref, dz_ref, dxc_ref, part_ref, go_ref, gdt_ref, ga_ref, vec_ref, gz_ref,
           h_scr, a_scr, q_scr, bcs_scr, bc_scr, pre_scr, st_scr, sd_scr, dx_scr, dy_scr, y_scr, da_scr, gb_scr, *, m, n, e):
    b = pl.program_id(0)
    @pl.when(b == 0)
    def _():
        q_scr[...] = qin_ref[...]
        for ref in (go_ref, gdt_ref, ga_ref, vec_ref, gz_ref):
            ref[...] = jnp.zeros_like(ref)
    fill(low_ref, bcs_scr, bc_scr, n)
    pre = mm(low_ref[0, :, :128], wdt_ref[...]) + dtb_ref[...]
    pre_scr[...] = pre
    step = softplus(pre)
    st_scr[...] = step
    sd_scr[...] = jnp.where(mask_ref[0, :, 0:1] > 0.0, step, 1e30)
    dx_scr[...] = step * xc_ref[0].astype(F32)
    z = xz_ref[0, :, e:].astype(F32)
    dy_scr[...] = dg_ref[0] * (z * jax.nn.sigmoid(z))
    a2 = a2_ref[...]
    sub = lax.broadcasted_iota(jnp.int32, (8, e), 0)
    rows = sd_scr.shape[0] // m
    lanes = lax.broadcasted_iota(jnp.int32, (n, rows), 1)
    un = 32
    for i in range(m):
        r0 = i * rows
        h0 = cks_ref[0, i] + ckp_ref[0, i] * hin_ref[i]
        h_scr[pl.ds(0, n), :] = h0

        def fwd(g, h, r0=r0):
            ys = []
            for j in range(un):
                t = g * un + j
                bc = bc_scr[at((r0 + t) * n, n, n), :]
                bb, cc = wide(bc[:, :128], e), wide(bc[:, 128:], e)
                a = jnp.exp2(sd_scr[pl.ds(r0 + t, 1), :] * a2)
                h = a * h + bb * dx_scr[pl.ds(r0 + t, 1), :]
                a_scr[at(t * n, n, n), :] = a
                h_scr[at(t * n + n, n, n), :] = h
                cy = cc * h
                ys.append(cy[:8] + cy[8:])
                if len(ys) == 8:
                    y_scr[at(r0 + t - 7, 8), :] = fold_rows(ys, sub)
                    ys = []
            return h
        lax.fori_loop(0, rows // un, fwd, h0)

        def bwd(g, carry, r0=r0):
            q, ga, hn, db, dc = carry
            das, gbs = [], []
            for j in range(un):
                t = rows - 1 - (g * un + j)
                bc = bc_scr[at((r0 + t) * n, n, n), :]
                bb, cc = wide(bc[:, :128], e), wide(bc[:, 128:], e)
                a = a_scr[at(t * n, n, n), :]
                hp = h_scr[at(t * n, n, n), :]
                dyr = dy_scr[pl.ds(r0 + t, 1), :]
                gt = cc * dyr + q
                q = a * gt
                da = q * hp
                ga = ga + da * st_scr[pl.ds(r0 + t, 1), :]
                d_a = da * a2
                g_b = gt * bb
                das.append(d_a[:8] + d_a[8:])
                gbs.append(g_b[:8] + g_b[8:])
                pb = gt * dx_scr[pl.ds(r0 + t, 1), :]
                pc = dyr * hn
                pb = sum(pb[:, k:k + 128] for k in range(0, e, 128))
                pc = sum(pc[:, k:k + 128] for k in range(0, e, 128))
                db = jnp.where(lanes == t, jnp.sum(pb, axis=1, keepdims=True), db)
                dc = jnp.where(lanes == t, jnp.sum(pc, axis=1, keepdims=True), dc)
                hn = hp
                if len(das) == 8:
                    da_scr[at(r0 + t, 8), :] = fold_rows(das[::-1], sub)
                    gb_scr[at(r0 + t, 8), :] = fold_rows(gbs[::-1], sub)
                    das, gbs = [], []
            return q, ga, hn, db, dc
        zero = jnp.zeros((n, rows), F32)
        q, ga, _, db, dc = lax.fori_loop(
            0, rows // un, bwd, (q_scr[i], ga_ref[...], h_scr[pl.ds(rows * n, n), :], zero, zero))
        q_scr[i] = q
        ga_ref[...] = ga
        part_ref[0, 128:128 + n, r0:r0 + rows] = db
        part_ref[0, 128 + n:128 + 2 * n, r0:r0 + rows] = dc

    z = xz_ref[0, :, e:].astype(F32)
    sz = jax.nn.sigmoid(z)
    xc = xc_ref[0].astype(F32)
    skip = skip_ref[...]
    y = y_scr[...] + skip * xc
    gated = (y * (z * sz)).astype(BF16)
    out_ref[0] = mm(gated, wo_ref[...]).astype(BF16)
    go_ref[...] += tn(gated, dy_ref[0])
    dz = (dg_ref[0] * y * (sz * (1.0 + z * (1.0 - sz)))).astype(BF16)
    dz_ref[0] = dz
    gz_ref[...] += tn(nu_ref[0], dz)
    gb = gb_scr[...]
    dy_y = dy_scr[...]
    dxc_ref[0] = dy_y * skip + st_scr[...] * gb
    d_pre = (da_scr[...] * LN2 + xc * gb) * jax.nn.sigmoid(pre_scr[...])
    d_low = d_pre.astype(BF16)
    gdt_ref[...] += tn(low_ref[0, :, :128], d_low)
    part_ref[0, :128, :] = nt(wdt_ref[...], d_low)
    vec_ref[0:1] += jnp.sum(d_pre, axis=0, keepdims=True)
    vec_ref[1:2] += jnp.sum(dy_y * xc, axis=0, keepdims=True)


def dsilu(v):
    s = jax.nn.sigmoid(v)
    return s * (1.0 + v * (1.0 - s))


def back(xz_ref, prev_ref, edge_ref, mask_ref, dxc_ref, ddbc_ref, dz_ref, nu_ref, next_ref, w_ref, xpt_ref, cw_ref, cb_ref,
         v_ref, gx_ref, vec_ref, carry, dx_scr, *, m, e):
    b = pl.program_id(0)
    @pl.when(b == 0)
    def _():
        carry[...] = next_ref[...]
        gx_ref[...] = jnp.zeros_like(gx_ref)
        vec_ref[...] = jnp.zeros_like(vec_ref)
    first = b == pl.num_programs(0) - 1
    rows = xz_ref.shape[1] // m
    cw, cb = cw_ref[...], cb_ref[...]
    dxc_all = dxc_ref[0] + mm(ddbc_ref[0], xpt_ref[...])
    for i in range(m):
        part = slice(i * rows, (i + 1) * rows)
        x = xz_ref[0, part, :e].astype(F32)
        before = prev_ref[0, (i + 1) * rows - 2 * EDGE:(i + 1) * rows, :e].astype(F32)[EDGE:]
        before = jnp.where(first, edge_ref[i * EDGE:(i + 1) * EDGE], before)
        lag = lags(jnp.concatenate([before, x], axis=0), rows)
        same = mask_ref[0, part]
        dconv = dxc_all[part] * dsilu(convolve(lag, same, cw, cb))
        vec_ref[4:5] += jnp.sum(dconv, axis=0, keepdims=True)
        vec_ref[3:4] += jnp.sum(dconv * x, axis=0, keepdims=True)
        dx = cw[3:4] * dconv
        for k in range(1, 4):
            masked = dconv * same[:, k - 1:k]
            vec_ref[3 - k:4 - k] += jnp.sum(masked * lag[k], axis=0, keepdims=True)
            sent = cw[3 - k:4 - k] * masked
            ext = jnp.concatenate([sent, carry[k - 1, i]], axis=0)
            dx = dx + ext[k:k + rows]
            carry[k - 1, i] = sent[:EDGE]
        dx_scr[part] = dx
    dx = dx_scr[...].astype(BF16)
    v_ref[0] = nt(jnp.concatenate([dx, dz_ref[0]], axis=1), w_ref[...]).astype(BF16)
    gx_ref[...] += tn(nu_ref[0], dx)


def shift_rep(value, steps):
    count = lax.axis_size("rep")
    first, last = max(0, -steps), min(count, count - steps)
    return lax.ppermute(value, "rep", [(i, i + steps) for i in range(first, last)])


def sum_rep(value):
    if lax.axis_size("rep") != 2:
        return lax.psum(value.astype(F32), "rep")
    low = value.astype(BF16)
    other = lax.ppermute(low, "rep", [(0, 1), (1, 0)])
    return low.astype(F32) + other.astype(F32)


def on_device(hidden_in, segment_ids, out_grad, norm_gain, in_proj, conv_weight, conv_bias, x_proj,
              dt_weight, dt_bias, a_log, d_skip, out_proj):
    peers, reps = lax.axis_size("shard"), lax.axis_size("rep")
    rep = lax.axis_index("rep")
    m, tl, d = hidden_in.shape
    t, w = tl * peers, m * tl
    dl = in_proj.shape[0]
    e = x_proj.shape[0]
    n, rank, taps = a_log.shape[0], dt_weight.shape[0], conv_weight.shape[0]
    w32 = lambda v: v.astype(F32)
    shp = jax.ShapeDtypeStruct
    rising = lambda i: i
    falling = lambda i: peers - 1 - i

    gain = w32(lax.all_gather(norm_gain, "shard", axis=0, tiled=True))
    u = w32(hidden_in)
    r = lax.rsqrt(jnp.mean(u * u, axis=2, keepdims=True) + 1e-5)
    nu = (u * r * gain).astype(BF16).reshape(w, d)
    nu_all = lax.all_gather(nu, "shard")
    dy_all = lax.all_gather(out_grad.reshape(w, d), "shard")
    w_split = in_proj.reshape(dl, 2, peers, e).transpose(2, 0, 1, 3).reshape(peers * dl, 2 * e)
    w_cols = lax.all_to_all(w_split, "shard", 0, 0, tiled=True)

    ids = lax.all_gather(segment_ids, "shard")
    row_ids = ids.transpose(1, 0, 2).reshape(m, t)
    before = jnp.where(rep > 0, shift_rep(row_ids[:, t - taps + 1:], 1), -1)
    ext = jnp.concatenate([before, row_ids], axis=1)
    same = jnp.stack([w32(ext[:, taps - 1 - k:taps - 1 - k + t] == row_ids) for k in range(1, taps)], axis=-1)
    mask = jnp.pad(same, ((0, 0), (0, 0), (0, 8 - same.shape[-1])))
    mask = mask.reshape(m, peers, tl, 8).transpose(1, 0, 2, 3).reshape(peers, w, 8)
    halo = shift_rep(nu_all[peers - 1].reshape(m, tl, d)[:, tl - EDGE:].reshape(m * EDGE, d), 1)

    cw, cb = w32(conv_weight), w32(conv_bias)[None]
    ins = [nu_all, w_cols, halo, mask, cw, cb, x_proj.T]
    outs = [shp((peers, w, 2 * e), BF16), shp((peers, w, e), BF16), shp((peers, rank + 2 * n, w), F32),
            shp((m * EDGE, e), BF16)]
    xz, xc, part, edge = call(
        functools.partial(front, m=m, e=e), (peers,),
        [block(nu_all, rising)] + [whole(a) for a in ins[1:3]] + [block(mask, rising)] + [whole(a) for a in ins[4:]],
        [block(a, rising) for a in outs[:3]] + [whole(outs[3])], outs,
        [pltpu.VMEM((m * EDGE, e), F32)], ins, flops=2 * peers * w * d * 2 * e)

    low = allsum(part, functools.partial(spread_low, n=n), 0)
    a_mat = -jnp.exp(w32(a_log))
    a2 = a_mat * LOG2E
    dtb, skip = w32(dt_bias)[None], w32(d_skip)[None]

    ins = [low, xz, xc, mask, dy_all, out_proj, dt_weight, dtb, a2]
    outs = [shp((peers, m, n, e), F32)] * 2 + [shp((3, m, n, e), F32), shp((peers, w, e), F32)]
    cks, ckp, end, dg = call(
        functools.partial(ahead, m=m, n=n, e=e), (peers,),
        [block(a, rising) for a in ins[:5]] + [whole(a) for a in ins[5:]],
        [block(outs[0], rising), block(outs[1], rising), whole(outs[2]), block(outs[3], rising)], outs,
        [pltpu.VMEM((m, n, e), F32)] * 3 + [pltpu.VMEM((w, e), F32)] * 3 + [pltpu.VMEM((w, 128), F32), pltpu.VMEM((w * n, 256), F32)],
        ins, flops=40 * 10 ** 9)

    ends = lax.all_gather(end, "rep")
    h_in = jnp.zeros((m, n, e), F32)
    q_in = jnp.zeros((m, n, e), F32)
    for k in range(reps - 1):
        o = reps - 1 - k
        h_in = jnp.where(k < rep, ends[k, 1] * h_in + ends[k, 0], h_in)
        q_in = jnp.where(o > rep, ends[o, 1] * q_in + ends[o, 2], q_in)

    ins = [low, xz, xc, mask, dy_all, dg, nu_all, cks, ckp, out_proj, dt_weight, dtb, a2, skip, h_in, q_in]
    outs = [shp((peers, w, d), BF16), shp((peers, w, e), BF16), shp((peers, w, e), F32),
            shp((peers, rank + 2 * n, w), F32), shp((e, d), F32), shp((rank, e), F32), shp((n, e), F32), shp((8, e), F32),
            shp((d, e), F32)]
    part_out, dz, dxc, part, g_out, g_dt, g_a, vec, g_z = call(
        functools.partial(behind, m=m, n=n, e=e), (peers,),
        [block(a, falling) for a in ins[:9]] + [whole(a) for a in ins[9:]],
        [block(a, falling) for a in outs[:4]] + [whole(a) for a in outs[4:]], outs,
        [pltpu.VMEM((tl * n + n, e), F32), pltpu.VMEM((tl * n, e), F32), pltpu.VMEM((m, n, e), F32),
         pltpu.VMEM((w, 128), F32), pltpu.VMEM((w * n, 256), F32)] + [pltpu.VMEM((w, e), F32)] * 8, ins, flops=100 * 10 ** 9)

    out_sum = scatter(part_out, 2).reshape(m, tl, d)
    layer_out = (u + out_sum).astype(BF16)

    ddbc = allsum(part, functools.partial(spread_plain, n=n), 1)
    xpt = jnp.pad(x_proj.T, ((0, 256 - x_proj.shape[1]), (0, 0)))

    x8 = w32(xz[0].reshape(m, tl, 2 * e)[:, :EDGE, :e])
    ext8 = jnp.concatenate([w32(edge).reshape(m, EDGE, e), x8], axis=1)
    same8 = mask[0].reshape(m, tl, 8)[:, :EDGE]
    conv8 = cb + cw[3] * x8
    for k in range(1, taps):
        conv8 = conv8 + cw[3 - k] * ext8[:, EDGE - k:2 * EDGE - k] * same8[:, :, k - 1:k]
    d8 = dxc[0].reshape(m, tl, e)[:, :EDGE] + mm(ddbc[0].reshape(m, tl, -1)[:, :EDGE].reshape(m * EDGE, -1), xpt).reshape(m, EDGE, e)
    d8 = d8 * dsilu(conv8)
    sent = jnp.stack([cw[3 - k] * d8 * same8[:, :, k - 1:k] for k in range(1, taps)])
    follow = shift_rep(sent, -1)

    ins = [xz, xz, w32(edge), mask, dxc, ddbc, dz, nu_all, follow, w_cols, xpt, cw, cb]
    outs = [shp((peers, w, d), BF16), shp((d, e), F32), shp((8, e), F32)]
    earlier = lambda i: jnp.maximum(peers - 2 - i, 0)
    specs = [block(a, falling) for a in ins[:8]] + [whole(a) for a in ins[8:]]
    specs[1], specs[2] = block(xz, earlier), whole(ins[2])
    v_part, g_x, vec2 = call(
        functools.partial(back, m=m, e=e), (peers,), specs,
        [block(outs[0], falling), whole(outs[1]), whole(outs[2])], outs,
        [pltpu.VMEM((taps - 1, m, EDGE, e), F32), pltpu.VMEM((w, e), F32)], ins, flops=2 * peers * w * d * 3 * e)

    v = scatter(v_part, 3).reshape(m, tl, d) * gain
    in_grad = w32(out_grad) + r * v - u * (r * r * r) * jnp.mean(v * u, axis=2, keepdims=True)

    def to_owner(g):
        own = lax.all_to_all(g.astype(BF16), "shard", 0, 0, tiled=True)
        own = own.reshape(peers, dl, e).transpose(1, 0, 2).reshape(dl, peers * e)
        return sum_rep(own)
    grad_in_proj = jnp.concatenate([to_owner(g_x), to_owner(g_z)], axis=1)
    grad_gain = jnp.sum(grad_in_proj * w32(in_proj), axis=1) / w32(norm_gain)

    small = jnp.concatenate([vec, vec2, g_a * a_mat, g_dt, tn(xc.reshape(peers * w, e), ddbc.reshape(peers * w, -1)).T], axis=0)
    small = sum_rep(small)
    vec, vec2, g_a, g_dt, g_xp = (small[:8], small[8:16], small[16:16 + n], small[16 + n:16 + n + rank], small[16 + n + rank:])
    return (layer_out, in_grad, grad_gain, grad_in_proj, vec2[:taps], vec2[taps], g_xp[:rank + 2 * n].T, g_dt, vec[0],
            g_a, vec[1], sum_rep(g_out))


def solution(mesh):
    tok, ids = P(None, ("rep", "shard"), None), P(None, ("rep", "shard"))
    row, col, one = P("shard", None), P(None, "shard"), P("shard")
    return jax.shard_map(
        on_device,
        mesh=mesh,
        in_specs=(tok, ids, tok, one, row, col, one, row, col, one, col, one, row),
        out_specs=(tok, tok, one, row, col, one, row, col, one, col, one, row),
        check_vma=False,
    )
```

```python
import functools
import jax
import jax.numpy as jnp
from jax import lax
from jax.sharding import PartitionSpec as P
from jax.experimental import pallas as pl
from jax.experimental.pallas import tpu as pltpu

F32, BF16 = jnp.float32, jnp.bfloat16
LOG2E, LN2 = 1.4426950408889634, 0.6931471805599453
EDGE = 8
VMEM = 56 << 20


def nt(a, b):
    return lax.dot_general(a, b, (((1,), (1,)), ((), ())), preferred_element_type=F32)


def tn(a, b):
    return lax.dot_general(a, b, (((0,), (0,)), ((), ())), preferred_element_type=F32)


def mm(a, b):
    return jnp.dot(a, b, preferred_element_type=F32)


def softplus(v):
    return jnp.maximum(v, 0.0) + jnp.log1p(jnp.exp(-jnp.abs(v)))


def wide(v, e):
    return jnp.concatenate([v] * (e // 128), axis=1) if e > 128 else v


def at(start, size, unit=8):
    return pl.ds(pl.multiple_of(start, unit), size)


def call(kernel, grid, in_specs, out_specs, out_shape, scratch, args, flops=0, **params):
    size = sum(a.size * a.dtype.itemsize for a in args) + sum(s.size * s.dtype.itemsize for s in out_shape)
    return pl.pallas_call(
        kernel, grid=grid, in_specs=in_specs, out_specs=out_specs, out_shape=out_shape,
        scratch_shapes=scratch, compiler_params=pltpu.CompilerParams(vmem_limit_bytes=VMEM, **params),
        cost_estimate=pl.CostEstimate(flops=flops, bytes_accessed=size, transcendentals=0))(*args)


def whole(a):
    return pl.BlockSpec(a.shape, lambda i, r=len(a.shape): (0,) * r)


def block(a, order):
    return pl.BlockSpec((1,) + a.shape[1:], lambda i, r=len(a.shape): (order(i),) + (0,) * (r - 1))


def lags(x_ext, rows):
    return [x_ext[EDGE - k:EDGE - k + rows] for k in range(4)]


def convolve(lag, same, cw, cb):
    out = cb + cw[3:4] * lag[0]
    for k in range(1, 4):
        out = out + cw[3 - k:4 - k] * lag[k] * same[:, k - 1:k]
    return out


def normalise(rows, gain):
    u = rows.astype(F32)
    return (u * lax.rsqrt(jnp.mean(u * u, axis=1, keepdims=True) + 1e-5) * gain).astype(BF16)


def front(hid_ref, w_ref, halo_ref, mask_ref, cw_ref, cb_ref, xp_ref, gain_ref, xz_ref, xc_ref, part_ref, nu_ref, edge_ref,
          carry, *, m, e):
    @pl.when(pl.program_id(0) == 0)
    def _():
        edge = mm(normalise(halo_ref[...], gain_ref[...]), w_ref[:, :e]).astype(BF16)
        edge_ref[...] = edge
        carry[...] = edge.astype(F32)
    nu = normalise(hid_ref[0], gain_ref[...])
    nu_ref[0] = nu
    xz = mm(nu, w_ref[...]).astype(BF16)
    xz_ref[0] = xz
    rows = xz.shape[0] // m
    cw, cb = cw_ref[...], cb_ref[...]
    for i in range(m):
        x = xz[i * rows:(i + 1) * rows, :e].astype(F32)
        ext = jnp.concatenate([carry[i * EDGE:(i + 1) * EDGE], x], axis=0)
        carry[i * EDGE:(i + 1) * EDGE] = x[rows - EDGE:]
        conv = convolve(lags(ext, rows), mask_ref[0, i * rows:(i + 1) * rows], cw, cb)
        xc_ref[0, i * rows:(i + 1) * rows] = (conv * jax.nn.sigmoid(conv)).astype(BF16)
    part_ref[0] = nt(xp_ref[...], xc_ref[0])


def lattice(peers):
    y = 2 if peers <= 16 else 4
    return peers // (2 * y), y, 2


def greet(targets):
    barrier = pltpu.get_barrier_semaphore()
    for target in targets:
        pl.semaphore_signal(barrier, inc=1, device_id={"shard": target}, device_id_type=pl.DeviceIdType.MESH)
    pl.semaphore_wait(barrier, len(targets))


def remote(src, dst, send, recv, target):
    return pltpu.make_async_remote_copy(src_ref=src, dst_ref=dst, send_sem=send, recv_sem=recv,
                                        device_id={"shard": target}, device_id_type=pl.DeviceIdType.MESH)


def spread_low(total, n):
    rows = jnp.concatenate([total, jnp.zeros((256 - total.shape[0], total.shape[1]), F32)], axis=0).T
    rank = total.shape[0] - 2 * n
    out = [rows[:, :rank].astype(BF16)]
    rest = rows[:, rank:]
    hi = rest.astype(BF16)
    mid = (rest - hi.astype(F32)).astype(BF16)
    lo = (rest - hi.astype(F32) - mid.astype(F32)).astype(BF16)
    for k in range(2):
        out += [p[:, k * n:(k + 1) * n] for p in (hi, mid, lo)]
    out.append(jnp.zeros((rows.shape[0], 128 - 6 * n), BF16))
    return jnp.concatenate(out, axis=1)


def spread_plain(total, n):
    return jnp.concatenate([total, jnp.zeros((256 - total.shape[0], total.shape[1]), F32)], axis=0).T.astype(BF16)


def allsum_kernel(part, out, rc, ac, ry, ay, rz, send, recv, *, dims, chunks, finish):
    nz, ny, _ = dims
    me = lax.axis_index("shard")
    c, y, z = me % 2, (me // 2) % ny, me // (2 * ny)
    where = lambda a, b, d: (a * ny + b) * 2 + d
    across = where(z, y, 1 - c)
    ys = [lax.rem(y + k, ny) for k in range(1, ny)]
    zs = [lax.rem(z + k, nz) for k in range(1, nz)]
    greet([across] + [where(z, b, c) for b in ys] + [where(a, y, c) for a in zs])
    width = part.shape[-1] // chunks
    lanes = [pl.ds(q * width, width) for q in range(chunks)]
    rows = [pl.ds(q * width, width) for q in range(chunks)]

    def start(copies):
        for copy in copies:
            copy.start()
        return copies

    def finish_all(copies):
        for copy in copies:
            copy.wait()
    base = [0]

    def sems(count):
        base[0] += count
        return [(send.at[base[0] - count + k], recv.at[base[0] - count + k]) for k in range(count)]

    first = []
    for q in range(chunks):
        (s, r), = sems(1)
        first.append(start([remote(part.at[:, :, 1 - c, :, lanes[q]], rc.at[q], s, r, across)]))
    second = []
    for q in range(chunks):
        finish_all(first[q])
        for a in range(nz):
            for b in range(ny):
                ac[q, a, b] = part[a, b, c, :, q * width:(q + 1) * width] + rc[q, a, b]
        second.append(start([remote(ac.at[q, :, b], ry.at[q, k], *sem, where(z, b, c))
                             for k, (b, sem) in enumerate(zip(ys, sems(ny - 1)))]))
    third = []
    for q in range(chunks):
        finish_all(second[q])
        for a in range(nz):
            got = ac[q, a, y]
            for k in range(ny - 1):
                got = got + ry[q, k, a]
            ay[q, a] = got
        third.append(start([remote(ay.at[q, a], rz.at[q, k], *sem, where(a, y, c))
                            for k, (a, sem) in enumerate(zip(zs, sems(nz - 1)))]))
    fourth = []
    for q in range(chunks):
        finish_all(third[q])
        got = ay[q, z]
        for k in range(nz - 1):
            got = got + rz[q, k]
        out[z, y, c, q * width:(q + 1) * width] = finish(got)
        mine = out.at[z, y, c, rows[q]]
        fourth.append(start([remote(mine, mine, *sem, where(a, y, c)) for a, sem in zip(zs, sems(nz - 1))]))
    fifth = []
    for q in range(chunks):
        finish_all(fourth[q])
        mine = out.at[:, y, c, rows[q]]
        fifth.append(start([remote(mine, mine, *sem, where(z, b, c)) for b, sem in zip(ys, sems(ny - 1))]))
    last = []
    for q in range(chunks):
        finish_all(fifth[q])
        mine = out.at[:, :, c, rows[q]]
        (s, r), = sems(1)
        last.append(start([remote(mine, mine, s, r, across)]))
    for q in range(chunks):
        finish_all(last[q])


def allsum(part, finish, collective_id):
    peers, cols, w = part.shape
    dims = lattice(peers)
    nz, ny, nc = dims
    chunks = w // 128
    copies = 2 * chunks * (1 + ny - 1 + nz - 1)
    out = pl.pallas_call(
        functools.partial(allsum_kernel, dims=dims, chunks=chunks, finish=finish),
        out_shape=jax.ShapeDtypeStruct((nz, ny, nc, w, 256), BF16),
        in_specs=[pl.BlockSpec(memory_space=pltpu.VMEM)],
        out_specs=pl.BlockSpec(memory_space=pltpu.VMEM),
        scratch_shapes=[pltpu.VMEM((chunks, nz, ny, cols, 128), F32), pltpu.VMEM((chunks, nz, ny, cols, 128), F32),
                        pltpu.VMEM((chunks, ny - 1, nz, cols, 128), F32), pltpu.VMEM((chunks, nz, cols, 128), F32),
                        pltpu.VMEM((chunks, nz - 1, cols, 128), F32),
                        pltpu.SemaphoreType.DMA((copies,)), pltpu.SemaphoreType.DMA((copies,))],
        compiler_params=pltpu.CompilerParams(collective_id=collective_id, has_side_effects=True, vmem_limit_bytes=VMEM),
    )(part.reshape(nz, ny, nc, cols, w))
    return out.reshape(peers, w, 256)


def gather_kernel(x, small, out, small_out, send, recv, s_send, s_recv, own_sem, *, dims, chunks):
    nz, ny, _ = dims
    me = lax.axis_index("shard")
    c, y, z = me % 2, (me // 2) % ny, me // (2 * ny)
    where = lambda a, b, d: (a * ny + b) * 2 + d
    across = where(z, y, 1 - c)
    ys = [lax.rem(y + k, ny) for k in range(1, ny)]
    ys_from = [lax.rem(y + ny - k, ny) for k in range(1, ny)]
    zs = [lax.rem(z + k, nz) for k in range(1, nz)]
    greet([across] + [where(z, b, c) for b in ys] + [where(a, y, c) for a in zs])
    size = x.shape[0] // chunks
    rows = [pl.ds(q * size, size) for q in range(chunks)]

    keep = pltpu.make_async_copy(small, small_out.at[z, y, c], own_sem.at[0])
    keep.start()
    whole_own = pltpu.make_async_copy(x, out.at[z, y, c], own_sem.at[1])
    whole_own.start()

    kinds = 2 * nz - 1
    offset = [0] + [-1 - j for j in range(nz - 1)] + [1 + j for j in range(nz - 1)]

    def valid(kind):
        return (z + offset[kind] >= 0) & (z + offset[kind] < nz)

    def sems(group, kind, q):
        at_ = (group * kinds + kind) * chunks + q
        return send.at[at_], recv.at[at_]

    def hop(kind, q, up):
        there = out.at[z + offset[kind], y, c, rows[q]]
        src = x.at[rows[q]] if kind == 0 else there
        j = -offset[kind] if up else offset[kind]
        to_kind = 1 + j if up else nz + j
        return remote(src, there, *sems(0, to_kind, q), where(z + 1 if up else z - 1, y, c))

    def can_hop(kind, up):
        return valid(kind) & ((z + 1 < nz) if up else (z >= 1))

    def over_y(kind, q, k):
        there = out.at[z + offset[kind], y, c, rows[q]]
        src = x.at[rows[q]] if kind == 0 else there
        return remote(src, there, *sems(1 + k, kind, q), where(z, ys[k], c))

    def over_core(kind, q, k):
        there = out.at[z + offset[kind], y if k == 0 else ys_from[k - 1], c, rows[q]]
        src = x.at[rows[q]] if kind == 0 and k == 0 else there
        return remote(src, there, *sems(ny + k, kind, q), across)

    def landed(kind, q, b, d, group):
        there = out.at[z + offset[kind], b, d, rows[q]]
        return remote(there, there, *sems(group, kind, q), across)

    def onward(kind, q):
        if kind == 0:
            ups = [True, False]
        elif kind < nz:
            ups = [True] if kind < nz - 1 else []
        else:
            ups = [False] if kind < kinds - 1 else []
        for up in ups:
            @pl.when(can_hop(kind, up))
            def _(up=up):
                hop(kind, q, up).start()
        for k in range(ny - 1):
            over_y(kind, q, k).start()
        over_core(kind, q, 0).start()

    tiny = []

    def tiny_start(copies):
        tiny.append(copies)
        for copy in copies:
            copy.start()

    def tiny_wait():
        for copy in tiny[-1]:
            copy.wait()

    tiny_start([remote(small, small_out.at[z, y, c], s_send.at[k], s_recv.at[k], where(a, y, c)) for k, a in enumerate(zs)])
    for q in range(chunks):
        onward(0, q)
    tiny_wait()
    keep.wait()
    tiny_start([remote(small_out.at[:, y, c], small_out.at[:, y, c], s_send.at[nz - 1 + k], s_recv.at[nz - 1 + k], where(z, b, c))
                for k, b in enumerate(ys)])

    def from_y(kind, q):
        @pl.when(valid(kind))
        def _():
            for k in range(1, ny):
                landed(kind, q, ys_from[k - 1], c, k).wait_recv()
                over_core(kind, q, k).start()

    waves = [[0]] + [[1 + j, nz + j] for j in range(nz - 1)]
    for number, wave in enumerate(waves):
        for q in range(chunks):
            for kind in wave:
                if kind:
                    @pl.when(valid(kind))
                    def _(kind=kind, q=q):
                        landed(kind, q, y, c, 0).wait_recv()
                        onward(kind, q)
        if number == 1:
            tiny_wait()
            last = small_out.at[:, :, c]
            tiny_start([remote(last, last, s_send.at[nz + ny - 2], s_recv.at[nz + ny - 2], across)])
        if number:
            for q in range(chunks):
                for kind in waves[number - 1]:
                    from_y(kind, q)
    for q in range(chunks):
        for kind in waves[-1]:
            from_y(kind, q)
    tiny_wait()
    for kind in range(kinds):
        @pl.when(valid(kind))
        def _(kind=kind):
            for q in range(chunks):
                for k in range(ny):
                    landed(kind, q, y if k == 0 else ys_from[k - 1], 1 - c, ny + k).wait_recv()
                    over_core(kind, q, k).wait_send()
                for k in range(ny - 1):
                    over_y(kind, q, k).wait_send()
        for up in (True, False):
            j = -offset[kind] if up else offset[kind]
            if 0 <= j < nz - 1:
                @pl.when(can_hop(kind, up))
                def _(kind=kind, up=up):
                    for q in range(chunks):
                        hop(kind, q, up).wait_send()
    whole_own.wait()


def gather(x, small, collective_id, chunks=4):
    w, d = x.shape
    peers = lax.axis_size("shard")
    dims = lattice(peers)
    nz, ny, nc = dims
    copies = 2 * ny * (2 * nz - 1) * chunks
    out, tiles = pl.pallas_call(
        functools.partial(gather_kernel, dims=dims, chunks=chunks),
        out_shape=[jax.ShapeDtypeStruct((nz, ny, nc, w, d), x.dtype), jax.ShapeDtypeStruct((nz, ny, nc, 8, 128), F32)],
        in_specs=[pl.BlockSpec(memory_space=pl.ANY), pl.BlockSpec(memory_space=pltpu.VMEM)],
        out_specs=[pl.BlockSpec(memory_space=pl.ANY), pl.BlockSpec(memory_space=pltpu.VMEM)],
        scratch_shapes=[pltpu.SemaphoreType.DMA((copies,)), pltpu.SemaphoreType.DMA((copies,)),
                        pltpu.SemaphoreType.DMA((nz + ny,)), pltpu.SemaphoreType.DMA((nz + ny,)), pltpu.SemaphoreType.DMA((2,))],
        compiler_params=pltpu.CompilerParams(collective_id=collective_id, has_side_effects=True, vmem_limit_bytes=VMEM),
        cost_estimate=pl.CostEstimate(flops=8 * 10 ** 10, bytes_accessed=2 * peers * w * d, transcendentals=0),
    )(x, small)
    return out.reshape(peers, w, d), tiles.reshape(peers, 8, 128)


def scatter_kernel(part, out, own, rc, ry, rz, load, send, recv, *, dims, chunks):
    nz, ny, _ = dims
    me = lax.axis_index("shard")
    c, y, z = me % 2, (me // 2) % ny, me // (2 * ny)
    where = lambda a, b, d: (a * ny + b) * 2 + d
    across = where(z, y, 1 - c)
    ys = [lax.rem(y + k, ny) for k in range(1, ny)]
    zs = [lax.rem(z + k, nz) for k in range(1, nz)]
    greet([across] + [where(z, b, c) for b in ys] + [where(a, y, c) for a in zs])
    size = part.shape[3] // chunks
    rows = [pl.ds(q * size, size) for q in range(chunks)]
    per = 1 + ny - 1 + nz - 1

    def pair(q, k):
        return send.at[q * per + k], recv.at[q * per + k]
    loads, first, second, third = [], [], [None] * chunks, [None] * chunks
    for q in range(chunks):
        loads.append(pltpu.make_async_copy(part.at[:, :, c, rows[q]], own.at[:, :, rows[q]], load.at[q]))
        first.append(remote(part.at[:, :, 1 - c, rows[q]], rc.at[:, :, rows[q]], *pair(q, 0), across))
        loads[q].start()
        first[q].start()

    def over_core(q):
        loads[q].wait()
        first[q].wait()

        def add(a, _):
            i, j = a // ny, a % ny
            own[i, j, rows[q]] = (own[i, j, rows[q]].astype(F32) + rc[i, j, rows[q]].astype(F32)).astype(BF16)
            return 0
        lax.fori_loop(0, nz * ny, add, 0)
        second[q] = [remote(own.at[:, b, rows[q]], ry.at[k, :, rows[q]], *pair(q, 1 + k), where(z, b, c))
                     for k, b in enumerate(ys)]
        for copy in second[q]:
            copy.start()

    def over_y(q):
        for copy in second[q]:
            copy.wait()

        def add(a, _):
            total = own[a, y, rows[q]].astype(F32)
            for k in range(ny - 1):
                total = total + ry[k, a, rows[q]].astype(F32)
            own[a, y, rows[q]] = total.astype(BF16)
            return 0
        lax.fori_loop(0, nz, add, 0)
        third[q] = [remote(own.at[a, y, rows[q]], rz.at[k, rows[q]], *pair(q, ny + k), where(a, y, c))
                    for k, a in enumerate(zs)]
        for copy in third[q]:
            copy.start()

    def over_z(q):
        for copy in third[q]:
            copy.wait()
        total = own[z, y, rows[q]].astype(F32)
        for k in range(nz - 1):
            total = total + rz[k, rows[q]].astype(F32)
        out[rows[q]] = total

    for s in range(chunks + 4):
        if s < chunks:
            over_core(s)
        if 0 <= s - 2 < chunks:
            over_y(s - 2)
        if 0 <= s - 4 < chunks:
            over_z(s - 4)


def scatter(part, collective_id):
    peers, w, d = part.shape
    dims = lattice(peers)
    nz, ny, nc = dims
    chunks = w // 32
    copies = chunks * (1 + ny - 1 + nz - 1)
    return pl.pallas_call(
        functools.partial(scatter_kernel, dims=dims, chunks=chunks),
        out_shape=jax.ShapeDtypeStruct((w, d), F32),
        in_specs=[pl.BlockSpec(memory_space=pl.ANY)],
        out_specs=pl.BlockSpec(memory_space=pltpu.VMEM),
        scratch_shapes=[pltpu.VMEM((nz, ny, w, d), BF16), pltpu.VMEM((nz, ny, w, d), BF16),
                        pltpu.VMEM((ny - 1, nz, w, d), BF16), pltpu.VMEM((nz - 1, w, d), BF16),
                        pltpu.SemaphoreType.DMA((chunks,)),
                        pltpu.SemaphoreType.DMA((copies,)), pltpu.SemaphoreType.DMA((copies,))],
        compiler_params=pltpu.CompilerParams(collective_id=collective_id, has_side_effects=True, vmem_limit_bytes=VMEM),
        cost_estimate=pl.CostEstimate(flops=8 * 10 ** 10, bytes_accessed=2 * peers * w * d, transcendentals=0),
    )(part.reshape(nz, ny, nc, w, d))


def fill(low_ref, bcs_scr, bc_scr, n):
    bcs_scr[...] = low_ref[0, :, 128:].astype(F32)
    lane = lax.broadcasted_iota(jnp.int32, (n, 128), 1)
    sub = lax.broadcasted_iota(jnp.int32, (n, 128), 0)
    mask = (lane % n) == sub
    r = lax.broadcasted_iota(jnp.int32, (128, 256), 0)
    c = lax.broadcasted_iota(jnp.int32, (128, 256), 1)
    ones = jnp.where((r >= 3 * n) == (c >= 128), 1.0, 0.0).astype(BF16)
    group = 128

    def body(g, _):
        rows = [jnp.where(mask, bcs_scr[pl.ds(g * group + j, 1), :], 0.0).astype(BF16) for j in range(group)]
        bc_scr[at(g * (group * n), group * n, 128), :] = mm(jnp.concatenate(rows, axis=0), ones)
        return 0
    lax.fori_loop(0, bcs_scr.shape[0] // group, body, 0)


def fold_rows(vals, sub):
    for k in (1, 2, 4):
        mask = (sub & k) == 0
        vals = [jnp.where(mask, a, b) + pltpu.roll(jnp.where(mask, b, a), 8 - k, 0)
                for a, b in zip(vals[::2], vals[1::2])]
    return vals[0]


def ahead(low_ref, xz_ref, xc_ref, mask_ref, dy_ref, wo_ref, wdt_ref, dtb_ref, a2_ref,
          cks_ref, ckp_ref, end_ref, dg_ref, s_scr, p_scr, f_scr, sd_scr, dx_scr, dy_scr, bcs_scr, bc_scr, *, m, n, e):
    b = pl.program_id(0)
    @pl.when(b == 0)
    def _():
        s_scr[...] = jnp.zeros_like(s_scr)
        p_scr[...] = jnp.ones_like(p_scr)
        f_scr[...] = jnp.zeros_like(f_scr)
    cks_ref[0] = s_scr[...]
    ckp_ref[0] = p_scr[...]
    fill(low_ref, bcs_scr, bc_scr, n)
    step = softplus(mm(low_ref[0, :, :128], wdt_ref[...]) + dtb_ref[...])
    sd_scr[...] = jnp.where(mask_ref[0, :, 0:1] > 0.0, step, 1e30)
    dx_scr[...] = step * xc_ref[0].astype(F32)
    dg = nt(dy_ref[0], wo_ref[...])
    dg_ref[0] = dg
    z = xz_ref[0, :, e:].astype(F32)
    dy_scr[...] = dg * (z * jax.nn.sigmoid(z))
    a2 = a2_ref[...]
    rows = sd_scr.shape[0] // m
    un = 16

    def group(g, carry):
        s, p, f = [list(c) for c in carry]
        for j in range(un):
            for i in range(m):
                t = i * rows + g * un + j
                bc = bc_scr[at(t * n, n, n), :]
                bb, cc = wide(bc[:, :128], e), wide(bc[:, 128:], e)
                a = jnp.exp2(sd_scr[pl.ds(t, 1), :] * a2)
                s[i] = a * s[i] + bb * dx_scr[pl.ds(t, 1), :]
                p[i] = p[i] * a
                f[i] = f[i] + p[i] * (cc * dy_scr[pl.ds(t, 1), :])
        return tuple(s), tuple(p), tuple(f)
    done = lax.fori_loop(0, rows // un, group,
                         tuple(tuple(scr[i] for i in range(m)) for scr in (s_scr, p_scr, f_scr)))
    for scr, vals in zip((s_scr, p_scr, f_scr), done):
        for i in range(m):
            scr[i] = vals[i]

    @pl.when(b == pl.num_programs(0) - 1)
    def _():
        end_ref[0] = s_scr[...]
        end_ref[1] = p_scr[...]
        end_ref[2] = f_scr[...]


def behind(low_ref, xz_ref, xc_ref, mask_ref, dy_ref, dg_ref, nu_ref, cks_ref, ckp_ref,
           wo_ref, wdt_ref, dtb_ref, a2_ref, skip_ref, hin_ref, qin_ref,
           out_ref, dz_ref, dxc_ref, part_ref, go_ref, gdt_ref, ga_ref, vec_ref, gz_ref,
           h_scr, a_scr, q_scr, bcs_scr, bc_scr, pre_scr, st_scr, sd_scr, dx_scr, dy_scr, y_scr, da_scr, gb_scr, *, m, n, e):
    b = pl.program_id(0)
    @pl.when(b == 0)
    def _():
        greet([lax.axis_index("shard") + 1 - 2 * (lax.axis_index("shard") % 2)])
        q_scr[...] = qin_ref[...]
        for ref in (go_ref, gdt_ref, ga_ref, vec_ref, gz_ref):
            ref[...] = jnp.zeros_like(ref)
    fill(low_ref, bcs_scr, bc_scr, n)
    pre = mm(low_ref[0, :, :128], wdt_ref[...]) + dtb_ref[...]
    pre_scr[...] = pre
    step = softplus(pre)
    st_scr[...] = step
    sd_scr[...] = jnp.where(mask_ref[0, :, 0:1] > 0.0, step, 1e30)
    dx_scr[...] = step * xc_ref[0].astype(F32)
    z = xz_ref[0, :, e:].astype(F32)
    dy_scr[...] = dg_ref[0] * (z * jax.nn.sigmoid(z))
    a2 = a2_ref[...]
    sub = lax.broadcasted_iota(jnp.int32, (8, e), 0)
    rows = sd_scr.shape[0] // m
    lanes = lax.broadcasted_iota(jnp.int32, (n, rows), 1)
    un = 32
    for i in range(m):
        r0 = i * rows
        h0 = cks_ref[0, i] + ckp_ref[0, i] * hin_ref[i]
        h_scr[pl.ds(0, n), :] = h0

        def fwd(g, h, r0=r0):
            ys = []
            for j in range(un):
                t = g * un + j
                bc = bc_scr[at((r0 + t) * n, n, n), :]
                bb, cc = wide(bc[:, :128], e), wide(bc[:, 128:], e)
                a = jnp.exp2(sd_scr[pl.ds(r0 + t, 1), :] * a2)
                h = a * h + bb * dx_scr[pl.ds(r0 + t, 1), :]
                a_scr[at(t * n, n, n), :] = a
                h_scr[at(t * n + n, n, n), :] = h
                cy = cc * h
                ys.append(cy[:8] + cy[8:])
                if len(ys) == 8:
                    y_scr[at(r0 + t - 7, 8), :] = fold_rows(ys, sub)
                    ys = []
            return h
        lax.fori_loop(0, rows // un, fwd, h0)

        def bwd(g, carry, r0=r0):
            q, ga, hn, db, dc = carry
            das, gbs = [], []
            for j in range(un):
                t = rows - 1 - (g * un + j)
                bc = bc_scr[at((r0 + t) * n, n, n), :]
                bb, cc = wide(bc[:, :128], e), wide(bc[:, 128:], e)
                a = a_scr[at(t * n, n, n), :]
                hp = h_scr[at(t * n, n, n), :]
                dyr = dy_scr[pl.ds(r0 + t, 1), :]
                gt = cc * dyr + q
                q = a * gt
                da = q * hp
                ga = ga + da * st_scr[pl.ds(r0 + t, 1), :]
                d_a = da * a2
                g_b = gt * bb
                das.append(d_a[:8] + d_a[8:])
                gbs.append(g_b[:8] + g_b[8:])
                pb = gt * dx_scr[pl.ds(r0 + t, 1), :]
                pc = dyr * hn
                pb = sum(pb[:, k:k + 128] for k in range(0, e, 128))
                pc = sum(pc[:, k:k + 128] for k in range(0, e, 128))
                db = jnp.where(lanes == t, jnp.sum(pb, axis=1, keepdims=True), db)
                dc = jnp.where(lanes == t, jnp.sum(pc, axis=1, keepdims=True), dc)
                hn = hp
                if len(das) == 8:
                    da_scr[at(r0 + t, 8), :] = fold_rows(das[::-1], sub)
                    gb_scr[at(r0 + t, 8), :] = fold_rows(gbs[::-1], sub)
                    das, gbs = [], []
            return q, ga, hn, db, dc
        zero = jnp.zeros((n, rows), F32)
        q, ga, _, db, dc = lax.fori_loop(
            0, rows // un, bwd, (q_scr[i], ga_ref[...], h_scr[pl.ds(rows * n, n), :], zero, zero))
        q_scr[i] = q
        ga_ref[...] = ga
        part_ref[0, 128:128 + n, r0:r0 + rows] = db
        part_ref[0, 128 + n:128 + 2 * n, r0:r0 + rows] = dc

    z = xz_ref[0, :, e:].astype(F32)
    sz = jax.nn.sigmoid(z)
    xc = xc_ref[0].astype(F32)
    skip = skip_ref[...]
    y = y_scr[...] + skip * xc
    gated = (y * (z * sz)).astype(BF16)
    out_ref[0] = mm(gated, wo_ref[...]).astype(BF16)
    go_ref[...] += tn(gated, dy_ref[0])
    dz = (dg_ref[0] * y * (sz * (1.0 + z * (1.0 - sz)))).astype(BF16)
    dz_ref[0] = dz
    gz_ref[...] += tn(nu_ref[0], dz)
    gb = gb_scr[...]
    dy_y = dy_scr[...]
    dxc_ref[0] = dy_y * skip + st_scr[...] * gb
    d_pre = (da_scr[...] * LN2 + xc * gb) * jax.nn.sigmoid(pre_scr[...])
    d_low = d_pre.astype(BF16)
    gdt_ref[...] += tn(low_ref[0, :, :128], d_low)
    part_ref[0, :128, :] = nt(wdt_ref[...], d_low)
    vec_ref[0:1] += jnp.sum(d_pre, axis=0, keepdims=True)
    vec_ref[1:2] += jnp.sum(dy_y * xc, axis=0, keepdims=True)


def dsilu(v):
    s = jax.nn.sigmoid(v)
    return s * (1.0 + v * (1.0 - s))


def back(xz_ref, prev_ref, edge_ref, mask_ref, dxc_ref, ddbc_ref, dz_ref, nu_ref, next_ref, w_ref, xpt_ref, cw_ref, cb_ref,
         v_ref, gx_ref, vec_ref, carry, dx_scr, *, m, e):
    b = pl.program_id(0)
    @pl.when(b == 0)
    def _():
        carry[...] = next_ref[...]
        gx_ref[...] = jnp.zeros_like(gx_ref)
        vec_ref[...] = jnp.zeros_like(vec_ref)
    first = b == pl.num_programs(0) - 1
    rows = xz_ref.shape[1] // m
    cw, cb = cw_ref[...], cb_ref[...]
    dxc_all = dxc_ref[0] + mm(ddbc_ref[0], xpt_ref[...])
    for i in range(m):
        part = slice(i * rows, (i + 1) * rows)
        x = xz_ref[0, part, :e].astype(F32)
        before = prev_ref[0, (i + 1) * rows - 2 * EDGE:(i + 1) * rows, :e].astype(F32)[EDGE:]
        before = jnp.where(first, edge_ref[i * EDGE:(i + 1) * EDGE], before)
        lag = lags(jnp.concatenate([before, x], axis=0), rows)
        same = mask_ref[0, part]
        dconv = dxc_all[part] * dsilu(convolve(lag, same, cw, cb))
        vec_ref[4:5] += jnp.sum(dconv, axis=0, keepdims=True)
        vec_ref[3:4] += jnp.sum(dconv * x, axis=0, keepdims=True)
        dx = cw[3:4] * dconv
        for k in range(1, 4):
            masked = dconv * same[:, k - 1:k]
            vec_ref[3 - k:4 - k] += jnp.sum(masked * lag[k], axis=0, keepdims=True)
            sent = cw[3 - k:4 - k] * masked
            ext = jnp.concatenate([sent, carry[k - 1, i]], axis=0)
            dx = dx + ext[k:k + rows]
            carry[k - 1, i] = sent[:EDGE]
        dx_scr[part] = dx
    dx = dx_scr[...].astype(BF16)
    v_ref[0] = nt(jnp.concatenate([dx, dz_ref[0]], axis=1), w_ref[...]).astype(BF16)
    gx_ref[...] += tn(nu_ref[0], dx)


def shift_rep(value, steps):
    count = lax.axis_size("rep")
    first, last = max(0, -steps), min(count, count - steps)
    return lax.ppermute(value, "rep", [(i, i + steps) for i in range(first, last)])


def sum_rep(value):
    if lax.axis_size("rep") != 2:
        return lax.psum(value.astype(F32), "rep")
    low = value.astype(BF16)
    other = lax.ppermute(low, "rep", [(0, 1), (1, 0)])
    return low.astype(F32) + other.astype(F32)


def on_device(hidden_in, segment_ids, out_grad, norm_gain, in_proj, conv_weight, conv_bias, x_proj,
              dt_weight, dt_bias, a_log, d_skip, out_proj):
    peers, reps = lax.axis_size("shard"), lax.axis_size("rep")
    rep = lax.axis_index("rep")
    m, tl, d = hidden_in.shape
    t, w = tl * peers, m * tl
    dl = in_proj.shape[0]
    e = x_proj.shape[0]
    n, rank, taps = a_log.shape[0], dt_weight.shape[0], conv_weight.shape[0]
    w32 = lambda v: v.astype(F32)
    shp = jax.ShapeDtypeStruct
    rising = lambda i: i
    falling = lambda i: peers - 1 - i

    own = jnp.pad(jnp.concatenate([w32(segment_ids), jnp.pad(w32(norm_gain)[None], ((0, 0), (0, 128 - dl)))], axis=0),
                  ((0, 7 - m), (0, 0)))
    w_split = in_proj.reshape(dl, 2, peers, e).transpose(2, 0, 1, 3).reshape(peers * dl, 2 * e)
    own, w_split = lax.optimization_barrier((own, w_split))
    w_cols = lax.all_to_all(w_split, "shard", 0, 0, tiled=True)
    hid_all, tiles = gather(hidden_in.reshape(w, d), own, 4)
    gain = tiles[:, m, :dl].reshape(1, d)
    ids = tiles[:, :m, :tl].astype(jnp.int32)
    later, hid_all = lax.optimization_barrier((out_grad, hid_all))
    dy_all = lax.all_gather(later.reshape(w, d), "shard")
    u = w32(hidden_in)
    r = lax.rsqrt(jnp.mean(u * u, axis=2, keepdims=True) + 1e-5)

    row_ids = ids.transpose(1, 0, 2).reshape(m, t)
    before = jnp.where(rep > 0, shift_rep(row_ids[:, t - taps + 1:], 1), -1)
    ext = jnp.concatenate([before, row_ids], axis=1)
    same = jnp.stack([w32(ext[:, taps - 1 - k:taps - 1 - k + t] == row_ids) for k in range(1, taps)], axis=-1)
    mask = jnp.pad(same, ((0, 0), (0, 0), (0, 8 - same.shape[-1])))
    mask = mask.reshape(m, peers, tl, 8).transpose(1, 0, 2, 3).reshape(peers, w, 8)
    halo = shift_rep(hid_all[peers - 1].reshape(m, tl, d)[:, tl - EDGE:].reshape(m * EDGE, d), 1)

    cw, cb = w32(conv_weight), w32(conv_bias)[None]
    ins = [hid_all, w_cols, halo, mask, cw, cb, x_proj.T, gain]
    outs = [shp((peers, w, 2 * e), BF16), shp((peers, w, e), BF16), shp((peers, rank + 2 * n, w), F32),
            shp((peers, w, d), BF16), shp((m * EDGE, e), BF16)]
    xz, xc, part, nu_all, edge = call(
        functools.partial(front, m=m, e=e), (peers,),
        [block(hid_all, rising)] + [whole(a) for a in ins[1:3]] + [block(mask, rising)] + [whole(a) for a in ins[4:]],
        [block(a, rising) for a in outs[:4]] + [whole(outs[4])], outs,
        [pltpu.VMEM((m * EDGE, e), F32)], ins, flops=2 * peers * w * d * 2 * e)

    low = allsum(part, functools.partial(spread_low, n=n), 0)
    a_mat = -jnp.exp(w32(a_log))
    a2 = a_mat * LOG2E
    dtb, skip = w32(dt_bias)[None], w32(d_skip)[None]

    ins = [low, xz, xc, mask, dy_all, out_proj, dt_weight, dtb, a2]
    outs = [shp((peers, m, n, e), F32)] * 2 + [shp((3, m, n, e), F32), shp((peers, w, e), F32)]
    cks, ckp, end, dg = call(
        functools.partial(ahead, m=m, n=n, e=e), (peers,),
        [block(a, rising) for a in ins[:5]] + [whole(a) for a in ins[5:]],
        [block(outs[0], rising), block(outs[1], rising), whole(outs[2]), block(outs[3], rising)], outs,
        [pltpu.VMEM((m, n, e), F32)] * 3 + [pltpu.VMEM((w, e), F32)] * 3 + [pltpu.VMEM((w, 128), F32), pltpu.VMEM((w * n, 256), F32)],
        ins, flops=40 * 10 ** 9)

    ends = lax.all_gather(end, "rep")
    h_in = jnp.zeros((m, n, e), F32)
    q_in = jnp.zeros((m, n, e), F32)
    for k in range(reps - 1):
        o = reps - 1 - k
        h_in = jnp.where(k < rep, ends[k, 1] * h_in + ends[k, 0], h_in)
        q_in = jnp.where(o > rep, ends[o, 1] * q_in + ends[o, 2], q_in)

    ins = [low, xz, xc, mask, dy_all, dg, nu_all, cks, ckp, out_proj, dt_weight, dtb, a2, skip, h_in, q_in]
    outs = [shp((peers, w, d), BF16), shp((peers, w, e), BF16), shp((peers, w, e), F32),
            shp((peers, rank + 2 * n, w), F32), shp((e, d), F32), shp((rank, e), F32), shp((n, e), F32), shp((8, e), F32),
            shp((d, e), F32)]
    part_out, dz, dxc, part, g_out, g_dt, g_a, vec, g_z = call(
        functools.partial(behind, m=m, n=n, e=e), (peers,),
        [block(a, falling) for a in ins[:9]] + [whole(a) for a in ins[9:]],
        [block(a, falling) for a in outs[:4]] + [whole(a) for a in outs[4:]], outs,
        [pltpu.VMEM((tl * n + n, e), F32), pltpu.VMEM((tl * n, e), F32), pltpu.VMEM((m, n, e), F32),
         pltpu.VMEM((w, 128), F32), pltpu.VMEM((w * n, 256), F32)] + [pltpu.VMEM((w, e), F32)] * 8, ins, flops=100 * 10 ** 9, collective_id=5, has_side_effects=True)

    out_sum = scatter(part_out, 2).reshape(m, tl, d)
    layer_out = (u + out_sum).astype(BF16)

    ddbc = allsum(part, functools.partial(spread_plain, n=n), 1)
    xpt = jnp.pad(x_proj.T, ((0, 256 - x_proj.shape[1]), (0, 0)))

    x8 = w32(xz[0].reshape(m, tl, 2 * e)[:, :EDGE, :e])
    ext8 = jnp.concatenate([w32(edge).reshape(m, EDGE, e), x8], axis=1)
    same8 = mask[0].reshape(m, tl, 8)[:, :EDGE]
    conv8 = cb + cw[3] * x8
    for k in range(1, taps):
        conv8 = conv8 + cw[3 - k] * ext8[:, EDGE - k:2 * EDGE - k] * same8[:, :, k - 1:k]
    d8 = dxc[0].reshape(m, tl, e)[:, :EDGE] + mm(ddbc[0].reshape(m, tl, -1)[:, :EDGE].reshape(m * EDGE, -1), xpt).reshape(m, EDGE, e)
    d8 = d8 * dsilu(conv8)
    sent = jnp.stack([cw[3 - k] * d8 * same8[:, :, k - 1:k] for k in range(1, taps)])
    follow = shift_rep(sent, -1)

    ins = [xz, xz, w32(edge), mask, dxc, ddbc, dz, nu_all, follow, w_cols, xpt, cw, cb]
    outs = [shp((peers, w, d), BF16), shp((d, e), F32), shp((8, e), F32)]
    earlier = lambda i: jnp.maximum(peers - 2 - i, 0)
    specs = [block(a, falling) for a in ins[:8]] + [whole(a) for a in ins[8:]]
    specs[1], specs[2] = block(xz, earlier), whole(ins[2])
    v_part, g_x, vec2 = call(
        functools.partial(back, m=m, e=e), (peers,), specs,
        [block(outs[0], falling), whole(outs[1]), whole(outs[2])], outs,
        [pltpu.VMEM((taps - 1, m, EDGE, e), F32), pltpu.VMEM((w, e), F32)], ins, flops=2 * peers * w * d * 3 * e)

    g_out = sum_rep(g_out)
    v_part, g_out = lax.optimization_barrier((v_part, g_out))
    v = scatter(v_part, 3).reshape(m, tl, d) * gain
    in_grad = w32(out_grad) + r * v - u * (r * r * r) * jnp.mean(v * u, axis=2, keepdims=True)

    def to_owner(g):
        own = lax.all_to_all(g.astype(BF16), "shard", 0, 0, tiled=True)
        own = own.reshape(peers, dl, e).transpose(1, 0, 2).reshape(dl, peers * e)
        return sum_rep(own)
    grad_in_proj = jnp.concatenate([to_owner(g_x), to_owner(g_z)], axis=1)
    grad_gain = jnp.sum(grad_in_proj * w32(in_proj), axis=1) / w32(norm_gain)

    small = jnp.concatenate([vec, vec2, g_a * a_mat, g_dt, tn(xc.reshape(peers * w, e), ddbc.reshape(peers * w, -1)).T], axis=0)
    small = sum_rep(small)
    vec, vec2, g_a, g_dt, g_xp = (small[:8], small[8:16], small[16:16 + n], small[16 + n:16 + n + rank], small[16 + n + rank:])
    return (layer_out, in_grad, grad_gain, grad_in_proj, vec2[:taps], vec2[taps], g_xp[:rank + 2 * n].T, g_dt, vec[0],
            g_a, vec[1], g_out)


def solution(mesh):
    tok, ids = P(None, ("rep", "shard"), None), P(None, ("rep", "shard"))
    row, col, one = P("shard", None), P(None, "shard"), P("shard")
    return jax.shard_map(
        on_device,
        mesh=mesh,
        in_specs=(tok, ids, tok, one, row, col, one, row, col, one, col, one, row),
        out_specs=(tok, tok, one, row, col, one, row, col, one, col, one, row),
        check_vma=False,
    )
```

```python
import functools
import jax
import jax.numpy as jnp
from jax import lax
from jax.sharding import PartitionSpec as P
from jax.experimental import pallas as pl
from jax.experimental.pallas import tpu as pltpu

F32, BF16 = jnp.float32, jnp.bfloat16
LOG2E, LN2 = 1.4426950408889634, 0.6931471805599453
EDGE = 8
VMEM = 56 << 20


def nt(a, b):
    return lax.dot_general(a, b, (((1,), (1,)), ((), ())), preferred_element_type=F32)


def tn(a, b):
    return lax.dot_general(a, b, (((0,), (0,)), ((), ())), preferred_element_type=F32)


def mm(a, b):
    return jnp.dot(a, b, preferred_element_type=F32)


def softplus(v):
    return jnp.maximum(v, 0.0) + jnp.log1p(jnp.exp(-jnp.abs(v)))


def wide(v, e):
    return jnp.concatenate([v] * (e // 128), axis=1) if e > 128 else v


def at(start, size, unit=8):
    return pl.ds(pl.multiple_of(start, unit), size)


def call(kernel, grid, in_specs, out_specs, out_shape, scratch, args, flops=0, **params):
    size = sum(a.size * a.dtype.itemsize for a in args) + sum(s.size * s.dtype.itemsize for s in out_shape)
    return pl.pallas_call(
        kernel, grid=grid, in_specs=in_specs, out_specs=out_specs, out_shape=out_shape,
        scratch_shapes=scratch, compiler_params=pltpu.CompilerParams(vmem_limit_bytes=VMEM, **params),
        cost_estimate=pl.CostEstimate(flops=flops, bytes_accessed=size, transcendentals=0))(*args)


def whole(a):
    return pl.BlockSpec(a.shape, lambda i, r=len(a.shape): (0,) * r)


def block(a, order):
    return pl.BlockSpec((1,) + a.shape[1:], lambda i, r=len(a.shape): (order(i),) + (0,) * (r - 1))


def lags(x_ext, rows):
    return [x_ext[EDGE - k:EDGE - k + rows] for k in range(4)]


def convolve(lag, same, cw, cb):
    out = cb + cw[3:4] * lag[0]
    for k in range(1, 4):
        out = out + cw[3 - k:4 - k] * lag[k] * same[:, k - 1:k]
    return out


def normalise(rows, gain):
    u = rows.astype(F32)
    return (u * lax.rsqrt(jnp.mean(u * u, axis=1, keepdims=True) + 1e-5) * gain).astype(BF16)


def front(hid_ref, w_ref, halo_ref, mask_ref, cw_ref, cb_ref, xp_ref, gain_ref, xz_ref, xc_ref, nu_ref, edge_ref,
          *rest, m, e):
    parts, carry = rest[:m], rest[m]
    @pl.when(pl.program_id(0) == 0)
    def _():
        edge = mm(normalise(halo_ref[...], gain_ref[...]), w_ref[:, :e]).astype(BF16)
        edge_ref[...] = edge
        carry[...] = edge.astype(F32)
    nu = normalise(hid_ref[0], gain_ref[...])
    nu_ref[0] = nu
    xz = mm(nu, w_ref[...]).astype(BF16)
    xz_ref[0] = xz
    rows = xz.shape[0] // m
    cw, cb = cw_ref[...], cb_ref[...]
    for i in range(m):
        x = xz[i * rows:(i + 1) * rows, :e].astype(F32)
        ext = jnp.concatenate([carry[i * EDGE:(i + 1) * EDGE], x], axis=0)
        carry[i * EDGE:(i + 1) * EDGE] = x[rows - EDGE:]
        conv = convolve(lags(ext, rows), mask_ref[0, i * rows:(i + 1) * rows], cw, cb)
        xc = (conv * jax.nn.sigmoid(conv)).astype(BF16)
        xc_ref[0, i * rows:(i + 1) * rows] = xc
        parts[i][0] = nt(xp_ref[...], xc)


def lattice(peers):
    y = 2 if peers <= 16 else 4
    return peers // (2 * y), y, 2


def place(target):
    return target if isinstance(target, dict) else {"shard": target}


def greet(targets):
    barrier = pltpu.get_barrier_semaphore()
    for target in targets:
        pl.semaphore_signal(barrier, inc=1, device_id=place(target), device_id_type=pl.DeviceIdType.MESH)
    pl.semaphore_wait(barrier, len(targets))


def remote(src, dst, send, recv, target):
    return pltpu.make_async_remote_copy(src_ref=src, dst_ref=dst, send_sem=send, recv_sem=recv,
                                        device_id=place(target), device_id_type=pl.DeviceIdType.MESH)


def spread_low(total, n):
    rows = jnp.concatenate([total, jnp.zeros((256 - total.shape[0], total.shape[1]), F32)], axis=0).T
    rank = total.shape[0] - 2 * n
    out = [rows[:, :rank].astype(BF16)]
    rest = rows[:, rank:]
    hi = rest.astype(BF16)
    mid = (rest - hi.astype(F32)).astype(BF16)
    lo = (rest - hi.astype(F32) - mid.astype(F32)).astype(BF16)
    for k in range(2):
        out += [p[:, k * n:(k + 1) * n] for p in (hi, mid, lo)]
    out.append(jnp.zeros((rows.shape[0], 128 - 6 * n), BF16))
    return jnp.concatenate(out, axis=1)


def spread_plain(total, n):
    return jnp.concatenate([total, jnp.zeros((256 - total.shape[0], total.shape[1]), F32)], axis=0).T.astype(BF16)


def allsum_kernel(*refs, dims, chunks, finish):
    parts = refs[:chunks]
    out, rc, ac, low, ry, rz, send, recv = refs[chunks:]
    nz, ny, _ = dims
    me = lax.axis_index("shard")
    c, y, z = me % 2, (me // 2) % ny, me // (2 * ny)
    where = lambda a, b, d: (a * ny + b) * 2 + d
    across = where(z, y, 1 - c)
    ys = [lax.rem(y + k, ny) for k in range(1, ny)]
    zs = [lax.rem(z + k, nz) for k in range(1, nz)]
    greet([across] + [where(z, b, c) for b in ys] + [where(a, y, c) for a in zs])
    width = parts[0].shape[-1]
    rows = [pl.ds(q * width, width) for q in range(chunks)]

    def start(copies):
        for copy in copies:
            copy.start()
        return copies

    def finish_all(copies):
        for copy in copies:
            copy.wait()
    base = [0]

    def sems(count):
        base[0] += count
        return [(send.at[base[0] - count + k], recv.at[base[0] - count + k]) for k in range(count)]

    first = []
    for q in range(chunks):
        (s, r), = sems(1)
        first.append(start([remote(parts[q].at[:, :, 1 - c], rc.at[q], s, r, across)]))
    second = []
    for q in range(chunks):
        finish_all(first[q])
        for a in range(nz):
            for b in range(ny):
                total = parts[q][a, b, c] + rc[q, a, b]
                ac[q, a, b] = total
                low[q, a, b] = total.astype(BF16)
        second.append(start([remote(low.at[q, :, b], ry.at[q, k], *sem, where(z, b, c))
                             for k, (b, sem) in enumerate(zip(ys, sems(ny - 1)))]))
    third = []
    for q in range(chunks):
        finish_all(second[q])
        for a in range(nz):
            got = ac[q, a, y]
            for k in range(ny - 1):
                got = got + ry[q, k, a].astype(F32)
            ac[q, a, y] = got
            low[q, a, y] = got.astype(BF16)
        third.append(start([remote(low.at[q, a, y], rz.at[q, k], *sem, where(a, y, c))
                            for k, (a, sem) in enumerate(zip(zs, sems(nz - 1)))]))
    fourth = []
    for q in range(chunks):
        finish_all(third[q])
        got = ac[q, z, y]
        for k in range(nz - 1):
            got = got + rz[q, k].astype(F32)
        out[z, y, c, q * width:(q + 1) * width] = finish(got)
        mine = out.at[z, y, c, rows[q]]
        fourth.append(start([remote(mine, mine, *sem, where(a, y, c)) for a, sem in zip(zs, sems(nz - 1))]))
    fifth = []
    for q in range(chunks):
        finish_all(fourth[q])
        mine = out.at[:, y, c, rows[q]]
        fifth.append(start([remote(mine, mine, *sem, where(z, b, c)) for b, sem in zip(ys, sems(ny - 1))]))
    last = []
    for q in range(chunks):
        finish_all(fifth[q])
        mine = out.at[:, :, c, rows[q]]
        (s, r), = sems(1)
        last.append(start([remote(mine, mine, s, r, across)]))
    for q in range(chunks):
        finish_all(last[q])


def allsum(parts, finish, collective_id):
    peers, cols, width = parts[0].shape
    w = width * len(parts)
    dims = lattice(peers)
    nz, ny, nc = dims
    chunks = len(parts)
    copies = 2 * chunks * (1 + ny - 1 + nz - 1)
    out = pl.pallas_call(
        functools.partial(allsum_kernel, dims=dims, chunks=chunks, finish=finish),
        out_shape=jax.ShapeDtypeStruct((nz, ny, nc, w, 256), BF16),
        in_specs=[pl.BlockSpec(memory_space=pltpu.VMEM)] * chunks,
        out_specs=pl.BlockSpec(memory_space=pltpu.VMEM),
        scratch_shapes=[pltpu.VMEM((chunks, nz, ny, cols, 128), F32), pltpu.VMEM((chunks, nz, ny, cols, 128), F32),
                        pltpu.VMEM((chunks, nz, ny, cols, 128), BF16), pltpu.VMEM((chunks, ny - 1, nz, cols, 128), BF16),
                        pltpu.VMEM((chunks, nz - 1, cols, 128), BF16),
                        pltpu.SemaphoreType.DMA((copies,)), pltpu.SemaphoreType.DMA((copies,))],
        compiler_params=pltpu.CompilerParams(collective_id=collective_id, has_side_effects=True, vmem_limit_bytes=VMEM),
    )(*[part.reshape(nz, ny, nc, cols, width) for part in parts])
    return out.reshape(peers, w, 256)


def gather_kernel(x, small, wts, out, small_out, cols, send, recv, s_send, s_recv, w_send, w_recv, own_sem, *, dims, chunks):
    nz, ny, _ = dims
    me = lax.axis_index("shard")
    c, y, z = me % 2, (me // 2) % ny, me // (2 * ny)
    where = lambda a, b, d: (a * ny + b) * 2 + d
    across = where(z, y, 1 - c)
    ys = [lax.rem(y + k, ny) for k in range(1, ny)]
    ys_from = [lax.rem(y + ny - k, ny) for k in range(1, ny)]
    zs = [lax.rem(z + k, nz) for k in range(1, nz)]
    peers = nz * ny * 2
    others = [lax.rem(me + k, peers) for k in range(1, peers)]
    greet(others)
    dl, e = wts.shape[0], wts.shape[1] // (2 * peers)
    size = x.shape[0] // chunks
    rows = [pl.ds(q * size, size) for q in range(chunks)]

    keep = pltpu.make_async_copy(small, small_out.at[z, y, c], own_sem.at[0])
    keep.start()
    whole_own = pltpu.make_async_copy(x, out.at[z, y, c], own_sem.at[1])
    whole_own.start()

    def piece(half, src, dst):
        return (wts.at[:, pl.ds(pl.multiple_of(half * peers * e + dst * e, 128), e)],
                cols.at[pl.ds(pl.multiple_of(src * dl, dl), dl), pl.ds(half * e, e)])
    kept = [pltpu.make_async_copy(*piece(half, me, me), own_sem.at[2 + half]) for half in range(2)]
    sent = [remote(*piece(half, me, p), w_send.at[2 * k + half], w_recv.at[2 * k + half], p)
            for k, p in enumerate(others) for half in range(2)]

    kinds = 2 * nz - 1
    offset = [0] + [-1 - j for j in range(nz - 1)] + [1 + j for j in range(nz - 1)]

    def valid(kind):
        return (z + offset[kind] >= 0) & (z + offset[kind] < nz)

    def sems(group, kind, q):
        at_ = (group * kinds + kind) * chunks + q
        return send.at[at_], recv.at[at_]

    def hop(kind, q, up):
        there = out.at[z + offset[kind], y, c, rows[q]]
        src = x.at[rows[q]] if kind == 0 else there
        j = -offset[kind] if up else offset[kind]
        to_kind = 1 + j if up else nz + j
        return remote(src, there, *sems(0, to_kind, q), where(z + 1 if up else z - 1, y, c))

    def can_hop(kind, up):
        return valid(kind) & ((z + 1 < nz) if up else (z >= 1))

    def over_y(kind, q, k):
        there = out.at[z + offset[kind], y, c, rows[q]]
        src = x.at[rows[q]] if kind == 0 else there
        return remote(src, there, *sems(1 + k, kind, q), where(z, ys[k], c))

    def over_core(kind, q, k):
        there = out.at[z + offset[kind], y if k == 0 else ys_from[k - 1], c, rows[q]]
        src = x.at[rows[q]] if kind == 0 and k == 0 else there
        return remote(src, there, *sems(ny + k, kind, q), across)

    def landed(kind, q, b, d, group):
        there = out.at[z + offset[kind], b, d, rows[q]]
        return remote(there, there, *sems(group, kind, q), across)

    def onward(kind, q):
        if kind == 0:
            ups = [True, False]
        elif kind < nz:
            ups = [True] if kind < nz - 1 else []
        else:
            ups = [False] if kind < kinds - 1 else []
        for up in ups:
            @pl.when(can_hop(kind, up))
            def _(up=up):
                hop(kind, q, up).start()
        for k in range(ny - 1):
            over_y(kind, q, k).start()
        over_core(kind, q, 0).start()

    tiny = []

    def tiny_start(copies):
        tiny.append(copies)
        for copy in copies:
            copy.start()

    def tiny_wait():
        for copy in tiny[-1]:
            copy.wait()

    tiny_start([remote(small, small_out.at[z, y, c], s_send.at[k], s_recv.at[k], where(a, y, c)) for k, a in enumerate(zs)])
    for q in range(chunks):
        onward(0, q)
    for copy in kept + sent:
        copy.start()
    tiny_wait()
    keep.wait()
    tiny_start([remote(small_out.at[:, y, c], small_out.at[:, y, c], s_send.at[nz - 1 + k], s_recv.at[nz - 1 + k], where(z, b, c))
                for k, b in enumerate(ys)])

    def from_y(kind, q):
        @pl.when(valid(kind))
        def _():
            for k in range(1, ny):
                landed(kind, q, ys_from[k - 1], c, k).wait_recv()
                over_core(kind, q, k).start()

    waves = [[0]] + [[1 + j, nz + j] for j in range(nz - 1)]
    for number, wave in enumerate(waves):
        for q in range(chunks):
            for kind in wave:
                if kind:
                    @pl.when(valid(kind))
                    def _(kind=kind, q=q):
                        landed(kind, q, y, c, 0).wait_recv()
                        onward(kind, q)
        if number == 1:
            tiny_wait()
            last = small_out.at[:, :, c]
            tiny_start([remote(last, last, s_send.at[nz + ny - 2], s_recv.at[nz + ny - 2], across)])
        if number:
            for q in range(chunks):
                for kind in waves[number - 1]:
                    from_y(kind, q)
    for q in range(chunks):
        for kind in waves[-1]:
            from_y(kind, q)
    tiny_wait()
    for kind in range(kinds):
        @pl.when(valid(kind))
        def _(kind=kind):
            for q in range(chunks):
                for k in range(ny):
                    landed(kind, q, y if k == 0 else ys_from[k - 1], 1 - c, ny + k).wait_recv()
                    over_core(kind, q, k).wait_send()
                for k in range(ny - 1):
                    over_y(kind, q, k).wait_send()
        for up in (True, False):
            j = -offset[kind] if up else offset[kind]
            if 0 <= j < nz - 1:
                @pl.when(can_hop(kind, up))
                def _(kind=kind, up=up):
                    for q in range(chunks):
                        hop(kind, q, up).wait_send()
    for copy in kept + sent:
        copy.wait()
    whole_own.wait()


def gather(x, small, wts, collective_id, chunks=4):
    w, d = x.shape
    peers = lax.axis_size("shard")
    dims = lattice(peers)
    nz, ny, nc = dims
    copies = 2 * ny * (2 * nz - 1) * chunks
    dl, e = wts.shape[0], wts.shape[1] // (2 * peers)
    out, tiles, cols = pl.pallas_call(
        functools.partial(gather_kernel, dims=dims, chunks=chunks),
        out_shape=[jax.ShapeDtypeStruct((nz, ny, nc, w, d), x.dtype), jax.ShapeDtypeStruct((nz, ny, nc, 8, 128), F32),
                   jax.ShapeDtypeStruct((peers * dl, 2 * e), BF16)],
        in_specs=[pl.BlockSpec(memory_space=pl.ANY), pl.BlockSpec(memory_space=pltpu.VMEM), pl.BlockSpec(memory_space=pl.ANY)],
        out_specs=[pl.BlockSpec(memory_space=pl.ANY), pl.BlockSpec(memory_space=pltpu.VMEM), pl.BlockSpec(memory_space=pl.ANY)],
        scratch_shapes=[pltpu.SemaphoreType.DMA((copies,)), pltpu.SemaphoreType.DMA((copies,)),
                        pltpu.SemaphoreType.DMA((nz + ny,)), pltpu.SemaphoreType.DMA((nz + ny,)),
                        pltpu.SemaphoreType.DMA((2 * peers - 2,)), pltpu.SemaphoreType.DMA((2 * peers - 2,)),
                        pltpu.SemaphoreType.DMA((4,))],
        compiler_params=pltpu.CompilerParams(collective_id=collective_id, has_side_effects=True, vmem_limit_bytes=VMEM),
        cost_estimate=pl.CostEstimate(flops=8 * 10 ** 10, bytes_accessed=2 * peers * w * d, transcendentals=0),
    )(x, small, wts)
    return out.reshape(peers, w, d), tiles.reshape(peers, 8, 128), cols


def scatter_steps(refs, dims, reps):
    part, g, out, g_out, rc, own, ry, rz, rg, load, send, recv, g_load, g_send, g_recv = refs
    nz, ny, _ = dims
    me, rep = lax.axis_index("shard"), lax.axis_index("rep")
    c, y, z = me % 2, (me // 2) % ny, me // (2 * ny)
    where = lambda a, b, d: (a * ny + b) * 2 + d
    across = where(z, y, 1 - c)
    ys = [lax.rem(y + k, ny) for k in range(1, ny)]
    zs = [lax.rem(z + k, nz) for k in range(1, nz)]
    peers = nz * ny * 2
    others = [lax.rem(me + k, peers) for k in range(1, peers)]
    far = [{"rep": lax.rem(rep + k, reps)} for k in range(1, reps)]
    slots, size = own.shape[0], own.shape[3]
    chunks = part.shape[3] // size
    rows = [pl.ds(q * size, size) for q in range(chunks)]
    per = ny + nz - 1

    def pair(q, k):
        return send.at[q * per + k], recv.at[q * per + k]

    def loads(q):
        return pltpu.make_async_copy(part.at[:, :, c, rows[q]], own.at[q % slots], load.at[q])

    def first(q):
        return remote(part.at[:, :, 1 - c, rows[q]], rc.at[:, :, rows[q]], *pair(q, 0), across)

    def second(q):
        return [remote(rc.at[:, b, rows[q]], ry.at[k, :, rows[q]], *pair(q, 1 + k), where(z, b, c))
                for k, b in enumerate(ys)]

    def third(q):
        return [remote(rc.at[a, y, rows[q]], rz.at[k, rows[q]], *pair(q, ny + k), where(a, y, c))
                for k, a in enumerate(zs)]

    def handed():
        dl = rg.shape[2]
        spot = lambda p: g.at[pl.ds(pl.multiple_of(p * dl, dl), dl)]
        return pltpu.make_async_copy(spot(me), rg.at[rep, me], g_load.at[0]), [
            remote(spot(p), rg.at[rep, me], g_send.at[k], g_recv.at[k], p) for k, p in enumerate(others)]

    def crossed():
        return [remote(rg.at[rep], rg.at[rep], g_send.at[peers - 1 + k], g_recv.at[peers - 1 + k], p)
                for k, p in enumerate(far)]

    def start():
        if g is None:
            greet([across] + [where(z, b, c) for b in ys] + [where(a, y, c) for a in zs])
        else:
            greet(others + far)
        for q in range(min(slots, chunks)):
            loads(q).start()
        for q in range(chunks):
            first(q).start()
        if g is not None:
            kept, sent = handed()
            for copy in [kept] + sent:
                copy.start()

    def over_core(q):
        loads(q).wait()
        first(q).wait()

        def add(a, _):
            i, j = a // ny, a % ny
            rc[i, j, rows[q]] = (own[q % slots, i, j].astype(F32) + rc[i, j, rows[q]].astype(F32)).astype(BF16)
            return 0
        lax.fori_loop(0, nz * ny, add, 0)
        if q + slots < chunks:
            loads(q + slots).start()
        for copy in second(q):
            copy.start()

    def over_y(q):
        for copy in second(q):
            copy.wait()

        def add(a, _):
            total = rc[a, y, rows[q]].astype(F32)
            for k in range(ny - 1):
                total = total + ry[k, a, rows[q]].astype(F32)
            rc[a, y, rows[q]] = total.astype(BF16)
            return 0
        lax.fori_loop(0, nz, add, 0)
        for copy in third(q):
            copy.start()

    def over_z(q):
        for copy in third(q):
            copy.wait()
        total = rc[z, y, rows[q]].astype(F32)
        for k in range(nz - 1):
            total = total + rz[k, rows[q]].astype(F32)
        out[rows[q]] = total

    def step(s):
        if s < chunks:
            over_core(s)
        if 0 <= s - 2 < chunks:
            over_y(s - 2)
        if 0 <= s - 4 < chunks:
            over_z(s - 4)
        if s == chunks // 2 + 1 and g is not None:
            kept, sent = handed()
            for copy in [kept] + sent:
                copy.wait()
            for copy in crossed():
                copy.start()

    def finish():
        if g is None:
            return
        for copy in crossed():
            copy.wait()
        e = rg.shape[3]
        for p in range(peers):
            total = rg[0, p].astype(F32)
            for k in range(1, reps):
                total = total + rg[k, p].astype(F32)
            g_out[:, p * e:(p + 1) * e] = total
    return start, [functools.partial(step, s) for s in range(chunks + 4)], finish


def scatter_scratch(peers, w, d, size, g=None):
    nz, ny, nc = lattice(peers)
    chunks = w // size
    dma = pltpu.SemaphoreType.DMA
    copies = chunks * (ny + nz - 1)
    out = [pltpu.VMEM((nz, ny, w, d), BF16), pltpu.VMEM((3, nz, ny, size, d), BF16),
           pltpu.VMEM((ny - 1, nz, w, d), BF16), pltpu.VMEM((nz - 1, w, d), BF16)]
    tail = [dma((chunks,)), dma((copies,)), dma((copies,))]
    if g is None:
        return out + tail
    reps = lax.axis_size("rep")
    count = peers + reps - 2
    return (out + [pltpu.VMEM((reps, peers, g.shape[0] // peers, g.shape[1]), BF16)] + tail
            + [dma((1,)), dma((count,)), dma((count,))])


def scatter_kernel(part, g, out, g_out, rc, own, ry, rz, rg, load, send, recv, g_load, g_send, g_recv, *, dims, reps):
    start, steps, finish = scatter_steps(
        (part, g, out, g_out, rc, own, ry, rz, rg, load, send, recv, g_load, g_send, g_recv), dims, reps)
    start()
    for step in steps:
        step()
    finish()


def scatter(part, g, collective_id, size=32):
    peers, w, d = part.shape
    dims = lattice(peers)
    reps = lax.axis_size("rep")
    dl, e = g.shape[0] // peers, g.shape[1]
    return pl.pallas_call(
        functools.partial(scatter_kernel, dims=dims, reps=reps),
        out_shape=[jax.ShapeDtypeStruct((w, d), F32), jax.ShapeDtypeStruct((dl, peers * e), F32)],
        in_specs=[pl.BlockSpec(memory_space=pl.ANY)] * 2,
        out_specs=[pl.BlockSpec(memory_space=pltpu.VMEM)] * 2,
        scratch_shapes=scatter_scratch(peers, w, d, size, g),
        compiler_params=pltpu.CompilerParams(collective_id=collective_id, has_side_effects=True, vmem_limit_bytes=VMEM),
        cost_estimate=pl.CostEstimate(flops=8 * 10 ** 10, bytes_accessed=2 * peers * w * d, transcendentals=0),
    )(part.reshape(dims + (w, d)), g)


def beside(b, grid, start, steps, finish):
    @pl.when(b == 0)
    def _():
        start()
    for s, step in enumerate(steps):
        @pl.when(b == (s * (grid - 1)) // len(steps) + 1)
        def _(step=step):
            step()
    @pl.when(b == grid - 1)
    def _():
        finish()


def fill(low_ref, bcs_scr, bc_scr, n):
    bcs_scr[...] = low_ref[0, :, 128:].astype(F32)
    lane = lax.broadcasted_iota(jnp.int32, (n, 128), 1)
    sub = lax.broadcasted_iota(jnp.int32, (n, 128), 0)
    mask = (lane % n) == sub
    r = lax.broadcasted_iota(jnp.int32, (128, 256), 0)
    c = lax.broadcasted_iota(jnp.int32, (128, 256), 1)
    ones = jnp.where((r >= 3 * n) == (c >= 128), 1.0, 0.0).astype(BF16)
    group = 128

    def body(g, _):
        rows = [jnp.where(mask, bcs_scr[pl.ds(g * group + j, 1), :], 0.0).astype(BF16) for j in range(group)]
        bc_scr[at(g * (group * n), group * n, 128), :] = mm(jnp.concatenate(rows, axis=0), ones)
        return 0
    lax.fori_loop(0, bcs_scr.shape[0] // group, body, 0)


def fold_rows(vals, sub):
    for k in (1, 2, 4):
        mask = (sub & k) == 0
        vals = [jnp.where(mask, a, b) + pltpu.roll(jnp.where(mask, b, a), 8 - k, 0)
                for a, b in zip(vals[::2], vals[1::2])]
    return vals[0]


def ahead(low_ref, xz_ref, xc_ref, mask_ref, dy_ref, wo_ref, wdt_ref, dtb_ref, a2_ref,
          cks_ref, ckp_ref, end_ref, dg_ref, s_scr, p_scr, f_scr, sd_scr, dx_scr, dy_scr, bcs_scr, bc_scr, *, m, n, e):
    b = pl.program_id(0)
    @pl.when(b == 0)
    def _():
        s_scr[...] = jnp.zeros_like(s_scr)
        p_scr[...] = jnp.ones_like(p_scr)
        f_scr[...] = jnp.zeros_like(f_scr)
    cks_ref[0] = s_scr[...]
    ckp_ref[0] = p_scr[...]
    fill(low_ref, bcs_scr, bc_scr, n)
    step = softplus(mm(low_ref[0, :, :128], wdt_ref[...]) + dtb_ref[...])
    sd_scr[...] = jnp.where(mask_ref[0, :, 0:1] > 0.0, step, 1e30)
    dx_scr[...] = step * xc_ref[0].astype(F32)
    dg = nt(dy_ref[0], wo_ref[...])
    dg_ref[0] = dg
    z = xz_ref[0, :, e:].astype(F32)
    dy_scr[...] = dg * (z * jax.nn.sigmoid(z))
    a2 = a2_ref[...]
    rows = sd_scr.shape[0] // m
    un = 16

    def group(g, carry):
        s, p, f = [list(c) for c in carry]
        for j in range(un):
            for i in range(m):
                t = i * rows + g * un + j
                bc = bc_scr[at(t * n, n, n), :]
                bb, cc = wide(bc[:, :128], e), wide(bc[:, 128:], e)
                a = jnp.exp2(sd_scr[pl.ds(t, 1), :] * a2)
                s[i] = a * s[i] + bb * dx_scr[pl.ds(t, 1), :]
                p[i] = p[i] * a
                f[i] = f[i] + p[i] * (cc * dy_scr[pl.ds(t, 1), :])
        return tuple(s), tuple(p), tuple(f)
    done = lax.fori_loop(0, rows // un, group,
                         tuple(tuple(scr[i] for i in range(m)) for scr in (s_scr, p_scr, f_scr)))
    for scr, vals in zip((s_scr, p_scr, f_scr), done):
        for i in range(m):
            scr[i] = vals[i]

    @pl.when(b == pl.num_programs(0) - 1)
    def _():
        end_ref[0] = s_scr[...]
        end_ref[1] = p_scr[...]
        end_ref[2] = f_scr[...]


def behind(*refs, n, e, dims, reps, sending):
    (low_ref, xz_ref, xc_ref, mask_ref, dy_ref, dg_ref, nu_ref, cks_ref, ckp_ref,
     wo_ref, wdt_ref, dtb_ref, a2_ref, skip_ref, hin_ref, qin_ref) = refs[:16]
    refs = refs[16:]
    if sending:
        before, refs = refs[0], refs[1:]
    out_ref, dz_ref, dxc_ref, part_ref, go_ref, gdt_ref, ga_ref, vec_ref, gz_ref = refs[:9]
    refs = refs[9:]
    if sending:
        summed, refs = refs[0], refs[1:]
    (h_scr, a_scr, q_scr, bcs_scr, bc_scr, pre_scr, st_scr, sd_scr, dx_scr, dy_scr, y_scr, da_scr, gb_scr) = refs[:13]
    b = pl.program_id(0)
    if sending:
        rc, own, ry, rz, load, send, recv = refs[13:]
        beside(b, dims[0] * dims[1] * dims[2], *scatter_steps(
            (before, None, summed, None, rc, own, ry, rz, None, load, send, recv, None, None, None), dims, reps))
    m = 1
    @pl.when(b == 0)
    def _():
        q_scr[...] = qin_ref[...]
        for ref in (go_ref, gdt_ref, ga_ref, vec_ref, gz_ref):
            ref[...] = jnp.zeros_like(ref)
    fill(low_ref, bcs_scr, bc_scr, n)
    pre = mm(low_ref[0, :, :128], wdt_ref[...]) + dtb_ref[...]
    pre_scr[...] = pre
    step = softplus(pre)
    st_scr[...] = step
    sd_scr[...] = jnp.where(mask_ref[0, :, 0:1] > 0.0, step, 1e30)
    dx_scr[...] = step * xc_ref[0].astype(F32)
    z = xz_ref[0, :, e:].astype(F32)
    dy_scr[...] = dg_ref[0] * (z * jax.nn.sigmoid(z))
    a2 = a2_ref[...]
    sub = lax.broadcasted_iota(jnp.int32, (8, e), 0)
    rows = sd_scr.shape[0] // m
    lanes = lax.broadcasted_iota(jnp.int32, (n, rows), 1)
    un = 32
    for i in range(m):
        r0 = i * rows
        h0 = cks_ref[0, i] + ckp_ref[0, i] * hin_ref[i]
        h_scr[pl.ds(0, n), :] = h0

        def fwd(g, h, r0=r0):
            ys = []
            for j in range(un):
                t = g * un + j
                bc = bc_scr[at((r0 + t) * n, n, n), :]
                bb, cc = wide(bc[:, :128], e), wide(bc[:, 128:], e)
                a = jnp.exp2(sd_scr[pl.ds(r0 + t, 1), :] * a2)
                h = a * h + bb * dx_scr[pl.ds(r0 + t, 1), :]
                a_scr[at(t * n, n, n), :] = a
                h_scr[at(t * n + n, n, n), :] = h
                cy = cc * h
                ys.append(cy[:8] + cy[8:])
                if len(ys) == 8:
                    y_scr[at(r0 + t - 7, 8), :] = fold_rows(ys, sub)
                    ys = []
            return h
        lax.fori_loop(0, rows // un, fwd, h0)

        def bwd(g, carry, r0=r0):
            q, ga, hn, db, dc = carry
            das, gbs = [], []
            for j in range(un):
                t = rows - 1 - (g * un + j)
                bc = bc_scr[at((r0 + t) * n, n, n), :]
                bb, cc = wide(bc[:, :128], e), wide(bc[:, 128:], e)
                a = a_scr[at(t * n, n, n), :]
                hp = h_scr[at(t * n, n, n), :]
                dyr = dy_scr[pl.ds(r0 + t, 1), :]
                gt = cc * dyr + q
                q = a * gt
                da = q * hp
                ga = ga + da * st_scr[pl.ds(r0 + t, 1), :]
                d_a = da * a2
                g_b = gt * bb
                das.append(d_a[:8] + d_a[8:])
                gbs.append(g_b[:8] + g_b[8:])
                pb = gt * dx_scr[pl.ds(r0 + t, 1), :]
                pc = dyr * hn
                pb = sum(pb[:, k:k + 128] for k in range(0, e, 128))
                pc = sum(pc[:, k:k + 128] for k in range(0, e, 128))
                db = jnp.where(lanes == t, jnp.sum(pb, axis=1, keepdims=True), db)
                dc = jnp.where(lanes == t, jnp.sum(pc, axis=1, keepdims=True), dc)
                hn = hp
                if len(das) == 8:
                    da_scr[at(r0 + t, 8), :] = fold_rows(das[::-1], sub)
                    gb_scr[at(r0 + t, 8), :] = fold_rows(gbs[::-1], sub)
                    das, gbs = [], []
            return q, ga, hn, db, dc
        zero = jnp.zeros((n, rows), F32)
        q, ga, _, db, dc = lax.fori_loop(
            0, rows // un, bwd, (q_scr[i], ga_ref[...], h_scr[pl.ds(rows * n, n), :], zero, zero))
        q_scr[i] = q
        ga_ref[...] = ga
        part_ref[0, 128:128 + n, r0:r0 + rows] = db
        part_ref[0, 128 + n:128 + 2 * n, r0:r0 + rows] = dc

    z = xz_ref[0, :, e:].astype(F32)
    sz = jax.nn.sigmoid(z)
    xc = xc_ref[0].astype(F32)
    skip = skip_ref[...]
    y = y_scr[...] + skip * xc
    gated = (y * (z * sz)).astype(BF16)
    out_ref[0] = mm(gated, wo_ref[...]).astype(BF16)
    go_ref[...] += tn(gated, dy_ref[0])
    dz = (dg_ref[0] * y * (sz * (1.0 + z * (1.0 - sz)))).astype(BF16)
    dz_ref[0] = dz
    gz_ref[...] += tn(nu_ref[0], dz)
    gb = gb_scr[...]
    dy_y = dy_scr[...]
    dxc_ref[0] = dy_y * skip + st_scr[...] * gb
    d_pre = (da_scr[...] * LN2 + xc * gb) * jax.nn.sigmoid(pre_scr[...])
    d_low = d_pre.astype(BF16)
    gdt_ref[...] += tn(low_ref[0, :, :128], d_low)
    part_ref[0, :128, :] = nt(wdt_ref[...], d_low)
    vec_ref[0:1] += jnp.sum(d_pre, axis=0, keepdims=True)
    vec_ref[1:2] += jnp.sum(dy_y * xc, axis=0, keepdims=True)


def dsilu(v):
    s = jax.nn.sigmoid(v)
    return s * (1.0 + v * (1.0 - s))


def back(*refs, m, e, dims, reps):
    (xz_ref, prev_ref, edge_ref, mask_ref, ddbc_ref, nu_ref, next_ref, w_ref, xpt_ref, cw_ref, cb_ref) = refs[:11]
    dxc_refs, dz_refs = refs[11:11 + m], refs[11 + m:11 + 2 * m]
    before, gz_ref = refs[11 + 2 * m:13 + 2 * m]
    v_ref, gxl_ref, vec_ref, summed, gz_out, gx_ref, carry, dx_scr = refs[13 + 2 * m:21 + 2 * m]
    rc, own, ry, rz, rg, *sems = refs[21 + 2 * m:]
    beside(pl.program_id(0), dims[0] * dims[1] * dims[2], *scatter_steps(
        (before, gz_ref, summed, gz_out, rc, own, ry, rz, rg, *sems), dims, reps))
    b = pl.program_id(0)
    @pl.when(b == 0)
    def _():
        carry[...] = next_ref[...]
        gx_ref[...] = jnp.zeros_like(gx_ref)
        vec_ref[...] = jnp.zeros_like(vec_ref)
    first = b == pl.num_programs(0) - 1
    rows = xz_ref.shape[1] // m
    cw, cb = cw_ref[...], cb_ref[...]
    dxc_all = mm(ddbc_ref[0], xpt_ref[...])
    for i in range(m):
        part = slice(i * rows, (i + 1) * rows)
        x = xz_ref[0, part, :e].astype(F32)
        before = prev_ref[0, (i + 1) * rows - 2 * EDGE:(i + 1) * rows, :e].astype(F32)[EDGE:]
        before = jnp.where(first, edge_ref[i * EDGE:(i + 1) * EDGE], before)
        lag = lags(jnp.concatenate([before, x], axis=0), rows)
        same = mask_ref[0, part]
        dconv = (dxc_refs[i][0] + dxc_all[part]) * dsilu(convolve(lag, same, cw, cb))
        vec_ref[4:5] += jnp.sum(dconv, axis=0, keepdims=True)
        vec_ref[3:4] += jnp.sum(dconv * x, axis=0, keepdims=True)
        dx = cw[3:4] * dconv
        for k in range(1, 4):
            masked = dconv * same[:, k - 1:k]
            vec_ref[3 - k:4 - k] += jnp.sum(masked * lag[k], axis=0, keepdims=True)
            sent = cw[3 - k:4 - k] * masked
            ext = jnp.concatenate([sent, carry[k - 1, i]], axis=0)
            dx = dx + ext[k:k + rows]
            carry[k - 1, i] = sent[:EDGE]
        dx_scr[part] = dx
    dx = dx_scr[...].astype(BF16)
    v_ref[0] = nt(jnp.concatenate([dx, jnp.concatenate([ref[0] for ref in dz_refs], axis=0)], axis=1), w_ref[...]).astype(BF16)
    gx_ref[...] += tn(nu_ref[0], dx)

    @pl.when(first)
    def _():
        gxl_ref[...] = gx_ref[...].astype(BF16)


def shift_rep(value, steps):
    count = lax.axis_size("rep")
    first, last = max(0, -steps), min(count, count - steps)
    return lax.ppermute(value, "rep", [(i, i + steps) for i in range(first, last)])


def sum_rep(value):
    if lax.axis_size("rep") != 2:
        return lax.psum(value.astype(F32), "rep")
    low = value.astype(BF16)
    other = lax.ppermute(low, "rep", [(0, 1), (1, 0)])
    return low.astype(F32) + other.astype(F32)


def on_device(hidden_in, segment_ids, out_grad, norm_gain, in_proj, conv_weight, conv_bias, x_proj,
              dt_weight, dt_bias, a_log, d_skip, out_proj):
    peers, reps = lax.axis_size("shard"), lax.axis_size("rep")
    rep = lax.axis_index("rep")
    m, tl, d = hidden_in.shape
    t, w = tl * peers, m * tl
    dl = in_proj.shape[0]
    e = x_proj.shape[0]
    n, rank, taps = a_log.shape[0], dt_weight.shape[0], conv_weight.shape[0]
    w32 = lambda v: v.astype(F32)
    shp = jax.ShapeDtypeStruct
    rising = lambda i: i
    falling = lambda i: peers - 1 - i

    own = jnp.pad(jnp.concatenate([w32(segment_ids), jnp.pad(w32(norm_gain)[None], ((0, 0), (0, 128 - dl)))], axis=0),
                  ((0, 7 - m), (0, 0)))
    hid_all, tiles, w_cols = gather(hidden_in.reshape(w, d), own, in_proj, 4)
    gain = tiles[:, m, :dl].reshape(1, d)
    ids = tiles[:, :m, :tl].astype(jnp.int32)
    later, hid_all = lax.optimization_barrier((out_grad, hid_all))
    dy_all = lax.all_gather(later.reshape(w, d), "shard")
    u = w32(hidden_in)
    r = lax.rsqrt(jnp.mean(u * u, axis=2, keepdims=True) + 1e-5)

    row_ids = ids.transpose(1, 0, 2).reshape(m, t)
    before = jnp.where(rep > 0, shift_rep(row_ids[:, t - taps + 1:], 1), -1)
    ext = jnp.concatenate([before, row_ids], axis=1)
    same = jnp.stack([w32(ext[:, taps - 1 - k:taps - 1 - k + t] == row_ids) for k in range(1, taps)], axis=-1)
    mask = jnp.pad(same, ((0, 0), (0, 0), (0, 8 - same.shape[-1])))
    mask = mask.reshape(m, peers, tl, 8).transpose(1, 0, 2, 3).reshape(peers, w, 8)
    halo = shift_rep(hid_all[peers - 1].reshape(m, tl, d)[:, tl - EDGE:].reshape(m * EDGE, d), 1)

    cw, cb = w32(conv_weight), w32(conv_bias)[None]
    ins = [hid_all, w_cols, halo, mask, cw, cb, x_proj.T, gain]
    outs = [shp((peers, w, 2 * e), BF16), shp((peers, w, e), BF16), shp((peers, w, d), BF16), shp((m * EDGE, e), BF16)]
    outs += [shp((peers, rank + 2 * n, tl), F32)] * m
    xz, xc, nu_all, edge, *parts = call(
        functools.partial(front, m=m, e=e), (peers,),
        [block(hid_all, rising)] + [whole(a) for a in ins[1:3]] + [block(mask, rising)] + [whole(a) for a in ins[4:]],
        [block(a, rising) for a in outs[:3]] + [whole(outs[3])] + [block(a, rising) for a in outs[4:]], outs,
        [pltpu.VMEM((m * EDGE, e), F32)], ins, flops=2 * peers * w * d * 2 * e)

    low = allsum(parts, functools.partial(spread_low, n=n), 0)
    a_mat = -jnp.exp(w32(a_log))
    a2 = a_mat * LOG2E
    dtb, skip = w32(dt_bias)[None], w32(d_skip)[None]

    ins = [low, xz, xc, mask, dy_all, out_proj, dt_weight, dtb, a2]
    outs = [shp((peers, m, n, e), F32)] * 2 + [shp((3, m, n, e), F32), shp((peers, w, e), F32)]
    cks, ckp, end, dg = call(
        functools.partial(ahead, m=m, n=n, e=e), (peers,),
        [block(a, rising) for a in ins[:5]] + [whole(a) for a in ins[5:]],
        [block(outs[0], rising), block(outs[1], rising), whole(outs[2]), block(outs[3], rising)], outs,
        [pltpu.VMEM((m, n, e), F32)] * 3 + [pltpu.VMEM((w, e), F32)] * 3 + [pltpu.VMEM((w, 128), F32), pltpu.VMEM((w * n, 256), F32)],
        ins, flops=40 * 10 ** 9)

    ends = lax.all_gather(end, "rep")
    h_in = jnp.zeros((m, n, e), F32)
    q_in = jnp.zeros((m, n, e), F32)
    for k in range(reps - 1):
        o = reps - 1 - k
        h_in = jnp.where(k < rep, ends[k, 1] * h_in + ends[k, 0], h_in)
        q_in = jnp.where(o > rep, ends[o, 1] * q_in + ends[o, 2], q_in)

    dims = lattice(peers)
    anywhere = pl.BlockSpec(memory_space=pl.ANY)
    rows_done = []
    for i in range(m):
        def row(a, order, i=i):
            shape = (1, tl) if a.ndim == 3 else (1, 1, a.shape[2])
            return pl.BlockSpec(shape + a.shape[len(shape):], lambda b, r=a.ndim: (order(b), i) + (0,) * (r - 2))

        def one(a, i=i):
            return pl.BlockSpec((1,) + a.shape[1:], lambda b: (i, 0, 0))
        ins = [low, xz, xc, mask, dy_all, dg, nu_all, cks, ckp, out_proj, dt_weight, dtb, a2, skip, h_in, q_in]
        specs = [row(a, falling) for a in ins[:9]] + [whole(a) for a in ins[9:14]] + [one(a) for a in ins[14:]]
        outs = [shp((peers, tl, d), BF16), shp((peers, tl, e), BF16), shp((peers, tl, e), F32),
                shp((peers, rank + 2 * n, tl), F32), shp((e, d), F32), shp((rank, e), F32), shp((n, e), F32), shp((8, e), F32),
                shp((d, e), F32)]
        out_specs = [block(a, falling) for a in outs[:4]] + [whole(a) for a in outs[4:]]
        scratch = [pltpu.VMEM((tl * n + n, e), F32), pltpu.VMEM((tl * n, e), F32), pltpu.VMEM((1, n, e), F32),
                   pltpu.VMEM((tl, 128), F32), pltpu.VMEM((tl * n, 256), F32)] + [pltpu.VMEM((tl, e), F32)] * 8
        params = {}
        if i:
            ins.append(rows_done[i - 1][0].reshape(dims + (tl, d)))
            specs.append(anywhere)
            outs.append(shp((tl, d), F32))
            out_specs.append(whole(outs[-1]))
            scratch += scatter_scratch(peers, tl, d, 16)
            params = dict(collective_id=5 + i, has_side_effects=True)
        rows_done.append(call(
            functools.partial(behind, n=n, e=e, dims=dims, reps=reps, sending=bool(i)), (peers,), specs, out_specs, outs,
            scratch, ins, flops=50 * 10 ** 9, **params))
    g_out, g_dt, g_a, vec, g_z = (sum(done[k] for done in rows_done) for k in range(4, 9))
    g_z = g_z.astype(BF16)

    ddbc = allsum([done[3] for done in rows_done], functools.partial(spread_plain, n=n), 1)
    xpt = jnp.pad(x_proj.T, ((0, 256 - x_proj.shape[1]), (0, 0)))
    dxc8 = jnp.stack([done[2][0, :EDGE] for done in rows_done])

    x8 = w32(xz[0].reshape(m, tl, 2 * e)[:, :EDGE, :e])
    ext8 = jnp.concatenate([w32(edge).reshape(m, EDGE, e), x8], axis=1)
    same8 = mask[0].reshape(m, tl, 8)[:, :EDGE]
    conv8 = cb + cw[3] * x8
    for k in range(1, taps):
        conv8 = conv8 + cw[3 - k] * ext8[:, EDGE - k:2 * EDGE - k] * same8[:, :, k - 1:k]
    d8 = dxc8 + mm(ddbc[0].reshape(m, tl, -1)[:, :EDGE].reshape(m * EDGE, -1), xpt).reshape(m, EDGE, e)
    d8 = d8 * dsilu(conv8)
    sent = jnp.stack([cw[3 - k] * d8 * same8[:, :, k - 1:k] for k in range(1, taps)])
    follow = shift_rep(sent, -1)

    last = rows_done[-1][0].reshape(dims + (tl, d))
    ins = [xz, xz, w32(edge), mask, ddbc, nu_all, follow, w_cols, xpt, cw, cb]
    ins += [done[2] for done in rows_done] + [done[1] for done in rows_done] + [last, g_z]
    outs = [shp((peers, w, d), BF16), shp((d, e), BF16), shp((8, e), F32), shp((tl, d), F32), shp((dl, peers * e), F32)]
    earlier = lambda i: jnp.maximum(peers - 2 - i, 0)
    specs = ([block(a, falling) for a in ins[:6]] + [whole(a) for a in ins[6:11]] + [block(a, falling) for a in ins[11:-2]]
             + [anywhere] * 2)
    specs[1], specs[2] = block(xz, earlier), whole(ins[2])
    v_part, g_x, vec2, last_sum, grad_z = call(
        functools.partial(back, m=m, e=e, dims=dims, reps=reps), (peers,), specs,
        [block(outs[0], falling)] + [whole(a) for a in outs[1:]], outs,
        [pltpu.VMEM((d, e), F32), pltpu.VMEM((taps - 1, m, EDGE, e), F32), pltpu.VMEM((w, e), F32)]
        + scatter_scratch(peers, tl, d, 16, g_z), ins, flops=2 * peers * w * d * 3 * e, collective_id=2, has_side_effects=True)
    out_sum = jnp.stack([done[9] for done in rows_done[1:]] + [last_sum])
    layer_out = (u + out_sum).astype(BF16)

    g_out = sum_rep(g_out)
    v_part, g_out = lax.optimization_barrier((v_part, g_out))
    v, grad_x = scatter(v_part, g_x, 3)
    v = v.reshape(m, tl, d) * gain
    in_grad = w32(out_grad) + r * v - u * (r * r * r) * jnp.mean(v * u, axis=2, keepdims=True)

    grad_in_proj = jnp.concatenate([grad_x, grad_z], axis=1)
    grad_gain = jnp.sum(grad_in_proj * w32(in_proj), axis=1) / w32(norm_gain)

    small = jnp.concatenate([vec, vec2, g_a * a_mat, g_dt, tn(xc.reshape(peers * w, e), ddbc.reshape(peers * w, -1)).T], axis=0)
    small = sum_rep(small)
    vec, vec2, g_a, g_dt, g_xp = (small[:8], small[8:16], small[16:16 + n], small[16 + n:16 + n + rank], small[16 + n + rank:])
    return (layer_out, in_grad, grad_gain, grad_in_proj, vec2[:taps], vec2[taps], g_xp[:rank + 2 * n].T, g_dt, vec[0],
            g_a, vec[1], g_out)


def solution(mesh):
    tok, ids = P(None, ("rep", "shard"), None), P(None, ("rep", "shard"))
    row, col, one = P("shard", None), P(None, "shard"), P("shard")
    return jax.shard_map(
        on_device,
        mesh=mesh,
        in_specs=(tok, ids, tok, one, row, col, one, row, col, one, col, one, row),
        out_specs=(tok, tok, one, row, col, one, row, col, one, col, one, row),
        check_vma=False,
    )
```

```python
import functools
import jax
import jax.numpy as jnp
from jax import lax
from jax.sharding import PartitionSpec as P
from jax.experimental import pallas as pl
from jax.experimental.pallas import tpu as pltpu

F32, BF16 = jnp.float32, jnp.bfloat16
LOG2E, LN2 = 1.4426950408889634, 0.6931471805599453
EDGE = 8
VMEM = 60 << 20


def nt(a, b):
    return lax.dot_general(a, b, (((1,), (1,)), ((), ())), preferred_element_type=F32)


def tn(a, b):
    return lax.dot_general(a, b, (((0,), (0,)), ((), ())), preferred_element_type=F32)


def mm(a, b):
    return jnp.dot(a, b, preferred_element_type=F32)


def softplus(v):
    return jnp.maximum(v, 0.0) + jnp.log1p(jnp.exp(-jnp.abs(v)))


def wide(v, e):
    return jnp.concatenate([v] * (e // 128), axis=1) if e > 128 else v


def at(start, size, unit=8):
    return pl.ds(pl.multiple_of(start, unit), size)


def call(kernel, grid, in_specs, out_specs, out_shape, scratch, args, flops=0, **params):
    size = sum(a.size * a.dtype.itemsize for a in args) + sum(s.size * s.dtype.itemsize for s in out_shape)
    return pl.pallas_call(
        kernel, grid=grid, in_specs=in_specs, out_specs=out_specs, out_shape=out_shape,
        scratch_shapes=scratch, compiler_params=pltpu.CompilerParams(vmem_limit_bytes=VMEM, **params),
        cost_estimate=pl.CostEstimate(flops=flops, bytes_accessed=size, transcendentals=0))(*args)


def whole(a):
    return pl.BlockSpec(a.shape, lambda i, r=len(a.shape): (0,) * r)


def block(a, order):
    return pl.BlockSpec((1,) + a.shape[1:], lambda i, r=len(a.shape): (order(i),) + (0,) * (r - 1))


def lags(x_ext, rows):
    return [x_ext[EDGE - k:EDGE - k + rows] for k in range(4)]


def convolve(lag, same, cw, cb):
    out = cb + cw[3:4] * lag[0]
    for k in range(1, 4):
        out = out + cw[3 - k:4 - k] * lag[k] * same[:, k - 1:k]
    return out


def normalise(rows, gain):
    u = rows.astype(F32)
    return (u * lax.rsqrt(jnp.mean(u * u, axis=1, keepdims=True) + 1e-5) * gain).astype(BF16)


def front(hid_ref, w_ref, halo_ref, mask_ref, cw_ref, cb_ref, xp_ref, gain_ref, xz_ref, xc_ref, nu_ref, edge_ref,
          *rest, m, e):
    parts, carry = rest[:m], rest[m]
    @pl.when(pl.program_id(0) == 0)
    def _():
        edge = mm(normalise(halo_ref[...], gain_ref[...]), w_ref[:, :e]).astype(BF16)
        edge_ref[...] = edge
        carry[...] = edge.astype(F32)
    nu = normalise(hid_ref[0], gain_ref[...])
    nu_ref[0] = nu
    xz = mm(nu, w_ref[...]).astype(BF16)
    xz_ref[0] = xz
    rows = xz.shape[0] // m
    cw, cb = cw_ref[...], cb_ref[...]
    for i in range(m):
        x = xz[i * rows:(i + 1) * rows, :e].astype(F32)
        ext = jnp.concatenate([carry[i * EDGE:(i + 1) * EDGE], x], axis=0)
        carry[i * EDGE:(i + 1) * EDGE] = x[rows - EDGE:]
        conv = convolve(lags(ext, rows), mask_ref[0, i * rows:(i + 1) * rows], cw, cb)
        xc = (conv * jax.nn.sigmoid(conv)).astype(BF16)
        xc_ref[0, i * rows:(i + 1) * rows] = xc
        parts[i][0] = nt(xp_ref[...], xc)


def lattice(peers):
    y = 2 if peers <= 16 else 4
    return peers // (2 * y), y, 2


def place(target):
    return target if isinstance(target, dict) else {"shard": target}


def greet(targets):
    barrier = pltpu.get_barrier_semaphore()
    for target in targets:
        pl.semaphore_signal(barrier, inc=1, device_id=place(target), device_id_type=pl.DeviceIdType.MESH)
    pl.semaphore_wait(barrier, len(targets))


def remote(src, dst, send, recv, target):
    return pltpu.make_async_remote_copy(src_ref=src, dst_ref=dst, send_sem=send, recv_sem=recv,
                                        device_id=place(target), device_id_type=pl.DeviceIdType.MESH)


def spread_low(total, n):
    rows = jnp.concatenate([total, jnp.zeros((256 - total.shape[0], total.shape[1]), F32)], axis=0).T
    rank = total.shape[0] - 2 * n
    out = [rows[:, :rank].astype(BF16)]
    rest = rows[:, rank:]
    hi = rest.astype(BF16)
    mid = (rest - hi.astype(F32)).astype(BF16)
    lo = (rest - hi.astype(F32) - mid.astype(F32)).astype(BF16)
    for k in range(2):
        out += [p[:, k * n:(k + 1) * n] for p in (hi, mid, lo)]
    out.append(jnp.zeros((rows.shape[0], 128 - 6 * n), BF16))
    return jnp.concatenate(out, axis=1)


def spread_plain(total, n):
    return jnp.concatenate([total, jnp.zeros((256 - total.shape[0], total.shape[1]), F32)], axis=0).T.astype(BF16)


def allsum_kernel(*refs, dims, chunks, finish):
    parts = refs[:chunks]
    out, rc, ac, low, ry, rz, send, recv = refs[chunks:]
    nz, ny, _ = dims
    me = lax.axis_index("shard")
    c, y, z = me % 2, (me // 2) % ny, me // (2 * ny)
    where = lambda a, b, d: (a * ny + b) * 2 + d
    across = where(z, y, 1 - c)
    ys = [lax.rem(y + k, ny) for k in range(1, ny)]
    zs = [lax.rem(z + k, nz) for k in range(1, nz)]
    greet([across] + [where(z, b, c) for b in ys] + [where(a, y, c) for a in zs])
    width = parts[0].shape[-1]
    rows = [pl.ds(q * width, width) for q in range(chunks)]

    def start(copies):
        for copy in copies:
            copy.start()
        return copies

    def finish_all(copies):
        for copy in copies:
            copy.wait()
    base = [0]

    def sems(count):
        base[0] += count
        return [(send.at[base[0] - count + k], recv.at[base[0] - count + k]) for k in range(count)]

    first = []
    for q in range(chunks):
        (s, r), = sems(1)
        first.append(start([remote(parts[q].at[:, :, 1 - c], rc.at[q], s, r, across)]))
    second = []
    for q in range(chunks):
        finish_all(first[q])
        for a in range(nz):
            for b in range(ny):
                total = parts[q][a, b, c] + rc[q, a, b]
                ac[q, a, b] = total
                low[q, a, b] = total.astype(BF16)
        second.append(start([remote(low.at[q, :, b], ry.at[q, k], *sem, where(z, b, c))
                             for k, (b, sem) in enumerate(zip(ys, sems(ny - 1)))]))
    third = []
    for q in range(chunks):
        finish_all(second[q])
        for a in range(nz):
            got = ac[q, a, y]
            for k in range(ny - 1):
                got = got + ry[q, k, a].astype(F32)
            ac[q, a, y] = got
            low[q, a, y] = got.astype(BF16)
        third.append(start([remote(low.at[q, a, y], rz.at[q, k], *sem, where(a, y, c))
                            for k, (a, sem) in enumerate(zip(zs, sems(nz - 1)))]))
    fourth = []
    for q in range(chunks):
        finish_all(third[q])
        got = ac[q, z, y]
        for k in range(nz - 1):
            got = got + rz[q, k].astype(F32)
        out[z, y, c, q * width:(q + 1) * width] = finish(got)
        mine = out.at[z, y, c, rows[q]]
        fourth.append(start([remote(mine, mine, *sem, where(a, y, c)) for a, sem in zip(zs, sems(nz - 1))]))
    fifth = []
    for q in range(chunks):
        finish_all(fourth[q])
        mine = out.at[:, y, c, rows[q]]
        fifth.append(start([remote(mine, mine, *sem, where(z, b, c)) for b, sem in zip(ys, sems(ny - 1))]))
    last = []
    for q in range(chunks):
        finish_all(fifth[q])
        mine = out.at[:, :, c, rows[q]]
        (s, r), = sems(1)
        last.append(start([remote(mine, mine, s, r, across)]))
    for q in range(chunks):
        finish_all(last[q])


def allsum(parts, finish, collective_id):
    peers, cols, width = parts[0].shape
    w = width * len(parts)
    dims = lattice(peers)
    nz, ny, nc = dims
    chunks = len(parts)
    copies = 2 * chunks * (1 + ny - 1 + nz - 1)
    out = pl.pallas_call(
        functools.partial(allsum_kernel, dims=dims, chunks=chunks, finish=finish),
        out_shape=jax.ShapeDtypeStruct((nz, ny, nc, w, 256), BF16),
        in_specs=[pl.BlockSpec(memory_space=pltpu.VMEM)] * chunks,
        out_specs=pl.BlockSpec(memory_space=pltpu.VMEM),
        scratch_shapes=[pltpu.VMEM((chunks, nz, ny, cols, 128), F32), pltpu.VMEM((chunks, nz, ny, cols, 128), F32),
                        pltpu.VMEM((chunks, nz, ny, cols, 128), BF16), pltpu.VMEM((chunks, ny - 1, nz, cols, 128), BF16),
                        pltpu.VMEM((chunks, nz - 1, cols, 128), BF16),
                        pltpu.SemaphoreType.DMA((copies,)), pltpu.SemaphoreType.DMA((copies,))],
        compiler_params=pltpu.CompilerParams(collective_id=collective_id, has_side_effects=True, vmem_limit_bytes=VMEM),
    )(*[part.reshape(nz, ny, nc, cols, width) for part in parts])
    return out.reshape(peers, w, 256)


def gather_kernel(x, small, wts, out, small_out, cols, send, recv, s_send, s_recv, w_send, w_recv, own_sem, *, dims, chunks):
    nz, ny, _ = dims
    me = lax.axis_index("shard")
    c, y, z = me % 2, (me // 2) % ny, me // (2 * ny)
    where = lambda a, b, d: (a * ny + b) * 2 + d
    across = where(z, y, 1 - c)
    ys = [lax.rem(y + k, ny) for k in range(1, ny)]
    ys_from = [lax.rem(y + ny - k, ny) for k in range(1, ny)]
    zs = [lax.rem(z + k, nz) for k in range(1, nz)]
    peers = nz * ny * 2
    others = [lax.rem(me + k, peers) for k in range(1, peers)]
    greet(others + [{"rep": lax.axis_index("rep") + 1 - 2 * lax.rem(lax.axis_index("rep"), 2)}])
    dl, e = wts.shape[0], wts.shape[1] // (2 * peers)
    size = x.shape[0] // chunks
    rows = [pl.ds(q * size, size) for q in range(chunks)]

    keep = pltpu.make_async_copy(small, small_out.at[z, y, c], own_sem.at[0])
    keep.start()
    whole_own = pltpu.make_async_copy(x, out.at[z, y, c], own_sem.at[1])
    whole_own.start()

    rep = lax.axis_index("rep")
    odd = lax.rem(rep, 2)
    hl = dl // 2

    def piece(half, src, dst):
        return (wts.at[pl.ds(pl.multiple_of(odd * hl, hl), hl), pl.ds(pl.multiple_of(half * peers * e + dst * e, 128), e)],
                cols.at[src, odd, :, pl.ds(half * e, e)])
    kept = [pltpu.make_async_copy(*piece(half, me, me), own_sem.at[2 + half]) for half in range(2)]
    swapped = remote(cols.at[:, odd], cols.at[:, odd], w_send.at[2 * peers - 2], w_recv.at[2 * peers - 2], {"rep": rep + 1 - 2 * odd})
    sent = [remote(*piece(half, me, p), w_send.at[2 * k + half], w_recv.at[2 * k + half], p)
            for k, p in enumerate(others) for half in range(2)]

    kinds = 2 * nz - 1
    offset = [0] + [-1 - j for j in range(nz - 1)] + [1 + j for j in range(nz - 1)]

    def valid(kind):
        return (z + offset[kind] >= 0) & (z + offset[kind] < nz)

    def sems(group, kind, q):
        at_ = (group * kinds + kind) * chunks + q
        return send.at[at_], recv.at[at_]

    def hop(kind, q, up):
        there = out.at[z + offset[kind], y, c, rows[q]]
        src = x.at[rows[q]] if kind == 0 else there
        j = -offset[kind] if up else offset[kind]
        to_kind = 1 + j if up else nz + j
        return remote(src, there, *sems(0, to_kind, q), where(z + 1 if up else z - 1, y, c))

    def can_hop(kind, up):
        return valid(kind) & ((z + 1 < nz) if up else (z >= 1))

    def over_y(kind, q, k):
        there = out.at[z + offset[kind], y, c, rows[q]]
        src = x.at[rows[q]] if kind == 0 else there
        return remote(src, there, *sems(1 + k, kind, q), where(z, ys[k], c))

    def over_core(kind, q, k):
        there = out.at[z + offset[kind], y if k == 0 else ys_from[k - 1], c, rows[q]]
        src = x.at[rows[q]] if kind == 0 and k == 0 else there
        return remote(src, there, *sems(ny + k, kind, q), across)

    def landed(kind, q, b, d, group):
        there = out.at[z + offset[kind], b, d, rows[q]]
        return remote(there, there, *sems(group, kind, q), across)

    def onward(kind, q):
        if kind == 0:
            ups = [True, False]
        elif kind < nz:
            ups = [True] if kind < nz - 1 else []
        else:
            ups = [False] if kind < kinds - 1 else []
        for up in ups:
            @pl.when(can_hop(kind, up))
            def _(up=up):
                hop(kind, q, up).start()
        for k in range(ny - 1):
            over_y(kind, q, k).start()
        over_core(kind, q, 0).start()

    tiny = []

    def tiny_start(copies):
        tiny.append(copies)
        for copy in copies:
            copy.start()

    def tiny_wait():
        for copy in tiny[-1]:
            copy.wait()

    tiny_start([remote(small, small_out.at[z, y, c], s_send.at[k], s_recv.at[k], where(a, y, c)) for k, a in enumerate(zs)])
    for q in range(chunks):
        onward(0, q)
    for copy in kept + sent:
        copy.start()
    tiny_wait()
    keep.wait()
    tiny_start([remote(small_out.at[:, y, c], small_out.at[:, y, c], s_send.at[nz - 1 + k], s_recv.at[nz - 1 + k], where(z, b, c))
                for k, b in enumerate(ys)])

    def from_y(kind, q):
        @pl.when(valid(kind))
        def _():
            for k in range(1, ny):
                landed(kind, q, ys_from[k - 1], c, k).wait_recv()
                over_core(kind, q, k).start()

    waves = [[0]] + [[1 + j, nz + j] for j in range(nz - 1)]
    for number, wave in enumerate(waves):
        for q in range(chunks):
            for kind in wave:
                if kind:
                    @pl.when(valid(kind))
                    def _(kind=kind, q=q):
                        landed(kind, q, y, c, 0).wait_recv()
                        onward(kind, q)
        if number == 2:
            for copy in kept + sent:
                copy.wait()
            swapped.start()
        if number == 1:
            tiny_wait()
            last = small_out.at[:, :, c]
            tiny_start([remote(last, last, s_send.at[nz + ny - 2], s_recv.at[nz + ny - 2], across)])
        if number:
            for q in range(chunks):
                for kind in waves[number - 1]:
                    from_y(kind, q)
    for q in range(chunks):
        for kind in waves[-1]:
            from_y(kind, q)
    tiny_wait()
    for kind in range(kinds):
        @pl.when(valid(kind))
        def _(kind=kind):
            for q in range(chunks):
                for k in range(ny):
                    landed(kind, q, y if k == 0 else ys_from[k - 1], 1 - c, ny + k).wait_recv()
                    over_core(kind, q, k).wait_send()
                for k in range(ny - 1):
                    over_y(kind, q, k).wait_send()
        for up in (True, False):
            j = -offset[kind] if up else offset[kind]
            if 0 <= j < nz - 1:
                @pl.when(can_hop(kind, up))
                def _(kind=kind, up=up):
                    for q in range(chunks):
                        hop(kind, q, up).wait_send()
    swapped.wait()
    whole_own.wait()


def gather(x, small, wts, collective_id, chunks=4):
    w, d = x.shape
    peers = lax.axis_size("shard")
    dims = lattice(peers)
    nz, ny, nc = dims
    copies = 2 * ny * (2 * nz - 1) * chunks
    dl, e = wts.shape[0], wts.shape[1] // (2 * peers)
    out, tiles, cols = pl.pallas_call(
        functools.partial(gather_kernel, dims=dims, chunks=chunks),
        out_shape=[jax.ShapeDtypeStruct((nz, ny, nc, w, d), x.dtype), jax.ShapeDtypeStruct((nz, ny, nc, 8, 128), F32),
                   jax.ShapeDtypeStruct((peers, 2, dl // 2, 2 * e), BF16)],
        in_specs=[pl.BlockSpec(memory_space=pl.ANY), pl.BlockSpec(memory_space=pltpu.VMEM), pl.BlockSpec(memory_space=pl.ANY)],
        out_specs=[pl.BlockSpec(memory_space=pl.ANY), pl.BlockSpec(memory_space=pltpu.VMEM), pl.BlockSpec(memory_space=pl.ANY)],
        scratch_shapes=[pltpu.SemaphoreType.DMA((copies,)), pltpu.SemaphoreType.DMA((copies,)),
                        pltpu.SemaphoreType.DMA((nz + ny,)), pltpu.SemaphoreType.DMA((nz + ny,)),
                        pltpu.SemaphoreType.DMA((2 * peers - 1,)), pltpu.SemaphoreType.DMA((2 * peers - 1,)),
                        pltpu.SemaphoreType.DMA((4,))],
        compiler_params=pltpu.CompilerParams(collective_id=collective_id, has_side_effects=True, vmem_limit_bytes=VMEM),
        cost_estimate=pl.CostEstimate(flops=8 * 10 ** 10, bytes_accessed=2 * peers * w * d, transcendentals=0),
    )(x, small, wts)
    return out.reshape(peers, w, d), tiles.reshape(peers, 8, 128), cols.reshape(peers * dl, 2 * e)


def meet(dims, reps):
    nz, ny, _ = dims
    me, rep = lax.axis_index("shard"), lax.axis_index("rep")
    c, y, z = me % 2, (me // 2) % ny, me // (2 * ny)
    if reps:
        greet([lax.rem(me + k, nz * ny * 2) for k in range(1, nz * ny * 2)]
              + [{"rep": lax.rem(rep + k, reps)} for k in range(1, reps)])
    else:
        greet([(z * ny + y) * 2 + 1 - c] + [(z * ny + lax.rem(y + k, ny)) * 2 + c for k in range(1, ny)]
              + [(lax.rem(z + k, nz) * ny + y) * 2 + c for k in range(1, nz)])


def scatter_steps(refs, dims, reps, lag_y=2, lag_z=4, sum_at=4, cross_at=9, first_col=0):
    part, g, out, g_out, rc, own, ry, rz, ga, gs, rg, load, send, recv, g_load, a_send, a_recv, b_send, b_recv, c_send, c_recv = refs
    nz, ny, _ = dims
    me, rep = lax.axis_index("shard"), lax.axis_index("rep")
    c, y, z = me % 2, (me // 2) % ny, me // (2 * ny)
    where = lambda a, b, d: (a * ny + b) * 2 + d
    across = where(z, y, 1 - c)
    ys = [lax.rem(y + k, ny) for k in range(1, ny)]
    zs = [lax.rem(z + k, nz) for k in range(1, nz)]
    peers = nz * ny * 2
    others = [lax.rem(me + k, peers) for k in range(1, peers)]
    far = [{"rep": lax.rem(rep + k, reps)} for k in range(1, reps)]
    slots, size = own.shape[0], own.shape[3]
    chunks = part.shape[3] // size
    rows = [pl.ds(q * size, size) for q in range(chunks)]
    per = ny + nz - 1

    def pair(q, k):
        return send.at[q * per + k], recv.at[q * per + k]

    def loads(q):
        return pltpu.make_async_copy(part.at[:, :, c, rows[q]], own.at[q % slots], load.at[q])

    def first(q):
        return remote(part.at[:, :, 1 - c, rows[q]], rc.at[:, :, rows[q]], *pair(q, 0), across)

    def second(q):
        return [remote(rc.at[:, b, rows[q]], ry.at[k, :, rows[q]], *pair(q, 1 + k), where(z, b, c))
                for k, b in enumerate(ys)]

    def third(q):
        return [remote(rc.at[a, y, rows[q]], rz.at[k, rows[q]], *pair(q, ny + k), where(a, y, c))
                for k, a in enumerate(zs)]

    groups = peers // reps
    owner_here = lax.rem(me, reps) == rep

    def shared():
        return pltpu.make_async_copy(g.at[:, rep], ga.at[rep], g_load.at[0]), [
            remote(g.at[:, lax.rem(rep + k, reps)], ga.at[rep], a_send.at[k - 1], a_recv.at[k - 1], far[k - 1])
            for k in range(1, reps)]

    def handed(k):
        p = lax.rem(me // reps + k, groups)
        return remote(gs.at[p], rg.at[me], b_send.at[k], b_recv.at[me], p * reps + rep)

    def arrived(k):
        src = lax.rem(me + k, peers)
        return remote(gs.at[0], rg.at[src], b_send.at[0], b_recv.at[src], lax.rem(me + 1, peers))

    def crossed(k):
        return remote(rg, rg, c_send.at[k - 1], c_recv, far[k - 1])

    def g_sum():
        kept, sent = shared()
        for copy in [kept] + sent:
            copy.wait()

        def add(p, _):
            total = ga[0, p].astype(F32)
            for k in range(1, reps):
                total = total + ga[k, p].astype(F32)
            gs[p] = total.astype(BF16)
            return 0
        lax.fori_loop(0, groups, add, 0)

        @pl.when(owner_here)
        def _():
            rg[me] = gs[me // reps]

        @pl.when(jnp.logical_not(owner_here))
        def _():
            handed(0).start()
        for k in range(1, groups):
            handed(k).start()

    def g_cross():
        @pl.when(owner_here)
        def _():
            for k in range(1, peers):
                arrived(k).wait_recv()
            for k in range(1, reps):
                crossed(k).start()

        @pl.when(jnp.logical_not(owner_here))
        def _():
            handed(0).wait_send()
        for k in range(1, groups):
            handed(k).wait_send()

    def g_end():
        @pl.when(owner_here)
        def _():
            for k in range(1, reps):
                crossed(k).wait_send()

        @pl.when(jnp.logical_not(owner_here))
        def _():
            crossed(1).wait_recv()
        e = rg.shape[2]
        for p in range(peers):
            g_out[:, first_col + p * e:first_col + (p + 1) * e] = rg[p].astype(F32)

    def start():
        for q in range(min(slots, chunks)):
            loads(q).start()
        for q in range(chunks):
            first(q).start()
        if g is not None:
            kept, sent = shared()
            for copy in [kept] + sent:
                copy.start()

    def over_core(q):
        loads(q).wait()
        first(q).wait()

        def add(a, _):
            i, j = a // ny, a % ny
            rc[i, j, rows[q]] = (own[q % slots, i, j].astype(F32) + rc[i, j, rows[q]].astype(F32)).astype(BF16)
            return 0
        lax.fori_loop(0, nz * ny, add, 0)
        if q + slots < chunks:
            loads(q + slots).start()
        for copy in second(q):
            copy.start()

    def over_y(q):
        for copy in second(q):
            copy.wait()

        def add(a, _):
            total = rc[a, y, rows[q]].astype(F32)
            for k in range(ny - 1):
                total = total + ry[k, a, rows[q]].astype(F32)
            rc[a, y, rows[q]] = total.astype(BF16)
            return 0
        lax.fori_loop(0, nz, add, 0)
        for copy in third(q):
            copy.start()

    def over_z(q):
        for copy in third(q):
            copy.wait()
        total = rc[z, y, rows[q]].astype(F32)
        for k in range(nz - 1):
            total = total + rz[k, rows[q]].astype(F32)
        out[rows[q]] = total

    def step(s):
        if s < chunks:
            over_core(s)
        if 0 <= s - lag_y < chunks:
            over_y(s - lag_y)
        if 0 <= s - lag_z < chunks:
            over_z(s - lag_z)
        if s == sum_at and g is not None:
            g_sum()
        if s == cross_at and g is not None:
            g_cross()

    def finish():
        if g is not None:
            g_end()
    return start, [functools.partial(step, s) for s in range(chunks + lag_z)], finish


def scatter_scratch(peers, w, d, size, g=None):
    nz, ny, nc = lattice(peers)
    chunks = w // size
    dma = pltpu.SemaphoreType.DMA
    copies = chunks * (ny + nz - 1)
    out = [pltpu.VMEM((nz, ny, w, d), BF16), pltpu.VMEM((3, nz, ny, size, d), BF16),
           pltpu.VMEM((ny - 1, nz, w, d), BF16), pltpu.VMEM((nz - 1, w, d), BF16)]
    tail = [dma((chunks,)), dma((copies,)), dma((copies,))]
    if g is None:
        return out + tail
    reps = lax.axis_size("rep")
    dl, e = g.shape[0] // peers, g.shape[1]
    return (out + [pltpu.VMEM((reps, peers // reps, dl, e), BF16), pltpu.VMEM((peers // reps, dl, e), BF16),
                   pltpu.VMEM((peers, dl, e), BF16)] + tail
            + [dma((1,)), dma((reps - 1,)), dma((reps - 1,)), dma((peers // reps,)), dma((peers,)), dma((reps - 1,)), dma])


def allsum_steps(refs, dims, finish):
    part, result, out, mine, rc, low, ry, rz, load, send, recv = refs
    nz, ny, _ = dims
    me = lax.axis_index("shard")
    c, y, z = me % 2, (me // 2) % ny, me // (2 * ny)
    where = lambda a, b, d: (a * ny + b) * 2 + d
    across = where(z, y, 1 - c)
    ys = [lax.rem(y + k, ny) for k in range(1, ny)]
    zs = [lax.rem(z + k, nz) for k in range(1, nz)]
    base = [0, 1, ny, ny + nz - 1, ny + 2 * nz - 2, 2 * ny + 2 * nz - 3]

    def sem(stage, k):
        return send.at[base[stage] + k], recv.at[base[stage] + k]

    def copies(stage):
        if stage == 0:
            return [remote(part.at[:, :, 1 - c], rc, *sem(0, 0), across)]
        if stage == 1:
            return [remote(low.at[:, b], ry.at[k], *sem(1, k), where(z, b, c)) for k, b in enumerate(ys)]
        if stage == 2:
            return [remote(low.at[a, y], rz.at[k], *sem(2, k), where(a, y, c)) for k, a in enumerate(zs)]
        if stage == 3:
            held, targets = out.at[z, y, c], [where(a, y, c) for a in zs]
        elif stage == 4:
            held, targets = out.at[:, y, c], [where(z, b, c) for b in ys]
        else:
            held, targets = out.at[:, :, c], [across]
        return [remote(held, held, *sem(stage, k), target) for k, target in enumerate(targets)]

    def own():
        return pltpu.make_async_copy(part.at[:, :, c], mine, load.at[0])

    def start():
        own().start()
        for copy in copies(0):
            copy.start()

    def step(s):
        if s == 0:
            own().wait()
        for copy in copies(s):
            copy.wait()
        if s == 0:
            def add(a, _):
                i, j = a // ny, a % ny
                total = mine[i, j] + rc[i, j]
                mine[i, j] = total
                low[i, j] = total.astype(BF16)
                return 0
            lax.fori_loop(0, nz * ny, add, 0)
        if s == 1:
            for a in range(nz):
                total = mine[a, y]
                for k in range(ny - 1):
                    total = total + ry[k, a].astype(F32)
                mine[a, y] = total
                low[a, y] = total.astype(BF16)
        if s == 2:
            total = mine[z, y]
            for k in range(nz - 1):
                total = total + rz[k].astype(F32)
            out[z, y, c] = finish(total)
        if s < 5:
            for copy in copies(s + 1):
                copy.start()

    def end():
        result[...] = out[...]
    return start, [functools.partial(step, s) for s in range(6)], end


def allsum_scratch(peers, cols, width):
    nz, ny, nc = lattice(peers)
    dma = pltpu.SemaphoreType.DMA
    count = 2 * (1 + ny - 1 + nz - 1)
    return [pltpu.VMEM((nz, ny, nc, width, 256), BF16), pltpu.VMEM((nz, ny, cols, width), F32),
            pltpu.VMEM((nz, ny, cols, width), F32),
            pltpu.VMEM((nz, ny, cols, width), BF16), pltpu.VMEM((ny - 1, nz, cols, width), BF16),
            pltpu.VMEM((nz - 1, cols, width), BF16), dma((1,)), dma((count,)), dma((count,))]


def beside(b, grid, dims, reps, transfers):
    @pl.when(b == 0)
    def _():
        meet(dims, reps)
        for start, _, _, _ in transfers:
            start()
    for _, steps, _, when in transfers:
        for s, step in enumerate(steps):
            @pl.when(b == (when[s] if when else (s * (grid - 1)) // len(steps) + 1))
            def _(step=step):
                step()

    @pl.when(b == grid - 1)
    def _():
        for _, _, finish, _ in transfers:
            finish()


PACED = [1, 1, 1, 1, 2, 2, 2, 2, 3, 5, 6, 8, 9, 11, 13, 14, 15, 15]


def fill(low_ref, bcs_scr, bc_scr, n):
    bcs_scr[...] = low_ref[0, :, 128:].astype(F32)
    lane = lax.broadcasted_iota(jnp.int32, (n, 128), 1)
    sub = lax.broadcasted_iota(jnp.int32, (n, 128), 0)
    mask = (lane % n) == sub
    r = lax.broadcasted_iota(jnp.int32, (128, 256), 0)
    c = lax.broadcasted_iota(jnp.int32, (128, 256), 1)
    ones = jnp.where((r >= 3 * n) == (c >= 128), 1.0, 0.0).astype(BF16)
    group = 128

    def body(g, _):
        rows = [jnp.where(mask, bcs_scr[pl.ds(g * group + j, 1), :], 0.0).astype(BF16) for j in range(group)]
        bc_scr[at(g * (group * n), group * n, 128), :] = mm(jnp.concatenate(rows, axis=0), ones)
        return 0
    lax.fori_loop(0, bcs_scr.shape[0] // group, body, 0)


def fold_rows(vals, sub):
    for k in (1, 2, 4):
        mask = (sub & k) == 0
        vals = [jnp.where(mask, a, b) + pltpu.roll(jnp.where(mask, b, a), 8 - k, 0)
                for a, b in zip(vals[::2], vals[1::2])]
    return vals[0]


def ahead(low_ref, xz_ref, xc_ref, mask_ref, dy_ref, wo_ref, wdt_ref, dtb_ref, a2_ref,
          cks_ref, ckp_ref, end_ref, dg_ref, s_scr, p_scr, f_scr, sd_scr, dx_scr, dy_scr, bcs_scr, bc_scr, *, m, n, e):
    b = pl.program_id(0)
    @pl.when(b == 0)
    def _():
        s_scr[...] = jnp.zeros_like(s_scr)
        p_scr[...] = jnp.ones_like(p_scr)
        f_scr[...] = jnp.zeros_like(f_scr)
    cks_ref[0] = s_scr[...]
    ckp_ref[0] = p_scr[...]
    fill(low_ref, bcs_scr, bc_scr, n)
    step = softplus(mm(low_ref[0, :, :128], wdt_ref[...]) + dtb_ref[...])
    sd_scr[...] = jnp.where(mask_ref[0, :, 0:1] > 0.0, step, 1e30)
    dx_scr[...] = step * xc_ref[0].astype(F32)
    dg = nt(dy_ref[0], wo_ref[...])
    dg_ref[0] = dg
    z = xz_ref[0, :, e:].astype(F32)
    dy_scr[...] = dg * (z * jax.nn.sigmoid(z))
    a2 = a2_ref[...]
    rows = sd_scr.shape[0] // m
    un = 16

    def group(g, carry):
        s, p, f = [list(c) for c in carry]
        for j in range(un):
            for i in range(m):
                t = i * rows + g * un + j
                bc = bc_scr[at(t * n, n, n), :]
                bb, cc = wide(bc[:, :128], e), wide(bc[:, 128:], e)
                a = jnp.exp2(sd_scr[pl.ds(t, 1), :] * a2)
                s[i] = a * s[i] + bb * dx_scr[pl.ds(t, 1), :]
                p[i] = p[i] * a
                f[i] = f[i] + p[i] * (cc * dy_scr[pl.ds(t, 1), :])
        return tuple(s), tuple(p), tuple(f)
    done = lax.fori_loop(0, rows // un, group,
                         tuple(tuple(scr[i] for i in range(m)) for scr in (s_scr, p_scr, f_scr)))
    for scr, vals in zip((s_scr, p_scr, f_scr), done):
        for i in range(m):
            scr[i] = vals[i]

    @pl.when(b == pl.num_programs(0) - 1)
    def _():
        end_ref[0] = s_scr[...]
        end_ref[1] = p_scr[...]
        end_ref[2] = f_scr[...]


def behind(*refs, n, e, dims, reps, sending):
    (low_ref, xz_ref, xc_ref, mask_ref, dg_ref, cks_ref, ckp_ref,
     wo_ref, wdt_ref, dtb_ref, a2_ref, skip_ref, hin_ref, qin_ref) = refs[:14]
    refs = refs[14:]
    if sending:
        before, adding, refs = refs[0], refs[1], refs[2:]
    out_ref, dz_ref, dxc_ref, part_ref, gated_ref, gdt_ref, ga_ref, vec_ref = refs[:8]
    refs = refs[8:]
    if sending:
        summed, added, refs = refs[0], refs[1], refs[2:]
    (h_scr, a_scr, q_scr, bcs_scr, bc_scr, pre_scr, st_scr, sd_scr, dx_scr, dy_scr, y_scr, da_scr, gb_scr) = refs[:13]
    b = pl.program_id(0)
    if sending:
        rc, own, ry, rz, load, send, recv = refs[13:20]
        beside(b, dims[0] * dims[1] * dims[2], dims, 0, [
            allsum_steps((adding, added) + refs[20:], dims, functools.partial(spread_plain, n=n)) + (None,),
            scatter_steps((before, None, summed, None, rc, own, ry, rz, None, None, None, load, send, recv) + (None,) * 7,
                          dims, reps, 8, 10) + (PACED,)])
    m = 1
    @pl.when(b == 0)
    def _():
        q_scr[...] = qin_ref[...]
        for ref in (gdt_ref, ga_ref, vec_ref):
            ref[...] = jnp.zeros_like(ref)
    fill(low_ref, bcs_scr, bc_scr, n)
    pre = mm(low_ref[0, :, :128], wdt_ref[...]) + dtb_ref[...]
    pre_scr[...] = pre
    step = softplus(pre)
    st_scr[...] = step
    sd_scr[...] = jnp.where(mask_ref[0, :, 0:1] > 0.0, step, 1e30)
    dx_scr[...] = step * xc_ref[0].astype(F32)
    z = xz_ref[0, :, e:].astype(F32)
    dy_scr[...] = dg_ref[0] * (z * jax.nn.sigmoid(z))
    a2 = a2_ref[...]
    sub = lax.broadcasted_iota(jnp.int32, (8, e), 0)
    rows = sd_scr.shape[0] // m
    lanes = lax.broadcasted_iota(jnp.int32, (n, rows), 1)
    un = 32
    for i in range(m):
        r0 = i * rows
        h0 = cks_ref[0, i] + ckp_ref[0, i] * hin_ref[i]
        h_scr[pl.ds(0, n), :] = h0

        def fwd(g, h, r0=r0):
            ys = []
            for j in range(un):
                t = g * un + j
                bc = bc_scr[at((r0 + t) * n, n, n), :]
                bb, cc = wide(bc[:, :128], e), wide(bc[:, 128:], e)
                a = jnp.exp2(sd_scr[pl.ds(r0 + t, 1), :] * a2)
                h = a * h + bb * dx_scr[pl.ds(r0 + t, 1), :]
                a_scr[at(t * n, n, n), :] = a
                h_scr[at(t * n + n, n, n), :] = h
                cy = cc * h
                ys.append(cy[:8] + cy[8:])
                if len(ys) == 8:
                    y_scr[at(r0 + t - 7, 8), :] = fold_rows(ys, sub)
                    ys = []
            return h
        lax.fori_loop(0, rows // un, fwd, h0)

        def bwd(g, carry, r0=r0):
            q, ga, hn, db, dc = carry
            das, gbs = [], []
            for j in range(un):
                t = rows - 1 - (g * un + j)
                bc = bc_scr[at((r0 + t) * n, n, n), :]
                bb, cc = wide(bc[:, :128], e), wide(bc[:, 128:], e)
                a = a_scr[at(t * n, n, n), :]
                hp = h_scr[at(t * n, n, n), :]
                dyr = dy_scr[pl.ds(r0 + t, 1), :]
                gt = cc * dyr + q
                q = a * gt
                da = q * hp
                ga = ga + da * st_scr[pl.ds(r0 + t, 1), :]
                d_a = da * a2
                g_b = gt * bb
                das.append(d_a[:8] + d_a[8:])
                gbs.append(g_b[:8] + g_b[8:])
                pb = gt * dx_scr[pl.ds(r0 + t, 1), :]
                pc = dyr * hn
                pb = sum(pb[:, k:k + 128] for k in range(0, e, 128))
                pc = sum(pc[:, k:k + 128] for k in range(0, e, 128))
                db = jnp.where(lanes == t, jnp.sum(pb, axis=1, keepdims=True), db)
                dc = jnp.where(lanes == t, jnp.sum(pc, axis=1, keepdims=True), dc)
                hn = hp
                if len(das) == 8:
                    da_scr[at(r0 + t, 8), :] = fold_rows(das[::-1], sub)
                    gb_scr[at(r0 + t, 8), :] = fold_rows(gbs[::-1], sub)
                    das, gbs = [], []
            return q, ga, hn, db, dc
        zero = jnp.zeros((n, rows), F32)
        q, ga, _, db, dc = lax.fori_loop(
            0, rows // un, bwd, (q_scr[i], ga_ref[...], h_scr[pl.ds(rows * n, n), :], zero, zero))
        q_scr[i] = q
        ga_ref[...] = ga
        part_ref[0, 128:128 + n, r0:r0 + rows] = db
        part_ref[0, 128 + n:128 + 2 * n, r0:r0 + rows] = dc

    z = xz_ref[0, :, e:].astype(F32)
    sz = jax.nn.sigmoid(z)
    xc = xc_ref[0].astype(F32)
    skip = skip_ref[...]
    y = y_scr[...] + skip * xc
    gated = (y * (z * sz)).astype(BF16)
    out_ref[0] = mm(gated, wo_ref[...]).astype(BF16)
    gated_ref[0] = gated
    dz = (dg_ref[0] * y * (sz * (1.0 + z * (1.0 - sz)))).astype(BF16)
    dz_ref[0] = dz
    gb = gb_scr[...]
    dy_y = dy_scr[...]
    dxc_ref[0] = dy_y * skip + st_scr[...] * gb
    d_pre = (da_scr[...] * LN2 + xc * gb) * jax.nn.sigmoid(pre_scr[...])
    d_low = d_pre.astype(BF16)
    gdt_ref[...] += tn(low_ref[0, :, :128], d_low)
    part_ref[0, :128, :] = nt(wdt_ref[...], d_low)
    vec_ref[0:1] += jnp.sum(d_pre, axis=0, keepdims=True)
    vec_ref[1:2] += jnp.sum(dy_y * xc, axis=0, keepdims=True)


def back(*refs, e, n, dims, reps, role):
    (xz_ref, prev_ref, edge_ref, mask_ref, ddbc_ref, nu_ref, next_ref, w_ref, xpt_ref, cw_ref, cb_ref, dxc_ref, dz_ref,
     before, extra) = refs[:15]
    b = pl.program_id(0)
    peers = dims[0] * dims[1] * dims[2]
    if role == "sum":
        nu_all, dy_all, dz0, dz1, gated0, gated1 = refs[15:21]
        v_ref, gx, vec_ref, summed, prod_z, prod_o, done, carry, acc_z, acc_o = refs[21:31]
        refs = refs[31:]
        rc, own, ry, rz, load, send, recv = refs[:7]
        beside(b, peers, dims, 0, [
            allsum_steps((extra, done) + refs[7:], dims, functools.partial(spread_plain, n=n)) + (None,),
            scatter_steps((before, None, summed, None, rc, own, ry, rz, None, None, None, load, send, recv) + (None,) * 7,
                          dims, reps) + (None,)])
    else:
        gx_before, v_out, vec_ref, summed, summed_own, g_done, carry, gx, gx_low, v_buf, v_sem, gx_sem = refs[15:27]
        refs = refs[27:]
        half = len(refs) // 2
        earlier = scatter_steps((before, extra, summed, g_done) + refs[:half], dims, reps, 8, 10, 8, 15, peers * e)
        latest = scatter_steps((v_out, gx_low, summed_own, g_done) + refs[half:], dims, reps, 8, 10, 4, 12)

        @pl.when(b == 0)
        def _():
            meet(dims, reps)
            earlier[0]()
            copy = pltpu.make_async_copy(gx_before, gx, gx_sem.at[0])
            copy.start()
            copy.wait()
        early = [1, 1, 1, 1, 2, 2, 2, 2, 7, 11, 14]
        for k, when in enumerate(early):
            @pl.when(b == when)
            def _(k=k):
                earlier[1][k]()

    @pl.when(b == 0)
    def _():
        carry[...] = next_ref[...]
        vec_ref[...] = jnp.zeros_like(vec_ref)
        if role == "sum":
            acc_z[...] = jnp.zeros_like(acc_z)
            acc_o[...] = jnp.zeros_like(acc_o)
            gx[...] = jnp.zeros_like(gx)
    rows = xz_ref.shape[1]
    cw, cb = cw_ref[...], cb_ref[...]
    x = xz_ref[0, :, :e].astype(F32)
    before_x = prev_ref[0, rows - 2 * EDGE:, :e].astype(F32)[EDGE:]
    before_x = jnp.where(b == peers - 1, edge_ref[...], before_x)
    lag = lags(jnp.concatenate([before_x, x], axis=0), rows)
    same = mask_ref[0]
    dconv = (dxc_ref[0] + mm(ddbc_ref[0], xpt_ref[...])) * dsilu(convolve(lag, same, cw, cb))
    vec_ref[4:5] += jnp.sum(dconv, axis=0, keepdims=True)
    vec_ref[3:4] += jnp.sum(dconv * x, axis=0, keepdims=True)
    dx = cw[3:4] * dconv
    for k in range(1, 4):
        masked = dconv * same[:, k - 1:k]
        vec_ref[3 - k:4 - k] += jnp.sum(masked * lag[k], axis=0, keepdims=True)
        sent = cw[3 - k:4 - k] * masked
        dx = dx + jnp.concatenate([sent, carry[k - 1]], axis=0)[k:k + rows]
        carry[k - 1] = sent[:EDGE]
    dx = dx.astype(BF16)
    v = nt(jnp.concatenate([dx, dz_ref[0]], axis=1), w_ref[...]).astype(BF16)
    gx[...] += tn(nu_ref[0], dx)
    if role == "sum":
        v_ref[0] = v
        acc_z[...] += tn(nu_all[0], jnp.concatenate([dz0[0], dz1[0]], axis=0))
        acc_o[...] += tn(jnp.concatenate([gated0[0], gated1[0]], axis=0), dy_all[0])

        @pl.when(b == peers - 1)
        def _():
            prod_z[...] = acc_z[...].astype(BF16)
            prod_o[...] = acc_o[...].astype(BF16)
        return

    slot, at_ = b % 2, peers - 1 - b

    def write(slot):
        return pltpu.make_async_copy(v_buf.at[slot], v_out.at[at_ // (2 * dims[1]), (at_ // 2) % dims[1], at_ % 2], v_sem.at[slot])

    @pl.when(b >= 2)
    def _():
        write(slot).wait()
    v_buf[slot] = v
    write(slot).start()

    @pl.when(b == peers - 1)
    def _():
        write(0).wait()
        write(1).wait()
        for p in range(peers // reps):
            for k in range(reps):
                first = (p * reps + k) * gx_low.shape[2]
                gx_low[p, k] = gx[first:first + gx_low.shape[2]].astype(BF16)
        latest[0]()
        for k, step in enumerate(latest[1]):
            if len(early) + k < len(earlier[1]):
                earlier[1][len(early) + k]()
            step()
        earlier[2]()
        latest[2]()


def dsilu(v):
    s = jax.nn.sigmoid(v)
    return s * (1.0 + v * (1.0 - s))


def shift_rep(value, steps):
    count = lax.axis_size("rep")
    first, last = max(0, -steps), min(count, count - steps)
    return lax.ppermute(value, "rep", [(i, i + steps) for i in range(first, last)])


def sum_rep(value):
    if lax.axis_size("rep") != 2:
        return lax.psum(value.astype(F32), "rep")
    low = value.astype(BF16)
    other = lax.ppermute(low, "rep", [(0, 1), (1, 0)])
    return low.astype(F32) + other.astype(F32)


def on_device(hidden_in, segment_ids, out_grad, norm_gain, in_proj, conv_weight, conv_bias, x_proj,
              dt_weight, dt_bias, a_log, d_skip, out_proj):
    peers, reps = lax.axis_size("shard"), lax.axis_size("rep")
    rep = lax.axis_index("rep")
    m, tl, d = hidden_in.shape
    t, w = tl * peers, m * tl
    dl = in_proj.shape[0]
    e = x_proj.shape[0]
    n, rank, taps = a_log.shape[0], dt_weight.shape[0], conv_weight.shape[0]
    w32 = lambda v: v.astype(F32)
    shp = jax.ShapeDtypeStruct
    rising = lambda i: i
    falling = lambda i: peers - 1 - i

    span = peers * reps
    before = lax.ppermute(segment_ids[:, tl - taps + 1:], ("rep", "shard"), [(k, k + 1) for k in range(span - 1)])
    before = jnp.where((rep > 0) | (lax.axis_index("shard") > 0), before, -1)
    ext = jnp.concatenate([before, segment_ids], axis=1)
    same = [w32(ext[:, taps - 1 - k:taps - 1 - k + tl] == segment_ids) for k in range(1, taps)]
    same = jnp.stack(same, axis=1).reshape(m * (taps - 1), tl)
    own = jnp.concatenate([same, jnp.pad(w32(norm_gain)[None], ((0, 0), (0, tl - dl))),
                           jnp.zeros((7 - m * (taps - 1), tl), F32)], axis=0)
    hid_all, tiles, w_cols = gather(hidden_in.reshape(w, d), own, in_proj, 4)
    gain = tiles[:, m * (taps - 1), :dl].reshape(1, d)
    later, hid_all = lax.optimization_barrier((out_grad, hid_all))
    dy_all = lax.all_gather(later.reshape(w, d), "shard")
    u = w32(hidden_in)
    r = lax.rsqrt(jnp.mean(u * u, axis=2, keepdims=True) + 1e-5)

    mask = tiles[:, :m * (taps - 1)].reshape(peers, m, taps - 1, tl).transpose(0, 1, 3, 2).reshape(peers, w, taps - 1)
    mask = jnp.pad(mask, ((0, 0), (0, 0), (0, 9 - taps)))
    halo = shift_rep(hid_all[peers - 1].reshape(m, tl, d)[:, tl - EDGE:].reshape(m * EDGE, d), 1)

    cw, cb = w32(conv_weight), w32(conv_bias)[None]
    ins = [hid_all, w_cols, halo, mask, cw, cb, x_proj.T, gain]
    outs = [shp((peers, w, 2 * e), BF16), shp((peers, w, e), BF16), shp((peers, w, d), BF16), shp((m * EDGE, e), BF16)]
    outs += [shp((peers, rank + 2 * n, tl), F32)] * m
    xz, xc, nu_all, edge, *parts = call(
        functools.partial(front, m=m, e=e), (peers,),
        [block(hid_all, rising)] + [whole(a) for a in ins[1:3]] + [block(mask, rising)] + [whole(a) for a in ins[4:]],
        [block(a, rising) for a in outs[:3]] + [whole(outs[3])] + [block(a, rising) for a in outs[4:]], outs,
        [pltpu.VMEM((m * EDGE, e), F32)], ins, flops=2 * peers * w * d * 2 * e)

    low = allsum(parts, functools.partial(spread_low, n=n), 0)
    a_mat = -jnp.exp(w32(a_log))
    a2 = a_mat * LOG2E
    dtb, skip = w32(dt_bias)[None], w32(d_skip)[None]

    ins = [low, xz, xc, mask, dy_all, out_proj, dt_weight, dtb, a2]
    outs = [shp((peers, m, n, e), F32)] * 2 + [shp((3, m, n, e), F32), shp((peers, w, e), F32)]
    cks, ckp, end, dg = call(
        functools.partial(ahead, m=m, n=n, e=e), (peers,),
        [block(a, rising) for a in ins[:5]] + [whole(a) for a in ins[5:]],
        [block(outs[0], rising), block(outs[1], rising), whole(outs[2]), block(outs[3], rising)], outs,
        [pltpu.VMEM((m, n, e), F32)] * 3 + [pltpu.VMEM((w, e), F32)] * 3 + [pltpu.VMEM((w, 128), F32), pltpu.VMEM((w * n, 256), F32)],
        ins, flops=40 * 10 ** 9)

    ends = lax.all_gather(end, "rep")
    h_in = jnp.zeros((m, n, e), F32)
    q_in = jnp.zeros((m, n, e), F32)
    for k in range(reps - 1):
        o = reps - 1 - k
        h_in = jnp.where(k < rep, ends[k, 1] * h_in + ends[k, 0], h_in)
        q_in = jnp.where(o > rep, ends[o, 1] * q_in + ends[o, 2], q_in)

    dims = lattice(peers)
    anywhere = pl.BlockSpec(memory_space=pl.ANY)
    rows_done = []
    for i in range(m):
        def row(a, order, i=i):
            shape = (1, tl) if a.ndim == 3 else (1, 1, a.shape[2])
            return pl.BlockSpec(shape + a.shape[len(shape):], lambda b, r=a.ndim: (order(b), i) + (0,) * (r - 2))

        def one(a, i=i):
            return pl.BlockSpec((1,) + a.shape[1:], lambda b: (i, 0, 0))
        ins = [low, xz, xc, mask, dg, cks, ckp, out_proj, dt_weight, dtb, a2, skip, h_in, q_in]
        specs = [row(a, falling) for a in ins[:7]] + [whole(a) for a in ins[7:12]] + [one(a) for a in ins[12:]]
        outs = [shp((peers, tl, d), BF16), shp((peers, tl, e), BF16), shp((peers, tl, e), F32),
                shp((peers, rank + 2 * n, tl), F32), shp((peers, tl, e), BF16), shp((rank, e), F32), shp((n, e), F32), shp((8, e), F32)]
        out_specs = [block(a, falling) for a in outs[:5]] + [whole(a) for a in outs[5:]]
        scratch = [pltpu.VMEM((tl * n + n, e), F32), pltpu.VMEM((tl * n, e), F32), pltpu.VMEM((1, n, e), F32),
                   pltpu.VMEM((tl, 128), F32), pltpu.VMEM((tl * n, 256), F32)] + [pltpu.VMEM((tl, e), F32)] * 8
        params = {}
        if i:
            ins += [rows_done[i - 1][0].reshape(dims + (tl, d)), rows_done[i - 1][3].reshape(dims + (rank + 2 * n, tl))]
            specs += [anywhere] * 2
            outs += [shp((tl, d), F32), shp(dims + (tl, 256), BF16)]
            out_specs += [whole(a) for a in outs[-2:]]
            scratch += scatter_scratch(peers, tl, d, 16) + allsum_scratch(peers, rank + 2 * n, tl)
            params = dict(collective_id=5 + i, has_side_effects=True)
        rows_done.append(call(
            functools.partial(behind, n=n, e=e, dims=dims, reps=reps, sending=bool(i)), (peers,), specs, out_specs, outs,
            scratch, ins, flops=50 * 10 ** 9, **params))
    g_dt, g_a, vec = (sum(done[k] for done in rows_done) for k in range(5, 8))

    xpt = jnp.pad(x_proj.T, ((0, 256 - x_proj.shape[1]), (0, 0)))
    xz_first = xz[0].reshape(m, tl, 2 * e)[:, :EDGE, :e]
    edges = w32(edge).reshape(m, EDGE, e)
    out_sums = [done[8] for done in rows_done[1:]]
    ddbcs = [done[9].reshape(peers, tl, 256) for done in rows_done[1:]]
    backs = []
    for i in range(m):
        ext8 = jnp.concatenate([edges[i], w32(xz_first[i])], axis=0)
        same8 = mask[0, i * tl:i * tl + EDGE]
        conv8 = cb + cw[3] * ext8[EDGE:]
        for k in range(1, taps):
            conv8 = conv8 + cw[3 - k] * ext8[EDGE - k:2 * EDGE - k] * same8[:, k - 1:k]
        d8 = (rows_done[i][2][0, :EDGE] + mm(ddbcs[i][0, :EDGE], xpt)) * dsilu(conv8)
        follow = shift_rep(jnp.stack([cw[3 - k] * d8 * same8[:, k - 1:k] for k in range(1, taps)]), -1)

        def row(a, order, i=i):
            return pl.BlockSpec((1, tl) + a.shape[2:], lambda b: (order(b), i, 0))
        earlier = lambda b: jnp.maximum(peers - 2 - b, 0)
        ins = [xz, xz, edges[i], mask, ddbcs[i], nu_all, follow, w_cols, xpt, cw, cb, rows_done[i][2], rows_done[i][1]]
        specs = [row(xz, falling), row(xz, earlier), whole(ins[2]), row(mask, falling), block(ins[4], falling), row(nu_all, falling)]
        specs += [whole(a) for a in ins[6:11]] + [block(a, falling) for a in ins[11:13]] + [anywhere] * 2
        carry = pltpu.VMEM((taps - 1, EDGE, e), F32)
        if i < m - 1:
            ins += [rows_done[i + 1][0].reshape(dims + (tl, d)), rows_done[i + 1][3].reshape(dims + (rank + 2 * n, tl))]
            more = [nu_all, dy_all] + [done[1] for done in rows_done] + [done[4] for done in rows_done]
            ins += more
            specs += [block(a, falling) for a in more]
            outs = [shp((peers, tl, d), BF16), shp((d, e), F32), shp((8, e), F32), shp((tl, d), F32), shp((d, e), BF16),
                    shp((e, d), BF16), shp(dims + (tl, 256), BF16)]
            out_specs = [block(outs[0], falling)] + [whole(a) for a in outs[1:]]
            scratch = [carry, pltpu.VMEM((d, e), F32), pltpu.VMEM((e, d), F32)]
            scratch += scatter_scratch(peers, tl, d, 16) + allsum_scratch(peers, rank + 2 * n, tl)
        else:
            g_z = backs[i - 1][4]
            ins += [backs[i - 1][0].reshape(dims + (tl, d)), g_z.reshape(peers // reps, reps, dl, e), backs[i - 1][1]]
            specs += [anywhere]
            outs = [shp(dims + (tl, d), BF16), shp((8, e), F32), shp((tl, d), F32), shp((tl, d), F32), shp((dl, 2 * peers * e), F32)]
            out_specs = [anywhere] + [whole(a) for a in outs[1:]]
            scratch = [carry, pltpu.VMEM((d, e), F32), pltpu.VMEM((peers // reps, reps, dl, e), BF16), pltpu.VMEM((2, tl, d), BF16),
                       pltpu.SemaphoreType.DMA((2,)), pltpu.SemaphoreType.DMA((1,))] + scatter_scratch(peers, tl, d, 16, g_z) * 2
        backs.append(call(
            functools.partial(back, e=e, n=n, dims=dims, reps=reps, role="sum" if i < m - 1 else "owner"), (peers,), specs,
            out_specs, outs, scratch, ins, flops=peers * w * d * 3 * e, collective_id=8 + i, has_side_effects=True))
        if i < m - 1:
            out_sums.append(backs[i][3])
            ddbcs.append(backs[i][6].reshape(peers, tl, 256))
    g_out, _ = lax.optimization_barrier((backs[0][5], follow))
    vec2 = backs[0][2] + backs[1][1]
    layer_out = (u + jnp.stack(out_sums)).astype(BF16)

    v = jnp.stack([backs[1][2], backs[1][3]]) * gain
    in_grad = w32(out_grad) + r * v - u * (r * r * r) * jnp.mean(v * u, axis=2, keepdims=True)

    grad_in_proj = backs[1][4]
    grad_gain = jnp.sum(grad_in_proj * w32(in_proj), axis=1) / w32(norm_gain)

    g_xproj = sum(tn(xc.reshape(peers, m, tl, e)[:, i].reshape(peers * tl, e), ddbcs[i].reshape(peers * tl, 256)) for i in range(m))
    small = jnp.concatenate([vec, g_a * a_mat, g_dt, g_xproj.T], axis=0)
    small, vec2 = sum_rep(small), sum_rep(vec2)
    vec, g_a, g_dt, g_xp = small[:8], small[8:8 + n], small[8 + n:8 + n + rank], small[8 + n + rank:]
    return (layer_out, in_grad, grad_gain, grad_in_proj, vec2[:taps], vec2[taps], g_xp[:rank + 2 * n].T, g_dt, vec[0],
            g_a, vec[1], sum_rep(g_out))


def solution(mesh):
    tok, ids = P(None, ("rep", "shard"), None), P(None, ("rep", "shard"))
    row, col, one = P("shard", None), P(None, "shard"), P("shard")
    return jax.shard_map(
        on_device,
        mesh=mesh,
        in_specs=(tok, ids, tok, one, row, col, one, row, col, one, col, one, row),
        out_specs=(tok, tok, one, row, col, one, row, col, one, col, one, row),
        check_vma=False,
    )
```

```python
import functools
import jax
import jax.numpy as jnp
from jax import lax
from jax.sharding import PartitionSpec as P
from jax.experimental import pallas as pl
from jax.experimental.pallas import tpu as pltpu

F32, BF16 = jnp.float32, jnp.bfloat16
LOG2E, LN2 = 1.4426950408889634, 0.6931471805599453
EDGE = 8
VMEM = 60 << 20


def nt(a, b):
    return lax.dot_general(a, b, (((1,), (1,)), ((), ())), preferred_element_type=F32)


def tn(a, b):
    return lax.dot_general(a, b, (((0,), (0,)), ((), ())), preferred_element_type=F32)


def mm(a, b):
    return jnp.dot(a, b, preferred_element_type=F32)


def softplus(v):
    return jnp.maximum(v, 0.0) + jnp.log1p(jnp.exp(-jnp.abs(v)))


def wide(v, e):
    return jnp.concatenate([v] * (e // 128), axis=1) if e > 128 else v


def at(start, size, unit=8):
    return pl.ds(pl.multiple_of(start, unit), size)


def call(kernel, grid, in_specs, out_specs, out_shape, scratch, args, flops=0, **params):
    size = sum(a.size * a.dtype.itemsize for a in args) + sum(s.size * s.dtype.itemsize for s in out_shape)
    return pl.pallas_call(
        kernel, grid=grid, in_specs=in_specs, out_specs=out_specs, out_shape=out_shape,
        scratch_shapes=scratch, compiler_params=pltpu.CompilerParams(vmem_limit_bytes=VMEM, **params),
        cost_estimate=pl.CostEstimate(flops=flops, bytes_accessed=size, transcendentals=0))(*args)


def whole(a):
    return pl.BlockSpec(a.shape, lambda i, r=len(a.shape): (0,) * r)


def block(a, order):
    return pl.BlockSpec((1,) + a.shape[1:], lambda i, r=len(a.shape): (order(i),) + (0,) * (r - 1))


def lags(x_ext, rows):
    return [x_ext[EDGE - k:EDGE - k + rows] for k in range(4)]


def convolve(lag, same, cw, cb):
    out = cb + cw[3:4] * lag[0]
    for k in range(1, 4):
        out = out + cw[3 - k:4 - k] * lag[k] * same[:, k - 1:k]
    return out


def normalise(rows, gain):
    u = rows.astype(F32)
    return (u * lax.rsqrt(jnp.mean(u * u, axis=1, keepdims=True) + 1e-5) * gain).astype(BF16)


def front(hid_ref, w_ref, halo_ref, mask_ref, cw_ref, cb_ref, xp_ref, gain_ref, xz_ref, xc_ref, nu_ref, edge_ref,
          *rest, m, e):
    parts, carry = rest[:m], rest[m]
    @pl.when(pl.program_id(0) == 0)
    def _():
        edge = mm(normalise(halo_ref[...], gain_ref[...]), w_ref[:, :e]).astype(BF16)
        edge_ref[...] = edge
        carry[...] = edge.astype(F32)
    nu = normalise(hid_ref[0], gain_ref[...])
    nu_ref[0] = nu
    xz = mm(nu, w_ref[...]).astype(BF16)
    xz_ref[0] = xz
    rows = xz.shape[0] // m
    cw, cb = cw_ref[...], cb_ref[...]
    for i in range(m):
        x = xz[i * rows:(i + 1) * rows, :e].astype(F32)
        ext = jnp.concatenate([carry[i * EDGE:(i + 1) * EDGE], x], axis=0)
        carry[i * EDGE:(i + 1) * EDGE] = x[rows - EDGE:]
        conv = convolve(lags(ext, rows), mask_ref[0, i * rows:(i + 1) * rows], cw, cb)
        xc = (conv * jax.nn.sigmoid(conv)).astype(BF16)
        xc_ref[0, i * rows:(i + 1) * rows] = xc
        parts[i][0] = nt(xp_ref[...], xc)


def lattice(peers):
    y = 2 if peers <= 16 else 4
    return peers // (2 * y), y, 2


def place(target):
    return target if isinstance(target, dict) else {"shard": target}


def greet(targets):
    barrier = pltpu.get_barrier_semaphore()
    for target in targets:
        pl.semaphore_signal(barrier, inc=1, device_id=place(target), device_id_type=pl.DeviceIdType.MESH)
    pl.semaphore_wait(barrier, len(targets))


def remote(src, dst, send, recv, target):
    return pltpu.make_async_remote_copy(src_ref=src, dst_ref=dst, send_sem=send, recv_sem=recv,
                                        device_id=place(target), device_id_type=pl.DeviceIdType.MESH)


def spread_low(total, n):
    rows = jnp.concatenate([total, jnp.zeros((256 - total.shape[0], total.shape[1]), F32)], axis=0).T
    rank = total.shape[0] - 2 * n
    out = [rows[:, :rank].astype(BF16)]
    rest = rows[:, rank:]
    hi = rest.astype(BF16)
    mid = (rest - hi.astype(F32)).astype(BF16)
    lo = (rest - hi.astype(F32) - mid.astype(F32)).astype(BF16)
    for k in range(2):
        out += [p[:, k * n:(k + 1) * n] for p in (hi, mid, lo)]
    out.append(jnp.zeros((rows.shape[0], 128 - 6 * n), BF16))
    return jnp.concatenate(out, axis=1)


def spread_plain(total, n):
    return jnp.concatenate([total, jnp.zeros((256 - total.shape[0], total.shape[1]), F32)], axis=0).T.astype(BF16)


def allsum_kernel(*refs, dims, chunks, finish):
    parts = refs[:chunks]
    out, rc, ac, low, ry, rz, send, recv = refs[chunks:]
    nz, ny, _ = dims
    me = lax.axis_index("shard")
    c, y, z = me % 2, (me // 2) % ny, me // (2 * ny)
    where = lambda a, b, d: (a * ny + b) * 2 + d
    across = where(z, y, 1 - c)
    ys = [lax.rem(y + k, ny) for k in range(1, ny)]
    zs = [lax.rem(z + k, nz) for k in range(1, nz)]
    greet([across] + [where(z, b, c) for b in ys] + [where(a, y, c) for a in zs])
    width = parts[0].shape[-1]
    rows = [pl.ds(q * width, width) for q in range(chunks)]

    def start(copies):
        for copy in copies:
            copy.start()
        return copies

    def finish_all(copies):
        for copy in copies:
            copy.wait()
    base = [0]

    def sems(count):
        base[0] += count
        return [(send.at[base[0] - count + k], recv.at[base[0] - count + k]) for k in range(count)]

    first = []
    for q in range(chunks):
        (s, r), = sems(1)
        first.append(start([remote(parts[q].at[:, :, 1 - c], rc.at[q], s, r, across)]))
    second = []
    for q in range(chunks):
        finish_all(first[q])
        for a in range(nz):
            for b in range(ny):
                total = parts[q][a, b, c] + rc[q, a, b]
                ac[q, a, b] = total
                low[q, a, b] = total.astype(BF16)
        second.append(start([remote(low.at[q, :, b], ry.at[q, k], *sem, where(z, b, c))
                             for k, (b, sem) in enumerate(zip(ys, sems(ny - 1)))]))
    third = []
    for q in range(chunks):
        finish_all(second[q])
        for a in range(nz):
            got = ac[q, a, y]
            for k in range(ny - 1):
                got = got + ry[q, k, a].astype(F32)
            ac[q, a, y] = got
            low[q, a, y] = got.astype(BF16)
        third.append(start([remote(low.at[q, a, y], rz.at[q, k], *sem, where(a, y, c))
                            for k, (a, sem) in enumerate(zip(zs, sems(nz - 1)))]))
    fourth = []
    for q in range(chunks):
        finish_all(third[q])
        got = ac[q, z, y]
        for k in range(nz - 1):
            got = got + rz[q, k].astype(F32)
        out[z, y, c, q * width:(q + 1) * width] = finish(got)
        mine = out.at[z, y, c, rows[q]]
        fourth.append(start([remote(mine, mine, *sem, where(a, y, c)) for a, sem in zip(zs, sems(nz - 1))]))
    fifth = []
    for q in range(chunks):
        finish_all(fourth[q])
        mine = out.at[:, y, c, rows[q]]
        fifth.append(start([remote(mine, mine, *sem, where(z, b, c)) for b, sem in zip(ys, sems(ny - 1))]))
    last = []
    for q in range(chunks):
        finish_all(fifth[q])
        mine = out.at[:, :, c, rows[q]]
        (s, r), = sems(1)
        last.append(start([remote(mine, mine, s, r, across)]))
    for q in range(chunks):
        finish_all(last[q])


def allsum(parts, finish, collective_id):
    peers, cols, width = parts[0].shape
    w = width * len(parts)
    dims = lattice(peers)
    nz, ny, nc = dims
    chunks = len(parts)
    copies = 2 * chunks * (1 + ny - 1 + nz - 1)
    out = pl.pallas_call(
        functools.partial(allsum_kernel, dims=dims, chunks=chunks, finish=finish),
        out_shape=jax.ShapeDtypeStruct((nz, ny, nc, w, 256), BF16),
        in_specs=[pl.BlockSpec(memory_space=pltpu.VMEM)] * chunks,
        out_specs=pl.BlockSpec(memory_space=pltpu.VMEM),
        scratch_shapes=[pltpu.VMEM((chunks, nz, ny, cols, 128), F32), pltpu.VMEM((chunks, nz, ny, cols, 128), F32),
                        pltpu.VMEM((chunks, nz, ny, cols, 128), BF16), pltpu.VMEM((chunks, ny - 1, nz, cols, 128), BF16),
                        pltpu.VMEM((chunks, nz - 1, cols, 128), BF16),
                        pltpu.SemaphoreType.DMA((copies,)), pltpu.SemaphoreType.DMA((copies,))],
        compiler_params=pltpu.CompilerParams(collective_id=collective_id, has_side_effects=True, vmem_limit_bytes=VMEM),
    )(*[part.reshape(nz, ny, nc, cols, width) for part in parts])
    return out.reshape(peers, w, 256)


def gather_kernel(x, small, wts, out, small_out, cols, send, recv, s_send, s_recv, w_send, w_recv, own_sem, *, dims, chunks):
    nz, ny, _ = dims
    me = lax.axis_index("shard")
    c, y, z = me % 2, (me // 2) % ny, me // (2 * ny)
    where = lambda a, b, d: (a * ny + b) * 2 + d
    across = where(z, y, 1 - c)
    ys = [lax.rem(y + k, ny) for k in range(1, ny)]
    ys_from = [lax.rem(y + ny - k, ny) for k in range(1, ny)]
    zs = [lax.rem(z + k, nz) for k in range(1, nz)]
    peers = nz * ny * 2
    others = [lax.rem(me + k, peers) for k in range(1, peers)]
    greet(others + [{"rep": lax.axis_index("rep") + 1 - 2 * lax.rem(lax.axis_index("rep"), 2)}])
    dl, e = wts.shape[0], wts.shape[1] // (2 * peers)
    size = x.shape[0] // chunks
    rows = [pl.ds(q * size, size) for q in range(chunks)]

    keep = pltpu.make_async_copy(small, small_out.at[z, y, c], own_sem.at[0])
    keep.start()
    whole_own = pltpu.make_async_copy(x, out.at[z, y, c], own_sem.at[1])
    whole_own.start()

    rep = lax.axis_index("rep")
    odd = lax.rem(rep, 2)
    hl = dl // 2

    def piece(half, src, dst):
        return (wts.at[pl.ds(pl.multiple_of(odd * hl, hl), hl), pl.ds(pl.multiple_of(half * peers * e + dst * e, 128), e)],
                cols.at[src, odd, :, pl.ds(half * e, e)])
    kept = [pltpu.make_async_copy(*piece(half, me, me), own_sem.at[2 + half]) for half in range(2)]
    swapped = remote(cols.at[:, odd], cols.at[:, odd], w_send.at[2 * peers - 2], w_recv.at[2 * peers - 2], {"rep": rep + 1 - 2 * odd})
    sent = [remote(*piece(half, me, p), w_send.at[2 * k + half], w_recv.at[2 * k + half], p)
            for k, p in enumerate(others) for half in range(2)]

    kinds = 2 * nz - 1
    offset = [0] + [-1 - j for j in range(nz - 1)] + [1 + j for j in range(nz - 1)]

    def valid(kind):
        return (z + offset[kind] >= 0) & (z + offset[kind] < nz)

    def sems(group, kind, q):
        at_ = (group * kinds + kind) * chunks + q
        return send.at[at_], recv.at[at_]

    def hop(kind, q, up):
        there = out.at[z + offset[kind], y, c, rows[q]]
        src = x.at[rows[q]] if kind == 0 else there
        j = -offset[kind] if up else offset[kind]
        to_kind = 1 + j if up else nz + j
        return remote(src, there, *sems(0, to_kind, q), where(z + 1 if up else z - 1, y, c))

    def can_hop(kind, up):
        return valid(kind) & ((z + 1 < nz) if up else (z >= 1))

    def over_y(kind, q, k):
        there = out.at[z + offset[kind], y, c, rows[q]]
        src = x.at[rows[q]] if kind == 0 else there
        return remote(src, there, *sems(1 + k, kind, q), where(z, ys[k], c))

    def over_core(kind, q, k):
        there = out.at[z + offset[kind], y if k == 0 else ys_from[k - 1], c, rows[q]]
        src = x.at[rows[q]] if kind == 0 and k == 0 else there
        return remote(src, there, *sems(ny + k, kind, q), across)

    def landed(kind, q, b, d, group):
        there = out.at[z + offset[kind], b, d, rows[q]]
        return remote(there, there, *sems(group, kind, q), across)

    def onward(kind, q):
        if kind == 0:
            ups = [True, False]
        elif kind < nz:
            ups = [True] if kind < nz - 1 else []
        else:
            ups = [False] if kind < kinds - 1 else []
        for up in ups:
            @pl.when(can_hop(kind, up))
            def _(up=up):
                hop(kind, q, up).start()
        for k in range(ny - 1):
            over_y(kind, q, k).start()
        over_core(kind, q, 0).start()

    tiny = []

    def tiny_start(copies):
        tiny.append(copies)
        for copy in copies:
            copy.start()

    def tiny_wait():
        for copy in tiny[-1]:
            copy.wait()

    tiny_start([remote(small, small_out.at[z, y, c], s_send.at[k], s_recv.at[k], where(a, y, c)) for k, a in enumerate(zs)])
    for q in range(chunks):
        onward(0, q)
    for copy in kept + sent:
        copy.start()
    tiny_wait()
    keep.wait()
    tiny_start([remote(small_out.at[:, y, c], small_out.at[:, y, c], s_send.at[nz - 1 + k], s_recv.at[nz - 1 + k], where(z, b, c))
                for k, b in enumerate(ys)])

    def from_y(kind, q):
        @pl.when(valid(kind))
        def _():
            for k in range(1, ny):
                landed(kind, q, ys_from[k - 1], c, k).wait_recv()
                over_core(kind, q, k).start()

    waves = [[0]] + [[1 + j, nz + j] for j in range(nz - 1)]
    for number, wave in enumerate(waves):
        for q in range(chunks):
            for kind in wave:
                if kind:
                    @pl.when(valid(kind))
                    def _(kind=kind, q=q):
                        landed(kind, q, y, c, 0).wait_recv()
                        onward(kind, q)
        if number == 2:
            for copy in kept + sent:
                copy.wait()
            swapped.start()
        if number == 1:
            tiny_wait()
            last = small_out.at[:, :, c]
            tiny_start([remote(last, last, s_send.at[nz + ny - 2], s_recv.at[nz + ny - 2], across)])
        if number:
            for q in range(chunks):
                for kind in waves[number - 1]:
                    from_y(kind, q)
    for q in range(chunks):
        for kind in waves[-1]:
            from_y(kind, q)
    tiny_wait()
    for kind in range(kinds):
        @pl.when(valid(kind))
        def _(kind=kind):
            for q in range(chunks):
                for k in range(ny):
                    landed(kind, q, y if k == 0 else ys_from[k - 1], 1 - c, ny + k).wait_recv()
                    over_core(kind, q, k).wait_send()
                for k in range(ny - 1):
                    over_y(kind, q, k).wait_send()
        for up in (True, False):
            j = -offset[kind] if up else offset[kind]
            if 0 <= j < nz - 1:
                @pl.when(can_hop(kind, up))
                def _(kind=kind, up=up):
                    for q in range(chunks):
                        hop(kind, q, up).wait_send()
    swapped.wait()
    whole_own.wait()


def gather(x, small, wts, collective_id, chunks=4):
    w, d = x.shape
    peers = lax.axis_size("shard")
    dims = lattice(peers)
    nz, ny, nc = dims
    copies = 2 * ny * (2 * nz - 1) * chunks
    dl, e = wts.shape[0], wts.shape[1] // (2 * peers)
    out, tiles, cols = pl.pallas_call(
        functools.partial(gather_kernel, dims=dims, chunks=chunks),
        out_shape=[jax.ShapeDtypeStruct((nz, ny, nc, w, d), x.dtype), jax.ShapeDtypeStruct((nz, ny, nc, 8, 128), F32),
                   jax.ShapeDtypeStruct((peers, 2, dl // 2, 2 * e), BF16)],
        in_specs=[pl.BlockSpec(memory_space=pl.ANY), pl.BlockSpec(memory_space=pltpu.VMEM), pl.BlockSpec(memory_space=pl.ANY)],
        out_specs=[pl.BlockSpec(memory_space=pl.ANY), pl.BlockSpec(memory_space=pltpu.VMEM), pl.BlockSpec(memory_space=pl.ANY)],
        scratch_shapes=[pltpu.SemaphoreType.DMA((copies,)), pltpu.SemaphoreType.DMA((copies,)),
                        pltpu.SemaphoreType.DMA((nz + ny,)), pltpu.SemaphoreType.DMA((nz + ny,)),
                        pltpu.SemaphoreType.DMA((2 * peers - 1,)), pltpu.SemaphoreType.DMA((2 * peers - 1,)),
                        pltpu.SemaphoreType.DMA((4,))],
        compiler_params=pltpu.CompilerParams(collective_id=collective_id, has_side_effects=True, vmem_limit_bytes=VMEM),
        cost_estimate=pl.CostEstimate(flops=8 * 10 ** 10, bytes_accessed=2 * peers * w * d, transcendentals=0),
    )(x, small, wts)
    return out.reshape(peers, w, d), tiles.reshape(peers, 8, 128), cols.reshape(peers * dl, 2 * e)


def meet(dims, reps):
    nz, ny, _ = dims
    me, rep = lax.axis_index("shard"), lax.axis_index("rep")
    c, y, z = me % 2, (me // 2) % ny, me // (2 * ny)
    if reps:
        greet([lax.rem(me + k, nz * ny * 2) for k in range(1, nz * ny * 2)]
              + [{"rep": lax.rem(rep + k, reps)} for k in range(1, reps)])
    else:
        greet([(z * ny + y) * 2 + 1 - c] + [(z * ny + lax.rem(y + k, ny)) * 2 + c for k in range(1, ny)]
              + [(lax.rem(z + k, nz) * ny + y) * 2 + c for k in range(1, nz)])


def scatter_steps(refs, dims, reps, lag_y=2, lag_z=4, sum_at=4, cross_at=9, first_col=0):
    part, g, out, g_out, rc, own, ry, rz, ga, gs, rg, load, send, recv, g_load, a_send, a_recv, b_send, b_recv, c_send, c_recv = refs
    nz, ny, _ = dims
    me, rep = lax.axis_index("shard"), lax.axis_index("rep")
    c, y, z = me % 2, (me // 2) % ny, me // (2 * ny)
    where = lambda a, b, d: (a * ny + b) * 2 + d
    across = where(z, y, 1 - c)
    ys = [lax.rem(y + k, ny) for k in range(1, ny)]
    zs = [lax.rem(z + k, nz) for k in range(1, nz)]
    peers = nz * ny * 2
    others = [lax.rem(me + k, peers) for k in range(1, peers)]
    far = [{"rep": lax.rem(rep + k, reps)} for k in range(1, reps)]
    slots, size = own.shape[0], own.shape[3]
    chunks = part.shape[3] // size
    rows = [pl.ds(q * size, size) for q in range(chunks)]
    per = ny + nz - 1

    def pair(q, k):
        return send.at[q * per + k], recv.at[q * per + k]

    def loads(q):
        return pltpu.make_async_copy(part.at[:, :, c, rows[q]], own.at[q % slots], load.at[q])

    def first(q):
        return remote(part.at[:, :, 1 - c, rows[q]], rc.at[:, :, rows[q]], *pair(q, 0), across)

    def second(q):
        return [remote(rc.at[:, b, rows[q]], ry.at[k, :, rows[q]], *pair(q, 1 + k), where(z, b, c))
                for k, b in enumerate(ys)]

    def third(q):
        return [remote(rc.at[a, y, rows[q]], rz.at[k, rows[q]], *pair(q, ny + k), where(a, y, c))
                for k, a in enumerate(zs)]

    groups = peers // reps
    owner_here = lax.rem(me, reps) == rep

    def shared():
        return pltpu.make_async_copy(g.at[:, rep], ga.at[rep], g_load.at[0]), [
            remote(g.at[:, lax.rem(rep + k, reps)], ga.at[rep], a_send.at[k - 1], a_recv.at[k - 1], far[k - 1])
            for k in range(1, reps)]

    def handed(k):
        p = lax.rem(me // reps + k, groups)
        return remote(gs.at[p], rg.at[me], b_send.at[k], b_recv.at[me], p * reps + rep)

    def arrived(k):
        src = lax.rem(me + k, peers)
        return remote(gs.at[0], rg.at[src], b_send.at[0], b_recv.at[src], lax.rem(me + 1, peers))

    def crossed(k):
        return remote(rg, rg, c_send.at[k - 1], c_recv, far[k - 1])

    def g_sum():
        kept, sent = shared()
        for copy in [kept] + sent:
            copy.wait()

        def add(p, _):
            total = ga[0, p].astype(F32)
            for k in range(1, reps):
                total = total + ga[k, p].astype(F32)
            gs[p] = total.astype(BF16)
            return 0
        lax.fori_loop(0, groups, add, 0)

        @pl.when(owner_here)
        def _():
            rg[me] = gs[me // reps]

        @pl.when(jnp.logical_not(owner_here))
        def _():
            handed(0).start()
        for k in range(1, groups):
            handed(k).start()

    def g_cross():
        @pl.when(owner_here)
        def _():
            for k in range(1, peers):
                arrived(k).wait_recv()
            for k in range(1, reps):
                crossed(k).start()

        @pl.when(jnp.logical_not(owner_here))
        def _():
            handed(0).wait_send()
        for k in range(1, groups):
            handed(k).wait_send()

    def g_end():
        @pl.when(owner_here)
        def _():
            for k in range(1, reps):
                crossed(k).wait_send()

        @pl.when(jnp.logical_not(owner_here))
        def _():
            crossed(1).wait_recv()
        e = rg.shape[2]
        for p in range(peers):
            g_out[:, first_col + p * e:first_col + (p + 1) * e] = rg[p].astype(F32)

    def start():
        for q in range(min(slots, chunks)):
            loads(q).start()
        for q in range(chunks):
            first(q).start()
        if g is not None:
            kept, sent = shared()
            for copy in [kept] + sent:
                copy.start()

    def over_core(q):
        loads(q).wait()
        first(q).wait()

        def add(a, _):
            i, j = a // ny, a % ny
            rc[i, j, rows[q]] = (own[q % slots, i, j].astype(F32) + rc[i, j, rows[q]].astype(F32)).astype(BF16)
            return 0
        lax.fori_loop(0, nz * ny, add, 0)
        if q + slots < chunks:
            loads(q + slots).start()
        for copy in second(q):
            copy.start()

    def over_y(q):
        for copy in second(q):
            copy.wait()

        def add(a, _):
            total = rc[a, y, rows[q]].astype(F32)
            for k in range(ny - 1):
                total = total + ry[k, a, rows[q]].astype(F32)
            rc[a, y, rows[q]] = total.astype(BF16)
            return 0
        lax.fori_loop(0, nz, add, 0)
        for copy in third(q):
            copy.start()

    def over_z(q):
        for copy in third(q):
            copy.wait()
        total = rc[z, y, rows[q]].astype(F32)
        for k in range(nz - 1):
            total = total + rz[k, rows[q]].astype(F32)
        out[rows[q]] = total

    def step(s):
        if s < chunks:
            over_core(s)
        if 0 <= s - lag_y < chunks:
            over_y(s - lag_y)
        if 0 <= s - lag_z < chunks:
            over_z(s - lag_z)
        if s == sum_at and g is not None:
            g_sum()
        if s == cross_at and g is not None:
            g_cross()

    def finish():
        if g is not None:
            g_end()
    return start, [functools.partial(step, s) for s in range(chunks + lag_z)], finish


def scatter_scratch(peers, w, d, size, g=None):
    nz, ny, nc = lattice(peers)
    chunks = w // size
    dma = pltpu.SemaphoreType.DMA
    copies = chunks * (ny + nz - 1)
    out = [pltpu.VMEM((nz, ny, w, d), BF16), pltpu.VMEM((3, nz, ny, size, d), BF16),
           pltpu.VMEM((ny - 1, nz, w, d), BF16), pltpu.VMEM((nz - 1, w, d), BF16)]
    tail = [dma((chunks,)), dma((copies,)), dma((copies,))]
    if g is None:
        return out + tail
    reps = lax.axis_size("rep")
    dl, e = g.shape[0] // peers, g.shape[1]
    return (out + [pltpu.VMEM((reps, peers // reps, dl, e), BF16), pltpu.VMEM((peers // reps, dl, e), BF16),
                   pltpu.VMEM((peers, dl, e), BF16)] + tail
            + [dma((1,)), dma((reps - 1,)), dma((reps - 1,)), dma((peers // reps,)), dma((peers,)), dma((reps - 1,)), dma])


def allsum_steps(refs, dims, finish):
    part, result, out, mine, rc, low, ry, rz, load, send, recv = refs
    nz, ny, _ = dims
    me = lax.axis_index("shard")
    c, y, z = me % 2, (me // 2) % ny, me // (2 * ny)
    where = lambda a, b, d: (a * ny + b) * 2 + d
    across = where(z, y, 1 - c)
    ys = [lax.rem(y + k, ny) for k in range(1, ny)]
    zs = [lax.rem(z + k, nz) for k in range(1, nz)]
    base = [0, 1, ny, ny + nz - 1, ny + 2 * nz - 2, 2 * ny + 2 * nz - 3]

    def sem(stage, k):
        return send.at[base[stage] + k], recv.at[base[stage] + k]

    def copies(stage):
        if stage == 0:
            return [remote(part.at[:, :, 1 - c], rc, *sem(0, 0), across)]
        if stage == 1:
            return [remote(low.at[:, b], ry.at[k], *sem(1, k), where(z, b, c)) for k, b in enumerate(ys)]
        if stage == 2:
            return [remote(low.at[a, y], rz.at[k], *sem(2, k), where(a, y, c)) for k, a in enumerate(zs)]
        if stage == 3:
            held, targets = out.at[z, y, c], [where(a, y, c) for a in zs]
        elif stage == 4:
            held, targets = out.at[:, y, c], [where(z, b, c) for b in ys]
        else:
            held, targets = out.at[:, :, c], [across]
        return [remote(held, held, *sem(stage, k), target) for k, target in enumerate(targets)]

    def own():
        return pltpu.make_async_copy(part.at[:, :, c], mine, load.at[0])

    def start():
        own().start()
        for copy in copies(0):
            copy.start()

    def step(s):
        if s == 0:
            own().wait()
        for copy in copies(s):
            copy.wait()
        if s == 0:
            def add(a, _):
                i, j = a // ny, a % ny
                total = mine[i, j] + rc[i, j]
                mine[i, j] = total
                low[i, j] = total.astype(BF16)
                return 0
            lax.fori_loop(0, nz * ny, add, 0)
        if s == 1:
            for a in range(nz):
                total = mine[a, y]
                for k in range(ny - 1):
                    total = total + ry[k, a].astype(F32)
                mine[a, y] = total
                low[a, y] = total.astype(BF16)
        if s == 2:
            total = mine[z, y]
            for k in range(nz - 1):
                total = total + rz[k].astype(F32)
            out[z, y, c] = finish(total)
        if s < 5:
            for copy in copies(s + 1):
                copy.start()

    def end():
        result[...] = out[...]
    return start, [functools.partial(step, s) for s in range(6)], end


def allsum_scratch(peers, cols, width):
    nz, ny, nc = lattice(peers)
    dma = pltpu.SemaphoreType.DMA
    count = 2 * (1 + ny - 1 + nz - 1)
    return [pltpu.VMEM((nz, ny, nc, width, 256), BF16), pltpu.VMEM((nz, ny, cols, width), F32),
            pltpu.VMEM((nz, ny, cols, width), F32),
            pltpu.VMEM((nz, ny, cols, width), BF16), pltpu.VMEM((ny - 1, nz, cols, width), BF16),
            pltpu.VMEM((nz - 1, cols, width), BF16), dma((1,)), dma((count,)), dma((count,))]


def beside(b, grid, dims, reps, transfers):
    @pl.when(b == 0)
    def _():
        meet(dims, reps)
        for start, _, _, _ in transfers:
            start()
    for _, steps, _, when in transfers:
        for s, step in enumerate(steps):
            @pl.when(b == (when[s] if when else (s * (grid - 1)) // len(steps) + 1))
            def _(step=step):
                step()

    @pl.when(b == grid - 1)
    def _():
        for _, _, finish, _ in transfers:
            finish()


PACED = [1, 1, 1, 1, 2, 2, 2, 2, 3, 5, 6, 8, 9, 11, 13, 14, 15, 15]


def fill(low_ref, bcs_scr, bc_scr, n):
    bcs_scr[...] = low_ref[0, :, 128:].astype(F32)
    lane = lax.broadcasted_iota(jnp.int32, (n, 128), 1)
    sub = lax.broadcasted_iota(jnp.int32, (n, 128), 0)
    mask = (lane % n) == sub
    r = lax.broadcasted_iota(jnp.int32, (128, 256), 0)
    c = lax.broadcasted_iota(jnp.int32, (128, 256), 1)
    ones = jnp.where((r >= 3 * n) == (c >= 128), 1.0, 0.0).astype(BF16)
    group = 128

    def body(g, _):
        rows = [jnp.where(mask, bcs_scr[pl.ds(g * group + j, 1), :], 0.0).astype(BF16) for j in range(group)]
        bc_scr[at(g * (group * n), group * n, 128), :] = mm(jnp.concatenate(rows, axis=0), ones)
        return 0
    lax.fori_loop(0, bcs_scr.shape[0] // group, body, 0)


def fold_rows(vals, sub):
    for k in (1, 2, 4):
        mask = (sub & k) == 0
        vals = [jnp.where(mask, a, b) + pltpu.roll(jnp.where(mask, b, a), 8 - k, 0)
                for a, b in zip(vals[::2], vals[1::2])]
    return vals[0]


def ahead(low_ref, xz_ref, xc_ref, mask_ref, dy_ref, wo_ref, wdt_ref, dtb_ref, a2_ref,
          cks_ref, ckp_ref, end_ref, dg_ref, s_scr, p_scr, f_scr, sd_scr, dx_scr, dy_scr, bcs_scr, bc_scr, *, m, n, e):
    b = pl.program_id(0)
    @pl.when(b == 0)
    def _():
        s_scr[...] = jnp.zeros_like(s_scr)
        p_scr[...] = jnp.ones_like(p_scr)
        f_scr[...] = jnp.zeros_like(f_scr)
    cks_ref[0] = s_scr[...]
    ckp_ref[0] = p_scr[...]
    fill(low_ref, bcs_scr, bc_scr, n)
    step = softplus(mm(low_ref[0, :, :128], wdt_ref[...]) + dtb_ref[...])
    sd_scr[...] = jnp.where(mask_ref[0, :, 0:1] > 0.0, step, 1e30)
    dx_scr[...] = step * xc_ref[0].astype(F32)
    dg = nt(dy_ref[0], wo_ref[...])
    dg_ref[0] = dg
    z = xz_ref[0, :, e:].astype(F32)
    dy_scr[...] = dg * (z * jax.nn.sigmoid(z))
    a2 = a2_ref[...]
    rows = sd_scr.shape[0] // m
    un = 16

    def group(g, carry):
        s, p, f = [list(c) for c in carry]
        for j in range(un):
            for i in range(m):
                t = i * rows + g * un + j
                bc = bc_scr[at(t * n, n, n), :]
                bb, cc = wide(bc[:, :128], e), wide(bc[:, 128:], e)
                a = jnp.exp2(sd_scr[pl.ds(t, 1), :] * a2)
                s[i] = a * s[i] + bb * dx_scr[pl.ds(t, 1), :]
                p[i] = p[i] * a
                f[i] = f[i] + p[i] * (cc * dy_scr[pl.ds(t, 1), :])
        return tuple(s), tuple(p), tuple(f)
    done = lax.fori_loop(0, rows // un, group,
                         tuple(tuple(scr[i] for i in range(m)) for scr in (s_scr, p_scr, f_scr)))
    for scr, vals in zip((s_scr, p_scr, f_scr), done):
        for i in range(m):
            scr[i] = vals[i]

    @pl.when(b == pl.num_programs(0) - 1)
    def _():
        end_ref[0] = s_scr[...]
        end_ref[1] = p_scr[...]
        end_ref[2] = f_scr[...]


def behind(*refs, n, e, dims, reps, sending):
    (low_ref, xz_ref, xc_ref, mask_ref, dg_ref, cks_ref, ckp_ref,
     wo_ref, wdt_ref, dtb_ref, a2_ref, skip_ref, hin_ref, qin_ref) = refs[:14]
    refs = refs[14:]
    if sending:
        before, adding, refs = refs[0], refs[1], refs[2:]
    out_ref, dz_ref, dxc_ref, part_ref, gated_ref, gdt_ref, ga_ref, vec_ref = refs[:8]
    refs = refs[8:]
    if sending:
        summed, added, refs = refs[0], refs[1], refs[2:]
    (h_scr, a_scr, q_scr, bcs_scr, bc_scr, pre_scr, st_scr, sd_scr, dx_scr, dy_scr, y_scr, da_scr, gb_scr) = refs[:13]
    b = pl.program_id(0)
    if sending:
        rc, own, ry, rz, load, send, recv = refs[13:20]
        beside(b, dims[0] * dims[1] * dims[2], dims, 0, [
            allsum_steps((adding, added) + refs[20:], dims, functools.partial(spread_plain, n=n)) + (None,),
            scatter_steps((before, None, summed, None, rc, own, ry, rz, None, None, None, load, send, recv) + (None,) * 7,
                          dims, reps, 8, 10) + (PACED,)])
    m = 1
    @pl.when(b == 0)
    def _():
        q_scr[...] = qin_ref[...]
        for ref in (gdt_ref, ga_ref, vec_ref):
            ref[...] = jnp.zeros_like(ref)
    fill(low_ref, bcs_scr, bc_scr, n)
    pre = mm(low_ref[0, :, :128], wdt_ref[...]) + dtb_ref[...]
    pre_scr[...] = pre
    step = softplus(pre)
    st_scr[...] = step
    sd_scr[...] = jnp.where(mask_ref[0, :, 0:1] > 0.0, step, 1e30)
    dx_scr[...] = step * xc_ref[0].astype(F32)
    z = xz_ref[0, :, e:].astype(F32)
    dy_scr[...] = dg_ref[0] * (z * jax.nn.sigmoid(z))
    a2 = a2_ref[...]
    sub = lax.broadcasted_iota(jnp.int32, (8, e), 0)
    rows = sd_scr.shape[0] // m
    lanes = lax.broadcasted_iota(jnp.int32, (n, rows), 1)
    un = 32
    for i in range(m):
        r0 = i * rows
        h0 = cks_ref[0, i] + ckp_ref[0, i] * hin_ref[i]
        h_scr[pl.ds(0, n), :] = h0

        def fwd(g, h, r0=r0):
            ys = []
            for j in range(un):
                t = g * un + j
                bc = bc_scr[at((r0 + t) * n, n, n), :]
                bb, cc = wide(bc[:, :128], e), wide(bc[:, 128:], e)
                a = jnp.exp2(sd_scr[pl.ds(r0 + t, 1), :] * a2)
                h = a * h + bb * dx_scr[pl.ds(r0 + t, 1), :]
                a_scr[at(t * n, n, n), :] = a
                h_scr[at(t * n + n, n, n), :] = h
                cy = cc * h
                ys.append(cy[:8] + cy[8:])
                if len(ys) == 8:
                    y_scr[at(r0 + t - 7, 8), :] = fold_rows(ys, sub)
                    ys = []
            return h
        lax.fori_loop(0, rows // un, fwd, h0)

        def bwd(g, carry, r0=r0):
            q, ga, hn, db, dc = carry
            das, gbs = [], []
            for j in range(un):
                t = rows - 1 - (g * un + j)
                bc = bc_scr[at((r0 + t) * n, n, n), :]
                bb, cc = wide(bc[:, :128], e), wide(bc[:, 128:], e)
                a = a_scr[at(t * n, n, n), :]
                hp = h_scr[at(t * n, n, n), :]
                dyr = dy_scr[pl.ds(r0 + t, 1), :]
                gt = cc * dyr + q
                q = a * gt
                da = q * hp
                ga = ga + da * st_scr[pl.ds(r0 + t, 1), :]
                d_a = da * a2
                g_b = gt * bb
                das.append(d_a[:8] + d_a[8:])
                gbs.append(g_b[:8] + g_b[8:])
                pb = gt * dx_scr[pl.ds(r0 + t, 1), :]
                pc = dyr * hn
                pb = sum(pb[:, k:k + 128] for k in range(0, e, 128))
                pc = sum(pc[:, k:k + 128] for k in range(0, e, 128))
                db = jnp.where(lanes == t, jnp.sum(pb, axis=1, keepdims=True), db)
                dc = jnp.where(lanes == t, jnp.sum(pc, axis=1, keepdims=True), dc)
                hn = hp
                if len(das) == 8:
                    da_scr[at(r0 + t, 8), :] = fold_rows(das[::-1], sub)
                    gb_scr[at(r0 + t, 8), :] = fold_rows(gbs[::-1], sub)
                    das, gbs = [], []
            return q, ga, hn, db, dc
        zero = jnp.zeros((n, rows), F32)
        q, ga, _, db, dc = lax.fori_loop(
            0, rows // un, bwd, (q_scr[i], ga_ref[...], h_scr[pl.ds(rows * n, n), :], zero, zero))
        q_scr[i] = q
        ga_ref[...] = ga
        part_ref[0, 128:128 + n, r0:r0 + rows] = db
        part_ref[0, 128 + n:128 + 2 * n, r0:r0 + rows] = dc

    z = xz_ref[0, :, e:].astype(F32)
    sz = jax.nn.sigmoid(z)
    xc = xc_ref[0].astype(F32)
    skip = skip_ref[...]
    y = y_scr[...] + skip * xc
    gated = (y * (z * sz)).astype(BF16)
    out_ref[0] = mm(gated, wo_ref[...]).astype(BF16)
    gated_ref[0] = gated
    dz = (dg_ref[0] * y * (sz * (1.0 + z * (1.0 - sz)))).astype(BF16)
    dz_ref[0] = dz
    gb = gb_scr[...]
    dy_y = dy_scr[...]
    dxc_ref[0] = dy_y * skip + st_scr[...] * gb
    d_pre = (da_scr[...] * LN2 + xc * gb) * jax.nn.sigmoid(pre_scr[...])
    d_low = d_pre.astype(BF16)
    gdt_ref[...] += tn(low_ref[0, :, :128], d_low)
    part_ref[0, :128, :] = nt(wdt_ref[...], d_low)
    vec_ref[0:1] += jnp.sum(d_pre, axis=0, keepdims=True)
    vec_ref[1:2] += jnp.sum(dy_y * xc, axis=0, keepdims=True)


def back(*refs, e, n, dims, reps, role):
    (xz_ref, prev_ref, edge_ref, mask_ref, ddbc_ref, nu_ref, next_ref, w_ref, xpt_ref, cw_ref, cb_ref, dxc_ref, dz_ref,
     before, extra) = refs[:15]
    b = pl.program_id(0)
    peers = dims[0] * dims[1] * dims[2]
    if role == "sum":
        nu_all, dy0, dy1, dz0, dz1, gated0, gated1 = refs[15:22]
        v_ref, gx, vec_ref, summed, prod_z, prod_o, done, carry, acc_z, acc_o = refs[22:32]
        refs = refs[32:]
        rc, own, ry, rz, load, send, recv = refs[:7]
        beside(b, peers, dims, 0, [
            allsum_steps((extra, done) + refs[7:], dims, functools.partial(spread_plain, n=n)) + (None,),
            scatter_steps((before, None, summed, None, rc, own, ry, rz, None, None, None, load, send, recv) + (None,) * 7,
                          dims, reps) + (None,)])
    else:
        gx_before, v_out, vec_ref, summed, summed_own, g_done, carry, gx, gx_low, v_buf, v_sem, gx_sem = refs[15:27]
        refs = refs[27:]
        half = len(refs) // 2
        earlier = scatter_steps((before, extra, summed, g_done) + refs[:half], dims, reps, 8, 10, 8, 15, peers * e)
        latest = scatter_steps((v_out, gx_low, summed_own, g_done) + refs[half:], dims, reps, 8, 10, 4, 12)

        @pl.when(b == 0)
        def _():
            meet(dims, reps)
            earlier[0]()
            copy = pltpu.make_async_copy(gx_before, gx, gx_sem.at[0])
            copy.start()
            copy.wait()
        early = [1, 1, 1, 1, 2, 2, 2, 2, 7, 11, 14]
        for k, when in enumerate(early):
            @pl.when(b == when)
            def _(k=k):
                earlier[1][k]()

    @pl.when(b == 0)
    def _():
        carry[...] = next_ref[...]
        vec_ref[...] = jnp.zeros_like(vec_ref)
        if role == "sum":
            acc_z[...] = jnp.zeros_like(acc_z)
            acc_o[...] = jnp.zeros_like(acc_o)
            gx[...] = jnp.zeros_like(gx)
    rows = xz_ref.shape[1]
    cw, cb = cw_ref[...], cb_ref[...]
    x = xz_ref[0, :, :e].astype(F32)
    before_x = prev_ref[0, rows - 2 * EDGE:, :e].astype(F32)[EDGE:]
    before_x = jnp.where(b == peers - 1, edge_ref[...], before_x)
    lag = lags(jnp.concatenate([before_x, x], axis=0), rows)
    same = mask_ref[0]
    dconv = (dxc_ref[0] + mm(ddbc_ref[0], xpt_ref[...])) * dsilu(convolve(lag, same, cw, cb))
    vec_ref[4:5] += jnp.sum(dconv, axis=0, keepdims=True)
    vec_ref[3:4] += jnp.sum(dconv * x, axis=0, keepdims=True)
    dx = cw[3:4] * dconv
    for k in range(1, 4):
        masked = dconv * same[:, k - 1:k]
        vec_ref[3 - k:4 - k] += jnp.sum(masked * lag[k], axis=0, keepdims=True)
        sent = cw[3 - k:4 - k] * masked
        dx = dx + jnp.concatenate([sent, carry[k - 1]], axis=0)[k:k + rows]
        carry[k - 1] = sent[:EDGE]
    dx = dx.astype(BF16)
    v = nt(jnp.concatenate([dx, dz_ref[0]], axis=1), w_ref[...]).astype(BF16)
    gx[...] += tn(nu_ref[0], dx)
    if role == "sum":
        v_ref[0] = v
        acc_z[...] += tn(nu_all[0], jnp.concatenate([dz0[0], dz1[0]], axis=0))
        acc_o[...] += tn(jnp.concatenate([gated0[0], gated1[0]], axis=0), jnp.concatenate([dy0[0], dy1[0]], axis=0))

        @pl.when(b == peers - 1)
        def _():
            prod_z[...] = acc_z[...].astype(BF16)
            prod_o[...] = acc_o[...].astype(BF16)
        return

    slot, at_ = b % 2, peers - 1 - b

    def write(slot):
        return pltpu.make_async_copy(v_buf.at[slot], v_out.at[at_ // (2 * dims[1]), (at_ // 2) % dims[1], at_ % 2], v_sem.at[slot])

    @pl.when(b >= 2)
    def _():
        write(slot).wait()
    v_buf[slot] = v
    write(slot).start()

    @pl.when(b == peers - 1)
    def _():
        write(0).wait()
        write(1).wait()
        for p in range(peers // reps):
            for k in range(reps):
                first = (p * reps + k) * gx_low.shape[2]
                gx_low[p, k] = gx[first:first + gx_low.shape[2]].astype(BF16)
        latest[0]()
        for k, step in enumerate(latest[1]):
            if len(early) + k < len(earlier[1]):
                earlier[1][len(early) + k]()
            step()
        earlier[2]()
        latest[2]()


def dsilu(v):
    s = jax.nn.sigmoid(v)
    return s * (1.0 + v * (1.0 - s))


def shift_rep(value, steps):
    count = lax.axis_size("rep")
    first, last = max(0, -steps), min(count, count - steps)
    return lax.ppermute(value, "rep", [(i, i + steps) for i in range(first, last)])


def sum_rep(value):
    if lax.axis_size("rep") != 2:
        return lax.psum(value.astype(F32), "rep")
    low = value.astype(BF16)
    other = lax.ppermute(low, "rep", [(0, 1), (1, 0)])
    return low.astype(F32) + other.astype(F32)


def on_device(hidden_in, segment_ids, out_grad, norm_gain, in_proj, conv_weight, conv_bias, x_proj,
              dt_weight, dt_bias, a_log, d_skip, out_proj):
    peers, reps = lax.axis_size("shard"), lax.axis_size("rep")
    rep = lax.axis_index("rep")
    m, tl, d = hidden_in.shape
    t, w = tl * peers, m * tl
    dl = in_proj.shape[0]
    e = x_proj.shape[0]
    n, rank, taps = a_log.shape[0], dt_weight.shape[0], conv_weight.shape[0]
    w32 = lambda v: v.astype(F32)
    shp = jax.ShapeDtypeStruct
    rising = lambda i: i
    falling = lambda i: peers - 1 - i

    span = peers * reps
    before = lax.ppermute(segment_ids[:, tl - taps + 1:], ("rep", "shard"), [(k, k + 1) for k in range(span - 1)])
    before = jnp.where((rep > 0) | (lax.axis_index("shard") > 0), before, -1)
    ext = jnp.concatenate([before, segment_ids], axis=1)
    same = [w32(ext[:, taps - 1 - k:taps - 1 - k + tl] == segment_ids) for k in range(1, taps)]
    same = jnp.stack(same, axis=1).reshape(m * (taps - 1), tl)
    own = jnp.concatenate([same, jnp.pad(w32(norm_gain)[None], ((0, 0), (0, tl - dl))),
                           jnp.zeros((7 - m * (taps - 1), tl), F32)], axis=0)
    hid_all, tiles, w_cols = gather(hidden_in.reshape(w, d), own, in_proj, 4)
    gain = tiles[:, m * (taps - 1), :dl].reshape(1, d)
    later, hid_all = lax.optimization_barrier((out_grad, hid_all))
    dy_rows = [lax.all_gather(later[i], "shard") for i in range(m)]
    u = w32(hidden_in)
    r = lax.rsqrt(jnp.mean(u * u, axis=2, keepdims=True) + 1e-5)

    mask = tiles[:, :m * (taps - 1)].reshape(peers, m, taps - 1, tl).transpose(0, 1, 3, 2).reshape(peers, w, taps - 1)
    mask = jnp.pad(mask, ((0, 0), (0, 0), (0, 9 - taps)))
    halo = shift_rep(hid_all[peers - 1].reshape(m, tl, d)[:, tl - EDGE:].reshape(m * EDGE, d), 1)

    cw, cb = w32(conv_weight), w32(conv_bias)[None]
    ins = [hid_all, w_cols, halo, mask, cw, cb, x_proj.T, gain]
    outs = [shp((peers, w, 2 * e), BF16), shp((peers, w, e), BF16), shp((peers, w, d), BF16), shp((m * EDGE, e), BF16)]
    outs += [shp((peers, rank + 2 * n, tl), F32)] * m
    xz, xc, nu_all, edge, *parts = call(
        functools.partial(front, m=m, e=e), (peers,),
        [block(hid_all, rising)] + [whole(a) for a in ins[1:3]] + [block(mask, rising)] + [whole(a) for a in ins[4:]],
        [block(a, rising) for a in outs[:3]] + [whole(outs[3])] + [block(a, rising) for a in outs[4:]], outs,
        [pltpu.VMEM((m * EDGE, e), F32)], ins, flops=2 * peers * w * d * 2 * e)

    low = allsum(parts, functools.partial(spread_low, n=n), 0)
    a_mat = -jnp.exp(w32(a_log))
    a2 = a_mat * LOG2E
    dtb, skip = w32(dt_bias)[None], w32(d_skip)[None]

    dims = lattice(peers)
    anywhere = pl.BlockSpec(memory_space=pl.ANY)
    rows_done = []
    for i in range(m):
        def row(a, order, i=i):
            shape = (1, tl) if a.ndim == 3 else (1, 1, a.shape[2])
            return pl.BlockSpec(shape + a.shape[len(shape):], lambda b, r=a.ndim: (order(b), i) + (0,) * (r - 2))

        if i:
            low, _ = lax.optimization_barrier((low, rows_done[i - 1][7]))
        ins = [low, xz, xc, mask, dy_rows[i], out_proj, dt_weight, dtb, a2]
        outs = [shp((peers, 1, n, e), F32)] * 2 + [shp((3, 1, n, e), F32), shp((peers, tl, e), F32)]
        cks, ckp, end, dg = call(
            functools.partial(ahead, m=1, n=n, e=e), (peers,),
            [row(a, rising) for a in ins[:4]] + [block(ins[4], rising)] + [whole(a) for a in ins[5:]],
            [block(outs[0], rising), block(outs[1], rising), whole(outs[2]), block(outs[3], rising)], outs,
            [pltpu.VMEM((1, n, e), F32)] * 3 + [pltpu.VMEM((tl, e), F32)] * 3
            + [pltpu.VMEM((tl, 128), F32), pltpu.VMEM((tl * n, 256), F32)], ins, flops=20 * 10 ** 9)
        ends = lax.all_gather(end, "rep")
        h_in = jnp.zeros((1, n, e), F32)
        q_in = jnp.zeros((1, n, e), F32)
        for k in range(reps - 1):
            o = reps - 1 - k
            h_in = jnp.where(k < rep, ends[k, 1] * h_in + ends[k, 0], h_in)
            q_in = jnp.where(o > rep, ends[o, 1] * q_in + ends[o, 2], q_in)
        ins = [low, xz, xc, mask, dg, cks, ckp, out_proj, dt_weight, dtb, a2, skip, h_in, q_in]
        specs = [row(a, falling) for a in ins[:4]] + [block(a, falling) for a in ins[4:7]] + [whole(a) for a in ins[7:]]
        outs = [shp((peers, tl, d), BF16), shp((peers, tl, e), BF16), shp((peers, tl, e), F32),
                shp((peers, rank + 2 * n, tl), F32), shp((peers, tl, e), BF16), shp((rank, e), F32), shp((n, e), F32), shp((8, e), F32)]
        out_specs = [block(a, falling) for a in outs[:5]] + [whole(a) for a in outs[5:]]
        scratch = [pltpu.VMEM((tl * n + n, e), F32), pltpu.VMEM((tl * n, e), F32), pltpu.VMEM((1, n, e), F32),
                   pltpu.VMEM((tl, 128), F32), pltpu.VMEM((tl * n, 256), F32)] + [pltpu.VMEM((tl, e), F32)] * 8
        params = {}
        if i:
            ins += [rows_done[i - 1][0].reshape(dims + (tl, d)), rows_done[i - 1][3].reshape(dims + (rank + 2 * n, tl))]
            specs += [anywhere] * 2
            outs += [shp((tl, d), F32), shp(dims + (tl, 256), BF16)]
            out_specs += [whole(a) for a in outs[-2:]]
            scratch += scatter_scratch(peers, tl, d, 16) + allsum_scratch(peers, rank + 2 * n, tl)
            params = dict(collective_id=5 + i, has_side_effects=True)
        rows_done.append(call(
            functools.partial(behind, n=n, e=e, dims=dims, reps=reps, sending=bool(i)), (peers,), specs, out_specs, outs,
            scratch, ins, flops=50 * 10 ** 9, **params))
    g_dt, g_a, vec = (sum(done[k] for done in rows_done) for k in range(5, 8))

    xpt = jnp.pad(x_proj.T, ((0, 256 - x_proj.shape[1]), (0, 0)))
    xz_first = xz[0].reshape(m, tl, 2 * e)[:, :EDGE, :e]
    edges = w32(edge).reshape(m, EDGE, e)
    out_sums = [done[8] for done in rows_done[1:]]
    ddbcs = [done[9].reshape(peers, tl, 256) for done in rows_done[1:]]
    backs = []
    for i in range(m):
        ext8 = jnp.concatenate([edges[i], w32(xz_first[i])], axis=0)
        same8 = mask[0, i * tl:i * tl + EDGE]
        conv8 = cb + cw[3] * ext8[EDGE:]
        for k in range(1, taps):
            conv8 = conv8 + cw[3 - k] * ext8[EDGE - k:2 * EDGE - k] * same8[:, k - 1:k]
        d8 = (rows_done[i][2][0, :EDGE] + mm(ddbcs[i][0, :EDGE], xpt)) * dsilu(conv8)
        follow = shift_rep(jnp.stack([cw[3 - k] * d8 * same8[:, k - 1:k] for k in range(1, taps)]), -1)

        def row(a, order, i=i):
            return pl.BlockSpec((1, tl) + a.shape[2:], lambda b: (order(b), i, 0))
        earlier = lambda b: jnp.maximum(peers - 2 - b, 0)
        ins = [xz, xz, edges[i], mask, ddbcs[i], nu_all, follow, w_cols, xpt, cw, cb, rows_done[i][2], rows_done[i][1]]
        specs = [row(xz, falling), row(xz, earlier), whole(ins[2]), row(mask, falling), block(ins[4], falling), row(nu_all, falling)]
        specs += [whole(a) for a in ins[6:11]] + [block(a, falling) for a in ins[11:13]] + [anywhere] * 2
        carry = pltpu.VMEM((taps - 1, EDGE, e), F32)
        if i < m - 1:
            ins += [rows_done[i + 1][0].reshape(dims + (tl, d)), rows_done[i + 1][3].reshape(dims + (rank + 2 * n, tl))]
            more = [nu_all] + dy_rows + [done[1] for done in rows_done] + [done[4] for done in rows_done]
            ins += more
            specs += [block(a, falling) for a in more]
            outs = [shp((peers, tl, d), BF16), shp((d, e), F32), shp((8, e), F32), shp((tl, d), F32), shp((d, e), BF16),
                    shp((e, d), BF16), shp(dims + (tl, 256), BF16)]
            out_specs = [block(outs[0], falling)] + [whole(a) for a in outs[1:]]
            scratch = [carry, pltpu.VMEM((d, e), F32), pltpu.VMEM((e, d), F32)]
            scratch += scatter_scratch(peers, tl, d, 16) + allsum_scratch(peers, rank + 2 * n, tl)
        else:
            g_z = backs[i - 1][4]
            ins += [backs[i - 1][0].reshape(dims + (tl, d)), g_z.reshape(peers // reps, reps, dl, e), backs[i - 1][1]]
            specs += [anywhere]
            outs = [shp(dims + (tl, d), BF16), shp((8, e), F32), shp((tl, d), F32), shp((tl, d), F32), shp((dl, 2 * peers * e), F32)]
            out_specs = [anywhere] + [whole(a) for a in outs[1:]]
            scratch = [carry, pltpu.VMEM((d, e), F32), pltpu.VMEM((peers // reps, reps, dl, e), BF16), pltpu.VMEM((2, tl, d), BF16),
                       pltpu.SemaphoreType.DMA((2,)), pltpu.SemaphoreType.DMA((1,))] + scatter_scratch(peers, tl, d, 16, g_z) * 2
        backs.append(call(
            functools.partial(back, e=e, n=n, dims=dims, reps=reps, role="sum" if i < m - 1 else "owner"), (peers,), specs,
            out_specs, outs, scratch, ins, flops=peers * w * d * 3 * e, collective_id=8 + i, has_side_effects=True))
        if i < m - 1:
            out_sums.append(backs[i][3])
            ddbcs.append(backs[i][6].reshape(peers, tl, 256))
    g_out, _ = lax.optimization_barrier((backs[0][5], follow))
    vec2 = backs[0][2] + backs[1][1]
    layer_out = (u + jnp.stack(out_sums)).astype(BF16)

    v = jnp.stack([backs[1][2], backs[1][3]]) * gain
    in_grad = w32(out_grad) + r * v - u * (r * r * r) * jnp.mean(v * u, axis=2, keepdims=True)

    grad_in_proj = backs[1][4]
    grad_gain = jnp.sum(grad_in_proj * w32(in_proj), axis=1) / w32(norm_gain)

    g_xproj = sum(tn(xc.reshape(peers, m, tl, e)[:, i].reshape(peers * tl, e), ddbcs[i].reshape(peers * tl, 256)) for i in range(m))
    small = jnp.concatenate([vec, g_a * a_mat, g_dt, g_xproj.T], axis=0)
    small, vec2 = sum_rep(small), sum_rep(vec2)
    vec, g_a, g_dt, g_xp = small[:8], small[8:8 + n], small[8 + n:8 + n + rank], small[8 + n + rank:]
    return (layer_out, in_grad, grad_gain, grad_in_proj, vec2[:taps], vec2[taps], g_xp[:rank + 2 * n].T, g_dt, vec[0],
            g_a, vec[1], sum_rep(g_out))


def solution(mesh):
    tok, ids = P(None, ("rep", "shard"), None), P(None, ("rep", "shard"))
    row, col, one = P("shard", None), P(None, "shard"), P("shard")
    return jax.shard_map(
        on_device,
        mesh=mesh,
        in_specs=(tok, ids, tok, one, row, col, one, row, col, one, col, one, row),
        out_specs=(tok, tok, one, row, col, one, row, col, one, col, one, row),
        check_vma=False,
    )
```

```python
import functools
import jax
import jax.numpy as jnp
from jax import lax
from jax.sharding import PartitionSpec as P
from jax.experimental import pallas as pl
from jax.experimental.pallas import tpu as pltpu

F32, BF16 = jnp.float32, jnp.bfloat16
LOG2E, LN2 = 1.4426950408889634, 0.6931471805599453
EDGE = 8
VMEM = 60 << 20


def nt(a, b):
    return lax.dot_general(a, b, (((1,), (1,)), ((), ())), preferred_element_type=F32)


def tn(a, b):
    return lax.dot_general(a, b, (((0,), (0,)), ((), ())), preferred_element_type=F32)


def mm(a, b):
    return jnp.dot(a, b, preferred_element_type=F32)


def softplus(v):
    return jnp.maximum(v, 0.0) + jnp.log1p(jnp.exp(-jnp.abs(v)))


def wide(v, e):
    return jnp.concatenate([v] * (e // 128), axis=1) if e > 128 else v


def at(start, size, unit=8):
    return pl.ds(pl.multiple_of(start, unit), size)


def call(kernel, grid, in_specs, out_specs, out_shape, scratch, args, flops=0, **params):
    size = sum(a.size * a.dtype.itemsize for a in args) + sum(s.size * s.dtype.itemsize for s in out_shape)
    return pl.pallas_call(
        kernel, grid=grid, in_specs=in_specs, out_specs=out_specs, out_shape=out_shape,
        scratch_shapes=scratch, compiler_params=pltpu.CompilerParams(vmem_limit_bytes=VMEM, **params),
        cost_estimate=pl.CostEstimate(flops=flops, bytes_accessed=size, transcendentals=0))(*args)


def whole(a):
    return pl.BlockSpec(a.shape, lambda i, r=len(a.shape): (0,) * r)


def block(a, order):
    return pl.BlockSpec((1,) + a.shape[1:], lambda i, r=len(a.shape): (order(i),) + (0,) * (r - 1))


def lags(x_ext, rows):
    return [x_ext[EDGE - k:EDGE - k + rows] for k in range(4)]


def convolve(lag, same, cw, cb):
    out = cb + cw[3:4] * lag[0]
    for k in range(1, 4):
        out = out + cw[3 - k:4 - k] * lag[k] * same[:, k - 1:k]
    return out


def normalise(rows, gain):
    u = rows.astype(F32)
    return (u * lax.rsqrt(jnp.mean(u * u, axis=1, keepdims=True) + 1e-5) * gain).astype(BF16)


def front(hid_ref, w_ref, halo_ref, mask_ref, cw_ref, cb_ref, xp_ref, gain_ref, xz_ref, xc_ref, nu_ref, edge_ref,
          *rest, m, e):
    parts, carry = rest[:m], rest[m]
    @pl.when(pl.program_id(0) == 0)
    def _():
        edge = mm(normalise(halo_ref[...], gain_ref[...]), w_ref[:, :e]).astype(BF16)
        edge_ref[...] = edge
        carry[...] = edge.astype(F32)
    nu = normalise(hid_ref[0], gain_ref[...])
    nu_ref[0] = nu
    xz = mm(nu, w_ref[...]).astype(BF16)
    xz_ref[0] = xz
    rows = xz.shape[0] // m
    cw, cb = cw_ref[...], cb_ref[...]
    for i in range(m):
        x = xz[i * rows:(i + 1) * rows, :e].astype(F32)
        ext = jnp.concatenate([carry[i * EDGE:(i + 1) * EDGE], x], axis=0)
        carry[i * EDGE:(i + 1) * EDGE] = x[rows - EDGE:]
        conv = convolve(lags(ext, rows), mask_ref[0, i * rows:(i + 1) * rows], cw, cb)
        xc = (conv * jax.nn.sigmoid(conv)).astype(BF16)
        xc_ref[0, i * rows:(i + 1) * rows] = xc
        parts[i][0] = nt(xp_ref[...], xc)


def lattice(peers):
    y = 2 if peers <= 16 else 4
    return peers // (2 * y), y, 2


def place(target):
    return target if isinstance(target, dict) else {"shard": target}


def greet(targets):
    barrier = pltpu.get_barrier_semaphore()
    for target in targets:
        pl.semaphore_signal(barrier, inc=1, device_id=place(target), device_id_type=pl.DeviceIdType.MESH)
    pl.semaphore_wait(barrier, len(targets))


def remote(src, dst, send, recv, target):
    return pltpu.make_async_remote_copy(src_ref=src, dst_ref=dst, send_sem=send, recv_sem=recv,
                                        device_id=place(target), device_id_type=pl.DeviceIdType.MESH)


def spread_low(total, n):
    rows = jnp.concatenate([total, jnp.zeros((256 - total.shape[0], total.shape[1]), F32)], axis=0).T
    rank = total.shape[0] - 2 * n
    out = [rows[:, :rank].astype(BF16)]
    rest = rows[:, rank:]
    hi = rest.astype(BF16)
    mid = (rest - hi.astype(F32)).astype(BF16)
    lo = (rest - hi.astype(F32) - mid.astype(F32)).astype(BF16)
    for k in range(2):
        out += [p[:, k * n:(k + 1) * n] for p in (hi, mid, lo)]
    out.append(jnp.zeros((rows.shape[0], 128 - 6 * n), BF16))
    return jnp.concatenate(out, axis=1)


def spread_plain(total, n):
    return jnp.concatenate([total, jnp.zeros((256 - total.shape[0], total.shape[1]), F32)], axis=0).T.astype(BF16)


def allsum_kernel(*refs, dims, chunks, finish):
    parts = refs[:chunks]
    out, rc, ac, low, ry, rz, send, recv = refs[chunks:]
    nz, ny, _ = dims
    me = lax.axis_index("shard")
    c, y, z = me % 2, (me // 2) % ny, me // (2 * ny)
    where = lambda a, b, d: (a * ny + b) * 2 + d
    across = where(z, y, 1 - c)
    ys = [lax.rem(y + k, ny) for k in range(1, ny)]
    zs = [lax.rem(z + k, nz) for k in range(1, nz)]
    greet([across] + [where(z, b, c) for b in ys] + [where(a, y, c) for a in zs])
    width = parts[0].shape[-1]
    rows = [pl.ds(q * width, width) for q in range(chunks)]

    def start(copies):
        for copy in copies:
            copy.start()
        return copies

    def finish_all(copies):
        for copy in copies:
            copy.wait()
    base = [0]

    def sems(count):
        base[0] += count
        return [(send.at[base[0] - count + k], recv.at[base[0] - count + k]) for k in range(count)]

    first = []
    for q in range(chunks):
        (s, r), = sems(1)
        first.append(start([remote(parts[q].at[:, :, 1 - c], rc.at[q], s, r, across)]))
    second = []
    for q in range(chunks):
        finish_all(first[q])
        for a in range(nz):
            for b in range(ny):
                total = parts[q][a, b, c] + rc[q, a, b]
                ac[q, a, b] = total
                low[q, a, b] = total.astype(BF16)
        second.append(start([remote(low.at[q, :, b], ry.at[q, k], *sem, where(z, b, c))
                             for k, (b, sem) in enumerate(zip(ys, sems(ny - 1)))]))
    third = []
    for q in range(chunks):
        finish_all(second[q])
        for a in range(nz):
            got = ac[q, a, y]
            for k in range(ny - 1):
                got = got + ry[q, k, a].astype(F32)
            ac[q, a, y] = got
            low[q, a, y] = got.astype(BF16)
        third.append(start([remote(low.at[q, a, y], rz.at[q, k], *sem, where(a, y, c))
                            for k, (a, sem) in enumerate(zip(zs, sems(nz - 1)))]))
    fourth = []
    for q in range(chunks):
        finish_all(third[q])
        got = ac[q, z, y]
        for k in range(nz - 1):
            got = got + rz[q, k].astype(F32)
        out[z, y, c, q * width:(q + 1) * width] = finish(got)
        mine = out.at[z, y, c, rows[q]]
        fourth.append(start([remote(mine, mine, *sem, where(a, y, c)) for a, sem in zip(zs, sems(nz - 1))]))
    fifth = []
    for q in range(chunks):
        finish_all(fourth[q])
        mine = out.at[:, y, c, rows[q]]
        fifth.append(start([remote(mine, mine, *sem, where(z, b, c)) for b, sem in zip(ys, sems(ny - 1))]))
    last = []
    for q in range(chunks):
        finish_all(fifth[q])
        mine = out.at[:, :, c, rows[q]]
        (s, r), = sems(1)
        last.append(start([remote(mine, mine, s, r, across)]))
    for q in range(chunks):
        finish_all(last[q])


def allsum(parts, finish, collective_id):
    peers, cols, width = parts[0].shape
    w = width * len(parts)
    dims = lattice(peers)
    nz, ny, nc = dims
    chunks = len(parts)
    copies = 2 * chunks * (1 + ny - 1 + nz - 1)
    out = pl.pallas_call(
        functools.partial(allsum_kernel, dims=dims, chunks=chunks, finish=finish),
        out_shape=jax.ShapeDtypeStruct((nz, ny, nc, w, 256), BF16),
        in_specs=[pl.BlockSpec(memory_space=pltpu.VMEM)] * chunks,
        out_specs=pl.BlockSpec(memory_space=pltpu.VMEM),
        scratch_shapes=[pltpu.VMEM((chunks, nz, ny, cols, 128), F32), pltpu.VMEM((chunks, nz, ny, cols, 128), F32),
                        pltpu.VMEM((chunks, nz, ny, cols, 128), BF16), pltpu.VMEM((chunks, ny - 1, nz, cols, 128), BF16),
                        pltpu.VMEM((chunks, nz - 1, cols, 128), BF16),
                        pltpu.SemaphoreType.DMA((copies,)), pltpu.SemaphoreType.DMA((copies,))],
        compiler_params=pltpu.CompilerParams(collective_id=collective_id, has_side_effects=True, vmem_limit_bytes=VMEM),
    )(*[part.reshape(nz, ny, nc, cols, width) for part in parts])
    return out.reshape(peers, w, 256)


def gather_kernel(x, small, wts, out, small_out, cols, send, recv, s_send, s_recv, w_send, w_recv, own_sem, *, dims, chunks):
    nz, ny, _ = dims
    me = lax.axis_index("shard")
    c, y, z = me % 2, (me // 2) % ny, me // (2 * ny)
    where = lambda a, b, d: (a * ny + b) * 2 + d
    across = where(z, y, 1 - c)
    ys = [lax.rem(y + k, ny) for k in range(1, ny)]
    ys_from = [lax.rem(y + ny - k, ny) for k in range(1, ny)]
    zs = [lax.rem(z + k, nz) for k in range(1, nz)]
    peers = nz * ny * 2
    others = [lax.rem(me + k, peers) for k in range(1, peers)]
    greet(others + [{"rep": lax.axis_index("rep") + 1 - 2 * lax.rem(lax.axis_index("rep"), 2)}])
    dl, e = wts.shape[0], wts.shape[1] // (2 * peers)
    size = x.shape[0] // chunks
    rows = [pl.ds(q * size, size) for q in range(chunks)]

    keep = pltpu.make_async_copy(small, small_out.at[z, y, c], own_sem.at[0])
    keep.start()
    whole_own = pltpu.make_async_copy(x, out.at[z, y, c], own_sem.at[1])
    whole_own.start()

    rep = lax.axis_index("rep")
    odd = lax.rem(rep, 2)
    hl = dl // 2

    def piece(half, src, dst):
        return (wts.at[pl.ds(pl.multiple_of(odd * hl, hl), hl), pl.ds(pl.multiple_of(half * peers * e + dst * e, 128), e)],
                cols.at[src, odd, :, pl.ds(half * e, e)])
    kept = [pltpu.make_async_copy(*piece(half, me, me), own_sem.at[2 + half]) for half in range(2)]
    swapped = remote(cols.at[:, odd], cols.at[:, odd], w_send.at[2 * peers - 2], w_recv.at[2 * peers - 2], {"rep": rep + 1 - 2 * odd})
    sent = [remote(*piece(half, me, p), w_send.at[2 * k + half], w_recv.at[2 * k + half], p)
            for k, p in enumerate(others) for half in range(2)]

    kinds = 2 * nz - 1
    offset = [0] + [-1 - j for j in range(nz - 1)] + [1 + j for j in range(nz - 1)]

    def valid(kind):
        return (z + offset[kind] >= 0) & (z + offset[kind] < nz)

    def sems(group, kind, q):
        at_ = (group * kinds + kind) * chunks + q
        return send.at[at_], recv.at[at_]

    def hop(kind, q, up):
        there = out.at[z + offset[kind], y, c, rows[q]]
        src = x.at[rows[q]] if kind == 0 else there
        j = -offset[kind] if up else offset[kind]
        to_kind = 1 + j if up else nz + j
        return remote(src, there, *sems(0, to_kind, q), where(z + 1 if up else z - 1, y, c))

    def can_hop(kind, up):
        return valid(kind) & ((z + 1 < nz) if up else (z >= 1))

    def over_y(kind, q, k):
        there = out.at[z + offset[kind], y, c, rows[q]]
        src = x.at[rows[q]] if kind == 0 else there
        return remote(src, there, *sems(1 + k, kind, q), where(z, ys[k], c))

    def over_core(kind, q, k):
        there = out.at[z + offset[kind], y if k == 0 else ys_from[k - 1], c, rows[q]]
        src = x.at[rows[q]] if kind == 0 and k == 0 else there
        return remote(src, there, *sems(ny + k, kind, q), across)

    def landed(kind, q, b, d, group):
        there = out.at[z + offset[kind], b, d, rows[q]]
        return remote(there, there, *sems(group, kind, q), across)

    def onward(kind, q):
        if kind == 0:
            ups = [True, False]
        elif kind < nz:
            ups = [True] if kind < nz - 1 else []
        else:
            ups = [False] if kind < kinds - 1 else []
        for up in ups:
            @pl.when(can_hop(kind, up))
            def _(up=up):
                hop(kind, q, up).start()
        for k in range(ny - 1):
            over_y(kind, q, k).start()
        over_core(kind, q, 0).start()

    tiny = []

    def tiny_start(copies):
        tiny.append(copies)
        for copy in copies:
            copy.start()

    def tiny_wait():
        for copy in tiny[-1]:
            copy.wait()

    tiny_start([remote(small, small_out.at[z, y, c], s_send.at[k], s_recv.at[k], where(a, y, c)) for k, a in enumerate(zs)])
    for q in range(chunks):
        onward(0, q)
    for copy in kept + sent:
        copy.start()
    tiny_wait()
    keep.wait()
    tiny_start([remote(small_out.at[:, y, c], small_out.at[:, y, c], s_send.at[nz - 1 + k], s_recv.at[nz - 1 + k], where(z, b, c))
                for k, b in enumerate(ys)])

    def from_y(kind, q):
        @pl.when(valid(kind))
        def _():
            for k in range(1, ny):
                landed(kind, q, ys_from[k - 1], c, k).wait_recv()
                over_core(kind, q, k).start()

    waves = [[0]] + [[1 + j, nz + j] for j in range(nz - 1)]
    for number, wave in enumerate(waves):
        for q in range(chunks):
            for kind in wave:
                if kind:
                    @pl.when(valid(kind))
                    def _(kind=kind, q=q):
                        landed(kind, q, y, c, 0).wait_recv()
                        onward(kind, q)
        if number == 2:
            for copy in kept + sent:
                copy.wait()
            swapped.start()
        if number == 1:
            tiny_wait()
            last = small_out.at[:, :, c]
            tiny_start([remote(last, last, s_send.at[nz + ny - 2], s_recv.at[nz + ny - 2], across)])
        if number:
            for q in range(chunks):
                for kind in waves[number - 1]:
                    from_y(kind, q)
    for q in range(chunks):
        for kind in waves[-1]:
            from_y(kind, q)
    tiny_wait()
    for kind in range(kinds):
        @pl.when(valid(kind))
        def _(kind=kind):
            for q in range(chunks):
                for k in range(ny):
                    landed(kind, q, y if k == 0 else ys_from[k - 1], 1 - c, ny + k).wait_recv()
                    over_core(kind, q, k).wait_send()
                for k in range(ny - 1):
                    over_y(kind, q, k).wait_send()
        for up in (True, False):
            j = -offset[kind] if up else offset[kind]
            if 0 <= j < nz - 1:
                @pl.when(can_hop(kind, up))
                def _(kind=kind, up=up):
                    for q in range(chunks):
                        hop(kind, q, up).wait_send()
    swapped.wait()
    whole_own.wait()


def gather(x, small, wts, collective_id, chunks=4):
    w, d = x.shape
    peers = lax.axis_size("shard")
    dims = lattice(peers)
    nz, ny, nc = dims
    copies = 2 * ny * (2 * nz - 1) * chunks
    dl, e = wts.shape[0], wts.shape[1] // (2 * peers)
    out, tiles, cols = pl.pallas_call(
        functools.partial(gather_kernel, dims=dims, chunks=chunks),
        out_shape=[jax.ShapeDtypeStruct((nz, ny, nc, w, d), x.dtype), jax.ShapeDtypeStruct((nz, ny, nc, 8, 128), F32),
                   jax.ShapeDtypeStruct((peers, 2, dl // 2, 2 * e), BF16)],
        in_specs=[pl.BlockSpec(memory_space=pl.ANY), pl.BlockSpec(memory_space=pltpu.VMEM), pl.BlockSpec(memory_space=pl.ANY)],
        out_specs=[pl.BlockSpec(memory_space=pl.ANY), pl.BlockSpec(memory_space=pltpu.VMEM), pl.BlockSpec(memory_space=pl.ANY)],
        scratch_shapes=[pltpu.SemaphoreType.DMA((copies,)), pltpu.SemaphoreType.DMA((copies,)),
                        pltpu.SemaphoreType.DMA((nz + ny,)), pltpu.SemaphoreType.DMA((nz + ny,)),
                        pltpu.SemaphoreType.DMA((2 * peers - 1,)), pltpu.SemaphoreType.DMA((2 * peers - 1,)),
                        pltpu.SemaphoreType.DMA((4,))],
        compiler_params=pltpu.CompilerParams(collective_id=collective_id, has_side_effects=True, vmem_limit_bytes=VMEM),
        cost_estimate=pl.CostEstimate(flops=8 * 10 ** 10, bytes_accessed=2 * peers * w * d, transcendentals=0),
    )(x, small, wts)
    return out.reshape(peers, w, d), tiles.reshape(peers, 8, 128), cols.reshape(peers * dl, 2 * e)


def meet(dims, reps):
    nz, ny, _ = dims
    me, rep = lax.axis_index("shard"), lax.axis_index("rep")
    c, y, z = me % 2, (me // 2) % ny, me // (2 * ny)
    if reps:
        greet([lax.rem(me + k, nz * ny * 2) for k in range(1, nz * ny * 2)]
              + [{"rep": lax.rem(rep + k, reps)} for k in range(1, reps)])
    else:
        greet([(z * ny + y) * 2 + 1 - c] + [(z * ny + lax.rem(y + k, ny)) * 2 + c for k in range(1, ny)]
              + [(lax.rem(z + k, nz) * ny + y) * 2 + c for k in range(1, nz)])


def scatter_steps(refs, dims, reps, lag_y=2, lag_z=4, sum_at=4, cross_at=9, first_col=0):
    part, g, out, g_out, rc, own, ry, rz, ga, gs, rg, load, send, recv, g_load, a_send, a_recv, b_send, b_recv, c_send, c_recv = refs
    nz, ny, _ = dims
    me, rep = lax.axis_index("shard"), lax.axis_index("rep")
    c, y, z = me % 2, (me // 2) % ny, me // (2 * ny)
    where = lambda a, b, d: (a * ny + b) * 2 + d
    across = where(z, y, 1 - c)
    ys = [lax.rem(y + k, ny) for k in range(1, ny)]
    zs = [lax.rem(z + k, nz) for k in range(1, nz)]
    peers = nz * ny * 2
    others = [lax.rem(me + k, peers) for k in range(1, peers)]
    far = [{"rep": lax.rem(rep + k, reps)} for k in range(1, reps)]
    slots, size = own.shape[0], own.shape[3]
    chunks = part.shape[3] // size
    rows = [pl.ds(q * size, size) for q in range(chunks)]
    per = ny + nz - 1

    def pair(q, k):
        return send.at[q * per + k], recv.at[q * per + k]

    def loads(q):
        return pltpu.make_async_copy(part.at[:, :, c, rows[q]], own.at[q % slots], load.at[q])

    def first(q):
        return remote(part.at[:, :, 1 - c, rows[q]], rc.at[:, :, rows[q]], *pair(q, 0), across)

    def second(q):
        return [remote(rc.at[:, b, rows[q]], ry.at[k, :, rows[q]], *pair(q, 1 + k), where(z, b, c))
                for k, b in enumerate(ys)]

    def third(q):
        return [remote(rc.at[a, y, rows[q]], rz.at[k, rows[q]], *pair(q, ny + k), where(a, y, c))
                for k, a in enumerate(zs)]

    groups = peers // reps
    owner_here = lax.rem(me, reps) == rep

    def shared():
        return pltpu.make_async_copy(g.at[:, rep], ga.at[rep], g_load.at[0]), [
            remote(g.at[:, lax.rem(rep + k, reps)], ga.at[rep], a_send.at[k - 1], a_recv.at[k - 1], far[k - 1])
            for k in range(1, reps)]

    def handed(k):
        p = lax.rem(me // reps + k, groups)
        return remote(gs.at[p], rg.at[me], b_send.at[k], b_recv.at[me], p * reps + rep)

    def arrived(k):
        src = lax.rem(me + k, peers)
        return remote(gs.at[0], rg.at[src], b_send.at[0], b_recv.at[src], lax.rem(me + 1, peers))

    def crossed(k):
        return remote(rg, rg, c_send.at[k - 1], c_recv, far[k - 1])

    def g_sum():
        kept, sent = shared()
        for copy in [kept] + sent:
            copy.wait()

        def add(p, _):
            total = ga[0, p].astype(F32)
            for k in range(1, reps):
                total = total + ga[k, p].astype(F32)
            gs[p] = total.astype(BF16)
            return 0
        lax.fori_loop(0, groups, add, 0)

        @pl.when(owner_here)
        def _():
            rg[me] = gs[me // reps]

        @pl.when(jnp.logical_not(owner_here))
        def _():
            handed(0).start()
        for k in range(1, groups):
            handed(k).start()

    def g_cross():
        @pl.when(owner_here)
        def _():
            for k in range(1, peers):
                arrived(k).wait_recv()
            for k in range(1, reps):
                crossed(k).start()

        @pl.when(jnp.logical_not(owner_here))
        def _():
            handed(0).wait_send()
        for k in range(1, groups):
            handed(k).wait_send()

    def g_end():
        @pl.when(owner_here)
        def _():
            for k in range(1, reps):
                crossed(k).wait_send()

        @pl.when(jnp.logical_not(owner_here))
        def _():
            crossed(1).wait_recv()
        e = rg.shape[2]
        for p in range(peers):
            g_out[:, first_col + p * e:first_col + (p + 1) * e] = rg[p].astype(F32)

    def start():
        for q in range(min(slots, chunks)):
            loads(q).start()
        for q in range(chunks):
            first(q).start()
        if g is not None:
            kept, sent = shared()
            for copy in [kept] + sent:
                copy.start()

    def over_core(q):
        loads(q).wait()
        first(q).wait()

        def add(a, _):
            i, j = a // ny, a % ny
            rc[i, j, rows[q]] = (own[q % slots, i, j].astype(F32) + rc[i, j, rows[q]].astype(F32)).astype(BF16)
            return 0
        lax.fori_loop(0, nz * ny, add, 0)
        if q + slots < chunks:
            loads(q + slots).start()
        for copy in second(q):
            copy.start()

    def over_y(q):
        for copy in second(q):
            copy.wait()

        def add(a, _):
            total = rc[a, y, rows[q]].astype(F32)
            for k in range(ny - 1):
                total = total + ry[k, a, rows[q]].astype(F32)
            rc[a, y, rows[q]] = total.astype(BF16)
            return 0
        lax.fori_loop(0, nz, add, 0)
        for copy in third(q):
            copy.start()

    def over_z(q):
        for copy in third(q):
            copy.wait()
        total = rc[z, y, rows[q]].astype(F32)
        for k in range(nz - 1):
            total = total + rz[k, rows[q]].astype(F32)
        out[rows[q]] = total

    def step(s):
        if s < chunks:
            over_core(s)
        if 0 <= s - lag_y < chunks:
            over_y(s - lag_y)
        if 0 <= s - lag_z < chunks:
            over_z(s - lag_z)
        if s == sum_at and g is not None:
            g_sum()
        if s == cross_at and g is not None:
            g_cross()

    def finish():
        if g is not None:
            g_end()
    return start, [functools.partial(step, s) for s in range(chunks + lag_z)], finish


def scatter_scratch(peers, w, d, size, g=None):
    nz, ny, nc = lattice(peers)
    chunks = w // size
    dma = pltpu.SemaphoreType.DMA
    copies = chunks * (ny + nz - 1)
    out = [pltpu.VMEM((nz, ny, w, d), BF16), pltpu.VMEM((3, nz, ny, size, d), BF16),
           pltpu.VMEM((ny - 1, nz, w, d), BF16), pltpu.VMEM((nz - 1, w, d), BF16)]
    tail = [dma((chunks,)), dma((copies,)), dma((copies,))]
    if g is None:
        return out + tail
    reps = lax.axis_size("rep")
    dl, e = g.shape[0] // peers, g.shape[1]
    return (out + [pltpu.VMEM((reps, peers // reps, dl, e), BF16), pltpu.VMEM((peers // reps, dl, e), BF16),
                   pltpu.VMEM((peers, dl, e), BF16)] + tail
            + [dma((1,)), dma((reps - 1,)), dma((reps - 1,)), dma((peers // reps,)), dma((peers,)), dma((reps - 1,)), dma])


def allsum_steps(refs, dims, finish):
    part, result, out, mine, rc, low, ry, rz, load, send, recv = refs
    nz, ny, _ = dims
    me = lax.axis_index("shard")
    c, y, z = me % 2, (me // 2) % ny, me // (2 * ny)
    where = lambda a, b, d: (a * ny + b) * 2 + d
    across = where(z, y, 1 - c)
    ys = [lax.rem(y + k, ny) for k in range(1, ny)]
    zs = [lax.rem(z + k, nz) for k in range(1, nz)]
    base = [0, 1, ny, ny + nz - 1, ny + 2 * nz - 2, 2 * ny + 2 * nz - 3]

    def sem(stage, k):
        return send.at[base[stage] + k], recv.at[base[stage] + k]

    def copies(stage):
        if stage == 0:
            return [remote(part.at[:, :, 1 - c], rc, *sem(0, 0), across)]
        if stage == 1:
            return [remote(low.at[:, b], ry.at[k], *sem(1, k), where(z, b, c)) for k, b in enumerate(ys)]
        if stage == 2:
            return [remote(low.at[a, y], rz.at[k], *sem(2, k), where(a, y, c)) for k, a in enumerate(zs)]
        if stage == 3:
            held, targets = out.at[z, y, c], [where(a, y, c) for a in zs]
        elif stage == 4:
            held, targets = out.at[:, y, c], [where(z, b, c) for b in ys]
        else:
            held, targets = out.at[:, :, c], [across]
        return [remote(held, held, *sem(stage, k), target) for k, target in enumerate(targets)]

    def own():
        return pltpu.make_async_copy(part.at[:, :, c], mine, load.at[0])

    def start():
        own().start()
        for copy in copies(0):
            copy.start()

    def step(s):
        if s == 0:
            own().wait()
        for copy in copies(s):
            copy.wait()
        if s == 0:
            def add(a, _):
                i, j = a // ny, a % ny
                total = mine[i, j] + rc[i, j]
                mine[i, j] = total
                low[i, j] = total.astype(BF16)
                return 0
            lax.fori_loop(0, nz * ny, add, 0)
        if s == 1:
            for a in range(nz):
                total = mine[a, y]
                for k in range(ny - 1):
                    total = total + ry[k, a].astype(F32)
                mine[a, y] = total
                low[a, y] = total.astype(BF16)
        if s == 2:
            total = mine[z, y]
            for k in range(nz - 1):
                total = total + rz[k].astype(F32)
            out[z, y, c] = finish(total)
        if s < 5:
            for copy in copies(s + 1):
                copy.start()

    def end():
        result[...] = out[...]
    return start, [functools.partial(step, s) for s in range(6)], end


def allsum_scratch(peers, cols, width):
    nz, ny, nc = lattice(peers)
    dma = pltpu.SemaphoreType.DMA
    count = 2 * (1 + ny - 1 + nz - 1)
    return [pltpu.VMEM((nz, ny, nc, width, 256), BF16), pltpu.VMEM((nz, ny, cols, width), F32),
            pltpu.VMEM((nz, ny, cols, width), F32),
            pltpu.VMEM((nz, ny, cols, width), BF16), pltpu.VMEM((ny - 1, nz, cols, width), BF16),
            pltpu.VMEM((nz - 1, cols, width), BF16), dma((1,)), dma((count,)), dma((count,))]


def beside(b, grid, dims, reps, transfers):
    @pl.when(b == 0)
    def _():
        meet(dims, reps)
        for start, _, _, _ in transfers:
            start()
    for _, steps, _, when in transfers:
        for s, step in enumerate(steps):
            @pl.when(b == (when[s] if when else (s * (grid - 1)) // len(steps) + 1))
            def _(step=step):
                step()

    @pl.when(b == grid - 1)
    def _():
        for _, _, finish, _ in transfers:
            finish()


PACED = [1, 1, 1, 1, 2, 2, 2, 2, 3, 5, 6, 8, 9, 11, 13, 14, 15, 15]


def fill(low_ref, bcs_scr, bc_scr, n):
    bcs_scr[...] = low_ref[0, :, 128:].astype(F32)
    lane = lax.broadcasted_iota(jnp.int32, (n, 128), 1)
    sub = lax.broadcasted_iota(jnp.int32, (n, 128), 0)
    mask = (lane % n) == sub
    r = lax.broadcasted_iota(jnp.int32, (128, 256), 0)
    c = lax.broadcasted_iota(jnp.int32, (128, 256), 1)
    ones = jnp.where((r >= 3 * n) == (c >= 128), 1.0, 0.0).astype(BF16)
    group = 128

    def body(g, _):
        rows = [jnp.where(mask, bcs_scr[pl.ds(g * group + j, 1), :], 0.0).astype(BF16) for j in range(group)]
        bc_scr[at(g * (group * n), group * n, 128), :] = mm(jnp.concatenate(rows, axis=0), ones)
        return 0
    lax.fori_loop(0, bcs_scr.shape[0] // group, body, 0)


def fold_rows(vals, sub):
    for k in (1, 2, 4):
        mask = (sub & k) == 0
        vals = [jnp.where(mask, a, b) + pltpu.roll(jnp.where(mask, b, a), 8 - k, 0)
                for a, b in zip(vals[::2], vals[1::2])]
    return vals[0]


def ahead(*refs, m, n, e, dims, sending):
    (low_ref, xz_ref, xc_ref, mask_ref, dy_ref, wo_ref, wdt_ref, dtb_ref, a2_ref) = refs[:9]
    refs = refs[9:]
    if sending:
        adding, refs = refs[0], refs[1:]
    cks_ref, ckp_ref, end_ref, dg_ref = refs[:4]
    refs = refs[4:]
    if sending:
        added, refs = refs[0], refs[1:]
    s_scr, p_scr, f_scr, sd_scr, dx_scr, dy_scr, bcs_scr, bc_scr = refs[:8]
    if sending:
        beside(pl.program_id(0), dims[0] * dims[1] * dims[2], dims, 0,
               [allsum_steps((adding, added) + refs[8:], dims, functools.partial(spread_plain, n=n)) + (None,)])
    b = pl.program_id(0)
    @pl.when(b == 0)
    def _():
        s_scr[...] = jnp.zeros_like(s_scr)
        p_scr[...] = jnp.ones_like(p_scr)
        f_scr[...] = jnp.zeros_like(f_scr)
    cks_ref[0] = s_scr[...]
    ckp_ref[0] = p_scr[...]
    fill(low_ref, bcs_scr, bc_scr, n)
    step = softplus(mm(low_ref[0, :, :128], wdt_ref[...]) + dtb_ref[...])
    sd_scr[...] = jnp.where(mask_ref[0, :, 0:1] > 0.0, step, 1e30)
    dx_scr[...] = step * xc_ref[0].astype(F32)
    dg = nt(dy_ref[0], wo_ref[...])
    dg_ref[0] = dg
    z = xz_ref[0, :, e:].astype(F32)
    dy_scr[...] = dg * (z * jax.nn.sigmoid(z))
    a2 = a2_ref[...]
    rows = sd_scr.shape[0] // m
    un = 16

    def group(g, carry):
        s, p, f = [list(c) for c in carry]
        for j in range(un):
            for i in range(m):
                t = i * rows + g * un + j
                bc = bc_scr[at(t * n, n, n), :]
                bb, cc = wide(bc[:, :128], e), wide(bc[:, 128:], e)
                a = jnp.exp2(sd_scr[pl.ds(t, 1), :] * a2)
                s[i] = a * s[i] + bb * dx_scr[pl.ds(t, 1), :]
                p[i] = p[i] * a
                f[i] = f[i] + p[i] * (cc * dy_scr[pl.ds(t, 1), :])
        return tuple(s), tuple(p), tuple(f)
    done = lax.fori_loop(0, rows // un, group,
                         tuple(tuple(scr[i] for i in range(m)) for scr in (s_scr, p_scr, f_scr)))
    for scr, vals in zip((s_scr, p_scr, f_scr), done):
        for i in range(m):
            scr[i] = vals[i]

    @pl.when(b == pl.num_programs(0) - 1)
    def _():
        end_ref[0] = s_scr[...]
        end_ref[1] = p_scr[...]
        end_ref[2] = f_scr[...]


def behind(*refs, n, e, dims, reps, sending):
    (low_ref, xz_ref, xc_ref, mask_ref, dg_ref, cks_ref, ckp_ref,
     wo_ref, wdt_ref, dtb_ref, a2_ref, skip_ref, hin_ref, qin_ref) = refs[:14]
    refs = refs[14:]
    if sending:
        before, refs = refs[0], refs[1:]
    out_ref, dz_ref, dxc_ref, part_ref, gated_ref, gdt_ref, ga_ref, vec_ref = refs[:8]
    refs = refs[8:]
    if sending:
        summed, refs = refs[0], refs[1:]
    (h_scr, a_scr, q_scr, bcs_scr, bc_scr, pre_scr, st_scr, sd_scr, dx_scr, dy_scr, y_scr, da_scr, gb_scr) = refs[:13]
    b = pl.program_id(0)
    if sending:
        rc, own, ry, rz, load, send, recv = refs[13:20]
        beside(b, dims[0] * dims[1] * dims[2], dims, 0, [
            scatter_steps((before, None, summed, None, rc, own, ry, rz, None, None, None, load, send, recv) + (None,) * 7,
                          dims, reps, 8, 10) + (PACED,)])
    m = 1
    @pl.when(b == 0)
    def _():
        q_scr[...] = qin_ref[...]
        for ref in (gdt_ref, ga_ref, vec_ref):
            ref[...] = jnp.zeros_like(ref)
    fill(low_ref, bcs_scr, bc_scr, n)
    pre = mm(low_ref[0, :, :128], wdt_ref[...]) + dtb_ref[...]
    pre_scr[...] = pre
    step = softplus(pre)
    st_scr[...] = step
    sd_scr[...] = jnp.where(mask_ref[0, :, 0:1] > 0.0, step, 1e30)
    dx_scr[...] = step * xc_ref[0].astype(F32)
    z = xz_ref[0, :, e:].astype(F32)
    dy_scr[...] = dg_ref[0] * (z * jax.nn.sigmoid(z))
    a2 = a2_ref[...]
    sub = lax.broadcasted_iota(jnp.int32, (8, e), 0)
    rows = sd_scr.shape[0] // m
    lanes = lax.broadcasted_iota(jnp.int32, (n, rows), 1)
    un = 32
    for i in range(m):
        r0 = i * rows
        h0 = cks_ref[0, i] + ckp_ref[0, i] * hin_ref[i]
        h_scr[pl.ds(0, n), :] = h0

        def fwd(g, h, r0=r0):
            ys = []
            for j in range(un):
                t = g * un + j
                bc = bc_scr[at((r0 + t) * n, n, n), :]
                bb, cc = wide(bc[:, :128], e), wide(bc[:, 128:], e)
                a = jnp.exp2(sd_scr[pl.ds(r0 + t, 1), :] * a2)
                h = a * h + bb * dx_scr[pl.ds(r0 + t, 1), :]
                a_scr[at(t * n, n, n), :] = a
                h_scr[at(t * n + n, n, n), :] = h
                cy = cc * h
                ys.append(cy[:8] + cy[8:])
                if len(ys) == 8:
                    y_scr[at(r0 + t - 7, 8), :] = fold_rows(ys, sub)
                    ys = []
            return h
        lax.fori_loop(0, rows // un, fwd, h0)

        def bwd(g, carry, r0=r0):
            q, ga, hn, db, dc = carry
            das, gbs = [], []
            for j in range(un):
                t = rows - 1 - (g * un + j)
                bc = bc_scr[at((r0 + t) * n, n, n), :]
                bb, cc = wide(bc[:, :128], e), wide(bc[:, 128:], e)
                a = a_scr[at(t * n, n, n), :]
                hp = h_scr[at(t * n, n, n), :]
                dyr = dy_scr[pl.ds(r0 + t, 1), :]
                gt = cc * dyr + q
                q = a * gt
                da = q * hp
                ga = ga + da * st_scr[pl.ds(r0 + t, 1), :]
                d_a = da * a2
                g_b = gt * bb
                das.append(d_a[:8] + d_a[8:])
                gbs.append(g_b[:8] + g_b[8:])
                pb = gt * dx_scr[pl.ds(r0 + t, 1), :]
                pc = dyr * hn
                pb = sum(pb[:, k:k + 128] for k in range(0, e, 128))
                pc = sum(pc[:, k:k + 128] for k in range(0, e, 128))
                db = jnp.where(lanes == t, jnp.sum(pb, axis=1, keepdims=True), db)
                dc = jnp.where(lanes == t, jnp.sum(pc, axis=1, keepdims=True), dc)
                hn = hp
                if len(das) == 8:
                    da_scr[at(r0 + t, 8), :] = fold_rows(das[::-1], sub)
                    gb_scr[at(r0 + t, 8), :] = fold_rows(gbs[::-1], sub)
                    das, gbs = [], []
            return q, ga, hn, db, dc
        zero = jnp.zeros((n, rows), F32)
        q, ga, _, db, dc = lax.fori_loop(
            0, rows // un, bwd, (q_scr[i], ga_ref[...], h_scr[pl.ds(rows * n, n), :], zero, zero))
        q_scr[i] = q
        ga_ref[...] = ga
        part_ref[0, 128:128 + n, r0:r0 + rows] = db
        part_ref[0, 128 + n:128 + 2 * n, r0:r0 + rows] = dc

    z = xz_ref[0, :, e:].astype(F32)
    sz = jax.nn.sigmoid(z)
    xc = xc_ref[0].astype(F32)
    skip = skip_ref[...]
    y = y_scr[...] + skip * xc
    gated = (y * (z * sz)).astype(BF16)
    out_ref[0] = mm(gated, wo_ref[...]).astype(BF16)
    gated_ref[0] = gated
    dz = (dg_ref[0] * y * (sz * (1.0 + z * (1.0 - sz)))).astype(BF16)
    dz_ref[0] = dz
    gb = gb_scr[...]
    dy_y = dy_scr[...]
    dxc_ref[0] = dy_y * skip + st_scr[...] * gb
    d_pre = (da_scr[...] * LN2 + xc * gb) * jax.nn.sigmoid(pre_scr[...])
    d_low = d_pre.astype(BF16)
    gdt_ref[...] += tn(low_ref[0, :, :128], d_low)
    part_ref[0, :128, :] = nt(wdt_ref[...], d_low)
    vec_ref[0:1] += jnp.sum(d_pre, axis=0, keepdims=True)
    vec_ref[1:2] += jnp.sum(dy_y * xc, axis=0, keepdims=True)


def back(*refs, e, n, dims, reps, role):
    (xz_ref, prev_ref, edge_ref, mask_ref, ddbc_ref, nu_ref, next_ref, w_ref, xpt_ref, cw_ref, cb_ref, dxc_ref, dz_ref,
     before, extra) = refs[:15]
    b = pl.program_id(0)
    peers = dims[0] * dims[1] * dims[2]
    if role == "sum":
        nu_all, dy0, dy1, dz0, dz1, gated0, gated1 = refs[15:22]
        v_ref, gx, vec_ref, summed, prod_z, prod_o, done, carry, acc_z, acc_o = refs[22:32]
        refs = refs[32:]
        rc, own, ry, rz, load, send, recv = refs[:7]
        beside(b, peers, dims, 0, [
            allsum_steps((extra, done) + refs[7:], dims, functools.partial(spread_plain, n=n)) + (None,),
            scatter_steps((before, None, summed, None, rc, own, ry, rz, None, None, None, load, send, recv) + (None,) * 7,
                          dims, reps) + (None,)])
    else:
        gx_before, go_part, v_out, vec_ref, summed, summed_own, g_done, go_done = refs[15:23]
        carry, gx, gx_low, v_buf, go_all, v_sem, gx_sem, go_send, go_recv = refs[23:32]
        refs = refs[32:]
        half = len(refs) // 2
        earlier = scatter_steps((before, extra, summed, g_done) + refs[:half], dims, reps, 8, 10, 8, 15, peers * e)
        latest = scatter_steps((v_out, gx_low, summed_own, g_done) + refs[half:], dims, reps, 8, 10, 4, 12)

        @pl.when(b == 0)
        def _():
            meet(dims, reps)
            earlier[0]()
            copy = pltpu.make_async_copy(gx_before, gx, gx_sem.at[0])
            copy.start()
            copy.wait()
        early = [1, 1, 1, 1, 2, 2, 2, 2, 7, 11, 14]
        for k, when in enumerate(early):
            @pl.when(b == when)
            def _(k=k):
                earlier[1][k]()

    @pl.when(b == 0)
    def _():
        carry[...] = next_ref[...]
        vec_ref[...] = jnp.zeros_like(vec_ref)
        if role == "sum":
            acc_z[...] = jnp.zeros_like(acc_z)
            acc_o[...] = jnp.zeros_like(acc_o)
            gx[...] = jnp.zeros_like(gx)
    rows = xz_ref.shape[1]
    cw, cb = cw_ref[...], cb_ref[...]
    x = xz_ref[0, :, :e].astype(F32)
    before_x = prev_ref[0, rows - 2 * EDGE:, :e].astype(F32)[EDGE:]
    before_x = jnp.where(b == peers - 1, edge_ref[...], before_x)
    lag = lags(jnp.concatenate([before_x, x], axis=0), rows)
    same = mask_ref[0]
    dconv = (dxc_ref[0] + mm(ddbc_ref[0], xpt_ref[...])) * dsilu(convolve(lag, same, cw, cb))
    vec_ref[4:5] += jnp.sum(dconv, axis=0, keepdims=True)
    vec_ref[3:4] += jnp.sum(dconv * x, axis=0, keepdims=True)
    dx = cw[3:4] * dconv
    for k in range(1, 4):
        masked = dconv * same[:, k - 1:k]
        vec_ref[3 - k:4 - k] += jnp.sum(masked * lag[k], axis=0, keepdims=True)
        sent = cw[3 - k:4 - k] * masked
        dx = dx + jnp.concatenate([sent, carry[k - 1]], axis=0)[k:k + rows]
        carry[k - 1] = sent[:EDGE]
    dx = dx.astype(BF16)
    v = nt(jnp.concatenate([dx, dz_ref[0]], axis=1), w_ref[...]).astype(BF16)
    gx[...] += tn(nu_ref[0], dx)
    if role == "sum":
        v_ref[0] = v
        acc_z[...] += tn(nu_all[0], jnp.concatenate([dz0[0], dz1[0]], axis=0))
        acc_o[...] += tn(jnp.concatenate([gated0[0], gated1[0]], axis=0), jnp.concatenate([dy0[0], dy1[0]], axis=0))

        @pl.when(b == peers - 1)
        def _():
            prod_z[...] = acc_z[...].astype(BF16)
            prod_o[...] = acc_o[...].astype(BF16)
        return

    slot, at_ = b % 2, peers - 1 - b

    def write(slot):
        return pltpu.make_async_copy(v_buf.at[slot], v_out.at[at_ // (2 * dims[1]), (at_ // 2) % dims[1], at_ % 2], v_sem.at[slot])

    @pl.when(b >= 2)
    def _():
        write(slot).wait()
    v_buf[slot] = v
    write(slot).start()

    @pl.when(b == peers - 1)
    def _():
        write(0).wait()
        write(1).wait()
        for p in range(peers // reps):
            for k in range(reps):
                first = (p * reps + k) * gx_low.shape[2]
                gx_low[p, k] = gx[first:first + gx_low.shape[2]].astype(BF16)
        latest[0]()
        rep = lax.axis_index("rep")
        kept = pltpu.make_async_copy(go_part, go_all.at[rep], gx_sem.at[0])
        swaps = [remote(go_part, go_all.at[rep], go_send.at[k - 1], go_recv.at[k - 1], {"rep": lax.rem(rep + k, reps)})
                 for k in range(1, reps)]
        for k, step in enumerate(latest[1]):
            if k == 6:
                for copy in [kept] + swaps:
                    copy.start()
            if len(early) + k < len(earlier[1]):
                earlier[1][len(early) + k]()
            step()
        earlier[2]()
        for copy in [kept] + swaps:
            copy.wait()
        total = go_all[0].astype(F32)
        for k in range(1, reps):
            total = total + go_all[k].astype(F32)
        go_done[...] = total
        latest[2]()


def dsilu(v):
    s = jax.nn.sigmoid(v)
    return s * (1.0 + v * (1.0 - s))


def shift_rep(value, steps):
    count = lax.axis_size("rep")
    first, last = max(0, -steps), min(count, count - steps)
    return lax.ppermute(value, "rep", [(i, i + steps) for i in range(first, last)])


def sum_rep(value):
    if lax.axis_size("rep") != 2:
        return lax.psum(value.astype(F32), "rep")
    low = value.astype(BF16)
    other = lax.ppermute(low, "rep", [(0, 1), (1, 0)])
    return low.astype(F32) + other.astype(F32)


def on_device(hidden_in, segment_ids, out_grad, norm_gain, in_proj, conv_weight, conv_bias, x_proj,
              dt_weight, dt_bias, a_log, d_skip, out_proj):
    peers, reps = lax.axis_size("shard"), lax.axis_size("rep")
    rep = lax.axis_index("rep")
    m, tl, d = hidden_in.shape
    t, w = tl * peers, m * tl
    dl = in_proj.shape[0]
    e = x_proj.shape[0]
    n, rank, taps = a_log.shape[0], dt_weight.shape[0], conv_weight.shape[0]
    w32 = lambda v: v.astype(F32)
    shp = jax.ShapeDtypeStruct
    rising = lambda i: i
    falling = lambda i: peers - 1 - i

    span = peers * reps
    before = lax.ppermute(segment_ids[:, tl - taps + 1:], ("rep", "shard"), [(k, k + 1) for k in range(span - 1)])
    before = jnp.where((rep > 0) | (lax.axis_index("shard") > 0), before, -1)
    ext = jnp.concatenate([before, segment_ids], axis=1)
    same = [w32(ext[:, taps - 1 - k:taps - 1 - k + tl] == segment_ids) for k in range(1, taps)]
    same = jnp.stack(same, axis=1).reshape(m * (taps - 1), tl)
    own = jnp.concatenate([same, jnp.pad(w32(norm_gain)[None], ((0, 0), (0, tl - dl))),
                           jnp.zeros((7 - m * (taps - 1), tl), F32)], axis=0)
    hid_all, tiles, w_cols = gather(hidden_in.reshape(w, d), own, in_proj, 4)
    gain = tiles[:, m * (taps - 1), :dl].reshape(1, d)
    later, hid_all = lax.optimization_barrier((out_grad, hid_all))
    dy_rows = [lax.all_gather(later[i], "shard") for i in range(m)]
    u = w32(hidden_in)
    r = lax.rsqrt(jnp.mean(u * u, axis=2, keepdims=True) + 1e-5)

    mask = tiles[:, :m * (taps - 1)].reshape(peers, m, taps - 1, tl).transpose(0, 1, 3, 2).reshape(peers, w, taps - 1)
    mask = jnp.pad(mask, ((0, 0), (0, 0), (0, 9 - taps)))
    halo = shift_rep(hid_all[peers - 1].reshape(m, tl, d)[:, tl - EDGE:].reshape(m * EDGE, d), 1)

    cw, cb = w32(conv_weight), w32(conv_bias)[None]
    ins = [hid_all, w_cols, halo, mask, cw, cb, x_proj.T, gain]
    outs = [shp((peers, w, 2 * e), BF16), shp((peers, w, e), BF16), shp((peers, w, d), BF16), shp((m * EDGE, e), BF16)]
    outs += [shp((peers, rank + 2 * n, tl), F32)] * m
    xz, xc, nu_all, edge, *parts = call(
        functools.partial(front, m=m, e=e), (peers,),
        [block(hid_all, rising)] + [whole(a) for a in ins[1:3]] + [block(mask, rising)] + [whole(a) for a in ins[4:]],
        [block(a, rising) for a in outs[:3]] + [whole(outs[3])] + [block(a, rising) for a in outs[4:]], outs,
        [pltpu.VMEM((m * EDGE, e), F32)], ins, flops=2 * peers * w * d * 2 * e)

    low = allsum(parts, functools.partial(spread_low, n=n), 0)
    a_mat = -jnp.exp(w32(a_log))
    a2 = a_mat * LOG2E
    dtb, skip = w32(dt_bias)[None], w32(d_skip)[None]

    dims = lattice(peers)
    anywhere = pl.BlockSpec(memory_space=pl.ANY)
    rows_done, ddbcs = [], []
    for i in range(m):
        def row(a, order, i=i):
            shape = (1, tl) if a.ndim == 3 else (1, 1, a.shape[2])
            return pl.BlockSpec(shape + a.shape[len(shape):], lambda b, r=a.ndim: (order(b), i) + (0,) * (r - 2))

        if i:
            low, _ = lax.optimization_barrier((low, rows_done[i - 1][7]))
        ins = [low, xz, xc, mask, dy_rows[i], out_proj, dt_weight, dtb, a2]
        outs = [shp((peers, 1, n, e), F32)] * 2 + [shp((3, 1, n, e), F32), shp((peers, tl, e), F32)]
        specs = [row(a, rising) for a in ins[:4]] + [block(ins[4], rising)] + [whole(a) for a in ins[5:]]
        out_specs = [block(outs[0], rising), block(outs[1], rising), whole(outs[2]), block(outs[3], rising)]
        scratch = ([pltpu.VMEM((1, n, e), F32)] * 3 + [pltpu.VMEM((tl, e), F32)] * 3
                   + [pltpu.VMEM((tl, 128), F32), pltpu.VMEM((tl * n, 256), F32)])
        params = {}
        if i:
            ins.append(rows_done[i - 1][3].reshape(dims + (rank + 2 * n, tl)))
            specs.append(anywhere)
            outs.append(shp(dims + (tl, 256), BF16))
            out_specs.append(whole(outs[-1]))
            scratch += allsum_scratch(peers, rank + 2 * n, tl)
            params = dict(collective_id=11 + i, has_side_effects=True)
        cks, ckp, end, dg, *sums = call(
            functools.partial(ahead, m=1, n=n, e=e, dims=dims, sending=bool(i)), (peers,), specs, out_specs, outs, scratch,
            ins, flops=20 * 10 ** 9, **params)
        ddbcs += [a.reshape(peers, tl, 256) for a in sums]
        ends = lax.all_gather(end, "rep")
        h_in = jnp.zeros((1, n, e), F32)
        q_in = jnp.zeros((1, n, e), F32)
        for k in range(reps - 1):
            o = reps - 1 - k
            h_in = jnp.where(k < rep, ends[k, 1] * h_in + ends[k, 0], h_in)
            q_in = jnp.where(o > rep, ends[o, 1] * q_in + ends[o, 2], q_in)
        ins = [low, xz, xc, mask, dg, cks, ckp, out_proj, dt_weight, dtb, a2, skip, h_in, q_in]
        specs = [row(a, falling) for a in ins[:4]] + [block(a, falling) for a in ins[4:7]] + [whole(a) for a in ins[7:]]
        outs = [shp((peers, tl, d), BF16), shp((peers, tl, e), BF16), shp((peers, tl, e), F32),
                shp((peers, rank + 2 * n, tl), F32), shp((peers, tl, e), BF16), shp((rank, e), F32), shp((n, e), F32), shp((8, e), F32)]
        out_specs = [block(a, falling) for a in outs[:5]] + [whole(a) for a in outs[5:]]
        scratch = [pltpu.VMEM((tl * n + n, e), F32), pltpu.VMEM((tl * n, e), F32), pltpu.VMEM((1, n, e), F32),
                   pltpu.VMEM((tl, 128), F32), pltpu.VMEM((tl * n, 256), F32)] + [pltpu.VMEM((tl, e), F32)] * 8
        params = {}
        if i:
            ins.append(rows_done[i - 1][0].reshape(dims + (tl, d)))
            specs.append(anywhere)
            outs.append(shp((tl, d), F32))
            out_specs.append(whole(outs[-1]))
            scratch += scatter_scratch(peers, tl, d, 16)
            params = dict(collective_id=5 + i, has_side_effects=True)
        rows_done.append(call(
            functools.partial(behind, n=n, e=e, dims=dims, reps=reps, sending=bool(i)), (peers,), specs, out_specs, outs,
            scratch, ins, flops=50 * 10 ** 9, **params))
    g_dt, g_a, vec = (sum(done[k] for done in rows_done) for k in range(5, 8))

    xpt = jnp.pad(x_proj.T, ((0, 256 - x_proj.shape[1]), (0, 0)))
    xz_first = xz[0].reshape(m, tl, 2 * e)[:, :EDGE, :e]
    edges = w32(edge).reshape(m, EDGE, e)
    out_sums = [done[8] for done in rows_done[1:]]
    backs = []
    for i in range(m):
        ext8 = jnp.concatenate([edges[i], w32(xz_first[i])], axis=0)
        same8 = mask[0, i * tl:i * tl + EDGE]
        conv8 = cb + cw[3] * ext8[EDGE:]
        for k in range(1, taps):
            conv8 = conv8 + cw[3 - k] * ext8[EDGE - k:2 * EDGE - k] * same8[:, k - 1:k]
        d8 = (rows_done[i][2][0, :EDGE] + mm(ddbcs[i][0, :EDGE], xpt)) * dsilu(conv8)
        follow = shift_rep(jnp.stack([cw[3 - k] * d8 * same8[:, k - 1:k] for k in range(1, taps)]), -1)

        def row(a, order, i=i):
            return pl.BlockSpec((1, tl) + a.shape[2:], lambda b: (order(b), i, 0))
        earlier = lambda b: jnp.maximum(peers - 2 - b, 0)
        ins = [xz, xz, edges[i], mask, ddbcs[i], nu_all, follow, w_cols, xpt, cw, cb, rows_done[i][2], rows_done[i][1]]
        specs = [row(xz, falling), row(xz, earlier), whole(ins[2]), row(mask, falling), block(ins[4], falling), row(nu_all, falling)]
        specs += [whole(a) for a in ins[6:11]] + [block(a, falling) for a in ins[11:13]] + [anywhere] * 2
        carry = pltpu.VMEM((taps - 1, EDGE, e), F32)
        if i < m - 1:
            ins += [rows_done[i + 1][0].reshape(dims + (tl, d)), rows_done[i + 1][3].reshape(dims + (rank + 2 * n, tl))]
            more = [nu_all] + dy_rows + [done[1] for done in rows_done] + [done[4] for done in rows_done]
            ins += more
            specs += [block(a, falling) for a in more]
            outs = [shp((peers, tl, d), BF16), shp((d, e), F32), shp((8, e), F32), shp((tl, d), F32), shp((d, e), BF16),
                    shp((e, d), BF16), shp(dims + (tl, 256), BF16)]
            out_specs = [block(outs[0], falling)] + [whole(a) for a in outs[1:]]
            scratch = [carry, pltpu.VMEM((d, e), F32), pltpu.VMEM((e, d), F32)]
            scratch += scatter_scratch(peers, tl, d, 16) + allsum_scratch(peers, rank + 2 * n, tl)
        else:
            g_z = backs[i - 1][4]
            ins += [backs[i - 1][0].reshape(dims + (tl, d)), g_z.reshape(peers // reps, reps, dl, e), backs[i - 1][1], backs[i - 1][5]]
            specs += [anywhere] * 2
            outs = [shp(dims + (tl, d), BF16), shp((8, e), F32), shp((tl, d), F32), shp((tl, d), F32), shp((dl, 2 * peers * e), F32),
                    shp((e, d), F32)]
            out_specs = [anywhere] + [whole(a) for a in outs[1:]]
            scratch = [carry, pltpu.VMEM((d, e), F32), pltpu.VMEM((peers // reps, reps, dl, e), BF16), pltpu.VMEM((2, tl, d), BF16),
                       pltpu.VMEM((reps, e, d), BF16), pltpu.SemaphoreType.DMA((2,)), pltpu.SemaphoreType.DMA((1,)),
                       pltpu.SemaphoreType.DMA((reps - 1,)), pltpu.SemaphoreType.DMA((reps - 1,))] + scatter_scratch(peers, tl, d, 16, g_z) * 2
        backs.append(call(
            functools.partial(back, e=e, n=n, dims=dims, reps=reps, role="sum" if i < m - 1 else "owner"), (peers,), specs,
            out_specs, outs, scratch, ins, flops=peers * w * d * 3 * e, collective_id=8 + i, has_side_effects=True))
        if i < m - 1:
            out_sums.append(backs[i][3])
            ddbcs.append(backs[i][6].reshape(peers, tl, 256))
    vec2 = backs[0][2] + backs[1][1]
    layer_out = (u + jnp.stack(out_sums)).astype(BF16)

    v = jnp.stack([backs[1][2], backs[1][3]]) * gain
    in_grad = w32(out_grad) + r * v - u * (r * r * r) * jnp.mean(v * u, axis=2, keepdims=True)

    grad_in_proj = backs[1][4]
    grad_gain = jnp.sum(grad_in_proj * w32(in_proj), axis=1) / w32(norm_gain)

    g_xproj = sum(tn(xc.reshape(peers, m, tl, e)[:, i].reshape(peers * tl, e), ddbcs[i].reshape(peers * tl, 256)) for i in range(m))
    small = jnp.concatenate([vec, g_a * a_mat, g_dt, g_xproj.T], axis=0)
    small, vec2 = sum_rep(small), sum_rep(vec2)
    vec, g_a, g_dt, g_xp = small[:8], small[8:8 + n], small[8 + n:8 + n + rank], small[8 + n + rank:]
    return (layer_out, in_grad, grad_gain, grad_in_proj, vec2[:taps], vec2[taps], g_xp[:rank + 2 * n].T, g_dt, vec[0],
            g_a, vec[1], backs[1][5])


def solution(mesh):
    tok, ids = P(None, ("rep", "shard"), None), P(None, ("rep", "shard"))
    row, col, one = P("shard", None), P(None, "shard"), P("shard")
    return jax.shard_map(
        on_device,
        mesh=mesh,
        in_specs=(tok, ids, tok, one, row, col, one, row, col, one, col, one, row),
        out_specs=(tok, tok, one, row, col, one, row, col, one, col, one, row),
        check_vma=False,
    )
```

```python
import functools
import jax
import jax.numpy as jnp
from jax import lax
from jax.sharding import PartitionSpec as P
from jax.experimental import pallas as pl
from jax.experimental.pallas import tpu as pltpu

F32, BF16 = jnp.float32, jnp.bfloat16
LOG2E, LN2 = 1.4426950408889634, 0.6931471805599453
EDGE = 8
VMEM = 60 << 20


def nt(a, b):
    return lax.dot_general(a, b, (((1,), (1,)), ((), ())), preferred_element_type=F32)


def tn(a, b):
    return lax.dot_general(a, b, (((0,), (0,)), ((), ())), preferred_element_type=F32)


def mm(a, b):
    return jnp.dot(a, b, preferred_element_type=F32)


def softplus(v):
    return jnp.maximum(v, 0.0) + jnp.log1p(jnp.exp(-jnp.abs(v)))


def wide(v, e):
    return jnp.concatenate([v] * (e // 128), axis=1) if e > 128 else v


def at(start, size, unit=8):
    return pl.ds(pl.multiple_of(start, unit), size)


def call(kernel, grid, in_specs, out_specs, out_shape, scratch, args, flops=0, **params):
    size = sum(a.size * a.dtype.itemsize for a in args) + sum(s.size * s.dtype.itemsize for s in out_shape)
    return pl.pallas_call(
        kernel, grid=grid, in_specs=in_specs, out_specs=out_specs, out_shape=out_shape,
        scratch_shapes=scratch, compiler_params=pltpu.CompilerParams(vmem_limit_bytes=VMEM, **params),
        cost_estimate=pl.CostEstimate(flops=flops, bytes_accessed=size, transcendentals=0))(*args)


def whole(a):
    return pl.BlockSpec(a.shape, lambda i, r=len(a.shape): (0,) * r)


def block(a, order):
    return pl.BlockSpec((1,) + a.shape[1:], lambda i, r=len(a.shape): (order(i),) + (0,) * (r - 1))


def lags(x_ext, rows):
    return [x_ext[EDGE - k:EDGE - k + rows] for k in range(4)]


def convolve(lag, same, cw, cb):
    out = cb + cw[3:4] * lag[0]
    for k in range(1, 4):
        out = out + cw[3 - k:4 - k] * lag[k] * same[:, k - 1:k]
    return out


def normalise(rows, gain):
    u = rows.astype(F32)
    return (u * lax.rsqrt(jnp.mean(u * u, axis=1, keepdims=True) + 1e-5) * gain).astype(BF16)


def front(hid_ref, w_ref, halo_ref, mask_ref, cw_ref, cb_ref, xp_ref, gain_ref, xz_ref, xc_ref, nu_ref, edge_ref,
          *rest, m, e):
    parts, carry = rest[:m], rest[m]
    @pl.when(pl.program_id(0) == 0)
    def _():
        edge = mm(normalise(halo_ref[...], gain_ref[...]), w_ref[:, :e]).astype(BF16)
        edge_ref[...] = edge
        carry[...] = edge.astype(F32)
    nu = normalise(hid_ref[0], gain_ref[...])
    nu_ref[0] = nu
    xz = mm(nu, w_ref[...]).astype(BF16)
    xz_ref[0] = xz
    rows = xz.shape[0] // m
    cw, cb = cw_ref[...], cb_ref[...]
    for i in range(m):
        x = xz[i * rows:(i + 1) * rows, :e].astype(F32)
        ext = jnp.concatenate([carry[i * EDGE:(i + 1) * EDGE], x], axis=0)
        carry[i * EDGE:(i + 1) * EDGE] = x[rows - EDGE:]
        conv = convolve(lags(ext, rows), mask_ref[0, i * rows:(i + 1) * rows], cw, cb)
        xc = (conv * jax.nn.sigmoid(conv)).astype(BF16)
        xc_ref[0, i * rows:(i + 1) * rows] = xc
        parts[i][0] = nt(xp_ref[...], xc)


def lattice(peers):
    y = 2 if peers <= 16 else 4
    return peers // (2 * y), y, 2


def place(target):
    return target if isinstance(target, dict) else {"shard": target}


def greet(targets):
    barrier = pltpu.get_barrier_semaphore()
    for target in targets:
        pl.semaphore_signal(barrier, inc=1, device_id=place(target), device_id_type=pl.DeviceIdType.MESH)
    pl.semaphore_wait(barrier, len(targets))


def remote(src, dst, send, recv, target):
    return pltpu.make_async_remote_copy(src_ref=src, dst_ref=dst, send_sem=send, recv_sem=recv,
                                        device_id=place(target), device_id_type=pl.DeviceIdType.MESH)


def spread_low(total, n):
    rows = jnp.concatenate([total, jnp.zeros((256 - total.shape[0], total.shape[1]), F32)], axis=0).T
    rank = total.shape[0] - 2 * n
    out = [rows[:, :rank].astype(BF16)]
    rest = rows[:, rank:]
    hi = rest.astype(BF16)
    mid = (rest - hi.astype(F32)).astype(BF16)
    lo = (rest - hi.astype(F32) - mid.astype(F32)).astype(BF16)
    for k in range(2):
        out += [p[:, k * n:(k + 1) * n] for p in (hi, mid, lo)]
    out.append(jnp.zeros((rows.shape[0], 128 - 6 * n), BF16))
    return jnp.concatenate(out, axis=1)


def spread_plain(total, n):
    return jnp.concatenate([total, jnp.zeros((256 - total.shape[0], total.shape[1]), F32)], axis=0).T.astype(BF16)


def allsum_kernel(*refs, dims, chunks, finish):
    parts = refs[:chunks]
    out, rc, ac, low, ry, rz, send, recv = refs[chunks:]
    nz, ny, _ = dims
    me = lax.axis_index("shard")
    c, y, z = me % 2, (me // 2) % ny, me // (2 * ny)
    where = lambda a, b, d: (a * ny + b) * 2 + d
    across = where(z, y, 1 - c)
    ys = [lax.rem(y + k, ny) for k in range(1, ny)]
    zs = [lax.rem(z + k, nz) for k in range(1, nz)]
    greet([across] + [where(z, b, c) for b in ys] + [where(a, y, c) for a in zs])
    width = parts[0].shape[-1]
    rows = [pl.ds(q * width, width) for q in range(chunks)]

    def start(copies):
        for copy in copies:
            copy.start()
        return copies

    def finish_all(copies):
        for copy in copies:
            copy.wait()
    base = [0]

    def sems(count):
        base[0] += count
        return [(send.at[base[0] - count + k], recv.at[base[0] - count + k]) for k in range(count)]

    first = []
    for q in range(chunks):
        (s, r), = sems(1)
        first.append(start([remote(parts[q].at[:, :, 1 - c], rc.at[q], s, r, across)]))
    second = []
    for q in range(chunks):
        finish_all(first[q])
        for a in range(nz):
            for b in range(ny):
                total = parts[q][a, b, c] + rc[q, a, b]
                ac[q, a, b] = total
                low[q, a, b] = total.astype(BF16)
        second.append(start([remote(low.at[q, :, b], ry.at[q, k], *sem, where(z, b, c))
                             for k, (b, sem) in enumerate(zip(ys, sems(ny - 1)))]))
    third = []
    for q in range(chunks):
        finish_all(second[q])
        for a in range(nz):
            got = ac[q, a, y]
            for k in range(ny - 1):
                got = got + ry[q, k, a].astype(F32)
            ac[q, a, y] = got
            low[q, a, y] = got.astype(BF16)
        third.append(start([remote(low.at[q, a, y], rz.at[q, k], *sem, where(a, y, c))
                            for k, (a, sem) in enumerate(zip(zs, sems(nz - 1)))]))
    fourth = []
    for q in range(chunks):
        finish_all(third[q])
        got = ac[q, z, y]
        for k in range(nz - 1):
            got = got + rz[q, k].astype(F32)
        out[z, y, c, q * width:(q + 1) * width] = finish(got)
        mine = out.at[z, y, c, rows[q]]
        fourth.append(start([remote(mine, mine, *sem, where(a, y, c)) for a, sem in zip(zs, sems(nz - 1))]))
    fifth = []
    for q in range(chunks):
        finish_all(fourth[q])
        mine = out.at[:, y, c, rows[q]]
        fifth.append(start([remote(mine, mine, *sem, where(z, b, c)) for b, sem in zip(ys, sems(ny - 1))]))
    last = []
    for q in range(chunks):
        finish_all(fifth[q])
        mine = out.at[:, :, c, rows[q]]
        (s, r), = sems(1)
        last.append(start([remote(mine, mine, s, r, across)]))
    for q in range(chunks):
        finish_all(last[q])


def allsum(parts, finish, collective_id):
    peers, cols, width = parts[0].shape
    w = width * len(parts)
    dims = lattice(peers)
    nz, ny, nc = dims
    chunks = len(parts)
    copies = 2 * chunks * (1 + ny - 1 + nz - 1)
    out = pl.pallas_call(
        functools.partial(allsum_kernel, dims=dims, chunks=chunks, finish=finish),
        out_shape=jax.ShapeDtypeStruct((nz, ny, nc, w, 256), BF16),
        in_specs=[pl.BlockSpec(memory_space=pltpu.VMEM)] * chunks,
        out_specs=pl.BlockSpec(memory_space=pltpu.VMEM),
        scratch_shapes=[pltpu.VMEM((chunks, nz, ny, cols, 128), F32), pltpu.VMEM((chunks, nz, ny, cols, 128), F32),
                        pltpu.VMEM((chunks, nz, ny, cols, 128), BF16), pltpu.VMEM((chunks, ny - 1, nz, cols, 128), BF16),
                        pltpu.VMEM((chunks, nz - 1, cols, 128), BF16),
                        pltpu.SemaphoreType.DMA((copies,)), pltpu.SemaphoreType.DMA((copies,))],
        compiler_params=pltpu.CompilerParams(collective_id=collective_id, has_side_effects=True, vmem_limit_bytes=VMEM),
    )(*[part.reshape(nz, ny, nc, cols, width) for part in parts])
    return out.reshape(peers, w, 256)


def gather_kernel(x, small, wts, out, small_out, cols, send, recv, s_send, s_recv, w_send, w_recv, own_sem, *, dims, chunks):
    nz, ny, _ = dims
    me = lax.axis_index("shard")
    c, y, z = me % 2, (me // 2) % ny, me // (2 * ny)
    where = lambda a, b, d: (a * ny + b) * 2 + d
    across = where(z, y, 1 - c)
    ys = [lax.rem(y + k, ny) for k in range(1, ny)]
    ys_from = [lax.rem(y + ny - k, ny) for k in range(1, ny)]
    zs = [lax.rem(z + k, nz) for k in range(1, nz)]
    peers = nz * ny * 2
    others = [lax.rem(me + k, peers) for k in range(1, peers)]
    greet(others + [{"rep": lax.axis_index("rep") + 1 - 2 * lax.rem(lax.axis_index("rep"), 2)}])
    dl, e = wts.shape[0], wts.shape[1] // (2 * peers)
    size = x.shape[0] // chunks
    rows = [pl.ds(q * size, size) for q in range(chunks)]

    keep = pltpu.make_async_copy(small, small_out.at[z, y, c], own_sem.at[0])
    keep.start()
    whole_own = pltpu.make_async_copy(x, out.at[z, y, c], own_sem.at[1])
    whole_own.start()

    rep = lax.axis_index("rep")
    odd = lax.rem(rep, 2)
    hl = dl // 2

    def piece(half, src, dst):
        return (wts.at[pl.ds(pl.multiple_of(odd * hl, hl), hl), pl.ds(pl.multiple_of(half * peers * e + dst * e, 128), e)],
                cols.at[src, odd, :, pl.ds(half * e, e)])
    kept = [pltpu.make_async_copy(*piece(half, me, me), own_sem.at[2 + half]) for half in range(2)]
    swapped = remote(cols.at[:, odd], cols.at[:, odd], w_send.at[2 * peers - 2], w_recv.at[2 * peers - 2], {"rep": rep + 1 - 2 * odd})
    sent = [remote(*piece(half, me, p), w_send.at[2 * k + half], w_recv.at[2 * k + half], p)
            for k, p in enumerate(others) for half in range(2)]

    kinds = 2 * nz - 1
    offset = [0] + [-1 - j for j in range(nz - 1)] + [1 + j for j in range(nz - 1)]

    def valid(kind):
        return (z + offset[kind] >= 0) & (z + offset[kind] < nz)

    def sems(group, kind, q):
        at_ = (group * kinds + kind) * chunks + q
        return send.at[at_], recv.at[at_]

    def hop(kind, q, up):
        there = out.at[z + offset[kind], y, c, rows[q]]
        src = x.at[rows[q]] if kind == 0 else there
        j = -offset[kind] if up else offset[kind]
        to_kind = 1 + j if up else nz + j
        return remote(src, there, *sems(0, to_kind, q), where(z + 1 if up else z - 1, y, c))

    def can_hop(kind, up):
        return valid(kind) & ((z + 1 < nz) if up else (z >= 1))

    def over_y(kind, q, k):
        there = out.at[z + offset[kind], y, c, rows[q]]
        src = x.at[rows[q]] if kind == 0 else there
        return remote(src, there, *sems(1 + k, kind, q), where(z, ys[k], c))

    def over_core(kind, q, k):
        there = out.at[z + offset[kind], y if k == 0 else ys_from[k - 1], c, rows[q]]
        src = x.at[rows[q]] if kind == 0 and k == 0 else there
        return remote(src, there, *sems(ny + k, kind, q), across)

    def landed(kind, q, b, d, group):
        there = out.at[z + offset[kind], b, d, rows[q]]
        return remote(there, there, *sems(group, kind, q), across)

    def onward(kind, q):
        if kind == 0:
            ups = [True, False]
        elif kind < nz:
            ups = [True] if kind < nz - 1 else []
        else:
            ups = [False] if kind < kinds - 1 else []
        for up in ups:
            @pl.when(can_hop(kind, up))
            def _(up=up):
                hop(kind, q, up).start()
        for k in range(ny - 1):
            over_y(kind, q, k).start()
        over_core(kind, q, 0).start()

    tiny = []

    def tiny_start(copies):
        tiny.append(copies)
        for copy in copies:
            copy.start()

    def tiny_wait():
        for copy in tiny[-1]:
            copy.wait()

    tiny_start([remote(small, small_out.at[z, y, c], s_send.at[k], s_recv.at[k], where(a, y, c)) for k, a in enumerate(zs)])
    for q in range(chunks):
        onward(0, q)
    for copy in kept + sent:
        copy.start()
    tiny_wait()
    keep.wait()
    tiny_start([remote(small_out.at[:, y, c], small_out.at[:, y, c], s_send.at[nz - 1 + k], s_recv.at[nz - 1 + k], where(z, b, c))
                for k, b in enumerate(ys)])

    def from_y(kind, q):
        @pl.when(valid(kind))
        def _():
            for k in range(1, ny):
                landed(kind, q, ys_from[k - 1], c, k).wait_recv()
                over_core(kind, q, k).start()

    waves = [[0]] + [[1 + j, nz + j] for j in range(nz - 1)]
    for number, wave in enumerate(waves):
        for q in range(chunks):
            for kind in wave:
                if kind:
                    @pl.when(valid(kind))
                    def _(kind=kind, q=q):
                        landed(kind, q, y, c, 0).wait_recv()
                        onward(kind, q)
        if number == 2:
            for copy in kept + sent:
                copy.wait()
            swapped.start()
        if number == 1:
            tiny_wait()
            last = small_out.at[:, :, c]
            tiny_start([remote(last, last, s_send.at[nz + ny - 2], s_recv.at[nz + ny - 2], across)])
        if number:
            for q in range(chunks):
                for kind in waves[number - 1]:
                    from_y(kind, q)
    for q in range(chunks):
        for kind in waves[-1]:
            from_y(kind, q)
    tiny_wait()
    for kind in range(kinds):
        @pl.when(valid(kind))
        def _(kind=kind):
            for q in range(chunks):
                for k in range(ny):
                    landed(kind, q, y if k == 0 else ys_from[k - 1], 1 - c, ny + k).wait_recv()
                    over_core(kind, q, k).wait_send()
                for k in range(ny - 1):
                    over_y(kind, q, k).wait_send()
        for up in (True, False):
            j = -offset[kind] if up else offset[kind]
            if 0 <= j < nz - 1:
                @pl.when(can_hop(kind, up))
                def _(kind=kind, up=up):
                    for q in range(chunks):
                        hop(kind, q, up).wait_send()
    swapped.wait()
    whole_own.wait()


def gather(x, small, wts, collective_id, chunks=4):
    w, d = x.shape
    peers = lax.axis_size("shard")
    dims = lattice(peers)
    nz, ny, nc = dims
    copies = 2 * ny * (2 * nz - 1) * chunks
    dl, e = wts.shape[0], wts.shape[1] // (2 * peers)
    out, tiles, cols = pl.pallas_call(
        functools.partial(gather_kernel, dims=dims, chunks=chunks),
        out_shape=[jax.ShapeDtypeStruct((nz, ny, nc, w, d), x.dtype), jax.ShapeDtypeStruct((nz, ny, nc, 8, 128), F32),
                   jax.ShapeDtypeStruct((peers, 2, dl // 2, 2 * e), BF16)],
        in_specs=[pl.BlockSpec(memory_space=pl.ANY), pl.BlockSpec(memory_space=pltpu.VMEM), pl.BlockSpec(memory_space=pl.ANY)],
        out_specs=[pl.BlockSpec(memory_space=pl.ANY), pl.BlockSpec(memory_space=pltpu.VMEM), pl.BlockSpec(memory_space=pl.ANY)],
        scratch_shapes=[pltpu.SemaphoreType.DMA((copies,)), pltpu.SemaphoreType.DMA((copies,)),
                        pltpu.SemaphoreType.DMA((nz + ny,)), pltpu.SemaphoreType.DMA((nz + ny,)),
                        pltpu.SemaphoreType.DMA((2 * peers - 1,)), pltpu.SemaphoreType.DMA((2 * peers - 1,)),
                        pltpu.SemaphoreType.DMA((4,))],
        compiler_params=pltpu.CompilerParams(collective_id=collective_id, has_side_effects=True, vmem_limit_bytes=VMEM),
        cost_estimate=pl.CostEstimate(flops=8 * 10 ** 10, bytes_accessed=2 * peers * w * d, transcendentals=0),
    )(x, small, wts)
    return out.reshape(peers, w, d), tiles.reshape(peers, 8, 128), cols.reshape(peers * dl, 2 * e)


def meet(dims, reps):
    nz, ny, _ = dims
    me, rep = lax.axis_index("shard"), lax.axis_index("rep")
    c, y, z = me % 2, (me // 2) % ny, me // (2 * ny)
    if reps:
        greet([lax.rem(me + k, nz * ny * 2) for k in range(1, nz * ny * 2)]
              + [{"rep": lax.rem(rep + k, reps)} for k in range(1, reps)])
    else:
        greet([(z * ny + y) * 2 + 1 - c] + [(z * ny + lax.rem(y + k, ny)) * 2 + c for k in range(1, ny)]
              + [(lax.rem(z + k, nz) * ny + y) * 2 + c for k in range(1, nz)])


def scatter_steps(refs, dims, reps, lag_y=2, lag_z=4, sum_at=4, cross_at=9, first_col=0):
    part, g, out, g_out, rc, own, ry, rz, ga, gs, rg, load, send, recv, g_load, a_send, a_recv, b_send, b_recv, c_send, c_recv = refs
    nz, ny, _ = dims
    me, rep = lax.axis_index("shard"), lax.axis_index("rep")
    c, y, z = me % 2, (me // 2) % ny, me // (2 * ny)
    where = lambda a, b, d: (a * ny + b) * 2 + d
    across = where(z, y, 1 - c)
    ys = [lax.rem(y + k, ny) for k in range(1, ny)]
    zs = [lax.rem(z + k, nz) for k in range(1, nz)]
    peers = nz * ny * 2
    others = [lax.rem(me + k, peers) for k in range(1, peers)]
    far = [{"rep": lax.rem(rep + k, reps)} for k in range(1, reps)]
    slots, size = own.shape[0], own.shape[3]
    chunks = part.shape[3] // size
    rows = [pl.ds(q * size, size) for q in range(chunks)]
    per = ny + nz - 1

    def pair(q, k):
        return send.at[q * per + k], recv.at[q * per + k]

    def loads(q):
        return pltpu.make_async_copy(part.at[:, :, c, rows[q]], own.at[q % slots], load.at[q])

    def first(q):
        return remote(part.at[:, :, 1 - c, rows[q]], rc.at[:, :, rows[q]], *pair(q, 0), across)

    def second(q):
        return [remote(rc.at[:, b, rows[q]], ry.at[k, :, rows[q]], *pair(q, 1 + k), where(z, b, c))
                for k, b in enumerate(ys)]

    def third(q):
        return [remote(rc.at[a, y, rows[q]], rz.at[k, rows[q]], *pair(q, ny + k), where(a, y, c))
                for k, a in enumerate(zs)]

    groups = peers // reps
    owner_here = lax.rem(me, reps) == rep

    def shared():
        return pltpu.make_async_copy(g.at[:, rep], ga.at[rep], g_load.at[0]), [
            remote(g.at[:, lax.rem(rep + k, reps)], ga.at[rep], a_send.at[k - 1], a_recv.at[k - 1], far[k - 1])
            for k in range(1, reps)]

    def handed(k):
        p = lax.rem(me // reps + k, groups)
        return remote(gs.at[p], rg.at[me], b_send.at[k], b_recv.at[me], p * reps + rep)

    def arrived(k):
        src = lax.rem(me + k, peers)
        return remote(gs.at[0], rg.at[src], b_send.at[0], b_recv.at[src], lax.rem(me + 1, peers))

    def crossed(k):
        return remote(rg, rg, c_send.at[k - 1], c_recv, far[k - 1])

    def g_sum():
        kept, sent = shared()
        for copy in [kept] + sent:
            copy.wait()

        def add(p, _):
            total = ga[0, p].astype(F32)
            for k in range(1, reps):
                total = total + ga[k, p].astype(F32)
            gs[p] = total.astype(BF16)
            return 0
        lax.fori_loop(0, groups, add, 0)

        @pl.when(owner_here)
        def _():
            rg[me] = gs[me // reps]

        @pl.when(jnp.logical_not(owner_here))
        def _():
            handed(0).start()
        for k in range(1, groups):
            handed(k).start()

    def g_cross():
        @pl.when(owner_here)
        def _():
            for k in range(1, peers):
                arrived(k).wait_recv()
            for k in range(1, reps):
                crossed(k).start()

        @pl.when(jnp.logical_not(owner_here))
        def _():
            handed(0).wait_send()
        for k in range(1, groups):
            handed(k).wait_send()

    def g_end():
        @pl.when(owner_here)
        def _():
            for k in range(1, reps):
                crossed(k).wait_send()

        @pl.when(jnp.logical_not(owner_here))
        def _():
            crossed(1).wait_recv()
        e = rg.shape[2]
        for p in range(peers):
            g_out[:, first_col + p * e:first_col + (p + 1) * e] = rg[p].astype(F32)

    def start():
        for q in range(min(slots, chunks)):
            loads(q).start()
        for q in range(chunks):
            first(q).start()
        if g is not None:
            kept, sent = shared()
            for copy in [kept] + sent:
                copy.start()

    def over_core(q):
        loads(q).wait()
        first(q).wait()

        def add(a, _):
            i, j = a // ny, a % ny
            rc[i, j, rows[q]] = (own[q % slots, i, j].astype(F32) + rc[i, j, rows[q]].astype(F32)).astype(BF16)
            return 0
        lax.fori_loop(0, nz * ny, add, 0)
        if q + slots < chunks:
            loads(q + slots).start()
        for copy in second(q):
            copy.start()

    def over_y(q):
        for copy in second(q):
            copy.wait()

        def add(a, _):
            total = rc[a, y, rows[q]].astype(F32)
            for k in range(ny - 1):
                total = total + ry[k, a, rows[q]].astype(F32)
            rc[a, y, rows[q]] = total.astype(BF16)
            return 0
        lax.fori_loop(0, nz, add, 0)
        for copy in third(q):
            copy.start()

    def over_z(q):
        for copy in third(q):
            copy.wait()
        total = rc[z, y, rows[q]].astype(F32)
        for k in range(nz - 1):
            total = total + rz[k, rows[q]].astype(F32)
        out[rows[q]] = total

    def step(s):
        if s < chunks:
            over_core(s)
        if 0 <= s - lag_y < chunks:
            over_y(s - lag_y)
        if 0 <= s - lag_z < chunks:
            over_z(s - lag_z)
        if s == sum_at and g is not None:
            g_sum()
        if s == cross_at and g is not None:
            g_cross()

    def finish():
        if g is not None:
            g_end()
    return start, [functools.partial(step, s) for s in range(chunks + lag_z)], finish


def scatter_scratch(peers, w, d, size, g=None):
    nz, ny, nc = lattice(peers)
    chunks = w // size
    dma = pltpu.SemaphoreType.DMA
    copies = chunks * (ny + nz - 1)
    out = [pltpu.VMEM((nz, ny, w, d), BF16), pltpu.VMEM((3, nz, ny, size, d), BF16),
           pltpu.VMEM((ny - 1, nz, w, d), BF16), pltpu.VMEM((nz - 1, w, d), BF16)]
    tail = [dma((chunks,)), dma((copies,)), dma((copies,))]
    if g is None:
        return out + tail
    reps = lax.axis_size("rep")
    dl, e = g.shape[0] // peers, g.shape[1]
    return (out + [pltpu.VMEM((reps, peers // reps, dl, e), BF16), pltpu.VMEM((peers // reps, dl, e), BF16),
                   pltpu.VMEM((peers, dl, e), BF16)] + tail
            + [dma((1,)), dma((reps - 1,)), dma((reps - 1,)), dma((peers // reps,)), dma((peers,)), dma((reps - 1,)), dma])


def allsum_steps(refs, dims, finish):
    part, result, out, mine, rc, low, ry, rz, load, send, recv = refs
    nz, ny, _ = dims
    me = lax.axis_index("shard")
    c, y, z = me % 2, (me // 2) % ny, me // (2 * ny)
    where = lambda a, b, d: (a * ny + b) * 2 + d
    across = where(z, y, 1 - c)
    ys = [lax.rem(y + k, ny) for k in range(1, ny)]
    zs = [lax.rem(z + k, nz) for k in range(1, nz)]
    base = [0, 1, ny, ny + nz - 1, ny + 2 * nz - 2, 2 * ny + 2 * nz - 3]

    def sem(stage, k):
        return send.at[base[stage] + k], recv.at[base[stage] + k]

    def copies(stage):
        if stage == 0:
            return [remote(part.at[:, :, 1 - c], rc, *sem(0, 0), across)]
        if stage == 1:
            return [remote(low.at[:, b], ry.at[k], *sem(1, k), where(z, b, c)) for k, b in enumerate(ys)]
        if stage == 2:
            return [remote(low.at[a, y], rz.at[k], *sem(2, k), where(a, y, c)) for k, a in enumerate(zs)]
        if stage == 3:
            held, targets = out.at[z, y, c], [where(a, y, c) for a in zs]
        elif stage == 4:
            held, targets = out.at[:, y, c], [where(z, b, c) for b in ys]
        else:
            held, targets = out.at[:, :, c], [across]
        return [remote(held, held, *sem(stage, k), target) for k, target in enumerate(targets)]

    def own():
        return pltpu.make_async_copy(part.at[:, :, c], mine, load.at[0])

    def start():
        own().start()
        for copy in copies(0):
            copy.start()

    def step(s):
        if s == 0:
            own().wait()
        for copy in copies(s):
            copy.wait()
        if s == 0:
            def add(a, _):
                i, j = a // ny, a % ny
                total = mine[i, j] + rc[i, j]
                mine[i, j] = total
                low[i, j] = total.astype(BF16)
                return 0
            lax.fori_loop(0, nz * ny, add, 0)
        if s == 1:
            for a in range(nz):
                total = mine[a, y]
                for k in range(ny - 1):
                    total = total + ry[k, a].astype(F32)
                mine[a, y] = total
                low[a, y] = total.astype(BF16)
        if s == 2:
            total = mine[z, y]
            for k in range(nz - 1):
                total = total + rz[k].astype(F32)
            out[z, y, c] = finish(total)
        if s < 5:
            for copy in copies(s + 1):
                copy.start()

    def end():
        result[...] = out[...]
    return start, [functools.partial(step, s) for s in range(6)], end


def allsum_scratch(peers, cols, width):
    nz, ny, nc = lattice(peers)
    dma = pltpu.SemaphoreType.DMA
    count = 2 * (1 + ny - 1 + nz - 1)
    return [pltpu.VMEM((nz, ny, nc, width, 256), BF16), pltpu.VMEM((nz, ny, cols, width), F32),
            pltpu.VMEM((nz, ny, cols, width), F32),
            pltpu.VMEM((nz, ny, cols, width), BF16), pltpu.VMEM((ny - 1, nz, cols, width), BF16),
            pltpu.VMEM((nz - 1, cols, width), BF16), dma((1,)), dma((count,)), dma((count,))]


def beside(b, grid, dims, reps, transfers):
    @pl.when(b == 0)
    def _():
        meet(dims, reps)
        for start, _, _, _ in transfers:
            start()
    for _, steps, _, when in transfers:
        for s, step in enumerate(steps):
            @pl.when(b == (when[s] if when else (s * (grid - 1)) // len(steps) + 1))
            def _(step=step):
                step()

    @pl.when(b == grid - 1)
    def _():
        for _, _, finish, _ in transfers:
            finish()


PACED = [1, 1, 1, 1, 2, 2, 2, 2, 3, 5, 6, 8, 9, 11, 13, 14, 15, 15]


def fill(low_ref, bcs_scr, bc_scr, n):
    bcs_scr[...] = low_ref[0, :, 128:].astype(F32)
    lane = lax.broadcasted_iota(jnp.int32, (n, 128), 1)
    sub = lax.broadcasted_iota(jnp.int32, (n, 128), 0)
    mask = (lane % n) == sub
    r = lax.broadcasted_iota(jnp.int32, (128, 256), 0)
    c = lax.broadcasted_iota(jnp.int32, (128, 256), 1)
    ones = jnp.where((r >= 3 * n) == (c >= 128), 1.0, 0.0).astype(BF16)
    group = 128

    def body(g, _):
        rows = [jnp.where(mask, bcs_scr[pl.ds(g * group + j, 1), :], 0.0).astype(BF16) for j in range(group)]
        bc_scr[at(g * (group * n), group * n, 128), :] = mm(jnp.concatenate(rows, axis=0), ones)
        return 0
    lax.fori_loop(0, bcs_scr.shape[0] // group, body, 0)


def fold_rows(vals, sub):
    for k in (1, 2, 4):
        mask = (sub & k) == 0
        vals = [jnp.where(mask, a, b) + pltpu.roll(jnp.where(mask, b, a), 8 - k, 0)
                for a, b in zip(vals[::2], vals[1::2])]
    return vals[0]


def ahead(*refs, m, n, e, dims, sending):
    (low_ref, xz_ref, xc_ref, mask_ref, dy_ref, wo_ref, wdt_ref, dtb_ref, a2_ref) = refs[:9]
    refs = refs[9:]
    if sending:
        adding, refs = refs[0], refs[1:]
    cks_ref, ckp_ref, end_ref, dg_ref = refs[:4]
    refs = refs[4:]
    if sending:
        added, refs = refs[0], refs[1:]
    s_scr, p_scr, f_scr, sd_scr, dx_scr, dy_scr, bcs_scr, bc_scr = refs[:8]
    if sending:
        beside(pl.program_id(0), dims[0] * dims[1] * dims[2], dims, 0,
               [allsum_steps((adding, added) + refs[8:], dims, functools.partial(spread_plain, n=n)) + ([1, 4, 7, 10, 13, 15],)])
    b = pl.program_id(0)
    @pl.when(b == 0)
    def _():
        s_scr[...] = jnp.zeros_like(s_scr)
        p_scr[...] = jnp.ones_like(p_scr)
        f_scr[...] = jnp.zeros_like(f_scr)
    cks_ref[0] = s_scr[...]
    ckp_ref[0] = p_scr[...]
    fill(low_ref, bcs_scr, bc_scr, n)
    step = softplus(mm(low_ref[0, :, :128], wdt_ref[...]) + dtb_ref[...])
    sd_scr[...] = jnp.where(mask_ref[0, :, 0:1] > 0.0, step, 1e30)
    dx_scr[...] = step * xc_ref[0].astype(F32)
    dg = nt(dy_ref[0], wo_ref[...])
    dg_ref[0] = dg
    z = xz_ref[0, :, e:].astype(F32)
    dy_scr[...] = dg * (z * jax.nn.sigmoid(z))
    a2 = a2_ref[...]
    rows = sd_scr.shape[0] // m
    un = 16

    def group(g, carry):
        s, p, f = [list(c) for c in carry]
        for j in range(un):
            for i in range(m):
                t = i * rows + g * un + j
                bc = bc_scr[at(t * n, n, n), :]
                bb, cc = wide(bc[:, :128], e), wide(bc[:, 128:], e)
                a = jnp.exp2(sd_scr[pl.ds(t, 1), :] * a2)
                s[i] = a * s[i] + bb * dx_scr[pl.ds(t, 1), :]
                p[i] = p[i] * a
                f[i] = f[i] + p[i] * (cc * dy_scr[pl.ds(t, 1), :])
        return tuple(s), tuple(p), tuple(f)
    done = lax.fori_loop(0, rows // un, group,
                         tuple(tuple(scr[i] for i in range(m)) for scr in (s_scr, p_scr, f_scr)))
    for scr, vals in zip((s_scr, p_scr, f_scr), done):
        for i in range(m):
            scr[i] = vals[i]

    @pl.when(b == pl.num_programs(0) - 1)
    def _():
        end_ref[0] = s_scr[...]
        end_ref[1] = p_scr[...]
        end_ref[2] = f_scr[...]


def behind(*refs, n, e, dims, reps, sending):
    (low_ref, xz_ref, xc_ref, mask_ref, dg_ref, cks_ref, ckp_ref,
     wo_ref, wdt_ref, dtb_ref, a2_ref, skip_ref, hin_ref, qin_ref) = refs[:14]
    refs = refs[14:]
    if sending:
        before, refs = refs[0], refs[1:]
    out_ref, dz_ref, dxc_ref, part_ref, gated_ref, gdt_ref, ga_ref, vec_ref = refs[:8]
    refs = refs[8:]
    if sending:
        summed, refs = refs[0], refs[1:]
    (h_scr, a_scr, q_scr, bcs_scr, bc_scr, pre_scr, st_scr, sd_scr, dx_scr, dy_scr, y_scr, da_scr, gb_scr) = refs[:13]
    b = pl.program_id(0)
    if sending:
        rc, own, ry, rz, load, send, recv = refs[13:20]
        beside(b, dims[0] * dims[1] * dims[2], dims, 0, [
            scatter_steps((before, None, summed, None, rc, own, ry, rz, None, None, None, load, send, recv) + (None,) * 7,
                          dims, reps, 8, 10) + (PACED,)])
    m = 1
    @pl.when(b == 0)
    def _():
        q_scr[...] = qin_ref[...]
        for ref in (gdt_ref, ga_ref, vec_ref):
            ref[...] = jnp.zeros_like(ref)
    fill(low_ref, bcs_scr, bc_scr, n)
    pre = mm(low_ref[0, :, :128], wdt_ref[...]) + dtb_ref[...]
    pre_scr[...] = pre
    step = softplus(pre)
    st_scr[...] = step
    sd_scr[...] = jnp.where(mask_ref[0, :, 0:1] > 0.0, step, 1e30)
    dx_scr[...] = step * xc_ref[0].astype(F32)
    z = xz_ref[0, :, e:].astype(F32)
    dy_scr[...] = dg_ref[0] * (z * jax.nn.sigmoid(z))
    a2 = a2_ref[...]
    sub = lax.broadcasted_iota(jnp.int32, (8, e), 0)
    rows = sd_scr.shape[0] // m
    lanes = lax.broadcasted_iota(jnp.int32, (n, rows), 1)
    un = 32
    for i in range(m):
        r0 = i * rows
        h0 = cks_ref[0, i] + ckp_ref[0, i] * hin_ref[i]
        h_scr[pl.ds(0, n), :] = h0

        def fwd(g, h, r0=r0):
            ys = []
            for j in range(un):
                t = g * un + j
                bc = bc_scr[at((r0 + t) * n, n, n), :]
                bb, cc = wide(bc[:, :128], e), wide(bc[:, 128:], e)
                a = jnp.exp2(sd_scr[pl.ds(r0 + t, 1), :] * a2)
                h = a * h + bb * dx_scr[pl.ds(r0 + t, 1), :]
                a_scr[at(t * n, n, n), :] = a
                h_scr[at(t * n + n, n, n), :] = h
                cy = cc * h
                ys.append(cy[:8] + cy[8:])
                if len(ys) == 8:
                    y_scr[at(r0 + t - 7, 8), :] = fold_rows(ys, sub)
                    ys = []
            return h
        lax.fori_loop(0, rows // un, fwd, h0)

        def bwd(g, carry, r0=r0):
            q, ga, hn, db, dc = carry
            das, gbs = [], []
            for j in range(un):
                t = rows - 1 - (g * un + j)
                bc = bc_scr[at((r0 + t) * n, n, n), :]
                bb, cc = wide(bc[:, :128], e), wide(bc[:, 128:], e)
                a = a_scr[at(t * n, n, n), :]
                hp = h_scr[at(t * n, n, n), :]
                dyr = dy_scr[pl.ds(r0 + t, 1), :]
                gt = cc * dyr + q
                q = a * gt
                da = q * hp
                ga = ga + da * st_scr[pl.ds(r0 + t, 1), :]
                d_a = da * a2
                g_b = gt * bb
                das.append(d_a[:8] + d_a[8:])
                gbs.append(g_b[:8] + g_b[8:])
                pb = gt * dx_scr[pl.ds(r0 + t, 1), :]
                pc = dyr * hn
                pb = sum(pb[:, k:k + 128] for k in range(0, e, 128))
                pc = sum(pc[:, k:k + 128] for k in range(0, e, 128))
                db = jnp.where(lanes == t, jnp.sum(pb, axis=1, keepdims=True), db)
                dc = jnp.where(lanes == t, jnp.sum(pc, axis=1, keepdims=True), dc)
                hn = hp
                if len(das) == 8:
                    da_scr[at(r0 + t, 8), :] = fold_rows(das[::-1], sub)
                    gb_scr[at(r0 + t, 8), :] = fold_rows(gbs[::-1], sub)
                    das, gbs = [], []
            return q, ga, hn, db, dc
        zero = jnp.zeros((n, rows), F32)
        q, ga, _, db, dc = lax.fori_loop(
            0, rows // un, bwd, (q_scr[i], ga_ref[...], h_scr[pl.ds(rows * n, n), :], zero, zero))
        q_scr[i] = q
        ga_ref[...] = ga
        part_ref[0, 128:128 + n, r0:r0 + rows] = db
        part_ref[0, 128 + n:128 + 2 * n, r0:r0 + rows] = dc

    z = xz_ref[0, :, e:].astype(F32)
    sz = jax.nn.sigmoid(z)
    xc = xc_ref[0].astype(F32)
    skip = skip_ref[...]
    y = y_scr[...] + skip * xc
    gated = (y * (z * sz)).astype(BF16)
    out_ref[0] = mm(gated, wo_ref[...]).astype(BF16)
    gated_ref[0] = gated
    dz = (dg_ref[0] * y * (sz * (1.0 + z * (1.0 - sz)))).astype(BF16)
    dz_ref[0] = dz
    gb = gb_scr[...]
    dy_y = dy_scr[...]
    dxc_ref[0] = dy_y * skip + st_scr[...] * gb
    d_pre = (da_scr[...] * LN2 + xc * gb) * jax.nn.sigmoid(pre_scr[...])
    d_low = d_pre.astype(BF16)
    gdt_ref[...] += tn(low_ref[0, :, :128], d_low)
    part_ref[0, :128, :] = nt(wdt_ref[...], d_low)
    vec_ref[0:1] += jnp.sum(d_pre, axis=0, keepdims=True)
    vec_ref[1:2] += jnp.sum(dy_y * xc, axis=0, keepdims=True)


def back(*refs, e, n, dims, reps, role):
    (xz_ref, prev_ref, edge_ref, mask_ref, ddbc_ref, nu_ref, next_ref, w_ref, xpt_ref, cw_ref, cb_ref, dxc_ref, dz_ref,
     before, extra) = refs[:15]
    b = pl.program_id(0)
    peers = dims[0] * dims[1] * dims[2]
    if role == "sum":
        nu_all, dy0, dy1, dz0, dz1, gated0, gated1 = refs[15:22]
        v_ref, gx, vec_ref, summed, prod_z, prod_o, done, carry, acc_z, acc_o = refs[22:32]
        refs = refs[32:]
        rc, own, ry, rz, load, send, recv = refs[:7]
        beside(b, peers, dims, 0, [
            allsum_steps((extra, done) + refs[7:], dims, functools.partial(spread_plain, n=n)) + (None,),
            scatter_steps((before, None, summed, None, rc, own, ry, rz, None, None, None, load, send, recv) + (None,) * 7,
                          dims, reps) + (None,)])
    else:
        gx_before, go_part, v_out, vec_ref, summed, summed_own, g_done, go_done = refs[15:23]
        carry, gx, gx_low, v_buf, go_all, v_sem, gx_sem, go_send, go_recv = refs[23:32]
        refs = refs[32:]
        half = len(refs) // 2
        earlier = scatter_steps((before, extra, summed, g_done) + refs[:half], dims, reps, 8, 10, 8, 15, peers * e)
        latest = scatter_steps((v_out, gx_low, summed_own, g_done) + refs[half:], dims, reps, 8, 10, 4, 12)

        @pl.when(b == 0)
        def _():
            meet(dims, reps)
            earlier[0]()
            copy = pltpu.make_async_copy(gx_before, gx, gx_sem.at[0])
            copy.start()
            copy.wait()
        early = [1, 1, 1, 1, 2, 2, 2, 2, 7, 11, 14]
        for k, when in enumerate(early):
            @pl.when(b == when)
            def _(k=k):
                earlier[1][k]()

    @pl.when(b == 0)
    def _():
        carry[...] = next_ref[...]
        vec_ref[...] = jnp.zeros_like(vec_ref)
        if role == "sum":
            acc_z[...] = jnp.zeros_like(acc_z)
            acc_o[...] = jnp.zeros_like(acc_o)
            gx[...] = jnp.zeros_like(gx)
    rows = xz_ref.shape[1]
    cw, cb = cw_ref[...], cb_ref[...]
    x = xz_ref[0, :, :e].astype(F32)
    before_x = prev_ref[0, rows - 2 * EDGE:, :e].astype(F32)[EDGE:]
    before_x = jnp.where(b == peers - 1, edge_ref[...], before_x)
    lag = lags(jnp.concatenate([before_x, x], axis=0), rows)
    same = mask_ref[0]
    dconv = (dxc_ref[0] + mm(ddbc_ref[0], xpt_ref[...])) * dsilu(convolve(lag, same, cw, cb))
    vec_ref[4:5] += jnp.sum(dconv, axis=0, keepdims=True)
    vec_ref[3:4] += jnp.sum(dconv * x, axis=0, keepdims=True)
    dx = cw[3:4] * dconv
    for k in range(1, 4):
        masked = dconv * same[:, k - 1:k]
        vec_ref[3 - k:4 - k] += jnp.sum(masked * lag[k], axis=0, keepdims=True)
        sent = cw[3 - k:4 - k] * masked
        dx = dx + jnp.concatenate([sent, carry[k - 1]], axis=0)[k:k + rows]
        carry[k - 1] = sent[:EDGE]
    dx = dx.astype(BF16)
    v = nt(jnp.concatenate([dx, dz_ref[0]], axis=1), w_ref[...]).astype(BF16)
    gx[...] += tn(nu_ref[0], dx)
    if role == "sum":
        v_ref[0] = v
        acc_z[...] += tn(nu_all[0], jnp.concatenate([dz0[0], dz1[0]], axis=0))
        acc_o[...] += tn(jnp.concatenate([gated0[0], gated1[0]], axis=0), jnp.concatenate([dy0[0], dy1[0]], axis=0))

        @pl.when(b == peers - 1)
        def _():
            prod_z[...] = acc_z[...].astype(BF16)
            prod_o[...] = acc_o[...].astype(BF16)
        return

    slot, at_ = b % 2, peers - 1 - b

    def write(slot):
        return pltpu.make_async_copy(v_buf.at[slot], v_out.at[at_ // (2 * dims[1]), (at_ // 2) % dims[1], at_ % 2], v_sem.at[slot])

    @pl.when(b >= 2)
    def _():
        write(slot).wait()
    v_buf[slot] = v
    write(slot).start()

    @pl.when(b == peers - 1)
    def _():
        write(0).wait()
        write(1).wait()
        for p in range(peers // reps):
            for k in range(reps):
                first = (p * reps + k) * gx_low.shape[2]
                gx_low[p, k] = gx[first:first + gx_low.shape[2]].astype(BF16)
        latest[0]()
        rep = lax.axis_index("rep")
        kept = pltpu.make_async_copy(go_part, go_all.at[rep], gx_sem.at[0])
        swaps = [remote(go_part, go_all.at[rep], go_send.at[k - 1], go_recv.at[k - 1], {"rep": lax.rem(rep + k, reps)})
                 for k in range(1, reps)]
        for k, step in enumerate(latest[1]):
            if k == 6:
                for copy in [kept] + swaps:
                    copy.start()
            if len(early) + k < len(earlier[1]):
                earlier[1][len(early) + k]()
            step()
        earlier[2]()
        for copy in [kept] + swaps:
            copy.wait()
        total = go_all[0].astype(F32)
        for k in range(1, reps):
            total = total + go_all[k].astype(F32)
        go_done[...] = total
        latest[2]()


def dsilu(v):
    s = jax.nn.sigmoid(v)
    return s * (1.0 + v * (1.0 - s))


def shift_rep(value, steps):
    count = lax.axis_size("rep")
    first, last = max(0, -steps), min(count, count - steps)
    return lax.ppermute(value, "rep", [(i, i + steps) for i in range(first, last)])


def sum_rep(value):
    if lax.axis_size("rep") != 2:
        return lax.psum(value.astype(F32), "rep")
    low = value.astype(BF16)
    other = lax.ppermute(low, "rep", [(0, 1), (1, 0)])
    return low.astype(F32) + other.astype(F32)


def on_device(hidden_in, segment_ids, out_grad, norm_gain, in_proj, conv_weight, conv_bias, x_proj,
              dt_weight, dt_bias, a_log, d_skip, out_proj):
    peers, reps = lax.axis_size("shard"), lax.axis_size("rep")
    rep = lax.axis_index("rep")
    m, tl, d = hidden_in.shape
    t, w = tl * peers, m * tl
    dl = in_proj.shape[0]
    e = x_proj.shape[0]
    n, rank, taps = a_log.shape[0], dt_weight.shape[0], conv_weight.shape[0]
    w32 = lambda v: v.astype(F32)
    shp = jax.ShapeDtypeStruct
    rising = lambda i: i
    falling = lambda i: peers - 1 - i

    span = peers * reps
    before = lax.ppermute(segment_ids[:, tl - taps + 1:], ("rep", "shard"), [(k, k + 1) for k in range(span - 1)])
    before = jnp.where((rep > 0) | (lax.axis_index("shard") > 0), before, -1)
    ext = jnp.concatenate([before, segment_ids], axis=1)
    same = [w32(ext[:, taps - 1 - k:taps - 1 - k + tl] == segment_ids) for k in range(1, taps)]
    same = jnp.stack(same, axis=1).reshape(m * (taps - 1), tl)
    own = jnp.concatenate([same, jnp.pad(w32(norm_gain)[None], ((0, 0), (0, tl - dl))),
                           jnp.zeros((7 - m * (taps - 1), tl), F32)], axis=0)
    hid_all, tiles, w_cols = gather(hidden_in.reshape(w, d), own, in_proj, 4)
    gain = tiles[:, m * (taps - 1), :dl].reshape(1, d)
    later, hid_all = lax.optimization_barrier((out_grad, hid_all))
    dy_rows = [lax.all_gather(later[i], "shard") for i in range(m)]
    u = w32(hidden_in)
    r = lax.rsqrt(jnp.mean(u * u, axis=2, keepdims=True) + 1e-5)

    mask = tiles[:, :m * (taps - 1)].reshape(peers, m, taps - 1, tl).transpose(0, 1, 3, 2).reshape(peers, w, taps - 1)
    mask = jnp.pad(mask, ((0, 0), (0, 0), (0, 9 - taps)))
    halo = shift_rep(hid_all[peers - 1].reshape(m, tl, d)[:, tl - EDGE:].reshape(m * EDGE, d), 1)

    cw, cb = w32(conv_weight), w32(conv_bias)[None]
    ins = [hid_all, w_cols, halo, mask, cw, cb, x_proj.T, gain]
    outs = [shp((peers, w, 2 * e), BF16), shp((peers, w, e), BF16), shp((peers, w, d), BF16), shp((m * EDGE, e), BF16)]
    outs += [shp((peers, rank + 2 * n, tl), F32)] * m
    xz, xc, nu_all, edge, *parts = call(
        functools.partial(front, m=m, e=e), (peers,),
        [block(hid_all, rising)] + [whole(a) for a in ins[1:3]] + [block(mask, rising)] + [whole(a) for a in ins[4:]],
        [block(a, rising) for a in outs[:3]] + [whole(outs[3])] + [block(a, rising) for a in outs[4:]], outs,
        [pltpu.VMEM((m * EDGE, e), F32)], ins, flops=2 * peers * w * d * 2 * e)

    low = allsum(parts, functools.partial(spread_low, n=n), 0)
    a_mat = -jnp.exp(w32(a_log))
    a2 = a_mat * LOG2E
    dtb, skip = w32(dt_bias)[None], w32(d_skip)[None]

    dims = lattice(peers)
    anywhere = pl.BlockSpec(memory_space=pl.ANY)
    rows_done, ddbcs = [], []
    for i in range(m):
        def row(a, order, i=i):
            shape = (1, tl) if a.ndim == 3 else (1, 1, a.shape[2])
            return pl.BlockSpec(shape + a.shape[len(shape):], lambda b, r=a.ndim: (order(b), i) + (0,) * (r - 2))

        if i:
            low, _ = lax.optimization_barrier((low, rows_done[i - 1][7]))
        ins = [low, xz, xc, mask, dy_rows[i], out_proj, dt_weight, dtb, a2]
        outs = [shp((peers, 1, n, e), F32)] * 2 + [shp((3, 1, n, e), F32), shp((peers, tl, e), F32)]
        specs = [row(a, rising) for a in ins[:4]] + [block(ins[4], rising)] + [whole(a) for a in ins[5:]]
        out_specs = [block(outs[0], rising), block(outs[1], rising), whole(outs[2]), block(outs[3], rising)]
        scratch = ([pltpu.VMEM((1, n, e), F32)] * 3 + [pltpu.VMEM((tl, e), F32)] * 3
                   + [pltpu.VMEM((tl, 128), F32), pltpu.VMEM((tl * n, 256), F32)])
        params = {}
        if i:
            ins.append(rows_done[i - 1][3].reshape(dims + (rank + 2 * n, tl)))
            specs.append(anywhere)
            outs.append(shp(dims + (tl, 256), BF16))
            out_specs.append(whole(outs[-1]))
            scratch += allsum_scratch(peers, rank + 2 * n, tl)
            params = dict(collective_id=11 + i, has_side_effects=True)
        cks, ckp, end, dg, *sums = call(
            functools.partial(ahead, m=1, n=n, e=e, dims=dims, sending=bool(i)), (peers,), specs, out_specs, outs, scratch,
            ins, flops=20 * 10 ** 9, **params)
        ddbcs += [a.reshape(peers, tl, 256) for a in sums]
        ends = lax.all_gather(end, "rep")
        h_in = jnp.zeros((1, n, e), F32)
        q_in = jnp.zeros((1, n, e), F32)
        for k in range(reps - 1):
            o = reps - 1 - k
            h_in = jnp.where(k < rep, ends[k, 1] * h_in + ends[k, 0], h_in)
            q_in = jnp.where(o > rep, ends[o, 1] * q_in + ends[o, 2], q_in)
        ins = [low, xz, xc, mask, dg, cks, ckp, out_proj, dt_weight, dtb, a2, skip, h_in, q_in]
        specs = [row(a, falling) for a in ins[:4]] + [block(a, falling) for a in ins[4:7]] + [whole(a) for a in ins[7:]]
        outs = [shp((peers, tl, d), BF16), shp((peers, tl, e), BF16), shp((peers, tl, e), F32),
                shp((peers, rank + 2 * n, tl), F32), shp((peers, tl, e), BF16), shp((rank, e), F32), shp((n, e), F32), shp((8, e), F32)]
        out_specs = [block(a, falling) for a in outs[:5]] + [whole(a) for a in outs[5:]]
        scratch = [pltpu.VMEM((tl * n + n, e), F32), pltpu.VMEM((tl * n, e), F32), pltpu.VMEM((1, n, e), F32),
                   pltpu.VMEM((tl, 128), F32), pltpu.VMEM((tl * n, 256), F32)] + [pltpu.VMEM((tl, e), F32)] * 8
        params = {}
        if i:
            ins.append(rows_done[i - 1][0].reshape(dims + (tl, d)))
            specs.append(anywhere)
            outs.append(shp((tl, d), F32))
            out_specs.append(whole(outs[-1]))
            scratch += scatter_scratch(peers, tl, d, 16)
            params = dict(collective_id=5 + i, has_side_effects=True)
        rows_done.append(call(
            functools.partial(behind, n=n, e=e, dims=dims, reps=reps, sending=bool(i)), (peers,), specs, out_specs, outs,
            scratch, ins, flops=50 * 10 ** 9, **params))
    g_dt, g_a, vec = (sum(done[k] for done in rows_done) for k in range(5, 8))

    xpt = jnp.pad(x_proj.T, ((0, 256 - x_proj.shape[1]), (0, 0)))
    xz_first = xz[0].reshape(m, tl, 2 * e)[:, :EDGE, :e]
    edges = w32(edge).reshape(m, EDGE, e)
    out_sums = [done[8] for done in rows_done[1:]]
    backs = []
    for i in range(m):
        ext8 = jnp.concatenate([edges[i], w32(xz_first[i])], axis=0)
        same8 = mask[0, i * tl:i * tl + EDGE]
        conv8 = cb + cw[3] * ext8[EDGE:]
        for k in range(1, taps):
            conv8 = conv8 + cw[3 - k] * ext8[EDGE - k:2 * EDGE - k] * same8[:, k - 1:k]
        d8 = (rows_done[i][2][0, :EDGE] + mm(ddbcs[i][0, :EDGE], xpt)) * dsilu(conv8)
        follow = shift_rep(jnp.stack([cw[3 - k] * d8 * same8[:, k - 1:k] for k in range(1, taps)]), -1)

        def row(a, order, i=i):
            return pl.BlockSpec((1, tl) + a.shape[2:], lambda b: (order(b), i, 0))
        earlier = lambda b: jnp.maximum(peers - 2 - b, 0)
        ins = [xz, xz, edges[i], mask, ddbcs[i], nu_all, follow, w_cols, xpt, cw, cb, rows_done[i][2], rows_done[i][1]]
        specs = [row(xz, falling), row(xz, earlier), whole(ins[2]), row(mask, falling), block(ins[4], falling), row(nu_all, falling)]
        specs += [whole(a) for a in ins[6:11]] + [block(a, falling) for a in ins[11:13]] + [anywhere] * 2
        carry = pltpu.VMEM((taps - 1, EDGE, e), F32)
        if i < m - 1:
            ins += [rows_done[i + 1][0].reshape(dims + (tl, d)), rows_done[i + 1][3].reshape(dims + (rank + 2 * n, tl))]
            more = [nu_all] + dy_rows + [done[1] for done in rows_done] + [done[4] for done in rows_done]
            ins += more
            specs += [block(a, falling) for a in more]
            outs = [shp((peers, tl, d), BF16), shp((d, e), F32), shp((8, e), F32), shp((tl, d), F32), shp((d, e), BF16),
                    shp((e, d), BF16), shp(dims + (tl, 256), BF16)]
            out_specs = [block(outs[0], falling)] + [whole(a) for a in outs[1:]]
            scratch = [carry, pltpu.VMEM((d, e), F32), pltpu.VMEM((e, d), F32)]
            scratch += scatter_scratch(peers, tl, d, 16) + allsum_scratch(peers, rank + 2 * n, tl)
        else:
            g_z = backs[i - 1][4]
            ins += [backs[i - 1][0].reshape(dims + (tl, d)), g_z.reshape(peers // reps, reps, dl, e), backs[i - 1][1], backs[i - 1][5]]
            specs += [anywhere] * 2
            outs = [shp(dims + (tl, d), BF16), shp((8, e), F32), shp((tl, d), F32), shp((tl, d), F32), shp((dl, 2 * peers * e), F32),
                    shp((e, d), F32)]
            out_specs = [anywhere] + [whole(a) for a in outs[1:]]
            scratch = [carry, pltpu.VMEM((d, e), F32), pltpu.VMEM((peers // reps, reps, dl, e), BF16), pltpu.VMEM((2, tl, d), BF16),
                       pltpu.VMEM((reps, e, d), BF16), pltpu.SemaphoreType.DMA((2,)), pltpu.SemaphoreType.DMA((1,)),
                       pltpu.SemaphoreType.DMA((reps - 1,)), pltpu.SemaphoreType.DMA((reps - 1,))] + scatter_scratch(peers, tl, d, 16, g_z) * 2
        backs.append(call(
            functools.partial(back, e=e, n=n, dims=dims, reps=reps, role="sum" if i < m - 1 else "owner"), (peers,), specs,
            out_specs, outs, scratch, ins, flops=peers * w * d * 3 * e, collective_id=8 + i, has_side_effects=True))
        if i < m - 1:
            out_sums.append(backs[i][3])
            ddbcs.append(backs[i][6].reshape(peers, tl, 256))
    vec2 = backs[0][2] + backs[1][1]
    layer_out = (u + jnp.stack(out_sums)).astype(BF16)

    v = jnp.stack([backs[1][2], backs[1][3]]) * gain
    in_grad = w32(out_grad) + r * v - u * (r * r * r) * jnp.mean(v * u, axis=2, keepdims=True)

    grad_in_proj = backs[1][4]
    grad_gain = jnp.sum(grad_in_proj * w32(in_proj), axis=1) / w32(norm_gain)

    g_xproj = sum(tn(xc.reshape(peers, m, tl, e)[:, i].reshape(peers * tl, e), ddbcs[i].reshape(peers * tl, 256)) for i in range(m))
    small = jnp.concatenate([vec, g_a * a_mat, g_dt, g_xproj.T], axis=0)
    small, vec2 = sum_rep(small), sum_rep(vec2)
    vec, g_a, g_dt, g_xp = small[:8], small[8:8 + n], small[8 + n:8 + n + rank], small[8 + n + rank:]
    return (layer_out, in_grad, grad_gain, grad_in_proj, vec2[:taps], vec2[taps], g_xp[:rank + 2 * n].T, g_dt, vec[0],
            g_a, vec[1], backs[1][5])


def solution(mesh):
    tok, ids = P(None, ("rep", "shard"), None), P(None, ("rep", "shard"))
    row, col, one = P("shard", None), P(None, "shard"), P("shard")
    return jax.shard_map(
        on_device,
        mesh=mesh,
        in_specs=(tok, ids, tok, one, row, col, one, row, col, one, col, one, row),
        out_specs=(tok, tok, one, row, col, one, row, col, one, col, one, row),
        check_vma=False,
    )
```
